32 devices in a mesh: dp: 16 (over z, y, core), tensor: 2 (over x).
Axes of the slice: x: 2, y: 2, z: 4, core: 2. Of those that a mesh axis runs over, the one named last changes fastest.
Arguments:
- tokens: bfloat16 [8192, 768], P(('dp', 'tensor')), may hold values from -6 to 6
- cotangent: bfloat16 [8192, 768], P(('dp', 'tensor')), may hold values from -6 to 6
- lengths: int32 [16, 3], P('dp'), may hold values from 0 to 512, as said below
- w_qkv: float32 [3, 768, 768], P(None, 'dp', 'tensor'), may hold values from -0.21875 to 0.21875
- m_qkv: float32 [3, 768, 768], P(None, 'dp', 'tensor'), may hold values from -12 to 12
- v_qkv: float32 [3, 768, 768], P(None, 'dp', 'tensor'), may hold values from 0.16384 to 1.31072
- w_out: float32 [768, 768], P('tensor', 'dp'), may hold values from -2.5 to 2.5
- m_out: float32 [768, 768], P('tensor', 'dp'), may hold values from -4 to 4
- v_out: float32 [768, 768], P('tensor', 'dp'), may hold values from 0.01024 to 0.08192
- w_in: float32 [768, 3072], P('dp', 'tensor'), may hold values from -0.21875 to 0.21875
- m_in: float32 [768, 3072], P('dp', 'tensor'), may hold values from -32 to 32
- v_in: float32 [768, 3072], P('dp', 'tensor'), may hold values from 1.024 to 8.192
- w_back: float32 [3072, 768], P('tensor', 'dp'), may hold values from -0.109375 to 0.109375
- m_back: float32 [3072, 768], P('tensor', 'dp'), may hold values from -20 to 20
- v_back: float32 [3072, 768], P('tensor', 'dp'), may hold values from 0.49152 to 4.096
- vectors: float32 [12, 768], P(None, ('dp', 'tensor'))
- m_vectors: float32 [12, 768], P(None, ('dp', 'tensor')), may hold values from -40 to 40
- v_vectors: float32 [12, 768], P(None, ('dp', 'tensor')), may hold values from 2.048 to 16.384
Outputs:
- mixed: bfloat16 [8192, 768], P(('dp', 'tensor'))
- input_grad: float32 [8192, 768], P(('dp', 'tensor'))
- new_qkv: float32 [3, 768, 768], P(None, 'dp', 'tensor')
- moment_qkv: float32 [3, 768, 768], P(None, 'dp', 'tensor')
- square_qkv: float32 [3, 768, 768], P(None, 'dp', 'tensor')
- new_out: float32 [768, 768], P('tensor', 'dp')
- moment_out: float32 [768, 768], P('tensor', 'dp')
- square_out: float32 [768, 768], P('tensor', 'dp')
- new_in: float32 [768, 3072], P('dp', 'tensor')
- moment_in: float32 [768, 3072], P('dp', 'tensor')
- square_in: float32 [768, 3072], P('dp', 'tensor')
- new_back: float32 [3072, 768], P('tensor', 'dp')
- moment_back: float32 [3072, 768], P('tensor', 'dp')
- square_back: float32 [3072, 768], P('tensor', 'dp')
- new_vectors: float32 [12, 768], P(None, ('dp', 'tensor'))
- moment_vectors: float32 [12, 768], P(None, ('dp', 'tensor'))
- square_vectors: float32 [12, 768], P(None, ('dp', 'tensor'))
The draws below stay inside these ranges and needn't reach their ends.
Inputs may be any that keep to these rules, and one draw needn't show every extreme that they name: In each group the lengths add up to more than 256 and at most 512; the first ends before slot 256 and the second after it; in one group a single sequence fills all 512 slots. Lengths may be 0.
All inputs are finite; a program needn't handle non-finite values.
Results may differ from the reference program's by a relative error of at most 0.015.
The reference program's roundings to bfloat16 on the way count: a program that leaves them out, or rounds other values in their place, can miss the bound.
Values may be sent and summed in bfloat16 or wider, within the bound.
No kernel may reach another device: no remote copies, remote signals or barrier semaphores. Data moves between devices by JAX's collectives and lax.ppermute only.
A program may use at most 128 MiB of HBM per device.

```python
import math
import jax
import jax.numpy as jnp
from jax import lax

D = 768
HEADS = 12
HEAD_DIM = 64
FF = 3072
TOK_GRP = 512
STEP = 10
GROUPS = 16
TOKENS = 8192


def draw_lengths(key, part):
    key = jax.random.fold_in(key, 11)
    key_fill, key_first, key_frac, key_full = jax.random.split(key, 4)
    half_rows = TOK_GRP // 2
    fill_end = jax.random.randint(key_fill, (GROUPS,), half_rows + 1, TOK_GRP + 1)
    first_end = jax.random.randint(key_first, (GROUPS,), 0, half_rows)
    fraction = jax.random.randint(key_frac, (GROUPS,), 0, 65536)
    second_end = half_rows + 1 + fraction * (fill_end - half_rows) // 65536
    second_end = jnp.minimum(second_end, fill_end)
    full_group = jax.random.randint(key_full, (), 0, GROUPS)
    is_full = jnp.arange(GROUPS) == full_group
    first_end = jnp.where(is_full, 0, first_end)
    second_end = jnp.where(is_full, TOK_GRP, second_end)
    fill_end = jnp.where(is_full, TOK_GRP, fill_end)
    return jnp.stack([first_end, second_end - first_end, fill_end - second_end], axis=1).astype(jnp.int32)


def draw_vectors(key, part):
    key = jax.random.fold_in(key, 5)
    noise = jnp.clip(jax.random.normal(key, (12, D), jnp.float32), -3.0, 3.0)
    row_index = jnp.arange(12)[:, None]
    is_gain = (row_index == 3) | (row_index == 6)
    return jnp.where(is_gain, 1.0 + 0.2 * noise, 0.3 * noise).astype(jnp.float32)


def with_spikes(drawn, stream_key, source, target, parts, factor):
    owner, partner = [(jnp.arange(drawn.shape[position]) // (drawn.shape[position] // parts)).reshape([-1 if axis == position else 1 for axis in range(drawn.ndim)]) for position in (source, target)]
    chosen = jax.random.permutation(stream_key, parts)[partner]
    strong = (owner == chosen) | (owner == (partner + parts // 2) % parts)
    return jnp.where(strong, factor * drawn, drawn)


def block_scale(own_key, extent, shards, least, top_value):
    factor_of, own = 1.0, jax.random.fold_in(own_key, 6)
    for axis_at, parts in shards:
        heights = jnp.exp(jax.random.uniform(jax.random.fold_in(own, axis_at), (parts,), jnp.float32, least / len(shards), top_value / len(shards)))
        factor_of = factor_of * jnp.repeat(heights, extent[axis_at] // parts).reshape([-1 if axis == axis_at else 1 for axis in range(len(extent))])
    return factor_of


def scatter_about(stream_key, extent, scale, bound, cuts=(), held_as=jnp.bfloat16):
    loudness = block_scale(stream_key, extent, cuts, -0.22, 0.18) if cuts else 1.0
    values = jax.random.normal(stream_key, extent, jnp.float32) * scale * loudness
    return jnp.minimum(jnp.maximum(values, -bound), bound).astype(held_as)


def gaussian_with(own_key, extent, spread, reach, pieces, heavy, kind=jnp.bfloat16):
    entries = spread * jax.random.normal(own_key, extent, jnp.float32)
    if pieces:
        entries = entries * block_scale(own_key, extent, pieces, -0.22, 0.18)
    return jnp.clip(with_spikes(entries, jax.random.fold_in(own_key, 3), *heavy), -reach, reach).astype(kind)


def setup_inputs(seed: int = 0) -> dict:
    splits = jax.random.split(jax.random.key(seed), 19)
    return {
        "tokens": gaussian_with(splits[0], (TOKENS, D), 1.0, 6.0, ((0, 32),), (0, 1, 32, 2.75)),
        "cotangent": scatter_about(splits[1], (TOKENS, D), 1.0, 6.0, ((0, 32),)),
        "lengths": draw_lengths(jax.random.fold_in(splits[18], 71), 0),
        "w_qkv": scatter_about(splits[3], (3, D, D), D ** -0.5, 0.21875, ((1, 16), (2, 2)), jnp.float32),
        "m_qkv": scatter_about(splits[4], (3, D, D), (0.022 * TOKENS ** 0.5), 12.0, ((1, 16), (2, 2)), jnp.float32),
        "v_qkv": jnp.clip(jnp.exp(math.log(1.31072) - 2.0794415 * jax.random.uniform(splits[5], (3, D, D), jnp.float32) ** block_scale(splits[5], (3, D, D), ((1, 16), (2, 2)), -0.2, 0.2)), 0.16384, 1.31072),
        "w_out": scatter_about(splits[6], (D, D), (4 * D // TOK_GRP) ** -0.5, 2.5, ((0, 2), (1, 16)), jnp.float32),
        "m_out": scatter_about(splits[7], (D, D), (0.0055 * TOKENS ** 0.5), 4.0, ((0, 2), (1, 16)), jnp.float32),
        "v_out": jnp.clip(jnp.exp(math.log(0.08192) - 2.0794415 * jax.random.uniform(splits[8], (D, D), jnp.float32) ** block_scale(splits[8], (D, D), ((0, 2), (1, 16)), -0.2, 0.2)), 0.01024, 0.08192),
        "w_in": scatter_about(splits[9], (D, FF), D ** -0.5, 0.21875, ((0, 16), (1, 2)), jnp.float32),
        "m_in": scatter_about(splits[10], (D, FF), (0.055 * TOKENS ** 0.5), 32.0, ((0, 16), (1, 2)), jnp.float32),
        "v_in": jnp.clip(jnp.exp(math.log(8.192) - 2.0794415 * jax.random.uniform(splits[11], (D, FF), jnp.float32) ** block_scale(splits[11], (D, FF), ((0, 16), (1, 2)), -0.2, 0.2)), 1.024, 8.192),
        "w_back": scatter_about(splits[12], (FF, D), FF ** -0.5, 0.109375, ((0, 2), (1, 16)), jnp.float32),
        "m_back": scatter_about(splits[13], (FF, D), (0.0385 * TOKENS ** 0.5), 20.0, ((0, 2), (1, 16)), jnp.float32),
        "v_back": jnp.clip(jnp.exp(math.log(4.096) - 2.1202636 * jax.random.uniform(splits[14], (FF, D), jnp.float32) ** block_scale(splits[14], (FF, D), ((0, 2), (1, 16)), -0.2, 0.2)), 0.49152, 4.096),
        "vectors": draw_vectors(jax.random.fold_in(splits[18], 71), 0),
        "m_vectors": scatter_about(splits[16], (12, D), (0.077 * TOKENS ** 0.5), 40.0, ((1, 32),), jnp.float32),
        "v_vectors": jnp.clip(jnp.exp(math.log(16.384) - 2.0794415 * jax.random.uniform(splits[17], (12, D), jnp.float32) ** block_scale(splits[17], (12, D), ((1, 32),), -0.2, 0.2)), 2.048, 16.384),
    }


@jax.custom_vjp
def low(v):
    return lax.optimization_barrier(v.astype(jnp.bfloat16)).astype(jnp.float32)

@jax.custom_vjp
def low_back(v):
    return v

def low_keep(v):
    return (low(v), None)

def low_pass(kept, grad):
    return (grad,)

def back_keep(v):
    return (v, None)

def back_low(kept, grad):
    return (low(grad),)
low.defvjp(low_keep, low_pass)
low_back.defvjp(back_keep, back_low)
HIGHEST_PREC = lax.Precision.HIGHEST
EPS_NORM = 1e-05
BETA_ONE = 0.9
BETA_TWO = 0.999
EPS_ADAM = 1e-08
WEIGHT_DECAY = 0.01
NEG_FILL = -1000000000.0

def normalize(values, gain_row, shift_row):
    row_mean = lax.optimization_barrier(jnp.mean(values, axis=-1, keepdims=True))
    centered = values - row_mean
    variance = lax.optimization_barrier(jnp.mean(centered * centered, axis=-1, keepdims=True))
    return centered * lax.rsqrt(variance + EPS_NORM) * gain_row + shift_row

def segments_of(lengths):
    seq_ends = jnp.cumsum(lengths, axis=1).astype(jnp.int32)
    positions = jnp.arange(TOK_GRP, dtype=jnp.int32)
    segment = lax.optimization_barrier(jnp.sum((positions[None, :, None] >= seq_ends[:, None, :]).astype(jnp.int32), axis=2)).astype(jnp.int32)
    valid = (positions[None, :] < seq_ends[:, -1:]).astype(jnp.float32)
    return (segment, valid)

def attend_group(operands):
    queries, key_rows, value_rows, segment = operands
    scores = jnp.einsum('qhe,khe->hqk', queries, key_rows, precision=HIGHEST_PREC) * 0.125
    scores = low_back(scores)
    same_seq = (segment[:, None] == segment[None, :])[None]
    scores = jnp.where(same_seq, scores, NEG_FILL)
    probabilities = low(jax.nn.softmax(scores, axis=-1))
    return jnp.einsum('hqk,khe->qhe', probabilities, value_rows, precision=HIGHEST_PREC)

def forward_layer(inputs, w_qkv, w_out, w_in, w_back, vectors, segment):
    w_qkv, w_out, w_in, w_back = (low(w_qkv), low(w_out), low(w_in), low(w_back))
    queries = jnp.dot(inputs, w_qkv[0], precision=HIGHEST_PREC) + vectors[0]
    key_rows = jnp.dot(inputs, w_qkv[1], precision=HIGHEST_PREC)
    value_rows = jnp.dot(inputs, w_qkv[2], precision=HIGHEST_PREC) + vectors[1]
    queries = low(low_back(queries))
    key_rows = low(low_back(key_rows))
    value_rows = low(low_back(value_rows))
    head_shape = (GROUPS, TOK_GRP, HEADS, HEAD_DIM)
    attended = lax.map(jax.checkpoint(attend_group), (queries.reshape(head_shape), key_rows.reshape(head_shape), value_rows.reshape(head_shape), segment))
    attended = low(low_back(attended.reshape(TOKENS, D)))
    attn_proj = low_back(jnp.dot(attended, w_out, precision=HIGHEST_PREC))
    first_norm = normalize(inputs + attn_proj + vectors[2], vectors[3], vectors[4])
    pre_act = jnp.dot(low(first_norm), w_in, precision=HIGHEST_PREC) + vectors[8:12].reshape(FF)
    pre_act = low_back(pre_act)
    activation = low(jax.nn.gelu(pre_act, approximate=False))
    mlp_proj = low_back(jnp.dot(activation, w_back, precision=HIGHEST_PREC))
    return normalize(first_norm + mlp_proj + vectors[5], vectors[6], vectors[7])

def adamw(weight, moment, square, gradient, step_rate, decay_rate):
    moment = BETA_ONE * moment + (1.0 - BETA_ONE) * gradient
    square = BETA_TWO * square + (1.0 - BETA_TWO) * gradient * gradient
    direction = moment / (1.0 - BETA_ONE ** STEP) / (jnp.sqrt(square / (1.0 - BETA_TWO ** STEP)) + EPS_ADAM)
    return (weight - step_rate * (direction + decay_rate * weight), moment, square)

def reference(tokens, cotangent, lengths, w_qkv, m_qkv, v_qkv, w_out, m_out, v_out, w_in, m_in, v_in, w_back, m_back, v_back, vectors, m_vectors, v_vectors):
    segment, valid = segments_of(lengths)
    inputs = tokens.astype(jnp.float32)

    def layer_of(inputs, w_qkv, w_out, w_in, w_back, vectors):
        return forward_layer(inputs, w_qkv, w_out, w_in, w_back, vectors, segment)
    result, pull = jax.vjp(layer_of, inputs, w_qkv, w_out, w_in, w_back, vectors)
    incoming = cotangent.astype(jnp.float32) * valid.reshape(TOKENS)[:, None]
    grad_x, grad_qkv, grad_out, grad_in, grad_back, grad_vec = pull(incoming)
    new_qkv, moment_qkv, square_qkv = adamw(w_qkv, m_qkv, v_qkv, grad_qkv, float(D) ** (-0.5), WEIGHT_DECAY)
    new_out, moment_out, square_out = adamw(w_out, m_out, v_out, grad_out, (4.0 * D / TOK_GRP) ** (-0.5), WEIGHT_DECAY)
    new_in, moment_in, square_in = adamw(w_in, m_in, v_in, grad_in, float(D) ** (-0.5), WEIGHT_DECAY)
    new_back, moment_back, square_back = adamw(w_back, m_back, v_back, grad_back, float(FF) ** (-0.5), WEIGHT_DECAY)
    new_vec, moment_vec, square_vec = adamw(vectors, m_vectors, v_vectors, grad_vec, 0.1, 0.0)
    return (result.astype(jnp.bfloat16), grad_x, new_qkv, moment_qkv, square_qkv, new_out, moment_out, square_out, new_in, moment_in, square_in, new_back, moment_back, square_back, new_vec, moment_vec, square_vec)
```

```python
import numpy as np

import jax
import jax.numpy as jnp
from jax import lax
from jax.sharding import PartitionSpec as P

HEAD_DIM = 64
STEP = 10


EPS_NORM = 1e-05
BETA_ONE = 0.9
BETA_TWO = 0.999
EPS_ADAM = 1e-08
WEIGHT_DECAY = 0.01
NEG_FILL = -1000000000.0
LOW = jnp.bfloat16
F32 = jnp.float32


def normalize_fwd(values, gain_row, shift_row):
    row_mean = jnp.mean(values, axis=-1, keepdims=True)
    centered = values - row_mean
    variance = jnp.mean(centered * centered, axis=-1, keepdims=True)
    inv_std = lax.rsqrt(variance + EPS_NORM)
    normed = centered * inv_std
    return (normed * gain_row + shift_row, normed, inv_std)


def normalize_back(gradient, normed, inv_std, gain_row):
    grad_norm = gradient * gain_row
    grad_in = inv_std * (
        grad_norm
        - jnp.mean(grad_norm, axis=-1, keepdims=True)
        - normed * jnp.mean(grad_norm * normed, axis=-1, keepdims=True)
    )
    return (grad_in, jnp.sum(gradient * normed, axis=0), jnp.sum(gradient, axis=0))


def gelu_exact(values):
    return jax.nn.gelu(values, approximate=False)


def adamw(weight, moment, square, gradient, step_rate, decay_rate):
    moment = BETA_ONE * moment + (1.0 - BETA_ONE) * gradient
    square = BETA_TWO * square + (1.0 - BETA_TWO) * gradient * gradient
    direction = (
        moment / (1.0 - BETA_ONE**STEP) / (jnp.sqrt(square / (1.0 - BETA_TWO**STEP)) + EPS_ADAM)
    )
    return (weight - step_rate * (direction + decay_rate * weight), moment, square)


def swap_dp(values, bit):
    size = lax.axis_size("dp")
    return lax.ppermute(values, "dp", [(i, i ^ (1 << bit)) for i in range(size)])


def swap_tensor(values):
    return lax.ppermute(values, "tensor", [(0, 1), (1, 0)])


def high_bits():
    return list(range(2, lax.axis_size("dp").bit_length() - 1))


def swap_total(values):
    for bit in range(lax.axis_size("dp").bit_length() - 1):
        values = values + swap_dp(values, bit)
    return values + swap_tensor(values)


def gather_shard(shard, tensor_first):
    for bit in high_bits():
        shard = jnp.concatenate([shard, swap_dp(shard, bit)], axis=0)
    for over_tensor in (tensor_first, not tensor_first):
        if over_tensor:
            shard = jnp.concatenate([shard, swap_tensor(shard)], axis=1)
        else:
            shard = jnp.concatenate([shard, swap_dp(shard, 1)], axis=0)
    return shard, swap_dp(shard, 0)


def halve(values, swap, axis):
    half = values.shape[axis] // 2
    keep = lax.slice_in_dim(values, 0, half, axis=axis)
    send = lax.slice_in_dim(values, half, 2 * half, axis=axis)
    return keep.astype(F32) + swap(send.astype(LOW)).astype(F32)


def scatter_grad(keep, send, tensor_first):
    total = keep.astype(F32) + swap_dp(send, 0).astype(F32)
    for over_tensor in (not tensor_first, tensor_first):
        total = total.astype(LOW)
        if over_tensor:
            total = halve(total, swap_tensor, 1)
        else:
            total = halve(total, lambda v: swap_dp(v, 1), 0)
    for bit in reversed(high_bits()):
        total = halve(total.astype(LOW), lambda v: swap_dp(v, bit), 0)
    return total


def relative_order(width):
    size = lax.axis_size("dp")
    rows = width // size
    inner_first = high_bits() + [1, 0]
    masks = np.zeros((size,), np.int32)
    for block in range(size):
        for place, bit in enumerate(inner_first):
            if (block >> place) & 1:
                masks[block] |= 1 << bit
    block_mask = jnp.asarray(np.repeat(masks, rows))
    offsets = jnp.asarray(np.tile(np.arange(rows, dtype=np.int32), size))
    return (lax.axis_index("dp") ^ block_mask) * rows + offsets


def dot(left, right):
    return jnp.dot(left, right, preferred_element_type=F32)


def dot_nt(left, right):
    return lax.dot_general(left, right, (((1,), (1,)), ((), ())), preferred_element_type=F32)


def dot_tn(left, right):
    return lax.dot_general(left, right, (((0,), (0,)), ((), ())), preferred_element_type=F32)


def on_device(
    tokens,
    cotangent,
    lengths,
    w_qkv,
    m_qkv,
    v_qkv,
    w_out,
    m_out,
    v_out,
    w_in,
    m_in,
    v_in,
    w_back,
    m_back,
    v_back,
    vectors,
    m_vectors,
    v_vectors,
):
    own_rows, width = tokens.shape
    tensor_rank = lax.axis_index("tensor")
    dp_rank = lax.axis_index("dp")
    group_rows = 2 * own_rows
    shard_width = vectors.shape[1]
    half_width = w_qkv.shape[2]
    hidden_half = w_in.shape[1]
    cut = hidden_half // 2
    full_inner = 2 * hidden_half

    low_qkv = w_qkv.astype(LOW)
    low_in = w_in.astype(LOW)
    low_back = w_back.T.astype(LOW)
    shards = [
        jnp.concatenate([low_qkv[0], low_qkv[1]], axis=1),
        jnp.concatenate([low_qkv[2], w_out.T.astype(LOW)], axis=1),
        low_in[:, :cut],
        low_in[:, cut:],
        low_back[:, :cut],
        low_back[:, cut:],
    ]
    gathered = [
        jnp.concatenate(gather_shard(shard, place % 2 == 0), axis=0)
        for place, shard in enumerate(shards)
    ]
    w_qk, w_vo, w_in_a, w_in_b, w_back_a, w_back_b = gathered

    vec_spread = lax.dynamic_update_slice(
        jnp.zeros((vectors.shape[0], width), F32),
        vectors,
        (0, (dp_rank * 2 + tensor_rank) * shard_width),
    )
    vec_all = swap_total(vec_spread)

    order = relative_order(width)
    permute = (jnp.arange(width, dtype=jnp.int32)[:, None] == order[None, :]).astype(LOW)
    permute_wide = permute.astype(F32)
    exact = lax.Precision.HIGHEST

    def own_first(row):
        pair = row.reshape(2, -1)
        return jnp.where(tensor_rank == 0, row, jnp.concatenate([pair[1], pair[0]]))

    vec_rel = lax.dot_general(
        vec_all[2:8], permute_wide, (((1,), (0,)), ((), ())), precision=exact
    )
    bias_out, gain_one, shift_one, bias_two, gain_two, shift_two = [vec_rel[i] for i in range(6)]
    bias_query = own_first(vec_all[0])
    bias_value = own_first(vec_all[1])
    bias_inner = own_first(vec_all[8:12].reshape(-1)).reshape(2, 2, cut)
    bias_inner = [bias_inner[:, 0].reshape(-1), bias_inner[:, 1].reshape(-1)]

    own = dot(tokens, permute).astype(LOW)
    rows_all = jnp.concatenate([own, dot(swap_tensor(tokens), permute).astype(LOW)], axis=0)
    cot = dot(cotangent, permute)

    seq_ends = jnp.cumsum(lengths[0])
    local = jnp.arange(own_rows, dtype=jnp.int32)
    own_positions = tensor_rank * own_rows + local
    key_positions = jnp.concatenate([own_positions, (1 - tensor_rank) * own_rows + local])

    def segments(positions):
        return jnp.sum((positions[:, None] >= seq_ends[None, :]).astype(jnp.int32), axis=1)

    same = (segments(own_positions)[:, None] == segments(key_positions)[None, :])[None]
    own_valid = (own_positions < seq_ends[-1]).astype(F32)[:, None]

    heads = width // HEAD_DIM

    def pick(values, first):
        return jnp.concatenate(
            [
                values[:, first * half_width : (first + 1) * half_width],
                values[:, (first + 2) * half_width : (first + 3) * half_width],
            ],
            axis=1,
        )

    weight_q, weight_k = pick(w_qk, 0), pick(w_qk, 1)
    weight_v, weight_o = pick(w_vo, 0), pick(w_vo, 1)
    queries = (dot(own, weight_q) + bias_query).astype(LOW).reshape(own_rows, heads, HEAD_DIM)
    key_rows = dot(rows_all, weight_k).astype(LOW).reshape(group_rows, heads, HEAD_DIM)
    value_rows = (dot(rows_all, weight_v) + bias_value).astype(LOW)
    value_rows = value_rows.reshape(group_rows, heads, HEAD_DIM)
    scores = jnp.einsum("qhe,khe->hqk", queries, key_rows, preferred_element_type=F32) * 0.125
    scores = jnp.where(same, scores, NEG_FILL)
    exp_scores = jnp.exp(scores - jnp.max(scores, axis=-1, keepdims=True))
    probabilities = exp_scores / jnp.sum(exp_scores, axis=-1, keepdims=True)
    prob_low = probabilities.astype(LOW)
    attended = jnp.einsum("hqk,khe->qhe", prob_low, value_rows, preferred_element_type=F32)
    attn_low = attended.reshape(own_rows, width).astype(LOW)

    first_norm, normed_one, inv_one = normalize_fwd(
        own.astype(F32) + dot_nt(attn_low, weight_o) + bias_out, gain_one, shift_one
    )
    first_low = first_norm.astype(LOW)
    pre_act = [
        dot(first_low, w_in_a) + bias_inner[0],
        dot(first_low, w_in_b) + bias_inner[1],
    ]
    activation = [gelu_exact(pre).astype(LOW) for pre in pre_act]
    mlp_proj = dot_nt(activation[0], w_back_a) + dot_nt(activation[1], w_back_b)
    result, normed_two, inv_two = normalize_fwd(
        first_norm + mlp_proj + bias_two, gain_two, shift_two
    )
    mixed = dot_nt(result.astype(LOW), permute).astype(LOW)

    half = width // 2
    grad_two, grad_gain_two, grad_shift_two = normalize_back(
        cot * own_valid, normed_two, inv_two, gain_two
    )
    grad_two_low = grad_two.astype(LOW)

    def weight_grad(left, right):
        return (
            dot_tn(left[:, :half], right).astype(LOW),
            dot_tn(left[:, half:], right).astype(LOW),
        )

    def reduced(left, right, tensor_first):
        keep, send = weight_grad(left, right)
        return scatter_grad(keep, send, tensor_first)

    sum_back = [
        reduced(grad_two_low, activation[0], True),
        reduced(grad_two_low, activation[1], False),
    ]
    grad_pre = [
        jax.vjp(gelu_exact, pre)[1](dot(grad_two_low, weight))[0].astype(LOW)
        for pre, weight in zip(pre_act, (w_back_a, w_back_b))
    ]
    sum_in = [
        reduced(first_low, grad_pre[0], True),
        reduced(first_low, grad_pre[1], False),
    ]
    grad_one, grad_gain_one, grad_shift_one = normalize_back(
        grad_two + dot_nt(grad_pre[0], w_in_a) + dot_nt(grad_pre[1], w_in_b),
        normed_one,
        inv_one,
        gain_one,
    )
    grad_one_low = grad_one.astype(LOW)
    grad_attn = dot(grad_one_low, weight_o).astype(LOW).reshape(own_rows, heads, HEAD_DIM)
    grad_probs = jnp.einsum("qhe,khe->hqk", grad_attn, value_rows, preferred_element_type=F32)
    row_delta = jnp.sum(grad_probs * probabilities, axis=-1, keepdims=True)
    grad_scores = (probabilities * (grad_probs - row_delta)).astype(LOW)

    def scaled(spec, left, right):
        return jnp.einsum(spec, left, right, preferred_element_type=F32)

    grad_q = (scaled("hqk,khe->qhe", grad_scores, key_rows) * 0.125).astype(LOW)
    grad_k = (scaled("hqk,qhe->khe", grad_scores, queries) * 0.125).astype(LOW)
    grad_v = scaled("hqk,qhe->khe", prob_low, grad_attn).astype(LOW)
    grad_q = grad_q.reshape(own_rows, width)
    grad_k = grad_k.reshape(group_rows, width)
    grad_v = grad_v.reshape(group_rows, width)

    def interleave(first, second):
        return jnp.concatenate(
            [
                first[:, :half_width],
                second[:, :half_width],
                first[:, half_width:],
                second[:, half_width:],
            ],
            axis=1,
        )

    parts_q = weight_grad(own, grad_q)
    parts_k = weight_grad(rows_all, grad_k)
    parts_v = weight_grad(rows_all, grad_v)
    parts_o = weight_grad(grad_one_low, attn_low)
    sum_qk = scatter_grad(*[interleave(a, b) for a, b in zip(parts_q, parts_k)], True)
    sum_vo = scatter_grad(*[interleave(a, b) for a, b in zip(parts_v, parts_o)], False)

    rows_kv = dot_nt(grad_k, weight_k) + dot_nt(grad_v, weight_v)
    from_partner = swap_tensor(rows_kv[own_rows:].astype(LOW)).astype(F32)
    grad_rel = grad_one + dot_nt(grad_q, weight_q) + rows_kv[:own_rows] + from_partner
    input_grad = lax.dot_general(
        grad_rel, permute_wide, (((1,), (1,)), ((), ())), precision=exact
    )

    def column_sum(values):
        return jnp.sum(values.astype(F32), axis=0)

    grad_inner = jnp.stack([column_sum(pre) for pre in grad_pre]).reshape(2, 2, cut)
    grad_inner = own_first(jnp.transpose(grad_inner, (1, 0, 2)).reshape(-1))
    rel_rows = jnp.stack(
        [
            column_sum(grad_one),
            grad_gain_one,
            grad_shift_one,
            column_sum(grad_two),
            grad_gain_two,
            grad_shift_two,
        ]
    )
    natural_rows = lax.dot_general(
        rel_rows, permute_wide, (((1,), (1,)), ((), ())), precision=exact
    )
    grad_vectors = jnp.concatenate(
        [
            own_first(column_sum(grad_q))[None],
            own_first(column_sum(grad_v))[None],
            natural_rows,
            grad_inner.reshape(full_inner // width, width),
        ],
        axis=0,
    )
    summed_vectors = lax.dynamic_slice_in_dim(
        swap_total(grad_vectors), (dp_rank * 2 + tensor_rank) * shard_width, shard_width, axis=1
    )

    summed_qkv = jnp.stack([sum_qk[:, :half_width], sum_qk[:, half_width:], sum_vo[:, :half_width]])
    summed_out = sum_vo[:, half_width:].T
    summed_in = jnp.concatenate(sum_in, axis=1)
    summed_back = jnp.concatenate(sum_back, axis=1).T
    new_qkv, moment_qkv, square_qkv = adamw(
        w_qkv, m_qkv, v_qkv, summed_qkv, float(width) ** (-0.5), WEIGHT_DECAY
    )
    new_out, moment_out, square_out = adamw(
        w_out, m_out, v_out, summed_out, (4.0 * width / group_rows) ** (-0.5), WEIGHT_DECAY
    )
    new_in, moment_in, square_in = adamw(
        w_in, m_in, v_in, summed_in, float(width) ** (-0.5), WEIGHT_DECAY
    )
    new_back, moment_back, square_back = adamw(
        w_back, m_back, v_back, summed_back, float(full_inner) ** (-0.5), WEIGHT_DECAY
    )
    new_vectors, moment_vectors, square_vectors = adamw(
        vectors, m_vectors, v_vectors, summed_vectors, 0.1, 0.0
    )
    return (
        mixed,
        input_grad,
        new_qkv,
        moment_qkv,
        square_qkv,
        new_out,
        moment_out,
        square_out,
        new_in,
        moment_in,
        square_in,
        new_back,
        moment_back,
        square_back,
        new_vectors,
        moment_vectors,
        square_vectors,
    )


def solution(mesh):
    placed = (
        P(("dp", "tensor"), None),
        P(("dp", "tensor"), None),
        P("dp", None),
        P(None, "dp", "tensor"),
        P(None, "dp", "tensor"),
        P(None, "dp", "tensor"),
        P("tensor", "dp"),
        P("tensor", "dp"),
        P("tensor", "dp"),
        P("dp", "tensor"),
        P("dp", "tensor"),
        P("dp", "tensor"),
        P("tensor", "dp"),
        P("tensor", "dp"),
        P("tensor", "dp"),
        P(None, ("dp", "tensor")),
        P(None, ("dp", "tensor")),
        P(None, ("dp", "tensor")),
    )
    return jax.shard_map(
        on_device,
        mesh=mesh,
        in_specs=placed,
        out_specs=(
            P(("dp", "tensor"), None),
            P(("dp", "tensor"), None),
            P(None, "dp", "tensor"),
            P(None, "dp", "tensor"),
            P(None, "dp", "tensor"),
            P("tensor", "dp"),
            P("tensor", "dp"),
            P("tensor", "dp"),
            P("dp", "tensor"),
            P("dp", "tensor"),
            P("dp", "tensor"),
            P("tensor", "dp"),
            P("tensor", "dp"),
            P("tensor", "dp"),
            P(None, ("dp", "tensor")),
            P(None, ("dp", "tensor")),
            P(None, ("dp", "tensor")),
        ),
        check_vma=False,
    )
```

```python
import numpy as np

import jax
import jax.numpy as jnp
from jax import lax
from jax.experimental import pallas as pl
from jax.experimental.pallas import tpu as pltpu
from jax.sharding import PartitionSpec as P

HEAD_DIM = 64
STEP = 10


EPS_NORM = 1e-05
BETA_ONE = 0.9
BETA_TWO = 0.999
EPS_ADAM = 1e-08
WEIGHT_DECAY = 0.01
NEG_FILL = -1000000000.0
LOW = jnp.bfloat16
F32 = jnp.float32


def normalize_fwd(values, gain_row, shift_row):
    row_mean = jnp.mean(values, axis=-1, keepdims=True)
    centered = values - row_mean
    variance = jnp.mean(centered * centered, axis=-1, keepdims=True)
    inv_std = lax.rsqrt(variance + EPS_NORM)
    normed = centered * inv_std
    return (normed * gain_row + shift_row, normed, inv_std)


def normalize_back(gradient, normed, inv_std, gain_row):
    grad_norm = gradient * gain_row
    grad_in = inv_std * (
        grad_norm
        - jnp.mean(grad_norm, axis=-1, keepdims=True)
        - normed * jnp.mean(grad_norm * normed, axis=-1, keepdims=True)
    )
    return (grad_in, jnp.sum(gradient * normed, axis=0), jnp.sum(gradient, axis=0))


def adamw(weight, moment, square, gradient, step_rate, decay_rate):
    moment = BETA_ONE * moment + (1.0 - BETA_ONE) * gradient
    square = BETA_TWO * square + (1.0 - BETA_TWO) * gradient * gradient
    direction = (
        moment / (1.0 - BETA_ONE**STEP) / (jnp.sqrt(square / (1.0 - BETA_TWO**STEP)) + EPS_ADAM)
    )
    return (weight - step_rate * (direction + decay_rate * weight), moment, square)


def swap_dp(values, mask):
    size = lax.axis_size("dp")
    return lax.ppermute(values, "dp", [(i, i ^ mask) for i in range(size)])


def swap_tensor(values):
    return lax.ppermute(values, "tensor", [(0, 1), (1, 0)])


def high_bits():
    return list(range(2, lax.axis_size("dp").bit_length() - 1))


def high_groups():
    bits = high_bits()
    return [[1 << bit for bit in bits[i : i + 2]] for i in range(0, len(bits), 2)]


def group_masks(group):
    return [0] + group + ([group[0] ^ group[1]] if len(group) == 2 else [])


def gather_high(shard, cut):
    groups = high_groups()
    for place, group in enumerate(groups):
        pieces = [shard if mask == 0 else swap_dp(shard, mask) for mask in group_masks(group)]
        if place < len(groups) - 1:
            shard = jnp.concatenate(pieces, axis=0)
    return (
        jnp.concatenate([piece[:, :cut] for piece in pieces], axis=0),
        jnp.concatenate([piece[:, cut:] for piece in pieces], axis=0),
    )


def gather_plane_first(first, second):
    return (
        jnp.concatenate([first, swap_tensor(first)], axis=1),
        jnp.concatenate([second, swap_dp(second, 2)], axis=0),
    )


def gather_plane_second(first, second):
    return (
        jnp.concatenate([first, swap_dp(first, 2)], axis=0),
        jnp.concatenate([second, swap_tensor(second)], axis=1),
    )


def gather_core(first, second):
    return (first, swap_dp(first, 1)), (second, swap_dp(second, 1))


def halve(values, swap, axis):
    half = values.shape[axis] // 2
    keep = lax.slice_in_dim(values, 0, half, axis=axis)
    send = lax.slice_in_dim(values, half, 2 * half, axis=axis)
    return (keep.astype(F32) + swap(send).astype(F32)).astype(LOW)


def reduce_core(keep, send):
    return (keep.astype(F32) + swap_dp(send, 1).astype(F32)).astype(LOW)


def reduce_plane_first(first, second):
    return halve(first, lambda v: swap_dp(v, 2), 0), halve(second, swap_tensor, 1)


def reduce_plane_second(first, second):
    return halve(first, swap_tensor, 1), halve(second, lambda v: swap_dp(v, 2), 0)


def reduce_high(first, second):
    total = jnp.concatenate([first, second], axis=1)
    for group in reversed(high_groups()):
        masks = group_masks(group)
        rows = total.shape[0] // len(masks)
        total = total.astype(LOW)
        parts = [total[i * rows : (i + 1) * rows] for i in range(len(masks))]
        total = parts[0].astype(F32)
        for part, mask in zip(parts[1:], masks[1:]):
            total = total + swap_dp(part, mask).astype(F32)
    return total


def relative_order(width):
    size = lax.axis_size("dp")
    rows = width // size
    inner_first = high_bits() + [1, 0]
    masks = np.zeros((size,), np.int32)
    for block in range(size):
        for place, bit in enumerate(inner_first):
            if (block >> place) & 1:
                masks[block] |= 1 << bit
    block_mask = jnp.asarray(np.repeat(masks, rows))
    offsets = jnp.asarray(np.tile(np.arange(rows, dtype=np.int32), size))
    return (lax.axis_index("dp") ^ block_mask) * rows + offsets


def dot(left, right):
    return jnp.dot(left, right, preferred_element_type=F32)


def dot_nt(left, right):
    return lax.dot_general(left, right, (((1,), (1,)), ((), ())), preferred_element_type=F32)


def dot_tn(left, right):
    return lax.dot_general(left, right, (((0,), (0,)), ((), ())), preferred_element_type=F32)


def shape_of(rows, columns, kind):
    return jax.ShapeDtypeStruct((rows, columns), kind)


def run(kernel, outs, operands, flops, after=(), grid=(), in_specs=None, out_specs=None):
    count = len(operands)

    def body(*refs):
        kernel(*refs[:count], *refs[count + len(after) :])

    whole = pl.BlockSpec(memory_space=pltpu.VMEM)
    in_specs = in_specs or [whole] * count
    size = sum(v.size * v.dtype.itemsize for v in list(operands) + list(outs))
    return pl.pallas_call(
        body,
        grid=grid,
        out_shape=list(outs),
        in_specs=list(in_specs) + [pl.BlockSpec(memory_space=pl.ANY)] * len(after),
        out_specs=list(out_specs or [whole] * len(outs)),
        compiler_params=pltpu.CompilerParams(vmem_limit_bytes=min(size + (16 << 20), 44 << 20)),
        cost_estimate=pl.CostEstimate(flops=flops, bytes_accessed=size, transcendentals=0),
    )(*operands, *after)


def cast_kernel(source, target):
    target[...] = source[...].astype(LOW)


def project_kernel(rows, a_own, a_far, b_own, b_far, bias_q, bias_v, q, k, v):
    half = a_own.shape[0]
    own_rows, width = q.shape
    part = width // 2
    low, high = rows[:, :half], rows[:, half:]
    a_half, b_half = a_own.shape[1] // 2, b_own.shape[1] // 2
    for side in range(2):
        cols = slice(side * part, (side + 1) * part)
        at = slice(side * a_half, side * a_half + part)
        q[:, cols] = (
            dot(low[:own_rows], a_own[:, at]) + dot(high[:own_rows], a_far[:, at]) + bias_q[:, cols]
        ).astype(LOW)
        at = slice(side * a_half + part, side * a_half + 2 * part)
        k[:, cols] = (dot(low, a_own[:, at]) + dot(high, a_far[:, at])).astype(LOW)
        at = slice(side * b_half, side * b_half + part)
        v[:, cols] = (dot(low, b_own[:, at]) + dot(high, b_far[:, at]) + bias_v[:, cols]).astype(
            LOW
        )


def attend_kernel(seg_q, seg_k, q, k, v, attended):
    same = seg_q[...] == seg_k[...]
    queries, key_rows, value_rows = q[...], k[...], v[...]
    first = lax.broadcasted_iota(jnp.int32, queries.shape, 1) < HEAD_DIM
    sides = []
    for mine in (first, jnp.logical_not(first)):
        scores = dot_nt(jnp.where(mine, queries, jnp.zeros_like(queries)), key_rows) * 0.125
        scores = jnp.where(same, scores, NEG_FILL)
        exp_scores = jnp.exp(scores - jnp.max(scores, axis=1, keepdims=True))
        inverse = 1.0 / jnp.sum(exp_scores, axis=1, keepdims=True)
        sides.append(dot((exp_scores * inverse).astype(LOW), value_rows))
    attended[...] = jnp.where(first, sides[0], sides[1]).astype(LOW)


def attend_back_kernel(seg_q, seg_k, q, k, v, grad, grad_q, grad_k, grad_v):
    same = seg_k[...] == seg_q[...]
    queries, key_rows, value_rows, grad_rows = q[...], k[...], v[...], grad[...]
    first = lax.broadcasted_iota(jnp.int32, queries.shape, 1) < HEAD_DIM
    first_all = lax.broadcasted_iota(jnp.int32, key_rows.shape, 1) < HEAD_DIM
    blank = jnp.zeros_like(queries)
    out_q, out_k, out_v = [], [], []
    for mine in (first, jnp.logical_not(first)):
        scores = dot_nt(key_rows, jnp.where(mine, queries, blank)) * 0.125
        scores = jnp.where(same, scores, NEG_FILL)
        exp_scores = jnp.exp(scores - jnp.max(scores, axis=0, keepdims=True))
        prob = exp_scores * (1.0 / jnp.sum(exp_scores, axis=0, keepdims=True))
        grad_prob = dot_nt(value_rows, jnp.where(mine, grad_rows, blank))
        delta = jnp.sum(grad_prob * prob, axis=0, keepdims=True)
        grad_score = (prob * (grad_prob - delta)).astype(LOW)
        out_q.append(dot_tn(grad_score, key_rows) * 0.125)
        out_k.append(dot(grad_score, queries) * 0.125)
        out_v.append(dot(prob.astype(LOW), grad_rows))
    grad_q[...] = jnp.where(first, out_q[0], out_q[1]).astype(LOW)
    grad_k[...] = jnp.where(first_all, out_k[0], out_k[1]).astype(LOW)
    grad_v[...] = jnp.where(first_all, out_v[0], out_v[1]).astype(LOW)


def out_norm_kernel(attended, rows, b_own, b_far, vec, y, y_low, normed, inv):
    half = b_own.shape[0]
    own_rows, width = y.shape
    part = width // 2
    b_half = b_own.shape[1] // 2
    near, far = attended[:, :part], attended[:, part:]
    out = []
    for weights in (b_own, b_far):
        out.append(
            dot_nt(near, weights[:, part : 2 * part])
            + dot_nt(far, weights[:, b_half + part : b_half + 2 * part])
        )
    total = rows[:own_rows, :].astype(F32) + jnp.concatenate(out, axis=1) + vec[0:1]
    y_new, normed[...], inv[...] = normalize_fwd(total, vec[1:2], vec[2:3])
    y[...] = y_new
    y_low[...] = y_new.astype(LOW)


def hidden_kernel(y_low, a_own, a_far, b_own, b_far, bias, activation, slope):
    half = a_own.shape[0]
    low, high = y_low[:, :half], y_low[:, half:]
    columns = a_own.shape[1]
    step = columns // 4
    for place, (own, far) in enumerate(((a_own, a_far), (b_own, b_far))):
        for start in range(0, columns, step):
            at = slice(start, start + step)
            to = slice(place * columns + start, place * columns + start + step)
            pre = dot(low, own[:, at]) + dot(high, far[:, at]) + bias[:, to]
            cdf = 0.5 + 0.5 * lax.erf(pre * (0.5**0.5))
            activation[:, to] = (pre * cdf).astype(LOW)
            slope[:, to] = cdf + pre * jnp.exp(-0.5 * pre * pre) * ((2.0 * np.pi) ** -0.5)


def out_back_kernel(
    activation, a_own, a_far, b_own, b_far, y, cot, valid, vec, mixed, grad, grad_low, sums
):
    columns = a_own.shape[1]
    act_a, act_b = activation[:, :columns], activation[:, columns:]
    out = [dot_nt(act_a, wa[...]) + dot_nt(act_b, wb[...]) for wa, wb in ((a_own, b_own), (a_far, b_far))]
    total = y[...] + jnp.concatenate(out, axis=1) + vec[3:4]
    result, normed, inv_std = normalize_fwd(total, vec[4:5], vec[5:6])
    mixed[...] = result.astype(LOW)
    grad_in, gain_sum, shift_sum = normalize_back(
        cot[...] * valid[...], normed, inv_std, vec[4:5]
    )
    grad[...] = grad_in
    grad_low[...] = grad_in.astype(LOW)
    sums[0:1] = jnp.sum(grad_in, axis=0, keepdims=True)
    sums[1:2] = gain_sum[None]
    sums[2:3] = shift_sum[None]


def hidden_back_kernel(grad_low, a_own, a_far, b_own, b_far, slope, grad_pre, sums):
    half = a_own.shape[0]
    low, high = grad_low[:, :half], grad_low[:, half:]
    columns = a_own.shape[1]
    step = columns // 4
    for place, (own, far) in enumerate(((a_own, a_far), (b_own, b_far))):
        for start in range(0, columns, step):
            at = slice(start, start + step)
            to = slice(place * columns + start, place * columns + start + step)
            value = ((dot(low, own[:, at]) + dot(high, far[:, at])) * slope[:, to]).astype(LOW)
            grad_pre[:, to] = value
            sums[:, to] = jnp.sum(value.astype(F32), axis=0, keepdims=True)


def norm_back_kernel(
    grad_pre, a_own, a_far, b_own, b_far, grad_two, normed, inv, vec, o_own, o_far,
    grad, grad_low, grad_attn, sums,
):
    columns = a_own.shape[1]
    pre_a, pre_b = grad_pre[:, :columns], grad_pre[:, columns:]
    out = [dot_nt(pre_a, wa[...]) + dot_nt(pre_b, wb[...]) for wa, wb in ((a_own, b_own), (a_far, b_far))]
    grad_in, gain_sum, shift_sum = normalize_back(
        grad_two[...] + jnp.concatenate(out, axis=1), normed[...], inv[...], vec[1:2]
    )
    grad[...] = grad_in
    low = grad_in.astype(LOW)
    grad_low[...] = low
    sums[0:1] = jnp.sum(grad_in, axis=0, keepdims=True)
    sums[1:2] = gain_sum[None]
    sums[2:3] = shift_sum[None]
    half = o_own.shape[0]
    part = grad.shape[1] // 2
    o_half = o_own.shape[1] // 2
    for side in range(2):
        at = slice(side * o_half + part, side * o_half + 2 * part)
        grad_attn[:, side * part : (side + 1) * part] = (
            dot(low[:, :half], o_own[:, at]) + dot(low[:, half:], o_far[:, at])
        ).astype(LOW)


def rows_back_kernel(grad_q, grad_k, grad_v, a_own, a_far, b_own, b_far, grad_one, own, away):
    own_rows, width = own.shape
    part = width // 2
    a_half, b_half = a_own.shape[1] // 2, b_own.shape[1] // 2
    half = a_own.shape[0]
    for place, (wa, wb) in enumerate(((a_own, b_own), (a_far, b_far))):
        to = slice(place * half, (place + 1) * half)
        both = jnp.zeros((2 * own_rows, half), F32)
        mine = grad_one[:, to]
        for side in range(2):
            cols = slice(side * part, (side + 1) * part)
            at = side * a_half
            mine = mine + dot_nt(grad_q[:, cols], wa[:, at : at + part])
            both = both + dot_nt(grad_k[:, cols], wa[:, at + part : at + 2 * part])
            at = side * b_half
            both = both + dot_nt(grad_v[:, cols], wb[:, at : at + part])
        own[:, to] = mine + both[:own_rows]
        away[:, to] = both[own_rows:].astype(LOW)


def first_grads_kernel(
    rows, grad_q, grad_k, grad_v, grad_low, attended, extra, a_keep, a_send, b_keep, b_send
):
    half = a_keep.shape[0]
    own_rows, width = grad_q.shape
    part = width // 2
    a_half, b_half = a_keep.shape[1] // 2, b_keep.shape[1] // 2
    for place, (to_a, to_b) in enumerate(((a_keep, b_keep), (a_send, b_send))):
        at = slice(place * half, (place + 1) * half)
        both = rows[:, at]
        mine = rows[:own_rows, at]
        low = grad_low[:, at]
        for side in range(2):
            cols = slice(side * part, (side + 1) * part)
            base = side * a_half
            to_a[:, base : base + part] = dot_tn(mine, grad_q[:, cols]).astype(LOW)
            to_a[:, base + part : base + 2 * part] = dot_tn(both, grad_k[:, cols]).astype(LOW)
            if a_half > 2 * part:
                lanes = a_half - 2 * part
                to_a[:, base + 2 * part : base + a_half] = extra[
                    at, side * lanes : (side + 1) * lanes
                ]
            base = side * b_half
            to_b[:, base : base + part] = dot_tn(both, grad_v[:, cols]).astype(LOW)
            to_b[:, base + part : base + 2 * part] = dot_tn(low, attended[:, cols]).astype(LOW)


LANES = 128


def on_device(
    tokens,
    cotangent,
    lengths,
    w_qkv,
    m_qkv,
    v_qkv,
    w_out,
    m_out,
    v_out,
    w_in,
    m_in,
    v_in,
    w_back,
    m_back,
    v_back,
    vectors,
    m_vectors,
    v_vectors,
):
    own_rows, width = tokens.shape
    tensor_rank = lax.axis_index("tensor")
    group_rows = 2 * own_rows
    shard_rows = w_qkv.shape[1]
    part = w_qkv.shape[2]
    hidden_half = w_in.shape[1]
    cut = hidden_half // 2
    full_inner = 2 * hidden_half
    half = width // 2
    count = vectors.shape[0]
    blocks = width // shard_rows
    shard_width = vectors.shape[1]
    per_row = count * shard_width // shard_rows

    vec_rows = vectors.T.reshape(shard_rows, per_row)
    vec_parts = [vec_rows.astype(LOW)]
    rest = vec_rows - vec_parts[0].astype(F32)
    vec_parts.append(rest.astype(LOW))
    vec_parts.append((rest - vec_parts[1].astype(F32)).astype(LOW))
    vec_lanes = jnp.concatenate(vec_parts, axis=1)
    vec_lanes = jnp.pad(vec_lanes, ((0, 0), (0, LANES - vec_lanes.shape[1])))
    low_qkv = w_qkv.astype(LOW)
    shard_one = jnp.concatenate(
        [low_qkv[0], low_qkv[1], vec_lanes, low_qkv[2], w_out.T.astype(LOW)], axis=1
    )
    a_width = 2 * part + LANES
    low_shape = shape_of(shard_rows, hidden_half, LOW)

    tokens_far = swap_tensor(tokens)
    one = gather_high(shard_one, a_width)
    shard_in = run(cast_kernel, [low_shape], [w_in], 0, after=one)[0]
    one = gather_plane_first(*one)
    inner = gather_high(shard_in, cut)
    one = gather_plane_second(*one)
    shard_back = run(cast_kernel, [low_shape], [w_back.T], 0, after=inner)[0]
    outer = gather_high(shard_back, cut)
    (a_own, a_far), (b_own, b_far) = gather_core(*one)
    inner = gather_plane_first(*inner)

    order = relative_order(width)
    permute = (jnp.arange(width, dtype=jnp.int32)[:, None] == order[None, :]).astype(LOW)
    permute_wide = permute.astype(F32)
    exact = lax.Precision.HIGHEST
    rows_all = jnp.concatenate([dot(tokens, permute), dot(tokens_far, permute)]).astype(LOW)
    cot = dot(cotangent, permute)

    def swap_sides(values, axis):
        first, second = jnp.split(values, 2, axis=axis)
        return jnp.where(tensor_rank == 0, values, jnp.concatenate([second, first], axis=axis))

    def lanes_of(side):
        at = side * a_width + 2 * part
        picked = jnp.concatenate([a_own[:, at : at + 3 * per_row], a_far[:, at : at + 3 * per_row]])
        picked = picked.astype(F32).reshape(width, 3, per_row)
        return (picked[:, 0] + picked[:, 1]) + picked[:, 2]

    spread = jnp.stack([lanes_of(0), lanes_of(1)]).reshape(2, blocks, shard_width, count)
    spread = swap_sides(spread, 0)
    vec_rel = jnp.transpose(spread, (3, 1, 0, 2)).reshape(count, width)
    vec_natural = lax.dot_general(
        jnp.concatenate([vec_rel[0:2], vec_rel[8:]]),
        permute_wide,
        (((1,), (1,)), ((), ())),
        precision=exact,
    )
    vec = vec_rel[2:8]
    bias_query = swap_sides(vec_natural[0:1], 1)
    bias_value = swap_sides(vec_natural[1:2], 1)
    bias_inner = swap_sides(vec_natural[2:].reshape(2, 2, cut), 0)
    bias_inner = jnp.transpose(bias_inner, (1, 0, 2)).reshape(1, full_inner)

    seq_ends = jnp.cumsum(lengths[0])
    local = jnp.arange(own_rows, dtype=jnp.int32)
    own_positions = tensor_rank * own_rows + local
    key_positions = jnp.concatenate([own_positions, (1 - tensor_rank) * own_rows + local])

    def segments(positions):
        return jnp.sum((positions[:, None] >= seq_ends[None, :]).astype(jnp.int32), axis=1)

    seg_own, seg_keys = segments(own_positions), segments(key_positions)
    valid = (own_positions < seq_ends[-1]).astype(F32)[:, None]

    wide_low = shape_of(own_rows, width, LOW)
    wide = shape_of(own_rows, width, F32)
    group_low = shape_of(group_rows, width, LOW)
    sums_shape = shape_of(8, width, F32)
    unit = 2 * own_rows * width * width
    queries, key_rows, value_rows = run(
        project_kernel,
        [wide_low, group_low, group_low],
        [rows_all, a_own, a_far, b_own, b_far, bias_query, bias_value],
        5 * unit,
        after=inner,
    )
    inner = gather_plane_second(*inner)
    pairs = width // LANES
    own_block = pl.BlockSpec((own_rows, LANES), lambda i: (0, i))
    all_block = pl.BlockSpec((group_rows, LANES), lambda i: (0, i))

    def fixed(shape):
        return pl.BlockSpec(shape, lambda i: (0, 0))

    attended = run(
        attend_kernel,
        [wide_low],
        [seg_own[:, None], seg_keys[None, :], queries, key_rows, value_rows],
        12 * unit,
        grid=(pairs,),
        in_specs=[fixed((own_rows, 1)), fixed((1, group_rows)), own_block, all_block, all_block],
        out_specs=[own_block],
    )[0]
    outer = gather_plane_first(*outer)
    first_norm, first_low, normed_one, inv_one = run(
        out_norm_kernel,
        [wide, wide_low, wide, shape_of(own_rows, 1, F32)],
        [attended, rows_all, b_own, b_far, vec],
        2 * unit,
        after=inner,
    )
    (c_own, c_far), (d_own, d_far) = gather_core(*inner)
    activation, slope = run(
        hidden_kernel,
        [shape_of(own_rows, full_inner, LOW), shape_of(own_rows, full_inner, F32)],
        [first_low, c_own, c_far, d_own, d_far, bias_inner],
        8 * unit,
        after=outer,
    )
    outer = gather_plane_second(*outer)
    (e_own, e_far), (f_own, f_far) = gather_core(*outer)
    mixed_rel, grad_two, grad_two_low, sums_two = run(
        out_back_kernel,
        [wide_low, wide, wide_low, sums_shape],
        [activation, e_own, e_far, f_own, f_far, first_norm, cot, valid, vec],
        5 * unit,
    )
    mixed = dot_nt(mixed_rel, permute).astype(LOW)

    def weight_grad(left, right):
        send = dot_tn(left[:, half:], right).astype(LOW)
        return dot_tn(left[:, :half], right).astype(LOW), send

    def halves(values):
        middle = values.shape[1] // 2
        return values[:, :middle], values[:, middle:]

    outer = halves(reduce_core(*weight_grad(grad_two_low, activation)))
    grad_pre, sums_inner = run(
        hidden_back_kernel,
        [shape_of(own_rows, full_inner, LOW), shape_of(1, full_inner, F32)],
        [grad_two_low, e_own, e_far, f_own, f_far, slope],
        6 * unit,
    )
    outer = reduce_plane_first(*outer)
    inner = halves(reduce_core(*weight_grad(first_low, grad_pre)))
    grad_one, grad_one_low, grad_attn, sums_one = run(
        norm_back_kernel,
        [wide, wide_low, wide_low, sums_shape],
        [grad_pre, c_own, c_far, d_own, d_far, grad_two, normed_one, inv_one, vec, b_own, b_far],
        6 * unit,
    )
    grad_q, grad_k, grad_v = run(
        attend_back_kernel,
        [wide_low, group_low, group_low],
        [seg_own[None, :], seg_keys[:, None], queries, key_rows, value_rows, grad_attn],
        25 * unit,
        after=outer,
        grid=(pairs,),
        in_specs=[fixed((1, own_rows)), fixed((group_rows, 1))]
        + [own_block, all_block, all_block, own_block],
        out_specs=[own_block, all_block, all_block],
    )
    outer = reduce_plane_second(*outer)

    def column_sum(values):
        return jnp.sum(values.astype(F32), axis=0, keepdims=True)

    inner_rows = jnp.transpose(sums_inner.reshape(2, 2, cut), (1, 0, 2))
    inner_rows = swap_sides(inner_rows, 0).reshape(full_inner // width, width)
    natural = jnp.concatenate(
        [swap_sides(column_sum(grad_q), 1), swap_sides(column_sum(grad_v), 1), inner_rows]
    )
    natural = lax.dot_general(natural, permute_wide, (((1,), (0,)), ((), ())), precision=exact)
    grad_vec = jnp.concatenate([natural[:2], sums_one[:3], sums_two[:3], natural[2:]])
    grad_vec = grad_vec.reshape(count, blocks, 2, shard_width)
    grad_vec = swap_sides(jnp.transpose(grad_vec, (1, 3, 0, 2)), 3)
    grad_vec = jnp.transpose(grad_vec, (3, 0, 1, 2)).reshape(2, width, per_row).astype(LOW)
    grad_vec = jnp.pad(grad_vec, ((0, 0), (0, 0), (0, LANES - per_row)))
    grad_vec = jnp.concatenate([grad_vec[0], grad_vec[1]], axis=1)

    a_shape, b_shape = shape_of(half, 2 * a_width, LOW), shape_of(half, 4 * part, LOW)
    a_keep, a_send, b_keep, b_send = run(
        first_grads_kernel,
        [a_shape, a_shape, b_shape, b_shape],
        [rows_all, grad_q, grad_k, grad_v, grad_one_low, attended, grad_vec],
        6 * unit,
        after=inner,
    )
    one = reduce_core(a_keep, a_send), reduce_core(b_keep, b_send)
    inner = reduce_plane_first(*inner)
    grad_own, grad_away = run(
        rows_back_kernel,
        [wide, wide_low],
        [grad_q, grad_k, grad_v, a_own, a_far, b_own, b_far, grad_one],
        5 * unit,
        after=outer,
    )
    grad_rel = grad_own + swap_tensor(grad_away).astype(F32)
    input_grad = lax.dot_general(
        grad_rel, permute_wide, (((1,), (1,)), ((), ())), precision=exact
    )
    summed_back = reduce_high(*outer).T
    inner = reduce_plane_second(*inner)
    one = reduce_plane_first(*one)
    summed_in = reduce_high(*inner)
    one = reduce_plane_second(*one)
    sum_one = reduce_high(*one)

    summed_vectors = sum_one[:, 2 * part : 2 * part + per_row].reshape(shard_width, count).T
    summed_qkv = jnp.stack(
        [
            sum_one[:, :part],
            sum_one[:, part : 2 * part],
            sum_one[:, a_width : a_width + part],
        ]
    )
    summed_out = sum_one[:, a_width + part :].T
    new_qkv, moment_qkv, square_qkv = adamw(
        w_qkv, m_qkv, v_qkv, summed_qkv, float(width) ** (-0.5), WEIGHT_DECAY
    )
    new_out, moment_out, square_out = adamw(
        w_out, m_out, v_out, summed_out, (4.0 * width / group_rows) ** (-0.5), WEIGHT_DECAY
    )
    new_in, moment_in, square_in = adamw(
        w_in, m_in, v_in, summed_in, float(width) ** (-0.5), WEIGHT_DECAY
    )
    new_back, moment_back, square_back = adamw(
        w_back, m_back, v_back, summed_back, float(full_inner) ** (-0.5), WEIGHT_DECAY
    )
    new_vectors, moment_vectors, square_vectors = adamw(
        vectors, m_vectors, v_vectors, summed_vectors, 0.1, 0.0
    )
    return (
        mixed,
        input_grad,
        new_qkv,
        moment_qkv,
        square_qkv,
        new_out,
        moment_out,
        square_out,
        new_in,
        moment_in,
        square_in,
        new_back,
        moment_back,
        square_back,
        new_vectors,
        moment_vectors,
        square_vectors,
    )


def solution(mesh):
    placed = (
        P(("dp", "tensor"), None),
        P(("dp", "tensor"), None),
        P("dp", None),
        P(None, "dp", "tensor"),
        P(None, "dp", "tensor"),
        P(None, "dp", "tensor"),
        P("tensor", "dp"),
        P("tensor", "dp"),
        P("tensor", "dp"),
        P("dp", "tensor"),
        P("dp", "tensor"),
        P("dp", "tensor"),
        P("tensor", "dp"),
        P("tensor", "dp"),
        P("tensor", "dp"),
        P(None, ("dp", "tensor")),
        P(None, ("dp", "tensor")),
        P(None, ("dp", "tensor")),
    )
    return jax.shard_map(
        on_device,
        mesh=mesh,
        in_specs=placed,
        out_specs=(
            P(("dp", "tensor"), None),
            P(("dp", "tensor"), None),
            P(None, "dp", "tensor"),
            P(None, "dp", "tensor"),
            P(None, "dp", "tensor"),
            P("tensor", "dp"),
            P("tensor", "dp"),
            P("tensor", "dp"),
            P("dp", "tensor"),
            P("dp", "tensor"),
            P("dp", "tensor"),
            P("tensor", "dp"),
            P("tensor", "dp"),
            P("tensor", "dp"),
            P(None, ("dp", "tensor")),
            P(None, ("dp", "tensor")),
            P(None, ("dp", "tensor")),
        ),
        check_vma=False,
    )
```

```python
import functools

import numpy as np

import jax
import jax.numpy as jnp
from jax import lax
from jax.experimental import pallas as pl
from jax.experimental.pallas import tpu as pltpu
from jax.sharding import PartitionSpec as P

HEAD_DIM = 64
LANES = 128
STEP = 10


EPS_NORM = 1e-05
BETA_ONE = 0.9
BETA_TWO = 0.999
EPS_ADAM = 1e-08
WEIGHT_DECAY = 0.01
NEG_FILL = -1000000000.0
LOW = jnp.bfloat16
F32 = jnp.float32


def normalize_fwd(values, gain_row, shift_row):
    row_mean = jnp.mean(values, axis=-1, keepdims=True)
    centered = values - row_mean
    variance = jnp.mean(centered * centered, axis=-1, keepdims=True)
    inv_std = lax.rsqrt(variance + EPS_NORM)
    normed = centered * inv_std
    return (normed * gain_row + shift_row, normed, inv_std)


def normalize_back(gradient, normed, inv_std, gain_row):
    grad_norm = gradient * gain_row
    grad_in = inv_std * (
        grad_norm
        - jnp.mean(grad_norm, axis=-1, keepdims=True)
        - normed * jnp.mean(grad_norm * normed, axis=-1, keepdims=True)
    )
    return (grad_in, jnp.sum(gradient * normed, axis=0), jnp.sum(gradient, axis=0))


def adamw(weight, moment, square, gradient, step_rate, decay_rate):
    moment = BETA_ONE * moment + (1.0 - BETA_ONE) * gradient
    square = BETA_TWO * square + (1.0 - BETA_TWO) * gradient * gradient
    direction = (
        moment / (1.0 - BETA_ONE**STEP) / (jnp.sqrt(square / (1.0 - BETA_TWO**STEP)) + EPS_ADAM)
    )
    return (weight - step_rate * (direction + decay_rate * weight), moment, square)


def swap_dp(values, mask):
    size = lax.axis_size("dp")
    return lax.ppermute(values, "dp", [(i, i ^ mask) for i in range(size)])


def swap_tensor(values):
    return lax.ppermute(values, "tensor", [(0, 1), (1, 0)])


def high_bits():
    return list(range(2, lax.axis_size("dp").bit_length() - 1))


def high_groups():
    bits = high_bits()
    return [[1 << bit for bit in bits[i : i + 2]] for i in range(0, len(bits), 2)]


def group_masks(group):
    return [0] + group + ([group[0] ^ group[1]] if len(group) == 2 else [])


def gather_high(shard):
    groups = high_groups()
    for place, group in enumerate(groups):
        pieces = [shard if mask == 0 else swap_dp(shard, mask) for mask in group_masks(group)]
        if place < len(groups) - 1:
            shard = jnp.concatenate(pieces, axis=0)
    return pieces


def send_high(parts):
    masks = group_masks(high_groups()[-1])
    return [parts[0]] + [swap_dp(part, mask) for part, mask in zip(parts[1:], masks[1:])]


def reduce_high(parts):
    total = sum(part.astype(F32) for part in parts)
    for group in reversed(high_groups()[:-1]):
        masks = group_masks(group)
        rows = total.shape[0] // len(masks)
        low = total.astype(LOW)
        total = total[:rows]
        for place, mask in enumerate(masks[1:], 1):
            total = total + swap_dp(low[place * rows : (place + 1) * rows], mask).astype(F32)
    return total


def relative_order(width):
    size = lax.axis_size("dp")
    rows = width // size
    inner_first = high_bits() + [1, 0]
    masks = np.zeros((size,), np.int32)
    for block in range(size):
        for place, bit in enumerate(inner_first):
            if (block >> place) & 1:
                masks[block] |= 1 << bit
    block_mask = jnp.asarray(np.repeat(masks, rows))
    offsets = jnp.asarray(np.tile(np.arange(rows, dtype=np.int32), size))
    return (lax.axis_index("dp") ^ block_mask) * rows + offsets


def dot(left, right):
    return jnp.dot(left, right, preferred_element_type=F32)


def dot_nt(left, right):
    return lax.dot_general(left, right, (((1,), (1,)), ((), ())), preferred_element_type=F32)


def dot_tn(left, right):
    return lax.dot_general(left, right, (((0,), (0,)), ((), ())), preferred_element_type=F32)


def shape_of(rows, columns, kind):
    return jax.ShapeDtypeStruct((rows, columns), kind)


def run(kernel, outs, operands, flops, after=(), grid=(), in_specs=None, out_specs=None, scratch=()):
    count = len(operands)

    def body(*refs):
        kernel(*refs[:count], *refs[count + len(after) :])

    whole = pl.BlockSpec(memory_space=pltpu.VMEM)
    in_specs = in_specs or [whole] * count
    size = sum(v.size * v.dtype.itemsize for v in list(operands) + list(outs))
    return pl.pallas_call(
        body,
        grid=grid,
        out_shape=list(outs),
        in_specs=list(in_specs) + [pl.BlockSpec(memory_space=pl.ANY)] * len(after),
        out_specs=list(out_specs or [whole] * len(outs)),
        scratch_shapes=list(scratch),
        compiler_params=pltpu.CompilerParams(
            vmem_limit_bytes=min(size + ((12 if flops else 4) << 20), 44 << 20)
        ),
        cost_estimate=pl.CostEstimate(flops=flops, bytes_accessed=size, transcendentals=0),
    )(*operands, *after)


def join_high_kernel(count, *refs):
    pieces, (first, second) = refs[:count], refs[count:]
    cut = first.shape[1]
    rows = pieces[0].shape[0]
    for place, piece in enumerate(pieces):
        to = slice(place * rows, (place + 1) * rows)
        first[to, :] = piece[:, :cut]
        second[to, :] = piece[:, cut:]


def join_high(pieces, cut, after=()):
    rows, columns = pieces[0].shape
    rows = rows * len(pieces)
    return run(
        functools.partial(join_high_kernel, len(pieces)),
        [shape_of(rows, cut, LOW), shape_of(rows, columns - cut, LOW)],
        pieces,
        0,
        after,
    )


def join_plane_kernel(across, down, across_far, down_far, across_all, down_all):
    columns, rows = across.shape[1], down.shape[0]
    across_all[:, :columns] = across[...]
    across_all[:, columns:] = across_far[...]
    down_all[:rows, :] = down[...]
    down_all[rows:, :] = down_far[...]


def join_plane(across, down, across_far, down_far, after=()):
    return run(
        join_plane_kernel,
        [
            shape_of(across.shape[0], 2 * across.shape[1], LOW),
            shape_of(2 * down.shape[0], down.shape[1], LOW),
        ],
        [across, down, across_far, down_far],
        0,
        after,
    )


def added(left, right, rows, columns):
    return (left[rows, columns].astype(F32) + right[rows, columns].astype(F32)).astype(LOW)


def split_core_kernel(keep, far, a_keep, a_send, b_keep, b_send):
    rows, cut = a_keep.shape
    half = b_keep.shape[1]
    every = slice(None)
    a_keep[...] = added(keep, far, slice(0, rows), slice(0, cut))
    a_send[...] = added(keep, far, slice(rows, 2 * rows), slice(0, cut))
    b_keep[...] = added(keep, far, every, slice(cut, cut + half))
    b_send[...] = added(keep, far, every, slice(cut + half, cut + 2 * half))


def split_core(keep, far, cut, after=()):
    rows, columns = keep.shape
    a_shape = shape_of(rows // 2, cut, LOW)
    b_shape = shape_of(rows, (columns - cut) // 2, LOW)
    return run(
        split_core_kernel, [a_shape, a_shape, b_shape, b_shape], [keep, far], 0, after
    )


def split_plane_kernel(a, a_far, b, b_far, a_keep, a_send, b_keep, b_send):
    half, rows = a_keep.shape[1], b_keep.shape[0]
    every = slice(None)
    a_keep[...] = added(a, a_far, every, slice(0, half))
    a_send[...] = added(a, a_far, every, slice(half, 2 * half))
    b_keep[...] = added(b, b_far, slice(0, rows), every)
    b_send[...] = added(b, b_far, slice(rows, 2 * rows), every)


def split_plane(a, a_far, b, b_far, after=()):
    a_shape = shape_of(a.shape[0], a.shape[1] // 2, LOW)
    b_shape = shape_of(b.shape[0] // 2, b.shape[1], LOW)
    return run(
        split_plane_kernel, [a_shape, a_shape, b_shape, b_shape], [a, a_far, b, b_far], 0, after
    )


def split_high_kernel(a, a_far, b, b_far, *parts):
    cut = a.shape[1]
    rows = parts[0].shape[0]
    for place, part in enumerate(parts):
        at = slice(place * rows, (place + 1) * rows)
        part[:, :cut] = added(a, a_far, at, slice(None))
        part[:, cut:] = added(b, b_far, at, slice(None))


def split_high(a, a_far, b, b_far, after=()):
    count = len(group_masks(high_groups()[-1]))
    part = shape_of(a.shape[0] // count, a.shape[1] + b.shape[1], LOW)
    return run(split_high_kernel, [part] * count, [a, a_far, b, b_far], 0, after)


def flip(rank, first, second):
    return jnp.where(rank == 0, first, second)


def vectors_kernel(rank_ref, permute, a_own, a_far, relative, bias_q, bias_v, bias_inner):
    rank = rank_ref[0]
    side = a_own.shape[1] // 2
    width = relative.shape[1]
    half = width // 2
    spread = jnp.concatenate(
        [
            (ref[:, side - LANES : side].astype(F32) + ref[:, 2 * side - LANES :].astype(F32))
            for ref in (a_own, a_far)
        ],
        axis=0,
    )
    parts = jnp.transpose(spread)
    parts = [parts[16 * i : 16 * (i + 1)] for i in range(3)]
    relative[...] = ((parts[0] + parts[1]) + parts[2])[2:8]
    natural = [dot_nt(part.astype(LOW), permute[...]) for part in parts]
    natural = (natural[0] + natural[1]) + natural[2]
    for row, target in ((0, bias_q), (1, bias_v)):
        first, second = natural[row : row + 1, :half], natural[row : row + 1, half:]
        target[:, :half] = flip(rank, first, second)
        target[:, half:] = flip(rank, second, first)
    for cut in range(2):
        for place in range(2):
            near, far = 8 + 2 * place + cut, 8 + 2 * (1 - place) + cut
            at = (2 * cut + place) * width
            bias_inner[:, at : at + width] = flip(
                rank, natural[near : near + 1], natural[far : far + 1]
            )


def vector_lanes(rank, permute, grad_q, grad_v, sums_one, sums_two, sums_inner, natural, relative):
    width = natural.shape[1]
    half = width // 2
    natural[...] = jnp.zeros_like(natural)
    relative[...] = jnp.zeros_like(relative)
    for row, source in ((0, grad_q), (1, grad_v)):
        total = jnp.sum(source[...].astype(F32), axis=0, keepdims=True)
        first, second = total[:, :half], total[:, half:]
        natural[row : row + 1, :half] = flip(rank, first, second)
        natural[row : row + 1, half:] = flip(rank, second, first)
    for cut in range(2):
        for place in range(2):
            near, far = (2 * cut + place) * width, (2 * cut + 1 - place) * width
            row = 8 + 2 * place + cut
            natural[row : row + 1, :] = flip(
                rank, sums_inner[:, near : near + width], sums_inner[:, far : far + width]
            )
    relative[:16, :] = dot(natural[...].astype(LOW), permute[...])
    relative[2:5, :] = sums_one[:3, :]
    relative[5:8, :] = sums_two[:3, :]
    return jnp.transpose(relative[...]).astype(LOW)


def cast_kernel(source, target):
    target[...] = source[...].astype(LOW)


def project_kernel(rows, a_own, a_far, b_own, b_far, bias_q, bias_v, q, k, v):
    half = a_own.shape[0]
    own_rows, width = q.shape
    part = width // 2
    low, high = rows[:, :half], rows[:, half:]
    a_half, b_half = a_own.shape[1] // 2, b_own.shape[1] // 2
    for side in range(2):
        cols = slice(side * part, (side + 1) * part)
        at = slice(side * a_half, side * a_half + part)
        q[:, cols] = (
            dot(low[:own_rows], a_own[:, at]) + dot(high[:own_rows], a_far[:, at]) + bias_q[:, cols]
        ).astype(LOW)
        at = slice(side * a_half + part, side * a_half + 2 * part)
        k[:, cols] = (dot(low, a_own[:, at]) + dot(high, a_far[:, at])).astype(LOW)
        at = slice(side * b_half, side * b_half + part)
        v[:, cols] = (dot(low, b_own[:, at]) + dot(high, b_far[:, at]) + bias_v[:, cols]).astype(
            LOW
        )


def softmax_down(seg_q, seg_k, key_rows, queries):
    scores = dot_nt(key_rows, queries) * 0.125
    scores = jnp.where(seg_k[...] == seg_q[...], scores, NEG_FILL)
    exp_scores = jnp.exp(scores - jnp.max(scores, axis=0, keepdims=True))
    return exp_scores * (1.0 / jnp.sum(exp_scores, axis=0, keepdims=True))


def two_heads(out):
    joined = jnp.concatenate([out[0][:HEAD_DIM], out[1][HEAD_DIM:]], axis=0)
    return jnp.transpose(joined).astype(LOW)


def attend_kernel(seg_q, seg_k, q, k, v, attended):
    queries, key_rows, value_rows = q[...], k[...], v[...]
    first = lax.broadcasted_iota(jnp.int32, queries.shape, 1) < HEAD_DIM
    out = []
    for mine in (first, jnp.logical_not(first)):
        prob = softmax_down(
            seg_q, seg_k, key_rows, jnp.where(mine, queries, jnp.zeros_like(queries))
        )
        out.append(dot_tn(value_rows, prob.astype(LOW)))
    attended[...] = two_heads(out)


def attend_back_kernel(seg_q, seg_k, q, k, v, grad, grad_q, grad_k, grad_v):
    queries, key_rows, value_rows, grad_rows = q[...], k[...], v[...], grad[...]
    first = lax.broadcasted_iota(jnp.int32, queries.shape, 1) < HEAD_DIM
    first_all = lax.broadcasted_iota(jnp.int32, key_rows.shape, 1) < HEAD_DIM
    blank = jnp.zeros_like(queries)
    out_q, out_k, out_v = [], [], []
    for mine in (first, jnp.logical_not(first)):
        prob = softmax_down(seg_q, seg_k, key_rows, jnp.where(mine, queries, blank))
        grad_prob = dot_nt(value_rows, jnp.where(mine, grad_rows, blank))
        delta = jnp.sum(grad_prob * prob, axis=0, keepdims=True)
        grad_score = (prob * (grad_prob - delta)).astype(LOW)
        out_q.append(dot_tn(key_rows, grad_score) * 0.125)
        out_k.append(dot(grad_score, queries) * 0.125)
        out_v.append(dot(prob.astype(LOW), grad_rows))
    grad_q[...] = two_heads(out_q)
    grad_k[...] = jnp.where(first_all, out_k[0], out_k[1]).astype(LOW)
    grad_v[...] = jnp.where(first_all, out_v[0], out_v[1]).astype(LOW)


def out_norm_kernel(attended, rows, b_own, b_far, vec, y, y_low, normed, inv):
    half = b_own.shape[0]
    own_rows, width = y.shape
    part = width // 2
    b_half = b_own.shape[1] // 2
    near, far = attended[:, :part], attended[:, part:]
    out = []
    for weights in (b_own, b_far):
        out.append(
            dot_nt(near, weights[:, part : 2 * part])
            + dot_nt(far, weights[:, b_half + part : b_half + 2 * part])
        )
    total = rows[:own_rows, :].astype(F32) + jnp.concatenate(out, axis=1) + vec[0:1]
    y_new, normed[...], inv[...] = normalize_fwd(total, vec[1:2], vec[2:3])
    y[...] = y_new
    y_low[...] = y_new.astype(LOW)


def hidden_kernel(y_low, a_own, a_far, b_own, b_far, bias, activation, slope):
    half = a_own.shape[0]
    low, high = y_low[:, :half], y_low[:, half:]
    columns = a_own.shape[1]
    step = columns // 4
    for place, (own, far) in enumerate(((a_own, a_far), (b_own, b_far))):
        for start in range(0, columns, step):
            at = slice(start, start + step)
            to = slice(place * columns + start, place * columns + start + step)
            pre = dot(low, own[:, at]) + dot(high, far[:, at]) + bias[:, to]
            cdf = 0.5 + 0.5 * lax.erf(pre * (0.5**0.5))
            activation[:, to] = (pre * cdf).astype(LOW)
            slope[:, to] = cdf + pre * jnp.exp(-0.5 * pre * pre) * ((2.0 * np.pi) ** -0.5)


def out_back_kernel(
    activation, a_own, a_far, b_own, b_far, y, cot, valid, vec, mixed, grad, grad_low, sums
):
    columns = a_own.shape[1]
    act_a, act_b = activation[:, :columns], activation[:, columns:]
    out = [dot_nt(act_a, wa[...]) + dot_nt(act_b, wb[...]) for wa, wb in ((a_own, b_own), (a_far, b_far))]
    total = y[...] + jnp.concatenate(out, axis=1) + vec[3:4]
    result, normed, inv_std = normalize_fwd(total, vec[4:5], vec[5:6])
    mixed[...] = result.astype(LOW)
    grad_in, gain_sum, shift_sum = normalize_back(
        cot[...] * valid[...], normed, inv_std, vec[4:5]
    )
    grad[...] = grad_in
    grad_low[...] = grad_in.astype(LOW)
    sums[0:1] = jnp.sum(grad_in, axis=0, keepdims=True)
    sums[1:2] = gain_sum[None]
    sums[2:3] = shift_sum[None]


def hidden_back_kernel(grad_low, a_own, a_far, b_own, b_far, slope, grad_pre, sums):
    half = a_own.shape[0]
    low, high = grad_low[:, :half], grad_low[:, half:]
    columns = a_own.shape[1]
    step = columns // 4
    for place, (own, far) in enumerate(((a_own, a_far), (b_own, b_far))):
        for start in range(0, columns, step):
            at = slice(start, start + step)
            to = slice(place * columns + start, place * columns + start + step)
            value = ((dot(low, own[:, at]) + dot(high, far[:, at])) * slope[:, to]).astype(LOW)
            grad_pre[:, to] = value
            sums[:, to] = jnp.sum(value.astype(F32), axis=0, keepdims=True)


def norm_back_kernel(
    grad_pre, a_own, a_far, b_own, b_far, grad_two, normed, inv, vec, o_own, o_far,
    grad, grad_low, grad_attn, sums,
):
    columns = a_own.shape[1]
    pre_a, pre_b = grad_pre[:, :columns], grad_pre[:, columns:]
    out = [dot_nt(pre_a, wa[...]) + dot_nt(pre_b, wb[...]) for wa, wb in ((a_own, b_own), (a_far, b_far))]
    grad_in, gain_sum, shift_sum = normalize_back(
        grad_two[...] + jnp.concatenate(out, axis=1), normed[...], inv[...], vec[1:2]
    )
    grad[...] = grad_in
    low = grad_in.astype(LOW)
    grad_low[...] = low
    sums[0:1] = jnp.sum(grad_in, axis=0, keepdims=True)
    sums[1:2] = gain_sum[None]
    sums[2:3] = shift_sum[None]
    half = o_own.shape[0]
    part = grad.shape[1] // 2
    o_half = o_own.shape[1] // 2
    for side in range(2):
        at = slice(side * o_half + part, side * o_half + 2 * part)
        grad_attn[:, side * part : (side + 1) * part] = (
            dot(low[:, :half], o_own[:, at]) + dot(low[:, half:], o_far[:, at])
        ).astype(LOW)


def rows_back_kernel(grad_q, grad_k, grad_v, a_own, a_far, b_own, b_far, grad_one, own, away):
    own_rows, width = own.shape
    part = width // 2
    a_half, b_half = a_own.shape[1] // 2, b_own.shape[1] // 2
    half = a_own.shape[0]
    for place, (wa, wb) in enumerate(((a_own, b_own), (a_far, b_far))):
        to = slice(place * half, (place + 1) * half)
        both = jnp.zeros((2 * own_rows, half), F32)
        mine = grad_one[:, to]
        for side in range(2):
            cols = slice(side * part, (side + 1) * part)
            at = side * a_half
            mine = mine + dot_nt(grad_q[:, cols], wa[:, at : at + part])
            both = both + dot_nt(grad_k[:, cols], wa[:, at + part : at + 2 * part])
            at = side * b_half
            both = both + dot_nt(grad_v[:, cols], wb[:, at : at + part])
        own[:, to] = mine + both[:own_rows]
        away[:, to] = both[own_rows:].astype(LOW)


def first_grads_kernel(
    a_half, rank_ref, permute, rows, grad_q, grad_k, grad_v, grad_low, attended,
    sums_one, sums_two, sums_inner, send, keep, natural, relative,
):
    half = keep.shape[0]
    own_rows, width = grad_q.shape
    part = width // 2
    extra = vector_lanes(
        rank_ref[0], permute, grad_q, grad_v, sums_one, sums_two, sums_inner, natural, relative
    )
    for place, to in ((1, send), (0, keep)):
        at = slice(place * half, (place + 1) * half)
        both = rows[:, at]
        mine = rows[:own_rows, at]
        low = grad_low[:, at]
        for side in range(2):
            cols = slice(side * part, (side + 1) * part)
            base = side * a_half
            to[:, base : base + part] = dot_tn(mine, grad_q[:, cols]).astype(LOW)
            to[:, base + part : base + 2 * part] = dot_tn(both, grad_k[:, cols]).astype(LOW)
            to[:, base + 2 * part : base + a_half] = extra[at, :]
            base = 2 * a_half + side * 2 * part
            to[:, base : base + part] = dot_tn(both, grad_v[:, cols]).astype(LOW)
            to[:, base + part : base + 2 * part] = dot_tn(low, attended[:, cols]).astype(LOW)


def on_device(
    tokens,
    cotangent,
    lengths,
    w_qkv,
    m_qkv,
    v_qkv,
    w_out,
    m_out,
    v_out,
    w_in,
    m_in,
    v_in,
    w_back,
    m_back,
    v_back,
    vectors,
    m_vectors,
    v_vectors,
):
    own_rows, width = tokens.shape
    tensor_rank = lax.axis_index("tensor")
    group_rows = 2 * own_rows
    shard_rows = w_qkv.shape[1]
    part = w_qkv.shape[2]
    hidden_half = w_in.shape[1]
    cut = hidden_half // 2
    full_inner = 2 * hidden_half
    half = width // 2
    count = vectors.shape[0]
    shard_width = vectors.shape[1]

    rest = vectors.T
    vec_parts = []
    for _ in range(3):
        vec_parts.append(jnp.pad(rest.astype(LOW), ((0, 0), (0, 16 - count))))
        rest = rest - rest.astype(LOW).astype(F32)
    vec_lanes = jnp.pad(jnp.concatenate(vec_parts, axis=1), ((0, 0), (0, LANES - 48)))
    blank = jnp.zeros_like(vec_lanes)
    vec_lanes = jnp.concatenate(
        [
            jnp.where(tensor_rank == 0, vec_lanes, blank),
            jnp.where(tensor_rank == 0, blank, vec_lanes),
        ],
        axis=0,
    )
    low_qkv = w_qkv.astype(LOW)
    shard_one = jnp.concatenate(
        [low_qkv[0], low_qkv[1], vec_lanes, low_qkv[2], w_out.T.astype(LOW)], axis=1
    )
    a_width = 2 * part + LANES
    low_shape = shape_of(shard_rows, hidden_half, LOW)
    rank = tensor_rank.astype(jnp.int32).reshape(1)
    scalar = pl.BlockSpec(memory_space=pltpu.SMEM)
    vmem = pl.BlockSpec(memory_space=pltpu.VMEM)

    tokens_far = swap_tensor(tokens)
    one_high = gather_high(shard_one)
    one = join_high(one_high, a_width)
    one_far = swap_tensor(one[0]), swap_dp(one[1], 2)
    shard_in = run(cast_kernel, [low_shape], [w_in], 0, after=one[:1])[0]
    inner_high = gather_high(shard_in)

    order = relative_order(width)
    permute = (jnp.arange(width, dtype=jnp.int32)[:, None] == order[None, :]).astype(LOW)
    permute_wide = permute.astype(F32)
    exact = lax.Precision.HIGHEST
    rows_all = jnp.concatenate([dot(tokens, permute), dot(tokens_far, permute)]).astype(LOW)
    cot = dot(cotangent, permute)

    one = join_plane(*one, *one_far, after=[shard_in])
    one_far = swap_dp(one[0], 2), swap_tensor(one[1])
    inner = join_high(inner_high, cut, after=one[:1])
    shard_back = run(cast_kernel, [low_shape], [w_back.T], 0, after=inner[:1])[0]
    outer_high = gather_high(shard_back)
    one = join_plane(one[1], one[0], one_far[1], one_far[0], after=inner[:1])[::-1]
    a_own, b_own = one
    a_far, b_far = swap_dp(a_own, 1), swap_dp(b_own, 1)
    inner_far = swap_tensor(inner[0]), swap_dp(inner[1], 2)

    vec, bias_query, bias_value, bias_inner = run(
        vectors_kernel,
        [
            shape_of(6, width, F32),
            shape_of(1, width, F32),
            shape_of(1, width, F32),
            shape_of(1, full_inner, F32),
        ],
        [rank, permute, a_own, a_far],
        1,
        after=[shard_back],
        in_specs=[scalar, vmem, vmem, vmem],
    )

    seq_ends = jnp.cumsum(lengths[0])
    local = jnp.arange(own_rows, dtype=jnp.int32)
    own_positions = tensor_rank * own_rows + local
    key_positions = jnp.concatenate([own_positions, (1 - tensor_rank) * own_rows + local])

    def segments(positions):
        return jnp.sum((positions[:, None] >= seq_ends[None, :]).astype(jnp.int32), axis=1)

    seg_own, seg_keys = segments(own_positions)[None, :], segments(key_positions)[:, None]
    valid = (own_positions < seq_ends[-1]).astype(F32)[:, None]

    wide_low = shape_of(own_rows, width, LOW)
    wide = shape_of(own_rows, width, F32)
    group_low = shape_of(group_rows, width, LOW)
    sums_shape = shape_of(8, width, F32)
    unit = 2 * own_rows * width * width
    queries, key_rows, value_rows = run(
        project_kernel,
        [wide_low, group_low, group_low],
        [rows_all, a_own, a_far, b_own, b_far, bias_query, bias_value],
        5 * unit,
    )
    inner = join_plane(*inner, *inner_far, after=[queries])
    inner_far = swap_dp(inner[0], 2), swap_tensor(inner[1])
    outer = join_high(outer_high, cut, after=[queries])
    pairs = width // LANES
    own_block = pl.BlockSpec((own_rows, LANES), lambda i: (0, i))
    all_block = pl.BlockSpec((group_rows, LANES), lambda i: (0, i))

    def fixed(shape):
        return pl.BlockSpec(shape, lambda i: (0, 0))

    attended = run(
        attend_kernel,
        [wide_low],
        [seg_own, seg_keys, queries, key_rows, value_rows],
        12 * unit,
        after=[inner[0], outer[0]],
        grid=(pairs,),
        in_specs=[fixed((1, own_rows)), fixed((group_rows, 1)), own_block, all_block, all_block],
        out_specs=[own_block],
    )[0]
    inner = join_plane(inner[1], inner[0], inner_far[1], inner_far[0], after=[attended])[::-1]
    c_own, d_own = inner
    c_far, d_far = swap_dp(c_own, 1), swap_dp(d_own, 1)
    outer_far = swap_tensor(outer[0]), swap_dp(outer[1], 2)
    first_norm, first_low, normed_one, inv_one = run(
        out_norm_kernel,
        [wide, wide_low, wide, shape_of(own_rows, 1, F32)],
        [attended, rows_all, b_own, b_far, vec],
        2 * unit,
        after=inner[:1],
    )
    outer = join_plane(*outer, *outer_far, after=[first_low])
    outer_far = swap_dp(outer[0], 2), swap_tensor(outer[1])
    activation, slope = run(
        hidden_kernel,
        [shape_of(own_rows, full_inner, LOW), shape_of(own_rows, full_inner, F32)],
        [first_low, c_own, c_far, d_own, d_far, bias_inner],
        8 * unit,
        after=outer[:1],
    )
    outer = join_plane(outer[1], outer[0], outer_far[1], outer_far[0], after=[activation])[::-1]
    e_own, f_own = outer
    e_far, f_far = swap_dp(e_own, 1), swap_dp(f_own, 1)
    mixed_rel, grad_two, grad_two_low, sums_two = run(
        out_back_kernel,
        [wide_low, wide, wide_low, sums_shape],
        [activation, e_own, e_far, f_own, f_far, first_norm, cot, valid, vec],
        5 * unit,
    )
    mixed = dot_nt(mixed_rel, permute).astype(LOW)

    def weight_grad(left, right):
        send = dot_tn(left[:, half:], right).astype(LOW)
        return dot_tn(left[:, :half], right).astype(LOW), swap_dp(send, 1)

    outer = weight_grad(grad_two_low, activation)
    grad_pre, sums_inner = run(
        hidden_back_kernel,
        [shape_of(own_rows, full_inner, LOW), shape_of(1, full_inner, F32)],
        [grad_two_low, e_own, e_far, f_own, f_far, slope],
        6 * unit,
    )
    a_keep, a_send, b_keep, b_send = split_core(*outer, hidden_half, after=[grad_pre])
    outer = a_keep, swap_dp(a_send, 2), b_keep, swap_tensor(b_send)
    inner = weight_grad(first_low, grad_pre)
    grad_one, grad_one_low, grad_attn, sums_one = run(
        norm_back_kernel,
        [wide, wide_low, wide_low, sums_shape],
        [grad_pre, c_own, c_far, d_own, d_far, grad_two, normed_one, inv_one, vec, b_own, b_far],
        6 * unit,
        after=[a_keep],
    )
    a_keep, a_send, b_keep, b_send = split_plane(*outer, after=[grad_attn])
    outer = a_keep, swap_tensor(a_send), b_keep, swap_dp(b_send, 2)
    inner_keep = split_core(*inner, hidden_half, after=[a_keep])
    grad_q, grad_k, grad_v = run(
        attend_back_kernel,
        [wide_low, group_low, group_low],
        [seg_own, seg_keys, queries, key_rows, value_rows, grad_attn],
        25 * unit,
        after=[a_keep, inner_keep[0]],
        grid=(pairs,),
        in_specs=[fixed((1, own_rows)), fixed((group_rows, 1))]
        + [own_block, all_block, all_block, own_block],
        out_specs=[own_block, all_block, all_block],
    )
    outer = send_high(split_high(*outer, after=[grad_q]))
    a_keep, a_send, b_keep, b_send = inner_keep
    inner = a_keep, swap_dp(a_send, 2), b_keep, swap_tensor(b_send)
    one_shape = shape_of(half, 2 * a_width + 4 * part, LOW)
    one_send, one_keep = run(
        functools.partial(first_grads_kernel, a_width),
        [one_shape, one_shape],
        [rank, permute, rows_all, grad_q, grad_k, grad_v, grad_one_low, attended]
        + [sums_one, sums_two, sums_inner],
        6 * unit,
        after=outer[:1],
        in_specs=[scalar] + [vmem] * 10,
        scratch=[pltpu.VMEM((16, width), F32), pltpu.VMEM((LANES, width), F32)],
    )
    one_far = swap_dp(one_send, 1)
    a_keep, a_send, b_keep, b_send = split_plane(*inner, after=[one_keep])
    inner = a_keep, swap_tensor(a_send), b_keep, swap_dp(b_send, 2)
    grad_own, grad_away = run(
        rows_back_kernel,
        [wide, wide_low],
        [grad_q, grad_k, grad_v, a_own, a_far, b_own, b_far, grad_one],
        5 * unit,
        after=[a_keep] + outer[1:],
    )
    grad_rel = grad_own + swap_tensor(grad_away).astype(F32)
    input_grad = lax.dot_general(
        grad_rel, permute_wide, (((1,), (1,)), ((), ())), precision=exact
    )
    summed_back = reduce_high(outer).T
    inner = send_high(split_high(*inner, after=[grad_own]))
    one_keep = split_core(one_keep, one_far, 2 * a_width, after=inner[:1])
    a_keep, a_send, b_keep, b_send = one_keep
    one = a_keep, swap_dp(a_send, 2), b_keep, swap_tensor(b_send)
    summed_in = reduce_high(inner)
    a_keep, a_send, b_keep, b_send = split_plane(*one)
    one = a_keep, swap_tensor(a_send), b_keep, swap_dp(b_send, 2)
    sum_one = reduce_high(send_high(split_high(*one, after=inner[1:])))

    summed_vectors = lax.dynamic_slice_in_dim(
        sum_one[:, 2 * part : a_width], tensor_rank * shard_width, shard_width, axis=0
    )[:, :count].T
    summed_qkv = jnp.stack(
        [
            sum_one[:, :part],
            sum_one[:, part : 2 * part],
            sum_one[:, a_width : a_width + part],
        ]
    )
    summed_out = sum_one[:, a_width + part :].T
    new_qkv, moment_qkv, square_qkv = adamw(
        w_qkv, m_qkv, v_qkv, summed_qkv, float(width) ** (-0.5), WEIGHT_DECAY
    )
    new_out, moment_out, square_out = adamw(
        w_out, m_out, v_out, summed_out, (4.0 * width / group_rows) ** (-0.5), WEIGHT_DECAY
    )
    new_in, moment_in, square_in = adamw(
        w_in, m_in, v_in, summed_in, float(width) ** (-0.5), WEIGHT_DECAY
    )
    new_back, moment_back, square_back = adamw(
        w_back, m_back, v_back, summed_back, float(full_inner) ** (-0.5), WEIGHT_DECAY
    )
    new_vectors, moment_vectors, square_vectors = adamw(
        vectors, m_vectors, v_vectors, summed_vectors, 0.1, 0.0
    )
    return (
        mixed,
        input_grad,
        new_qkv,
        moment_qkv,
        square_qkv,
        new_out,
        moment_out,
        square_out,
        new_in,
        moment_in,
        square_in,
        new_back,
        moment_back,
        square_back,
        new_vectors,
        moment_vectors,
        square_vectors,
    )


def solution(mesh):
    placed = (
        P(("dp", "tensor"), None),
        P(("dp", "tensor"), None),
        P("dp", None),
        P(None, "dp", "tensor"),
        P(None, "dp", "tensor"),
        P(None, "dp", "tensor"),
        P("tensor", "dp"),
        P("tensor", "dp"),
        P("tensor", "dp"),
        P("dp", "tensor"),
        P("dp", "tensor"),
        P("dp", "tensor"),
        P("tensor", "dp"),
        P("tensor", "dp"),
        P("tensor", "dp"),
        P(None, ("dp", "tensor")),
        P(None, ("dp", "tensor")),
        P(None, ("dp", "tensor")),
    )
    return jax.shard_map(
        on_device,
        mesh=mesh,
        in_specs=placed,
        out_specs=(
            P(("dp", "tensor"), None),
            P(("dp", "tensor"), None),
            P(None, "dp", "tensor"),
            P(None, "dp", "tensor"),
            P(None, "dp", "tensor"),
            P("tensor", "dp"),
            P("tensor", "dp"),
            P("tensor", "dp"),
            P("dp", "tensor"),
            P("dp", "tensor"),
            P("dp", "tensor"),
            P("tensor", "dp"),
            P("tensor", "dp"),
            P("tensor", "dp"),
            P(None, ("dp", "tensor")),
            P(None, ("dp", "tensor")),
            P(None, ("dp", "tensor")),
        ),
        check_vma=False,
    )
```

```python
import functools

import numpy as np

import jax
import jax.numpy as jnp
from jax import lax
from jax.experimental import pallas as pl
from jax.experimental.pallas import tpu as pltpu
from jax.sharding import PartitionSpec as P

HEAD_DIM = 64
LANES = 128
STEP = 10


EPS_NORM = 1e-05
BETA_ONE = 0.9
BETA_TWO = 0.999
EPS_ADAM = 1e-08
WEIGHT_DECAY = 0.01
NEG_FILL = -1000000000.0
LOW = jnp.bfloat16
F32 = jnp.float32


def normalize_fwd(values, gain_row, shift_row):
    row_mean = jnp.mean(values, axis=-1, keepdims=True)
    centered = values - row_mean
    variance = jnp.mean(centered * centered, axis=-1, keepdims=True)
    inv_std = lax.rsqrt(variance + EPS_NORM)
    normed = centered * inv_std
    return (normed * gain_row + shift_row, normed, inv_std)


def normalize_back(gradient, normed, inv_std, gain_row):
    grad_norm = gradient * gain_row
    grad_in = inv_std * (
        grad_norm
        - jnp.mean(grad_norm, axis=-1, keepdims=True)
        - normed * jnp.mean(grad_norm * normed, axis=-1, keepdims=True)
    )
    return (grad_in, jnp.sum(gradient * normed, axis=0), jnp.sum(gradient, axis=0))


def adamw(weight, moment, square, gradient, step_rate, decay_rate):
    moment = BETA_ONE * moment + (1.0 - BETA_ONE) * gradient
    square = BETA_TWO * square + (1.0 - BETA_TWO) * gradient * gradient
    direction = (
        moment / (1.0 - BETA_ONE**STEP) / (jnp.sqrt(square / (1.0 - BETA_TWO**STEP)) + EPS_ADAM)
    )
    return (weight - step_rate * (direction + decay_rate * weight), moment, square)


def swap_dp(values, mask):
    size = lax.axis_size("dp")
    return lax.ppermute(values, "dp", [(i, i ^ mask) for i in range(size)])


def swap_tensor(values):
    return lax.ppermute(values, "tensor", [(0, 1), (1, 0)])


def high_bits():
    return list(range(2, lax.axis_size("dp").bit_length() - 1))


def high_groups():
    bits = high_bits()
    return [[1 << bit for bit in bits[i : i + 2]] for i in range(0, len(bits), 2)]


def group_masks(group):
    return [0] + group + ([group[0] ^ group[1]] if len(group) == 2 else [])


def gather_high(shard):
    groups = high_groups()
    for place, group in enumerate(groups):
        pieces = [shard if mask == 0 else swap_dp(shard, mask) for mask in group_masks(group)]
        if place < len(groups) - 1:
            shard = jnp.concatenate(pieces, axis=0)
    return pieces


def send_high(parts):
    masks = group_masks(high_groups()[-1])
    return [parts[0]] + [swap_dp(part, mask) for part, mask in zip(parts[1:], masks[1:])]


def reduce_high(parts):
    total = sum(part.astype(F32) for part in parts)
    for group in reversed(high_groups()[:-1]):
        masks = group_masks(group)
        rows = total.shape[0] // len(masks)
        low = total.astype(LOW)
        total = total[:rows]
        for place, mask in enumerate(masks[1:], 1):
            total = total + swap_dp(low[place * rows : (place + 1) * rows], mask).astype(F32)
    return total


def relative_order(width):
    size = lax.axis_size("dp")
    rows = width // size
    inner_first = high_bits() + [1, 0]
    masks = np.zeros((size,), np.int32)
    for block in range(size):
        for place, bit in enumerate(inner_first):
            if (block >> place) & 1:
                masks[block] |= 1 << bit
    block_mask = jnp.asarray(np.repeat(masks, rows))
    offsets = jnp.asarray(np.tile(np.arange(rows, dtype=np.int32), size))
    return (lax.axis_index("dp") ^ block_mask) * rows + offsets


def dot(left, right):
    return jnp.dot(left, right, preferred_element_type=F32)


def dot_nt(left, right):
    return lax.dot_general(left, right, (((1,), (1,)), ((), ())), preferred_element_type=F32)


def dot_tn(left, right):
    return lax.dot_general(left, right, (((0,), (0,)), ((), ())), preferred_element_type=F32)


def shape_of(rows, columns, kind):
    return jax.ShapeDtypeStruct((rows, columns), kind)


def run(kernel, outs, operands, flops, after=(), grid=(), in_specs=None, out_specs=None, scratch=()):
    count = len(operands)

    def body(*refs):
        kernel(*refs[:count], *refs[count + len(after) :])

    whole = pl.BlockSpec(memory_space=pltpu.VMEM)
    in_specs = in_specs or [whole] * count
    size = sum(v.size * v.dtype.itemsize for v in list(operands) + list(outs))
    return pl.pallas_call(
        body,
        grid=grid,
        out_shape=list(outs),
        in_specs=list(in_specs) + [pl.BlockSpec(memory_space=pl.ANY)] * len(after),
        out_specs=list(out_specs or [whole] * len(outs)),
        scratch_shapes=list(scratch),
        compiler_params=pltpu.CompilerParams(
            vmem_limit_bytes=min(size + ((12 if flops else 4) << 20), 44 << 20)
        ),
        cost_estimate=pl.CostEstimate(flops=flops, bytes_accessed=size, transcendentals=0),
    )(*operands, *after)


def join_high_kernel(count, *refs):
    pieces, (first, second) = refs[:count], refs[count:]
    cut = first.shape[1]
    rows = pieces[0].shape[0]
    for place, piece in enumerate(pieces):
        to = slice(place * rows, (place + 1) * rows)
        first[to, :] = piece[:, :cut]
        second[to, :] = piece[:, cut:]


def join_high(pieces, cut, after=()):
    rows, columns = pieces[0].shape
    rows = rows * len(pieces)
    return run(
        functools.partial(join_high_kernel, len(pieces)),
        [shape_of(rows, cut, LOW), shape_of(rows, columns - cut, LOW)],
        pieces,
        0,
        after,
    )


def join_plane_kernel(across, down, across_far, down_far, across_all, down_all):
    columns, rows = across.shape[1], down.shape[0]
    across_all[:, :columns] = across[...]
    across_all[:, columns:] = across_far[...]
    down_all[:rows, :] = down[...]
    down_all[rows:, :] = down_far[...]


def join_plane(across, down, across_far, down_far, after=()):
    return run(
        join_plane_kernel,
        [
            shape_of(across.shape[0], 2 * across.shape[1], LOW),
            shape_of(2 * down.shape[0], down.shape[1], LOW),
        ],
        [across, down, across_far, down_far],
        0,
        after,
    )


def added(left, right, rows, columns):
    return (left[rows, columns].astype(F32) + right[rows, columns].astype(F32)).astype(LOW)


def split_core_kernel(keep, far, a_keep, a_send, b_keep, b_send):
    rows, cut = a_keep.shape
    half = b_keep.shape[1]
    every = slice(None)
    a_keep[...] = added(keep, far, slice(0, rows), slice(0, cut))
    a_send[...] = added(keep, far, slice(rows, 2 * rows), slice(0, cut))
    b_keep[...] = added(keep, far, every, slice(cut, cut + half))
    b_send[...] = added(keep, far, every, slice(cut + half, cut + 2 * half))


def split_core(keep, far, cut, after=()):
    rows, columns = keep.shape
    a_shape = shape_of(rows // 2, cut, LOW)
    b_shape = shape_of(rows, (columns - cut) // 2, LOW)
    return run(
        split_core_kernel, [a_shape, a_shape, b_shape, b_shape], [keep, far], 0, after
    )


def split_plane_kernel(a, a_far, b, b_far, a_keep, a_send, b_keep, b_send):
    half, rows = a_keep.shape[1], b_keep.shape[0]
    every = slice(None)
    a_keep[...] = added(a, a_far, every, slice(0, half))
    a_send[...] = added(a, a_far, every, slice(half, 2 * half))
    b_keep[...] = added(b, b_far, slice(0, rows), every)
    b_send[...] = added(b, b_far, slice(rows, 2 * rows), every)


def split_plane(a, a_far, b, b_far, after=()):
    a_shape = shape_of(a.shape[0], a.shape[1] // 2, LOW)
    b_shape = shape_of(b.shape[0] // 2, b.shape[1], LOW)
    return run(
        split_plane_kernel, [a_shape, a_shape, b_shape, b_shape], [a, a_far, b, b_far], 0, after
    )


def split_high_kernel(a, a_far, b, b_far, *parts):
    cut = a.shape[1]
    rows = parts[0].shape[0]
    for place, part in enumerate(parts):
        at = slice(place * rows, (place + 1) * rows)
        part[:, :cut] = added(a, a_far, at, slice(None))
        part[:, cut:] = added(b, b_far, at, slice(None))


def split_high(a, a_far, b, b_far, after=()):
    count = len(group_masks(high_groups()[-1]))
    part = shape_of(a.shape[0] // count, a.shape[1] + b.shape[1], LOW)
    return run(split_high_kernel, [part] * count, [a, a_far, b, b_far], 0, after)


def flip(rank, first, second):
    return jnp.where(rank == 0, first, second)


def vectors_kernel(rank_ref, permute, a_own, a_far, relative, bias_q, bias_v, bias_inner):
    rank = rank_ref[0]
    side = a_own.shape[1] // 2
    width = relative.shape[1]
    half = width // 2
    spread = jnp.concatenate(
        [
            (ref[:, side - LANES : side].astype(F32) + ref[:, 2 * side - LANES :].astype(F32))
            for ref in (a_own, a_far)
        ],
        axis=0,
    )
    parts = jnp.transpose(spread)
    parts = [parts[16 * i : 16 * (i + 1)] for i in range(3)]
    relative[...] = ((parts[0] + parts[1]) + parts[2])[2:8]
    natural = [dot_nt(part.astype(LOW), permute[...]) for part in parts]
    natural = (natural[0] + natural[1]) + natural[2]
    for row, target in ((0, bias_q), (1, bias_v)):
        first, second = natural[row : row + 1, :half], natural[row : row + 1, half:]
        target[:, :half] = flip(rank, first, second)
        target[:, half:] = flip(rank, second, first)
    for cut in range(2):
        for place in range(2):
            near, far = 8 + 2 * place + cut, 8 + 2 * (1 - place) + cut
            at = (2 * cut + place) * width
            bias_inner[:, at : at + width] = flip(
                rank, natural[near : near + 1], natural[far : far + 1]
            )


def vector_lanes(rank, permute, grad_q, grad_v, sums_one, sums_two, sums_inner, natural, relative):
    width = natural.shape[1]
    half = width // 2
    natural[...] = jnp.zeros_like(natural)
    relative[...] = jnp.zeros_like(relative)
    for row, source in ((0, grad_q), (1, grad_v)):
        total = jnp.sum(source[...].astype(F32), axis=0, keepdims=True)
        first, second = total[:, :half], total[:, half:]
        natural[row : row + 1, :half] = flip(rank, first, second)
        natural[row : row + 1, half:] = flip(rank, second, first)
    for cut in range(2):
        for place in range(2):
            near, far = (2 * cut + place) * width, (2 * cut + 1 - place) * width
            row = 8 + 2 * place + cut
            natural[row : row + 1, :] = flip(
                rank, sums_inner[:, near : near + width], sums_inner[:, far : far + width]
            )
    relative[:16, :] = dot(natural[...].astype(LOW), permute[...])
    relative[2:5, :] = sums_one[:3, :]
    relative[5:8, :] = sums_two[:3, :]
    return jnp.transpose(relative[...]).astype(LOW)


def cast_kernel(source, target):
    target[...] = source[...].astype(LOW)


def project_kernel(rows, a_own, a_far, b_own, b_far, bias_q, bias_v, q, k, v):
    half = a_own.shape[0]
    own_rows, width = q.shape
    part = width // 2
    low, high = rows[:, :half], rows[:, half:]
    a_half, b_half = a_own.shape[1] // 2, b_own.shape[1] // 2
    for side in range(2):
        cols = slice(side * part, (side + 1) * part)
        at = slice(side * a_half, side * a_half + part)
        q[:, cols] = (
            dot(low[:own_rows], a_own[:, at]) + dot(high[:own_rows], a_far[:, at]) + bias_q[:, cols]
        ).astype(LOW)
        at = slice(side * a_half + part, side * a_half + 2 * part)
        k[:, cols] = (dot(low, a_own[:, at]) + dot(high, a_far[:, at])).astype(LOW)
        at = slice(side * b_half, side * b_half + part)
        v[:, cols] = (dot(low, b_own[:, at]) + dot(high, b_far[:, at]) + bias_v[:, cols]).astype(
            LOW
        )


def softmax_down(seg_q, seg_k, key_rows, queries):
    scores = dot_nt(key_rows, queries) * 0.125
    scores = jnp.where(seg_k[...] == seg_q[...], scores, NEG_FILL)
    exp_scores = jnp.exp(scores - jnp.max(scores, axis=0, keepdims=True))
    return exp_scores * (1.0 / jnp.sum(exp_scores, axis=0, keepdims=True))


def two_heads(out):
    joined = jnp.concatenate([out[0][:HEAD_DIM], out[1][HEAD_DIM:]], axis=0)
    return jnp.transpose(joined).astype(LOW)


def attend_kernel(seg_q, seg_k, q, k, v, attended):
    queries, key_rows, value_rows = q[...], k[...], v[...]
    first = lax.broadcasted_iota(jnp.int32, queries.shape, 1) < HEAD_DIM
    out = []
    for mine in (first, jnp.logical_not(first)):
        prob = softmax_down(
            seg_q, seg_k, key_rows, jnp.where(mine, queries, jnp.zeros_like(queries))
        )
        out.append(dot_tn(value_rows, prob.astype(LOW)))
    attended[...] = two_heads(out)


def attend_back_kernel(seg_q, seg_k, q, k, v, grad, grad_q, grad_k, grad_v):
    queries, key_rows, value_rows, grad_rows = q[...], k[...], v[...], grad[...]
    first = lax.broadcasted_iota(jnp.int32, queries.shape, 1) < HEAD_DIM
    first_all = lax.broadcasted_iota(jnp.int32, key_rows.shape, 1) < HEAD_DIM
    blank = jnp.zeros_like(queries)
    out_q, out_k, out_v = [], [], []
    for mine in (first, jnp.logical_not(first)):
        prob = softmax_down(seg_q, seg_k, key_rows, jnp.where(mine, queries, blank))
        grad_prob = dot_nt(value_rows, jnp.where(mine, grad_rows, blank))
        delta = jnp.sum(grad_prob * prob, axis=0, keepdims=True)
        grad_score = (prob * (grad_prob - delta)).astype(LOW)
        out_q.append(dot_tn(key_rows, grad_score) * 0.125)
        out_k.append(dot(grad_score, queries) * 0.125)
        out_v.append(dot(prob.astype(LOW), grad_rows))
    grad_q[...] = two_heads(out_q)
    grad_k[...] = jnp.where(first_all, out_k[0], out_k[1]).astype(LOW)
    grad_v[...] = jnp.where(first_all, out_v[0], out_v[1]).astype(LOW)


def out_norm_kernel(attended, rows, b_own, b_far, vec, y, y_low, normed, inv):
    half = b_own.shape[0]
    own_rows, width = y.shape
    part = width // 2
    b_half = b_own.shape[1] // 2
    near, far = attended[:, :part], attended[:, part:]
    out = []
    for weights in (b_own, b_far):
        out.append(
            dot_nt(near, weights[:, part : 2 * part])
            + dot_nt(far, weights[:, b_half + part : b_half + 2 * part])
        )
    total = rows[:own_rows, :].astype(F32) + jnp.concatenate(out, axis=1) + vec[0:1]
    y_new, normed[...], inv[...] = normalize_fwd(total, vec[1:2], vec[2:3])
    y[...] = y_new
    y_low[...] = y_new.astype(LOW)


def hidden_kernel(y_low, a_own, a_far, b_own, b_far, bias, activation, slope):
    half = a_own.shape[0]
    low, high = y_low[:, :half], y_low[:, half:]
    columns = a_own.shape[1]
    step = columns // 4
    for place, (own, far) in enumerate(((a_own, a_far), (b_own, b_far))):
        for start in range(0, columns, step):
            at = slice(start, start + step)
            to = slice(place * columns + start, place * columns + start + step)
            pre = dot(low, own[:, at]) + dot(high, far[:, at]) + bias[:, to]
            cdf = 0.5 + 0.5 * lax.erf(pre * (0.5**0.5))
            activation[:, to] = (pre * cdf).astype(LOW)
            slope[:, to] = cdf + pre * jnp.exp(-0.5 * pre * pre) * ((2.0 * np.pi) ** -0.5)


def out_back_kernel(
    activation, a_own, a_far, b_own, b_far, y, cot, valid, vec, mixed, grad, grad_low, sums
):
    columns = a_own.shape[1]
    act_a, act_b = activation[:, :columns], activation[:, columns:]
    out = [dot_nt(act_a, wa[...]) + dot_nt(act_b, wb[...]) for wa, wb in ((a_own, b_own), (a_far, b_far))]
    total = y[...] + jnp.concatenate(out, axis=1) + vec[3:4]
    result, normed, inv_std = normalize_fwd(total, vec[4:5], vec[5:6])
    mixed[...] = result.astype(LOW)
    grad_in, gain_sum, shift_sum = normalize_back(
        cot[...] * valid[...], normed, inv_std, vec[4:5]
    )
    grad[...] = grad_in
    grad_low[...] = grad_in.astype(LOW)
    sums[0:1] = jnp.sum(grad_in, axis=0, keepdims=True)
    sums[1:2] = gain_sum[None]
    sums[2:3] = shift_sum[None]


def hidden_back_kernel(grad_low, a_own, a_far, b_own, b_far, slope, grad_pre, sums):
    half = a_own.shape[0]
    low, high = grad_low[:, :half], grad_low[:, half:]
    columns = a_own.shape[1]
    step = columns // 4
    for place, (own, far) in enumerate(((a_own, a_far), (b_own, b_far))):
        for start in range(0, columns, step):
            at = slice(start, start + step)
            to = slice(place * columns + start, place * columns + start + step)
            value = ((dot(low, own[:, at]) + dot(high, far[:, at])) * slope[:, to]).astype(LOW)
            grad_pre[:, to] = value
            sums[:, to] = jnp.sum(value.astype(F32), axis=0, keepdims=True)


def norm_back_kernel(
    grad_pre, a_own, a_far, b_own, b_far, grad_two, normed, inv, vec, o_own, o_far,
    grad, grad_low, grad_attn, sums,
):
    columns = a_own.shape[1]
    pre_a, pre_b = grad_pre[:, :columns], grad_pre[:, columns:]
    out = [dot_nt(pre_a, wa[...]) + dot_nt(pre_b, wb[...]) for wa, wb in ((a_own, b_own), (a_far, b_far))]
    grad_in, gain_sum, shift_sum = normalize_back(
        grad_two[...] + jnp.concatenate(out, axis=1), normed[...], inv[...], vec[1:2]
    )
    grad[...] = grad_in
    low = grad_in.astype(LOW)
    grad_low[...] = low
    sums[0:1] = jnp.sum(grad_in, axis=0, keepdims=True)
    sums[1:2] = gain_sum[None]
    sums[2:3] = shift_sum[None]
    half = o_own.shape[0]
    part = grad.shape[1] // 2
    o_half = o_own.shape[1] // 2
    for side in range(2):
        at = slice(side * o_half + part, side * o_half + 2 * part)
        grad_attn[:, side * part : (side + 1) * part] = (
            dot(low[:, :half], o_own[:, at]) + dot(low[:, half:], o_far[:, at])
        ).astype(LOW)


def rows_back_kernel(grad_q, grad_k, grad_v, a_own, a_far, b_own, b_far, grad_one, own, away):
    own_rows, width = own.shape
    part = width // 2
    a_half, b_half = a_own.shape[1] // 2, b_own.shape[1] // 2
    half = a_own.shape[0]
    for place, (wa, wb) in enumerate(((a_own, b_own), (a_far, b_far))):
        to = slice(place * half, (place + 1) * half)
        both = jnp.zeros((2 * own_rows, half), F32)
        mine = grad_one[:, to]
        for side in range(2):
            cols = slice(side * part, (side + 1) * part)
            at = side * a_half
            mine = mine + dot_nt(grad_q[:, cols], wa[:, at : at + part])
            both = both + dot_nt(grad_k[:, cols], wa[:, at + part : at + 2 * part])
            at = side * b_half
            both = both + dot_nt(grad_v[:, cols], wb[:, at : at + part])
        own[:, to] = mine + both[:own_rows]
        away[:, to] = both[own_rows:].astype(LOW)


def first_grads_kernel(
    a_half, rank_ref, permute, rows, grad_q, grad_k, grad_v, grad_low, attended,
    sums_one, sums_two, sums_inner, send, keep, natural, relative,
):
    half = keep.shape[0]
    own_rows, width = grad_q.shape
    part = width // 2
    extra = vector_lanes(
        rank_ref[0], permute, grad_q, grad_v, sums_one, sums_two, sums_inner, natural, relative
    )
    for place, to in ((1, send), (0, keep)):
        at = slice(place * half, (place + 1) * half)
        both = rows[:, at]
        mine = rows[:own_rows, at]
        low = grad_low[:, at]
        for side in range(2):
            cols = slice(side * part, (side + 1) * part)
            base = side * a_half
            to[:, base : base + part] = dot_tn(mine, grad_q[:, cols]).astype(LOW)
            to[:, base + part : base + 2 * part] = dot_tn(both, grad_k[:, cols]).astype(LOW)
            to[:, base + 2 * part : base + a_half] = extra[at, :]
            base = 2 * a_half + side * 2 * part
            to[:, base : base + part] = dot_tn(both, grad_v[:, cols]).astype(LOW)
            to[:, base + part : base + 2 * part] = dot_tn(low, attended[:, cols]).astype(LOW)


def on_device(
    tokens,
    cotangent,
    lengths,
    w_qkv,
    m_qkv,
    v_qkv,
    w_out,
    m_out,
    v_out,
    w_in,
    m_in,
    v_in,
    w_back,
    m_back,
    v_back,
    vectors,
    m_vectors,
    v_vectors,
):
    own_rows, width = tokens.shape
    tensor_rank = lax.axis_index("tensor")
    group_rows = 2 * own_rows
    shard_rows = w_qkv.shape[1]
    part = w_qkv.shape[2]
    hidden_half = w_in.shape[1]
    cut = hidden_half // 2
    full_inner = 2 * hidden_half
    half = width // 2
    count = vectors.shape[0]
    shard_width = vectors.shape[1]

    rest = vectors.T
    vec_parts = []
    for _ in range(3):
        vec_parts.append(jnp.pad(rest.astype(LOW), ((0, 0), (0, 16 - count))))
        rest = rest - rest.astype(LOW).astype(F32)
    vec_lanes = jnp.pad(jnp.concatenate(vec_parts, axis=1), ((0, 0), (0, LANES - 48)))
    blank = jnp.zeros_like(vec_lanes)
    vec_lanes = jnp.concatenate(
        [
            jnp.where(tensor_rank == 0, vec_lanes, blank),
            jnp.where(tensor_rank == 0, blank, vec_lanes),
        ],
        axis=0,
    )
    low_qkv = w_qkv.astype(LOW)
    shard_one = jnp.concatenate(
        [low_qkv[0], low_qkv[1], vec_lanes, low_qkv[2], w_out.T.astype(LOW)], axis=1
    )
    a_width = 2 * part + LANES
    low_shape = shape_of(shard_rows, hidden_half, LOW)
    rank = tensor_rank.astype(jnp.int32).reshape(1)
    scalar = pl.BlockSpec(memory_space=pltpu.SMEM)
    vmem = pl.BlockSpec(memory_space=pltpu.VMEM)

    tokens_far = swap_tensor(tokens)
    one_high = gather_high(shard_one)
    one = join_high(one_high, a_width)
    one_far = swap_tensor(one[0]), swap_dp(one[1], 2)
    shard_in = run(cast_kernel, [low_shape], [w_in], 0, after=one[:1])[0]
    inner_high = gather_high(shard_in)

    order = relative_order(width)
    permute = (jnp.arange(width, dtype=jnp.int32)[:, None] == order[None, :]).astype(LOW)
    permute_wide = permute.astype(F32)
    exact = lax.Precision.HIGHEST
    rows_all = jnp.concatenate([dot(tokens, permute), dot(tokens_far, permute)]).astype(LOW)
    cot = dot(cotangent, permute)

    one = join_plane(*one, *one_far, after=[shard_in, rows_all])
    one_far = swap_dp(one[0], 2), swap_tensor(one[1])
    inner = join_high(inner_high, cut, after=one[:1])
    shard_back = run(cast_kernel, [low_shape], [w_back.T], 0, after=inner[:1])[0]
    outer_high = gather_high(shard_back)
    one = join_plane(one[1], one[0], one_far[1], one_far[0], after=[shard_back])[::-1]
    a_own, b_own = one
    a_far, b_far = swap_dp(a_own, 1), swap_dp(b_own, 1)
    inner_far = swap_tensor(inner[0]), swap_dp(inner[1], 2)
    outer = join_high(outer_high, cut, after=[a_own])
    inner = join_plane(*inner, *inner_far, after=[a_own])
    inner_far = swap_dp(inner[0], 2), swap_tensor(inner[1])
    outer_far = swap_tensor(outer[0]), swap_dp(outer[1], 2)

    vec, bias_query, bias_value, bias_inner = run(
        vectors_kernel,
        [
            shape_of(6, width, F32),
            shape_of(1, width, F32),
            shape_of(1, width, F32),
            shape_of(1, full_inner, F32),
        ],
        [rank, permute, a_own, a_far],
        1,
        in_specs=[scalar, vmem, vmem, vmem],
    )

    seq_ends = jnp.cumsum(lengths[0])
    local = jnp.arange(own_rows, dtype=jnp.int32)
    own_positions = tensor_rank * own_rows + local
    key_positions = jnp.concatenate([own_positions, (1 - tensor_rank) * own_rows + local])

    def segments(positions):
        return jnp.sum((positions[:, None] >= seq_ends[None, :]).astype(jnp.int32), axis=1)

    seg_own, seg_keys = segments(own_positions)[None, :], segments(key_positions)[:, None]
    valid = (own_positions < seq_ends[-1]).astype(F32)[:, None]

    wide_low = shape_of(own_rows, width, LOW)
    wide = shape_of(own_rows, width, F32)
    group_low = shape_of(group_rows, width, LOW)
    sums_shape = shape_of(8, width, F32)
    unit = 2 * own_rows * width * width
    queries, key_rows, value_rows = run(
        project_kernel,
        [wide_low, group_low, group_low],
        [rows_all, a_own, a_far, b_own, b_far, bias_query, bias_value],
        5 * unit,
        after=[inner[0], outer[0]],
    )
    pairs = width // LANES
    own_block = pl.BlockSpec((own_rows, LANES), lambda i: (0, i))
    all_block = pl.BlockSpec((group_rows, LANES), lambda i: (0, i))

    def fixed(shape):
        return pl.BlockSpec(shape, lambda i: (0, 0))

    attended = run(
        attend_kernel,
        [wide_low],
        [seg_own, seg_keys, queries, key_rows, value_rows],
        3 * unit,
        grid=(pairs,),
        in_specs=[fixed((1, own_rows)), fixed((group_rows, 1)), own_block, all_block, all_block],
        out_specs=[own_block],
    )[0]
    inner = join_plane(inner[1], inner[0], inner_far[1], inner_far[0], after=[attended])[::-1]
    c_own, d_own = inner
    c_far, d_far = swap_dp(c_own, 1), swap_dp(d_own, 1)
    outer = join_plane(*outer, *outer_far, after=[attended])
    outer_far = swap_dp(outer[0], 2), swap_tensor(outer[1])
    first_norm, first_low, normed_one, inv_one = run(
        out_norm_kernel,
        [wide, wide_low, wide, shape_of(own_rows, 1, F32)],
        [attended, rows_all, b_own, b_far, vec],
        400 * unit,
        after=[inner[0], outer[0]],
    )
    activation, slope = run(
        hidden_kernel,
        [shape_of(own_rows, full_inner, LOW), shape_of(own_rows, full_inner, F32)],
        [first_low, c_own, c_far, d_own, d_far, bias_inner],
        8 * unit,
    )
    outer = join_plane(outer[1], outer[0], outer_far[1], outer_far[0], after=[activation])[::-1]
    e_own, f_own = outer
    e_far, f_far = swap_dp(e_own, 1), swap_dp(f_own, 1)
    mixed_rel, grad_two, grad_two_low, sums_two = run(
        out_back_kernel,
        [wide_low, wide, wide_low, sums_shape],
        [activation, e_own, e_far, f_own, f_far, first_norm, cot, valid, vec],
        5 * unit,
    )
    mixed = dot_nt(mixed_rel, permute).astype(LOW)

    def weight_grad(left, right):
        send = dot_tn(left[:, half:], right).astype(LOW)
        return dot_tn(left[:, :half], right).astype(LOW), swap_dp(send, 1)

    outer = weight_grad(grad_two_low, activation)
    grad_pre, sums_inner = run(
        hidden_back_kernel,
        [shape_of(own_rows, full_inner, LOW), shape_of(1, full_inner, F32)],
        [grad_two_low, e_own, e_far, f_own, f_far, slope],
        6 * unit,
    )
    a_keep, a_send, b_keep, b_send = split_core(*outer, hidden_half, after=[grad_pre])
    outer = a_keep, swap_dp(a_send, 2), b_keep, swap_tensor(b_send)
    inner = weight_grad(first_low, grad_pre)
    inner_keep = split_core(*inner, hidden_half, after=[a_keep])
    a_keep, a_send, b_keep, b_send = inner_keep
    inner = a_keep, swap_dp(a_send, 2), b_keep, swap_tensor(b_send)
    grad_one, grad_one_low, grad_attn, sums_one = run(
        norm_back_kernel,
        [wide, wide_low, wide_low, sums_shape],
        [grad_pre, c_own, c_far, d_own, d_far, grad_two, normed_one, inv_one, vec, b_own, b_far],
        6 * unit,
        after=[a_keep],
    )
    grad_q, grad_k, grad_v = run(
        attend_back_kernel,
        [wide_low, group_low, group_low],
        [seg_own, seg_keys, queries, key_rows, value_rows, grad_attn],
        25 * unit,
        grid=(pairs,),
        in_specs=[fixed((1, own_rows)), fixed((group_rows, 1))]
        + [own_block, all_block, all_block, own_block],
        out_specs=[own_block, all_block, all_block],
    )
    a_keep, a_send, b_keep, b_send = split_plane(*outer, after=[grad_q])
    outer = a_keep, swap_tensor(a_send), b_keep, swap_dp(b_send, 2)
    one_shape = shape_of(half, 2 * a_width + 4 * part, LOW)
    one_send, one_keep = run(
        functools.partial(first_grads_kernel, a_width),
        [one_shape, one_shape],
        [rank, permute, rows_all, grad_q, grad_k, grad_v, grad_one_low, attended]
        + [sums_one, sums_two, sums_inner],
        6 * unit,
        after=[a_keep],
        in_specs=[scalar] + [vmem] * 10,
        scratch=[pltpu.VMEM((16, width), F32), pltpu.VMEM((LANES, width), F32)],
    )
    one_far = swap_dp(one_send, 1)
    a_keep, a_send, b_keep, b_send = split_plane(*inner, after=[one_keep])
    inner = a_keep, swap_tensor(a_send), b_keep, swap_dp(b_send, 2)
    grad_own, grad_away = run(
        rows_back_kernel,
        [wide, wide_low],
        [grad_q, grad_k, grad_v, a_own, a_far, b_own, b_far, grad_one],
        400 * unit,
        after=[a_keep],
    )
    grad_rel = grad_own + swap_tensor(grad_away).astype(F32)
    input_grad = lax.dot_general(
        grad_rel, permute_wide, (((1,), (1,)), ((), ())), precision=exact
    )
    one_keep = split_core(one_keep, one_far, 2 * a_width, after=[grad_own])
    outer = send_high(split_high(*outer, after=one_keep[:1]))
    inner = send_high(split_high(*inner, after=outer[:1]))
    summed_back = reduce_high(outer).T
    a_keep, a_send, b_keep, b_send = one_keep
    one = a_keep, swap_dp(a_send, 2), b_keep, swap_tensor(b_send)
    summed_in = reduce_high(inner)
    a_keep, a_send, b_keep, b_send = split_plane(*one, after=inner[:1] + outer[1:])
    one = a_keep, swap_tensor(a_send), b_keep, swap_dp(b_send, 2)
    sum_one = reduce_high(send_high(split_high(*one, after=inner[1:])))

    summed_vectors = lax.dynamic_slice_in_dim(
        sum_one[:, 2 * part : a_width], tensor_rank * shard_width, shard_width, axis=0
    )[:, :count].T
    summed_qkv = jnp.stack(
        [
            sum_one[:, :part],
            sum_one[:, part : 2 * part],
            sum_one[:, a_width : a_width + part],
        ]
    )
    summed_out = sum_one[:, a_width + part :].T
    new_qkv, moment_qkv, square_qkv = adamw(
        w_qkv, m_qkv, v_qkv, summed_qkv, float(width) ** (-0.5), WEIGHT_DECAY
    )
    new_out, moment_out, square_out = adamw(
        w_out, m_out, v_out, summed_out, (4.0 * width / group_rows) ** (-0.5), WEIGHT_DECAY
    )
    new_in, moment_in, square_in = adamw(
        w_in, m_in, v_in, summed_in, float(width) ** (-0.5), WEIGHT_DECAY
    )
    new_back, moment_back, square_back = adamw(
        w_back, m_back, v_back, summed_back, float(full_inner) ** (-0.5), WEIGHT_DECAY
    )
    new_vectors, moment_vectors, square_vectors = adamw(
        vectors, m_vectors, v_vectors, summed_vectors, 0.1, 0.0
    )
    return (
        mixed,
        input_grad,
        new_qkv,
        moment_qkv,
        square_qkv,
        new_out,
        moment_out,
        square_out,
        new_in,
        moment_in,
        square_in,
        new_back,
        moment_back,
        square_back,
        new_vectors,
        moment_vectors,
        square_vectors,
    )


def solution(mesh):
    placed = (
        P(("dp", "tensor"), None),
        P(("dp", "tensor"), None),
        P("dp", None),
        P(None, "dp", "tensor"),
        P(None, "dp", "tensor"),
        P(None, "dp", "tensor"),
        P("tensor", "dp"),
        P("tensor", "dp"),
        P("tensor", "dp"),
        P("dp", "tensor"),
        P("dp", "tensor"),
        P("dp", "tensor"),
        P("tensor", "dp"),
        P("tensor", "dp"),
        P("tensor", "dp"),
        P(None, ("dp", "tensor")),
        P(None, ("dp", "tensor")),
        P(None, ("dp", "tensor")),
    )
    return jax.shard_map(
        on_device,
        mesh=mesh,
        in_specs=placed,
        out_specs=(
            P(("dp", "tensor"), None),
            P(("dp", "tensor"), None),
            P(None, "dp", "tensor"),
            P(None, "dp", "tensor"),
            P(None, "dp", "tensor"),
            P("tensor", "dp"),
            P("tensor", "dp"),
            P("tensor", "dp"),
            P("dp", "tensor"),
            P("dp", "tensor"),
            P("dp", "tensor"),
            P("tensor", "dp"),
            P("tensor", "dp"),
            P("tensor", "dp"),
            P(None, ("dp", "tensor")),
            P(None, ("dp", "tensor")),
            P(None, ("dp", "tensor")),
        ),
        check_vma=False,
    )
```

```python
import functools

import numpy as np

import jax
import jax.numpy as jnp
from jax import lax
from jax.experimental import pallas as pl
from jax.experimental.pallas import tpu as pltpu
from jax.sharding import PartitionSpec as P

HEAD_DIM = 64
LANES = 128
STEP = 10


EPS_NORM = 1e-05
BETA_ONE = 0.9
BETA_TWO = 0.999
EPS_ADAM = 1e-08
WEIGHT_DECAY = 0.01
NEG_FILL = -1000000000.0
LOW = jnp.bfloat16
F32 = jnp.float32


def normalize_fwd(values, gain_row, shift_row):
    row_mean = jnp.mean(values, axis=-1, keepdims=True)
    centered = values - row_mean
    variance = jnp.mean(centered * centered, axis=-1, keepdims=True)
    inv_std = lax.rsqrt(variance + EPS_NORM)
    normed = centered * inv_std
    return (normed * gain_row + shift_row, normed, inv_std)


def normalize_back(gradient, normed, inv_std, gain_row):
    grad_norm = gradient * gain_row
    grad_in = inv_std * (
        grad_norm
        - jnp.mean(grad_norm, axis=-1, keepdims=True)
        - normed * jnp.mean(grad_norm * normed, axis=-1, keepdims=True)
    )
    return (grad_in, jnp.sum(gradient * normed, axis=0), jnp.sum(gradient, axis=0))


def adamw(weight, moment, square, gradient, step_rate, decay_rate):
    moment = BETA_ONE * moment + (1.0 - BETA_ONE) * gradient
    square = BETA_TWO * square + (1.0 - BETA_TWO) * gradient * gradient
    direction = (
        moment / (1.0 - BETA_ONE**STEP) / (jnp.sqrt(square / (1.0 - BETA_TWO**STEP)) + EPS_ADAM)
    )
    return (weight - step_rate * (direction + decay_rate * weight), moment, square)


def swap_dp(values, mask):
    size = lax.axis_size("dp")
    return lax.ppermute(values, "dp", [(i, i ^ mask) for i in range(size)])


def swap_tensor(values):
    return lax.ppermute(values, "tensor", [(0, 1), (1, 0)])


def high_bits():
    return list(range(2, lax.axis_size("dp").bit_length() - 1))


def high_groups():
    bits = high_bits()
    return [[1 << bit for bit in bits[i : i + 2]] for i in range(0, len(bits), 2)]


def group_masks(group):
    return [0] + group + ([group[0] ^ group[1]] if len(group) == 2 else [])


def gather_high(shard):
    groups = high_groups()
    for place, group in enumerate(groups):
        pieces = [shard if mask == 0 else swap_dp(shard, mask) for mask in group_masks(group)]
        if place < len(groups) - 1:
            shard = jnp.concatenate(pieces, axis=0)
    return pieces


def send_high(parts):
    masks = group_masks(high_groups()[-1])
    return [parts[0]] + [swap_dp(part, mask) for part, mask in zip(parts[1:], masks[1:])]


def reduce_high(parts):
    total = sum(part.astype(F32) for part in parts)
    for group in reversed(high_groups()[:-1]):
        masks = group_masks(group)
        rows = total.shape[0] // len(masks)
        low = total.astype(LOW)
        total = total[:rows]
        for place, mask in enumerate(masks[1:], 1):
            total = total + swap_dp(low[place * rows : (place + 1) * rows], mask).astype(F32)
    return total


def relative_order(width):
    size = lax.axis_size("dp")
    rows = width // size
    inner_first = high_bits() + [1, 0]
    masks = np.zeros((size,), np.int32)
    for block in range(size):
        for place, bit in enumerate(inner_first):
            if (block >> place) & 1:
                masks[block] |= 1 << bit
    block_mask = jnp.asarray(np.repeat(masks, rows))
    offsets = jnp.asarray(np.tile(np.arange(rows, dtype=np.int32), size))
    return (lax.axis_index("dp") ^ block_mask) * rows + offsets


def dot(left, right):
    return jnp.dot(left, right, preferred_element_type=F32)


def dot_nt(left, right):
    return lax.dot_general(left, right, (((1,), (1,)), ((), ())), preferred_element_type=F32)


def dot_tn(left, right):
    return lax.dot_general(left, right, (((0,), (0,)), ((), ())), preferred_element_type=F32)


def shape_of(rows, columns, kind):
    return jax.ShapeDtypeStruct((rows, columns), kind)


def run(kernel, outs, operands, flops, after=(), grid=(), in_specs=None, out_specs=None, scratch=()):
    count = len(operands)

    def body(*refs):
        kernel(*refs[:count], *refs[count + len(after) :])

    whole = pl.BlockSpec(memory_space=pltpu.VMEM)
    in_specs = in_specs or [whole] * count
    size = sum(v.size * v.dtype.itemsize for v in list(operands) + list(outs))
    return pl.pallas_call(
        body,
        grid=grid,
        out_shape=list(outs),
        in_specs=list(in_specs) + [pl.BlockSpec(memory_space=pl.ANY)] * len(after),
        out_specs=list(out_specs or [whole] * len(outs)),
        scratch_shapes=list(scratch),
        compiler_params=pltpu.CompilerParams(
            vmem_limit_bytes=min(size + ((12 if flops else 4) << 20), 44 << 20)
        ),
        cost_estimate=pl.CostEstimate(flops=flops, bytes_accessed=size, transcendentals=0),
    )(*operands, *after)


def join_high_kernel(count, *refs):
    pieces, (first, second) = refs[:count], refs[count:]
    cut = first.shape[1]
    rows = pieces[0].shape[0]
    for place, piece in enumerate(pieces):
        to = slice(place * rows, (place + 1) * rows)
        first[to, :] = piece[:, :cut]
        second[to, :] = piece[:, cut:]


def join_high(pieces, cut, after=()):
    rows, columns = pieces[0].shape
    rows = rows * len(pieces)
    return run(
        functools.partial(join_high_kernel, len(pieces)),
        [shape_of(rows, cut, LOW), shape_of(rows, columns - cut, LOW)],
        pieces,
        0,
        after,
    )


def join_plane_kernel(across, down, across_far, down_far, across_all, down_all):
    columns, rows = across.shape[1], down.shape[0]
    across_all[:, :columns] = across[...]
    across_all[:, columns:] = across_far[...]
    down_all[:rows, :] = down[...]
    down_all[rows:, :] = down_far[...]


def join_plane(across, down, across_far, down_far, after=()):
    return run(
        join_plane_kernel,
        [
            shape_of(across.shape[0], 2 * across.shape[1], LOW),
            shape_of(2 * down.shape[0], down.shape[1], LOW),
        ],
        [across, down, across_far, down_far],
        0,
        after,
    )


def added(left, right, rows, columns):
    return (left[rows, columns].astype(F32) + right[rows, columns].astype(F32)).astype(LOW)


def split_core_kernel(cut, *refs):
    count = len(refs) - 4
    a_keep, a_send, b_keep, b_send = refs[count:]
    a, a_far, b, b_far = refs[:4] if count == 4 else refs[:2] * 2
    base = 0 if count == 4 else cut
    rows, half = a_keep.shape[0], b_keep.shape[1]
    every = slice(None)
    a_keep[...] = added(a, a_far, slice(0, rows), slice(0, cut))
    a_send[...] = added(a, a_far, slice(rows, 2 * rows), slice(0, cut))
    b_keep[...] = added(b, b_far, every, slice(base, base + half))
    b_send[...] = added(b, b_far, every, slice(base + half, base + 2 * half))


def split_core(arrays, cut, b_columns, after=()):
    rows = arrays[0].shape[0]
    a_shape = shape_of(rows // 2, cut, LOW)
    b_shape = shape_of(rows, b_columns // 2, LOW)
    return run(
        functools.partial(split_core_kernel, cut),
        [a_shape, a_shape, b_shape, b_shape],
        arrays,
        0,
        after,
    )


def split_plane_kernel(a, a_far, b, b_far, a_keep, a_send, b_keep, b_send):
    half, rows = a_keep.shape[1], b_keep.shape[0]
    every = slice(None)
    a_keep[...] = added(a, a_far, every, slice(0, half))
    a_send[...] = added(a, a_far, every, slice(half, 2 * half))
    b_keep[...] = added(b, b_far, slice(0, rows), every)
    b_send[...] = added(b, b_far, slice(rows, 2 * rows), every)


def split_plane(a, a_far, b, b_far, after=()):
    a_shape = shape_of(a.shape[0], a.shape[1] // 2, LOW)
    b_shape = shape_of(b.shape[0] // 2, b.shape[1], LOW)
    return run(
        split_plane_kernel, [a_shape, a_shape, b_shape, b_shape], [a, a_far, b, b_far], 0, after
    )


def split_high_kernel(a, a_far, b, b_far, *parts):
    cut = a.shape[1]
    rows = parts[0].shape[0]
    for place, part in enumerate(parts):
        at = slice(place * rows, (place + 1) * rows)
        part[:, :cut] = added(a, a_far, at, slice(None))
        part[:, cut:] = added(b, b_far, at, slice(None))


def split_high(a, a_far, b, b_far, after=()):
    count = len(group_masks(high_groups()[-1]))
    part = shape_of(a.shape[0] // count, a.shape[1] + b.shape[1], LOW)
    return run(split_high_kernel, [part] * count, [a, a_far, b, b_far], 0, after)


def flip(rank, first, second):
    return jnp.where(rank == 0, first, second)


def vectors_kernel(rank_ref, permute, a_own, a_far, relative, bias_q, bias_v, bias_inner):
    rank = rank_ref[0]
    side = a_own.shape[1] // 2
    width = relative.shape[1]
    half = width // 2
    spread = jnp.concatenate(
        [
            (ref[:, side - LANES : side].astype(F32) + ref[:, 2 * side - LANES :].astype(F32))
            for ref in (a_own, a_far)
        ],
        axis=0,
    )
    parts = jnp.transpose(spread)
    parts = [parts[16 * i : 16 * (i + 1)] for i in range(3)]
    relative[...] = ((parts[0] + parts[1]) + parts[2])[2:8]
    natural = [dot_nt(part.astype(LOW), permute[...]) for part in parts]
    natural = (natural[0] + natural[1]) + natural[2]
    for row, target in ((0, bias_q), (1, bias_v)):
        first, second = natural[row : row + 1, :half], natural[row : row + 1, half:]
        target[:, :half] = flip(rank, first, second)
        target[:, half:] = flip(rank, second, first)
    for place in range(2):
        for cut in range(2):
            near, far = 8 + 2 * place + cut, 8 + 2 * (1 - place) + cut
            at = (2 * place + cut) * width
            bias_inner[:, at : at + width] = flip(
                rank, natural[near : near + 1], natural[far : far + 1]
            )


def vector_lanes(rank, permute, grad_q, grad_v, sums_one, sums_two, sums_inner, natural, relative):
    width = natural.shape[1]
    half = width // 2
    natural[...] = jnp.zeros_like(natural)
    relative[...] = jnp.zeros_like(relative)
    for row, source in ((0, grad_q), (1, grad_v)):
        total = jnp.sum(source[...].astype(F32), axis=0, keepdims=True)
        first, second = total[:, :half], total[:, half:]
        natural[row : row + 1, :half] = flip(rank, first, second)
        natural[row : row + 1, half:] = flip(rank, second, first)
    for place in range(2):
        for cut in range(2):
            near, far = (2 * place + cut) * width, (2 * (1 - place) + cut) * width
            row = 8 + 2 * place + cut
            natural[row : row + 1, :] = flip(
                rank, sums_inner[:, near : near + width], sums_inner[:, far : far + width]
            )
    relative[:16, :] = dot(natural[...].astype(LOW), permute[...])
    relative[2:5, :] = sums_one[:3, :]
    relative[5:8, :] = sums_two[:3, :]
    return jnp.transpose(relative[...]).astype(LOW)


def cast_kernel(first, second, target):
    columns = first.shape[1]
    target[:, :columns] = first[...].astype(LOW)
    target[:, columns:] = second[...].astype(LOW)


def project_kernel(rows, a_own, a_far, b_own, b_far, bias_q, bias_v, q, k, v):
    half = a_own.shape[0]
    own_rows, width = q.shape
    part = width // 2
    low, high = rows[:, :half], rows[:, half:]
    a_half, b_half = a_own.shape[1] // 2, b_own.shape[1] // 2
    for side in range(2):
        cols = slice(side * part, (side + 1) * part)
        at = slice(side * a_half, side * a_half + part)
        q[:, cols] = (
            dot(low[:own_rows], a_own[:, at]) + dot(high[:own_rows], a_far[:, at]) + bias_q[:, cols]
        ).astype(LOW)
        at = slice(side * a_half + part, side * a_half + 2 * part)
        k[:, cols] = (dot(low, a_own[:, at]) + dot(high, a_far[:, at])).astype(LOW)
        at = slice(side * b_half, side * b_half + part)
        v[:, cols] = (dot(low, b_own[:, at]) + dot(high, b_far[:, at]) + bias_v[:, cols]).astype(
            LOW
        )


def softmax_down(seg_q, seg_k, key_rows, queries):
    scores = dot_nt(key_rows, queries) * 0.125
    scores = jnp.where(seg_k[...] == seg_q[...], scores, NEG_FILL)
    exp_scores = jnp.exp(scores - jnp.max(scores, axis=0, keepdims=True))
    return exp_scores * (1.0 / jnp.sum(exp_scores, axis=0, keepdims=True))


def two_heads(out):
    joined = jnp.concatenate([out[0][:HEAD_DIM], out[1][HEAD_DIM:]], axis=0)
    return jnp.transpose(joined).astype(LOW)


def attend_kernel(seg_q, seg_k, q, k, v, attended):
    queries, key_rows, value_rows = q[...], k[...], v[...]
    first = lax.broadcasted_iota(jnp.int32, queries.shape, 1) < HEAD_DIM
    out = []
    for mine in (first, jnp.logical_not(first)):
        prob = softmax_down(
            seg_q, seg_k, key_rows, jnp.where(mine, queries, jnp.zeros_like(queries))
        )
        out.append(dot_tn(value_rows, prob.astype(LOW)))
    attended[...] = two_heads(out)


def attend_back_kernel(seg_q, seg_k, q, k, v, grad, grad_q, grad_k, grad_v):
    queries, key_rows, value_rows, grad_rows = q[...], k[...], v[...], grad[...]
    first = lax.broadcasted_iota(jnp.int32, queries.shape, 1) < HEAD_DIM
    first_all = lax.broadcasted_iota(jnp.int32, key_rows.shape, 1) < HEAD_DIM
    blank = jnp.zeros_like(queries)
    out_q, out_k, out_v = [], [], []
    for mine in (first, jnp.logical_not(first)):
        prob = softmax_down(seg_q, seg_k, key_rows, jnp.where(mine, queries, blank))
        grad_prob = dot_nt(value_rows, jnp.where(mine, grad_rows, blank))
        delta = jnp.sum(grad_prob * prob, axis=0, keepdims=True)
        grad_score = (prob * (grad_prob - delta)).astype(LOW)
        out_q.append(dot_tn(key_rows, grad_score) * 0.125)
        out_k.append(dot(grad_score, queries) * 0.125)
        out_v.append(dot(prob.astype(LOW), grad_rows))
    grad_q[...] = two_heads(out_q)
    grad_k[...] = jnp.where(first_all, out_k[0], out_k[1]).astype(LOW)
    grad_v[...] = jnp.where(first_all, out_v[0], out_v[1]).astype(LOW)


def out_norm_kernel(attended, rows, b_own, b_far, vec, y, y_low, normed, inv):
    half = b_own.shape[0]
    own_rows, width = y.shape
    part = width // 2
    b_half = b_own.shape[1] // 2
    near, far = attended[:, :part], attended[:, part:]
    out = []
    for weights in (b_own, b_far):
        out.append(
            dot_nt(near, weights[:, part : 2 * part])
            + dot_nt(far, weights[:, b_half + part : b_half + 2 * part])
        )
    total = rows[:own_rows, :].astype(F32) + jnp.concatenate(out, axis=1) + vec[0:1]
    y_new, normed[...], inv[...] = normalize_fwd(total, vec[1:2], vec[2:3])
    y[...] = y_new
    y_low[...] = y_new.astype(LOW)


def hidden_kernel(y_low, own, far, bias, activation, slope):
    half = own.shape[0]
    low, high = y_low[:, :half], y_low[:, half:]
    columns = own.shape[1]
    step = columns // 8
    for start in range(0, columns, step):
        at = slice(start, start + step)
        pre = dot(low, own[:, at]) + dot(high, far[:, at]) + bias[:, at]
        cdf = 0.5 + 0.5 * lax.erf(pre * (0.5**0.5))
        activation[:, at] = (pre * cdf).astype(LOW)
        slope[:, at] = cdf + pre * jnp.exp(-0.5 * pre * pre) * ((2.0 * np.pi) ** -0.5)


def out_back_kernel(activation, own, far, y, cot, valid, vec, mixed, grad, grad_low, sums):
    out = [dot_nt(activation[...], weights[...]) for weights in (own, far)]
    total = y[...] + jnp.concatenate(out, axis=1) + vec[3:4]
    result, normed, inv_std = normalize_fwd(total, vec[4:5], vec[5:6])
    mixed[...] = result.astype(LOW)
    grad_in, gain_sum, shift_sum = normalize_back(
        cot[...] * valid[...], normed, inv_std, vec[4:5]
    )
    grad[...] = grad_in
    grad_low[...] = grad_in.astype(LOW)
    sums[0:1] = jnp.sum(grad_in, axis=0, keepdims=True)
    sums[1:2] = gain_sum[None]
    sums[2:3] = shift_sum[None]


def hidden_back_kernel(grad_low, own, far, slope, grad_pre, sums):
    half = own.shape[0]
    low, high = grad_low[:, :half], grad_low[:, half:]
    columns = own.shape[1]
    step = columns // 8
    for start in range(0, columns, step):
        at = slice(start, start + step)
        value = ((dot(low, own[:, at]) + dot(high, far[:, at])) * slope[:, at]).astype(LOW)
        grad_pre[:, at] = value
        sums[:, at] = jnp.sum(value.astype(F32), axis=0, keepdims=True)


def norm_back_kernel(
    grad_pre, own, far, grad_two, normed, inv, vec, o_own, o_far, grad, grad_low, grad_attn, sums
):
    out = [dot_nt(grad_pre[...], weights[...]) for weights in (own, far)]
    grad_in, gain_sum, shift_sum = normalize_back(
        grad_two[...] + jnp.concatenate(out, axis=1), normed[...], inv[...], vec[1:2]
    )
    grad[...] = grad_in
    low = grad_in.astype(LOW)
    grad_low[...] = low
    sums[0:1] = jnp.sum(grad_in, axis=0, keepdims=True)
    sums[1:2] = gain_sum[None]
    sums[2:3] = shift_sum[None]
    half = o_own.shape[0]
    part = grad.shape[1] // 2
    o_half = o_own.shape[1] // 2
    for side in range(2):
        at = slice(side * o_half + part, side * o_half + 2 * part)
        grad_attn[:, side * part : (side + 1) * part] = (
            dot(low[:, :half], o_own[:, at]) + dot(low[:, half:], o_far[:, at])
        ).astype(LOW)


def rows_back_kernel(grad_q, grad_k, grad_v, a_own, a_far, b_own, b_far, grad_one, own, away):
    own_rows, width = own.shape
    part = width // 2
    a_half, b_half = a_own.shape[1] // 2, b_own.shape[1] // 2
    half = a_own.shape[0]
    for place, (wa, wb) in enumerate(((a_own, b_own), (a_far, b_far))):
        to = slice(place * half, (place + 1) * half)
        both = jnp.zeros((2 * own_rows, half), F32)
        mine = grad_one[:, to]
        for side in range(2):
            cols = slice(side * part, (side + 1) * part)
            at = side * a_half
            mine = mine + dot_nt(grad_q[:, cols], wa[:, at : at + part])
            both = both + dot_nt(grad_k[:, cols], wa[:, at + part : at + 2 * part])
            at = side * b_half
            both = both + dot_nt(grad_v[:, cols], wb[:, at : at + part])
        own[:, to] = mine + both[:own_rows]
        away[:, to] = both[own_rows:].astype(LOW)


def first_grads_kernel(
    a_half, rank_ref, permute, rows, grad_q, grad_k, grad_v, grad_low, attended,
    sums_one, sums_two, sums_inner, send, keep, natural, relative,
):
    half = keep.shape[0]
    own_rows, width = grad_q.shape
    part = width // 2
    extra = vector_lanes(
        rank_ref[0], permute, grad_q, grad_v, sums_one, sums_two, sums_inner, natural, relative
    )
    for place, to in ((1, send), (0, keep)):
        at = slice(place * half, (place + 1) * half)
        both = rows[:, at]
        mine = rows[:own_rows, at]
        low = grad_low[:, at]
        for side in range(2):
            cols = slice(side * part, (side + 1) * part)
            base = side * a_half
            to[:, base : base + part] = dot_tn(mine, grad_q[:, cols]).astype(LOW)
            to[:, base + part : base + 2 * part] = dot_tn(both, grad_k[:, cols]).astype(LOW)
            to[:, base + 2 * part : base + a_half] = extra[at, :]
            base = 2 * a_half + side * 2 * part
            to[:, base : base + part] = dot_tn(both, grad_v[:, cols]).astype(LOW)
            to[:, base + part : base + 2 * part] = dot_tn(low, attended[:, cols]).astype(LOW)


def on_device(
    tokens,
    cotangent,
    lengths,
    w_qkv,
    m_qkv,
    v_qkv,
    w_out,
    m_out,
    v_out,
    w_in,
    m_in,
    v_in,
    w_back,
    m_back,
    v_back,
    vectors,
    m_vectors,
    v_vectors,
):
    own_rows, width = tokens.shape
    tensor_rank = lax.axis_index("tensor")
    group_rows = 2 * own_rows
    shard_rows = w_qkv.shape[1]
    part = w_qkv.shape[2]
    hidden_half = w_in.shape[1]
    full_inner = 2 * hidden_half
    half = width // 2
    count = vectors.shape[0]
    shard_width = vectors.shape[1]

    rest = vectors.T
    vec_parts = []
    for _ in range(3):
        vec_parts.append(jnp.pad(rest.astype(LOW), ((0, 0), (0, 16 - count))))
        rest = rest - rest.astype(LOW).astype(F32)
    vec_lanes = jnp.pad(jnp.concatenate(vec_parts, axis=1), ((0, 0), (0, LANES - 48)))
    blank = jnp.zeros_like(vec_lanes)
    vec_lanes = jnp.concatenate(
        [
            jnp.where(tensor_rank == 0, vec_lanes, blank),
            jnp.where(tensor_rank == 0, blank, vec_lanes),
        ],
        axis=0,
    )
    low_qkv = w_qkv.astype(LOW)
    shard_one = jnp.concatenate(
        [low_qkv[0], low_qkv[1], vec_lanes, low_qkv[2], w_out.T.astype(LOW)], axis=1
    )
    a_width = 2 * part + LANES
    rank = tensor_rank.astype(jnp.int32).reshape(1)
    scalar = pl.BlockSpec(memory_space=pltpu.SMEM)
    vmem = pl.BlockSpec(memory_space=pltpu.VMEM)

    tokens_far = swap_tensor(tokens)
    one_high = gather_high(shard_one)
    one = join_high(one_high, a_width)
    one_far = swap_tensor(one[0]), swap_dp(one[1], 2)
    shard_pair = run(
        cast_kernel,
        [shape_of(shard_rows, full_inner, LOW)],
        [w_in, w_back.T],
        0,
        after=one[:1],
    )[0]
    pair_high = gather_high(shard_pair)

    order = relative_order(width)
    permute = (jnp.arange(width, dtype=jnp.int32)[:, None] == order[None, :]).astype(LOW)
    permute_wide = permute.astype(F32)
    exact = lax.Precision.HIGHEST
    rows_all = jnp.concatenate([dot(tokens, permute), dot(tokens_far, permute)]).astype(LOW)
    cot = dot(cotangent, permute)

    one = join_plane(*one, *one_far, after=[rows_all, pair_high[1]])
    one_far = swap_dp(one[0], 2), swap_tensor(one[1])
    one = join_plane(one[1], one[0], one_far[1], one_far[0], after=pair_high[2:])[::-1]
    a_own, b_own = one
    a_far, b_far = swap_dp(a_own, 1), swap_dp(b_own, 1)
    pair = join_high(pair_high, hidden_half, after=[a_own])
    pair_far = swap_tensor(pair[0]), swap_dp(pair[1], 2)

    vec, bias_query, bias_value, bias_inner = run(
        vectors_kernel,
        [
            shape_of(6, width, F32),
            shape_of(1, width, F32),
            shape_of(1, width, F32),
            shape_of(1, full_inner, F32),
        ],
        [rank, permute, a_own, a_far],
        1,
        after=pair[:1],
        in_specs=[scalar, vmem, vmem, vmem],
    )

    seq_ends = jnp.cumsum(lengths[0])
    local = jnp.arange(own_rows, dtype=jnp.int32)
    own_positions = tensor_rank * own_rows + local
    key_positions = jnp.concatenate([own_positions, (1 - tensor_rank) * own_rows + local])

    def segments(positions):
        return jnp.sum((positions[:, None] >= seq_ends[None, :]).astype(jnp.int32), axis=1)

    seg_own, seg_keys = segments(own_positions)[None, :], segments(key_positions)[:, None]
    valid = (own_positions < seq_ends[-1]).astype(F32)[:, None]

    wide_low = shape_of(own_rows, width, LOW)
    wide = shape_of(own_rows, width, F32)
    group_low = shape_of(group_rows, width, LOW)
    sums_shape = shape_of(8, width, F32)
    unit = 2 * own_rows * width * width
    queries, key_rows, value_rows = run(
        project_kernel,
        [wide_low, group_low, group_low],
        [rows_all, a_own, a_far, b_own, b_far, bias_query, bias_value],
        5 * unit,
    )
    pair = join_plane(*pair, *pair_far, after=[queries])
    pair_far = swap_dp(pair[0], 2), swap_tensor(pair[1])
    pairs = width // LANES
    own_block = pl.BlockSpec((own_rows, LANES), lambda i: (0, i))
    all_block = pl.BlockSpec((group_rows, LANES), lambda i: (0, i))

    def fixed(shape):
        return pl.BlockSpec(shape, lambda i: (0, 0))

    attended = run(
        attend_kernel,
        [wide_low],
        [seg_own, seg_keys, queries, key_rows, value_rows],
        3 * unit,
        after=pair[:1],
        grid=(pairs,),
        in_specs=[fixed((1, own_rows)), fixed((group_rows, 1)), own_block, all_block, all_block],
        out_specs=[own_block],
    )[0]
    first_norm, first_low, normed_one, inv_one = run(
        out_norm_kernel,
        [wide, wide_low, wide, shape_of(own_rows, 1, F32)],
        [attended, rows_all, b_own, b_far, vec],
        2 * unit,
    )
    pair = join_plane(pair[1], pair[0], pair_far[1], pair_far[0], after=[first_low])[::-1]
    c_own, d_own = pair
    c_far, d_far = swap_dp(c_own, 1), swap_dp(d_own, 1)
    activation, slope = run(
        hidden_kernel,
        [shape_of(own_rows, full_inner, LOW), shape_of(own_rows, full_inner, F32)],
        [first_low, c_own, c_far, bias_inner],
        8 * unit,
    )
    mixed_rel, grad_two, grad_two_low, sums_two = run(
        out_back_kernel,
        [wide_low, wide, wide_low, sums_shape],
        [activation, d_own, d_far, first_norm, cot, valid, vec],
        5 * unit,
    )
    mixed = dot_nt(mixed_rel, permute).astype(LOW)

    def weight_grad(left, right):
        send = dot_tn(left[:, half:], right).astype(LOW)
        return dot_tn(left[:, :half], right).astype(LOW), swap_dp(send, 1)

    outer = weight_grad(grad_two_low, activation)
    grad_pre, sums_inner = run(
        hidden_back_kernel,
        [shape_of(own_rows, full_inner, LOW), shape_of(1, full_inner, F32)],
        [grad_two_low, d_own, d_far, slope],
        6 * unit,
    )
    inner = weight_grad(first_low, grad_pre)
    a_keep, a_send, b_keep, b_send = split_core([*inner, *outer], full_inner, full_inner)
    pair = a_keep, swap_dp(a_send, 2), b_keep, swap_tensor(b_send)
    grad_one, grad_one_low, grad_attn, sums_one = run(
        norm_back_kernel,
        [wide, wide_low, wide_low, sums_shape],
        [grad_pre, c_own, c_far, grad_two, normed_one, inv_one, vec, b_own, b_far],
        6 * unit,
        after=[a_keep],
    )
    grad_q, grad_k, grad_v = run(
        attend_back_kernel,
        [wide_low, group_low, group_low],
        [seg_own, seg_keys, queries, key_rows, value_rows, grad_attn],
        5 * unit,
        grid=(pairs,),
        in_specs=[fixed((1, own_rows)), fixed((group_rows, 1))]
        + [own_block, all_block, all_block, own_block],
        out_specs=[own_block, all_block, all_block],
    )
    one_shape = shape_of(half, 2 * a_width + 4 * part, LOW)
    one_send, one_keep = run(
        functools.partial(first_grads_kernel, a_width),
        [one_shape, one_shape],
        [rank, permute, rows_all, grad_q, grad_k, grad_v, grad_one_low, attended]
        + [sums_one, sums_two, sums_inner],
        6 * unit,
        in_specs=[scalar] + [vmem] * 10,
        scratch=[pltpu.VMEM((16, width), F32), pltpu.VMEM((LANES, width), F32)],
    )
    one_far = swap_dp(one_send, 1)
    a_keep, a_send, b_keep, b_send = split_plane(*pair, after=[one_keep])
    pair = a_keep, swap_tensor(a_send), b_keep, swap_dp(b_send, 2)
    grad_own, grad_away = run(
        rows_back_kernel,
        [wide, wide_low],
        [grad_q, grad_k, grad_v, a_own, a_far, b_own, b_far, grad_one],
        400 * unit,
        after=[a_keep],
    )
    grad_rel = grad_own + swap_tensor(grad_away).astype(F32)
    input_grad = lax.dot_general(
        grad_rel, permute_wide, (((1,), (1,)), ((), ())), precision=exact
    )
    a_keep, a_send, b_keep, b_send = split_core(
        [one_keep, one_far], 2 * a_width, 4 * part, after=[grad_own, mixed]
    )
    one = a_keep, swap_dp(a_send, 2), b_keep, swap_tensor(b_send)
    pair = send_high(split_high(*pair, after=[a_keep, input_grad]))
    a_keep, a_send, b_keep, b_send = split_plane(*one, after=pair[:1])
    one = a_keep, swap_tensor(a_send), b_keep, swap_dp(b_send, 2)
    sum_pair = reduce_high(pair)
    summed_in, summed_back = sum_pair[:, :hidden_half], sum_pair[:, hidden_half:].T
    sum_one = reduce_high(send_high(split_high(*one)))

    summed_vectors = lax.dynamic_slice_in_dim(
        sum_one[:, 2 * part : a_width], tensor_rank * shard_width, shard_width, axis=0
    )[:, :count].T
    summed_qkv = jnp.stack(
        [
            sum_one[:, :part],
            sum_one[:, part : 2 * part],
            sum_one[:, a_width : a_width + part],
        ]
    )
    summed_out = sum_one[:, a_width + part :].T
    new_qkv, moment_qkv, square_qkv = adamw(
        w_qkv, m_qkv, v_qkv, summed_qkv, float(width) ** (-0.5), WEIGHT_DECAY
    )
    new_out, moment_out, square_out = adamw(
        w_out, m_out, v_out, summed_out, (4.0 * width / group_rows) ** (-0.5), WEIGHT_DECAY
    )
    new_in, moment_in, square_in = adamw(
        w_in, m_in, v_in, summed_in, float(width) ** (-0.5), WEIGHT_DECAY
    )
    new_back, moment_back, square_back = adamw(
        w_back, m_back, v_back, summed_back, float(full_inner) ** (-0.5), WEIGHT_DECAY
    )
    new_vectors, moment_vectors, square_vectors = adamw(
        vectors, m_vectors, v_vectors, summed_vectors, 0.1, 0.0
    )
    return (
        mixed,
        input_grad,
        new_qkv,
        moment_qkv,
        square_qkv,
        new_out,
        moment_out,
        square_out,
        new_in,
        moment_in,
        square_in,
        new_back,
        moment_back,
        square_back,
        new_vectors,
        moment_vectors,
        square_vectors,
    )


def solution(mesh):
    placed = (
        P(("dp", "tensor"), None),
        P(("dp", "tensor"), None),
        P("dp", None),
        P(None, "dp", "tensor"),
        P(None, "dp", "tensor"),
        P(None, "dp", "tensor"),
        P("tensor", "dp"),
        P("tensor", "dp"),
        P("tensor", "dp"),
        P("dp", "tensor"),
        P("dp", "tensor"),
        P("dp", "tensor"),
        P("tensor", "dp"),
        P("tensor", "dp"),
        P("tensor", "dp"),
        P(None, ("dp", "tensor")),
        P(None, ("dp", "tensor")),
        P(None, ("dp", "tensor")),
    )
    return jax.shard_map(
        on_device,
        mesh=mesh,
        in_specs=placed,
        out_specs=(
            P(("dp", "tensor"), None),
            P(("dp", "tensor"), None),
            P(None, "dp", "tensor"),
            P(None, "dp", "tensor"),
            P(None, "dp", "tensor"),
            P("tensor", "dp"),
            P("tensor", "dp"),
            P("tensor", "dp"),
            P("dp", "tensor"),
            P("dp", "tensor"),
            P("dp", "tensor"),
            P("tensor", "dp"),
            P("tensor", "dp"),
            P("tensor", "dp"),
            P(None, ("dp", "tensor")),
            P(None, ("dp", "tensor")),
            P(None, ("dp", "tensor")),
        ),
        check_vma=False,
    )
```

```python
import functools

import numpy as np

import jax
import jax.numpy as jnp
from jax import lax
from jax.experimental import pallas as pl
from jax.experimental.pallas import tpu as pltpu
from jax.sharding import PartitionSpec as P

HEAD_DIM = 64
LANES = 128
STEP = 10


EPS_NORM = 1e-05
BETA_ONE = 0.9
BETA_TWO = 0.999
EPS_ADAM = 1e-08
WEIGHT_DECAY = 0.01
NEG_FILL = -1000000000.0
LOW = jnp.bfloat16
F32 = jnp.float32


def normalize_fwd(values, gain_row, shift_row):
    row_mean = jnp.mean(values, axis=-1, keepdims=True)
    centered = values - row_mean
    variance = jnp.mean(centered * centered, axis=-1, keepdims=True)
    inv_std = lax.rsqrt(variance + EPS_NORM)
    normed = centered * inv_std
    return (normed * gain_row + shift_row, normed, inv_std)


def normalize_back(gradient, normed, inv_std, gain_row):
    grad_norm = gradient * gain_row
    grad_in = inv_std * (
        grad_norm
        - jnp.mean(grad_norm, axis=-1, keepdims=True)
        - normed * jnp.mean(grad_norm * normed, axis=-1, keepdims=True)
    )
    return (grad_in, jnp.sum(gradient * normed, axis=0), jnp.sum(gradient, axis=0))


def adamw(weight, moment, square, gradient, step_rate, decay_rate):
    moment = BETA_ONE * moment + (1.0 - BETA_ONE) * gradient
    square = BETA_TWO * square + (1.0 - BETA_TWO) * gradient * gradient
    direction = (
        moment / (1.0 - BETA_ONE**STEP) / (jnp.sqrt(square / (1.0 - BETA_TWO**STEP)) + EPS_ADAM)
    )
    return (weight - step_rate * (direction + decay_rate * weight), moment, square)


def swap_dp(values, mask):
    size = lax.axis_size("dp")
    return lax.ppermute(values, "dp", [(i, i ^ mask) for i in range(size)])


def swap_tensor(values):
    return lax.ppermute(values, "tensor", [(0, 1), (1, 0)])


def high_bits():
    return list(range(2, lax.axis_size("dp").bit_length() - 1))


def high_groups():
    bits = high_bits()
    return [[1 << bit for bit in bits[i : i + 2]] for i in range(0, len(bits), 2)]


def group_masks(group):
    return [0] + group + ([group[0] ^ group[1]] if len(group) == 2 else [])


def gather_high(shard):
    groups = high_groups()
    for place, group in enumerate(groups):
        pieces = [shard if mask == 0 else swap_dp(shard, mask) for mask in group_masks(group)]
        if place < len(groups) - 1:
            shard = jnp.concatenate(pieces, axis=0)
    return pieces


def send_high(parts):
    masks = group_masks(high_groups()[-1])
    return [parts[0]] + [swap_dp(part, mask) for part, mask in zip(parts[1:], masks[1:])]


def reduce_rest(total):
    for group in reversed(high_groups()[:-1]):
        masks = group_masks(group)
        rows = total.shape[0] // len(masks)
        low = total.astype(LOW)
        total = total[:rows]
        for place, mask in enumerate(masks[1:], 1):
            total = total + swap_dp(low[place * rows : (place + 1) * rows], mask).astype(F32)
    return total


def relative_order(width):
    size = lax.axis_size("dp")
    rows = width // size
    inner_first = high_bits() + [1, 0]
    masks = np.zeros((size,), np.int32)
    for block in range(size):
        for place, bit in enumerate(inner_first):
            if (block >> place) & 1:
                masks[block] |= 1 << bit
    block_mask = jnp.asarray(np.repeat(masks, rows))
    offsets = jnp.asarray(np.tile(np.arange(rows, dtype=np.int32), size))
    return (lax.axis_index("dp") ^ block_mask) * rows + offsets


def dot(left, right):
    return jnp.dot(left, right, preferred_element_type=F32)


def dot_nt(left, right):
    return lax.dot_general(left, right, (((1,), (1,)), ((), ())), preferred_element_type=F32)


def dot_tn(left, right):
    return lax.dot_general(left, right, (((0,), (0,)), ((), ())), preferred_element_type=F32)


def shape_of(rows, columns, kind):
    return jax.ShapeDtypeStruct((rows, columns), kind)


def run(kernel, outs, operands, flops, after=(), grid=(), in_specs=None, out_specs=None, scratch=()):
    count = len(operands)

    def body(*refs):
        kernel(*refs[:count], *refs[count + len(after) :])

    whole = pl.BlockSpec(memory_space=pltpu.VMEM)
    in_specs = in_specs or [whole] * count
    size = sum(v.size * v.dtype.itemsize for v in list(operands) + list(outs))
    return pl.pallas_call(
        body,
        grid=grid,
        out_shape=list(outs),
        in_specs=list(in_specs) + [pl.BlockSpec(memory_space=pl.ANY)] * len(after),
        out_specs=list(out_specs or [whole] * len(outs)),
        scratch_shapes=list(scratch),
        compiler_params=pltpu.CompilerParams(
            vmem_limit_bytes=min(size + ((12 if flops else 4) << 20), 44 << 20)
        ),
        cost_estimate=pl.CostEstimate(flops=flops, bytes_accessed=size, transcendentals=0),
    )(*operands, *after)


def join_high_kernel(count, *refs):
    pieces, (first, second) = refs[:count], refs[count:]
    cut = first.shape[1]
    rows = pieces[0].shape[0]
    for place, piece in enumerate(pieces):
        to = slice(place * rows, (place + 1) * rows)
        first[to, :] = piece[:, :cut]
        second[to, :] = piece[:, cut:]


def join_high(pieces, cut, flops=0, after=()):
    rows, columns = pieces[0].shape
    rows = rows * len(pieces)
    return run(
        functools.partial(join_high_kernel, len(pieces)),
        [shape_of(rows, cut, LOW), shape_of(rows, columns - cut, LOW)],
        pieces,
        flops,
        after,
    )


def join_plane_kernel(across, down, across_far, down_far, across_all, down_all):
    columns, rows = across.shape[1], down.shape[0]
    across_all[:, :columns] = across[...]
    across_all[:, columns:] = across_far[...]
    down_all[:rows, :] = down[...]
    down_all[rows:, :] = down_far[...]


def join_plane(across, down, across_far, down_far, after=()):
    return run(
        join_plane_kernel,
        [
            shape_of(across.shape[0], 2 * across.shape[1], LOW),
            shape_of(2 * down.shape[0], down.shape[1], LOW),
        ],
        [across, down, across_far, down_far],
        0,
        after,
    )


def added(left, right, rows, columns):
    return (left[rows, columns].astype(F32) + right[rows, columns].astype(F32)).astype(LOW)


def split_rows_kernel(array, far, keep, send):
    rows = keep.shape[0]
    keep[...] = added(array, far, slice(0, rows), slice(None))
    send[...] = added(array, far, slice(rows, 2 * rows), slice(None))


def split_columns_kernel(array, far, keep, send):
    columns = keep.shape[1]
    keep[...] = added(array, far, slice(None), slice(0, columns))
    send[...] = added(array, far, slice(None), slice(columns, 2 * columns))


def split_rows(array, far, flops=0, after=()):
    part = shape_of(array.shape[0] // 2, array.shape[1], LOW)
    return run(split_rows_kernel, [part, part], [array, far], flops, after)


def split_columns(array, far, flops=0, after=()):
    part = shape_of(array.shape[0], array.shape[1] // 2, LOW)
    return run(split_columns_kernel, [part, part], [array, far], flops, after)


def split_core_kernel(a, a_far, b, b_far, a_keep, a_send, b_keep, b_send):
    split_rows_kernel(a, a_far, a_keep, a_send)
    split_columns_kernel(b, b_far, b_keep, b_send)


def split_core(a, a_far, b, b_far, after=()):
    a_shape = shape_of(a.shape[0] // 2, a.shape[1], LOW)
    b_shape = shape_of(b.shape[0], b.shape[1] // 2, LOW)
    return run(
        split_core_kernel, [a_shape, a_shape, b_shape, b_shape], [a, a_far, b, b_far], 0, after
    )


def sum_kernel(*refs):
    total = refs[0][...].astype(F32)
    for ref in refs[1:-1]:
        total = total + ref[...].astype(F32)
    refs[-1][...] = total


def sum_parts(parts, flops, after=()):
    return run(sum_kernel, [shape_of(*parts[0].shape, F32)], parts, flops, after)


def split_plane_kernel(a, a_far, b, b_far, a_keep, a_send, b_keep, b_send):
    half, rows = a_keep.shape[1], b_keep.shape[0]
    every = slice(None)
    a_keep[...] = added(a, a_far, every, slice(0, half))
    a_send[...] = added(a, a_far, every, slice(half, 2 * half))
    b_keep[...] = added(b, b_far, slice(0, rows), every)
    b_send[...] = added(b, b_far, slice(rows, 2 * rows), every)


def split_plane(a, a_far, b, b_far, after=()):
    a_shape = shape_of(a.shape[0], a.shape[1] // 2, LOW)
    b_shape = shape_of(b.shape[0] // 2, b.shape[1], LOW)
    return run(
        split_plane_kernel, [a_shape, a_shape, b_shape, b_shape], [a, a_far, b, b_far], 0, after
    )


def split_high_kernel(a, a_far, b, b_far, *parts):
    cut = a.shape[1]
    rows = parts[0].shape[0]
    for place, part in enumerate(parts):
        at = slice(place * rows, (place + 1) * rows)
        part[:, :cut] = added(a, a_far, at, slice(None))
        part[:, cut:] = added(b, b_far, at, slice(None))


def split_high(a, a_far, b, b_far, after=()):
    count = len(group_masks(high_groups()[-1]))
    part = shape_of(a.shape[0] // count, a.shape[1] + b.shape[1], LOW)
    return run(split_high_kernel, [part] * count, [a, a_far, b, b_far], 0, after)


def flip(rank, first, second):
    return jnp.where(rank == 0, first, second)


def vectors_kernel(rank_ref, permute, a_own, a_far, relative, bias_q, bias_v, bias_inner):
    rank = rank_ref[0]
    side = a_own.shape[1] // 2
    width = relative.shape[1]
    half = width // 2
    spread = jnp.concatenate(
        [
            (ref[:, side - LANES : side].astype(F32) + ref[:, 2 * side - LANES :].astype(F32))
            for ref in (a_own, a_far)
        ],
        axis=0,
    )
    parts = jnp.transpose(spread)
    parts = [parts[16 * i : 16 * (i + 1)] for i in range(3)]
    relative[...] = ((parts[0] + parts[1]) + parts[2])[2:8]
    natural = [dot_nt(part.astype(LOW), permute[...]) for part in parts]
    natural = (natural[0] + natural[1]) + natural[2]
    for row, target in ((0, bias_q), (1, bias_v)):
        first, second = natural[row : row + 1, :half], natural[row : row + 1, half:]
        target[:, :half] = flip(rank, first, second)
        target[:, half:] = flip(rank, second, first)
    for place in range(2):
        for cut in range(2):
            near, far = 8 + 2 * place + cut, 8 + 2 * (1 - place) + cut
            at = (2 * place + cut) * width
            bias_inner[:, at : at + width] = flip(
                rank, natural[near : near + 1], natural[far : far + 1]
            )


def vector_lanes(rank, permute, grad_q, grad_v, sums_one, sums_two, sums_inner, natural, relative):
    width = natural.shape[1]
    half = width // 2
    natural[...] = jnp.zeros_like(natural)
    relative[...] = jnp.zeros_like(relative)
    for row, source in ((0, grad_q), (1, grad_v)):
        total = jnp.sum(source[...].astype(F32), axis=0, keepdims=True)
        first, second = total[:, :half], total[:, half:]
        natural[row : row + 1, :half] = flip(rank, first, second)
        natural[row : row + 1, half:] = flip(rank, second, first)
    for place in range(2):
        for cut in range(2):
            near, far = (2 * place + cut) * width, (2 * (1 - place) + cut) * width
            row = 8 + 2 * place + cut
            natural[row : row + 1, :] = flip(
                rank, sums_inner[:, near : near + width], sums_inner[:, far : far + width]
            )
    relative[:16, :] = dot(natural[...].astype(LOW), permute[...])
    relative[2:5, :] = sums_one[:3, :]
    relative[5:8, :] = sums_two[:3, :]
    return jnp.transpose(relative[...]).astype(LOW)


def cast_kernel(first, second, target):
    columns = first.shape[1]
    target[:, :columns] = first[...].astype(LOW)
    target[:, columns:] = second[...].astype(LOW)


def project_kernel(rows, a_own, a_far, b_own, b_far, bias_q, bias_v, q, k, v):
    half = a_own.shape[0]
    own_rows, width = q.shape
    part = width // 2
    low, high = rows[:, :half], rows[:, half:]
    a_half, b_half = a_own.shape[1] // 2, b_own.shape[1] // 2
    for side in range(2):
        cols = slice(side * part, (side + 1) * part)
        at = slice(side * a_half, side * a_half + part)
        q[:, cols] = (
            dot(low[:own_rows], a_own[:, at]) + dot(high[:own_rows], a_far[:, at]) + bias_q[:, cols]
        ).astype(LOW)
        at = slice(side * a_half + part, side * a_half + 2 * part)
        k[:, cols] = (dot(low, a_own[:, at]) + dot(high, a_far[:, at])).astype(LOW)
        at = slice(side * b_half, side * b_half + part)
        v[:, cols] = (dot(low, b_own[:, at]) + dot(high, b_far[:, at]) + bias_v[:, cols]).astype(
            LOW
        )


def softmax_down(seg_q, seg_k, key_rows, queries):
    scores = dot_nt(key_rows, queries) * 0.125
    scores = jnp.where(seg_k[...] == seg_q[...], scores, NEG_FILL)
    exp_scores = jnp.exp(scores - jnp.max(scores, axis=0, keepdims=True))
    return exp_scores * (1.0 / jnp.sum(exp_scores, axis=0, keepdims=True))


def two_heads(out):
    joined = jnp.concatenate([out[0][:HEAD_DIM], out[1][HEAD_DIM:]], axis=0)
    return jnp.transpose(joined).astype(LOW)


def attend_kernel(seg_q, seg_k, q, k, v, attended):
    queries, key_rows, value_rows = q[...], k[...], v[...]
    first = lax.broadcasted_iota(jnp.int32, queries.shape, 1) < HEAD_DIM
    out = []
    for mine in (first, jnp.logical_not(first)):
        prob = softmax_down(
            seg_q, seg_k, key_rows, jnp.where(mine, queries, jnp.zeros_like(queries))
        )
        out.append(dot_tn(value_rows, prob.astype(LOW)))
    attended[...] = two_heads(out)


def attend_back_kernel(seg_q, seg_k, q, k, v, grad, grad_q, grad_k, grad_v):
    queries, key_rows, value_rows, grad_rows = q[...], k[...], v[...], grad[...]
    first = lax.broadcasted_iota(jnp.int32, queries.shape, 1) < HEAD_DIM
    first_all = lax.broadcasted_iota(jnp.int32, key_rows.shape, 1) < HEAD_DIM
    blank = jnp.zeros_like(queries)
    out_q, out_k, out_v = [], [], []
    for mine in (first, jnp.logical_not(first)):
        prob = softmax_down(seg_q, seg_k, key_rows, jnp.where(mine, queries, blank))
        grad_prob = dot_nt(value_rows, jnp.where(mine, grad_rows, blank))
        delta = jnp.sum(grad_prob * prob, axis=0, keepdims=True)
        grad_score = (prob * (grad_prob - delta)).astype(LOW)
        out_q.append(dot_tn(key_rows, grad_score) * 0.125)
        out_k.append(dot(grad_score, queries) * 0.125)
        out_v.append(dot(prob.astype(LOW), grad_rows))
    grad_q[...] = two_heads(out_q)
    grad_k[...] = jnp.where(first_all, out_k[0], out_k[1]).astype(LOW)
    grad_v[...] = jnp.where(first_all, out_v[0], out_v[1]).astype(LOW)


def out_norm_kernel(attended, rows, b_own, b_far, vec, y, y_low, normed, inv):
    half = b_own.shape[0]
    own_rows, width = y.shape
    part = width // 2
    b_half = b_own.shape[1] // 2
    near, far = attended[:, :part], attended[:, part:]
    out = []
    for weights in (b_own, b_far):
        out.append(
            dot_nt(near, weights[:, part : 2 * part])
            + dot_nt(far, weights[:, b_half + part : b_half + 2 * part])
        )
    total = rows[:own_rows, :].astype(F32) + jnp.concatenate(out, axis=1) + vec[0:1]
    y_new, normed[...], inv[...] = normalize_fwd(total, vec[1:2], vec[2:3])
    y[...] = y_new
    y_low[...] = y_new.astype(LOW)


def hidden_kernel(y_low, own, far, bias, activation, slope):
    half = own.shape[0]
    low, high = y_low[:, :half], y_low[:, half:]
    columns = own.shape[1]
    step = columns // 8
    for start in range(0, columns, step):
        at = slice(start, start + step)
        pre = dot(low, own[:, at]) + dot(high, far[:, at]) + bias[:, at]
        cdf = 0.5 + 0.5 * lax.erf(pre * (0.5**0.5))
        activation[:, at] = (pre * cdf).astype(LOW)
        slope[:, at] = cdf + pre * jnp.exp(-0.5 * pre * pre) * ((2.0 * np.pi) ** -0.5)


def out_back_kernel(activation, own, far, y, cot, valid, vec, mixed, grad, grad_low, sums):
    out = [dot_nt(activation[...], weights[...]) for weights in (own, far)]
    total = y[...] + jnp.concatenate(out, axis=1) + vec[3:4]
    result, normed, inv_std = normalize_fwd(total, vec[4:5], vec[5:6])
    mixed[...] = result.astype(LOW)
    grad_in, gain_sum, shift_sum = normalize_back(
        cot[...] * valid[...], normed, inv_std, vec[4:5]
    )
    grad[...] = grad_in
    grad_low[...] = grad_in.astype(LOW)
    sums[0:1] = jnp.sum(grad_in, axis=0, keepdims=True)
    sums[1:2] = gain_sum[None]
    sums[2:3] = shift_sum[None]


def hidden_back_kernel(grad_low, own, far, slope, grad_pre, sums):
    half = own.shape[0]
    low, high = grad_low[:, :half], grad_low[:, half:]
    columns = own.shape[1]
    step = columns // 8
    for start in range(0, columns, step):
        at = slice(start, start + step)
        value = ((dot(low, own[:, at]) + dot(high, far[:, at])) * slope[:, at]).astype(LOW)
        grad_pre[:, at] = value
        sums[:, at] = jnp.sum(value.astype(F32), axis=0, keepdims=True)


def norm_back_kernel(
    grad_pre, own, far, grad_two, normed, inv, vec, o_own, o_far, grad, grad_low, grad_attn, sums
):
    out = [dot_nt(grad_pre[...], weights[...]) for weights in (own, far)]
    grad_in, gain_sum, shift_sum = normalize_back(
        grad_two[...] + jnp.concatenate(out, axis=1), normed[...], inv[...], vec[1:2]
    )
    grad[...] = grad_in
    low = grad_in.astype(LOW)
    grad_low[...] = low
    sums[0:1] = jnp.sum(grad_in, axis=0, keepdims=True)
    sums[1:2] = gain_sum[None]
    sums[2:3] = shift_sum[None]
    half = o_own.shape[0]
    part = grad.shape[1] // 2
    o_half = o_own.shape[1] // 2
    for side in range(2):
        at = slice(side * o_half + part, side * o_half + 2 * part)
        grad_attn[:, side * part : (side + 1) * part] = (
            dot(low[:, :half], o_own[:, at]) + dot(low[:, half:], o_far[:, at])
        ).astype(LOW)


def rows_back_kernel(grad_q, grad_k, grad_v, a_own, a_far, b_own, b_far, grad_one, own, away):
    own_rows, width = own.shape
    part = width // 2
    a_half, b_half = a_own.shape[1] // 2, b_own.shape[1] // 2
    half = a_own.shape[0]
    for place, (wa, wb) in enumerate(((a_own, b_own), (a_far, b_far))):
        to = slice(place * half, (place + 1) * half)
        both = jnp.zeros((2 * own_rows, half), F32)
        mine = grad_one[:, to]
        for side in range(2):
            cols = slice(side * part, (side + 1) * part)
            at = side * a_half
            mine = mine + dot_nt(grad_q[:, cols], wa[:, at : at + part])
            both = both + dot_nt(grad_k[:, cols], wa[:, at + part : at + 2 * part])
            at = side * b_half
            both = both + dot_nt(grad_v[:, cols], wb[:, at : at + part])
        own[:, to] = mine + both[:own_rows]
        away[:, to] = both[own_rows:].astype(LOW)


def rows_out_kernel(own, away, permute, out):
    rest = own[...] + away[...].astype(F32)
    total = None
    for _ in range(3):
        part = rest.astype(LOW)
        rest = rest - part.astype(F32)
        moved = dot_nt(part, permute[...])
        total = moved if total is None else total + moved
    out[...] = total


def first_grads_kernel(
    a_half, rank_ref, permute, rows, grad_q, grad_k, grad_v, grad_low, attended,
    sums_one, sums_two, sums_inner, a_send, b_send, a_keep, b_keep, natural, relative,
):
    half = a_keep.shape[0]
    own_rows, width = grad_q.shape
    part = width // 2
    extra = vector_lanes(
        rank_ref[0], permute, grad_q, grad_v, sums_one, sums_two, sums_inner, natural, relative
    )
    for place, to, to_b in ((1, a_send, b_send), (0, a_keep, b_keep)):
        at = slice(place * half, (place + 1) * half)
        both = rows[:, at]
        mine = rows[:own_rows, at]
        low = grad_low[:, at]
        for side in range(2):
            cols = slice(side * part, (side + 1) * part)
            base = side * a_half
            to[:, base : base + part] = dot_tn(mine, grad_q[:, cols]).astype(LOW)
            to[:, base + part : base + 2 * part] = dot_tn(both, grad_k[:, cols]).astype(LOW)
            to[:, base + 2 * part : base + a_half] = extra[at, :]
            base = side * 2 * part
            to_b[:, base : base + part] = dot_tn(both, grad_v[:, cols]).astype(LOW)
            to_b[:, base + part : base + 2 * part] = dot_tn(low, attended[:, cols]).astype(LOW)


def on_device(
    tokens,
    cotangent,
    lengths,
    w_qkv,
    m_qkv,
    v_qkv,
    w_out,
    m_out,
    v_out,
    w_in,
    m_in,
    v_in,
    w_back,
    m_back,
    v_back,
    vectors,
    m_vectors,
    v_vectors,
):
    own_rows, width = tokens.shape
    tensor_rank = lax.axis_index("tensor")
    group_rows = 2 * own_rows
    shard_rows = w_qkv.shape[1]
    part = w_qkv.shape[2]
    hidden_half = w_in.shape[1]
    full_inner = 2 * hidden_half
    half = width // 2
    count = vectors.shape[0]
    shard_width = vectors.shape[1]

    rest = vectors.T
    vec_parts = []
    for _ in range(3):
        vec_parts.append(jnp.pad(rest.astype(LOW), ((0, 0), (0, 16 - count))))
        rest = rest - rest.astype(LOW).astype(F32)
    vec_lanes = jnp.pad(jnp.concatenate(vec_parts, axis=1), ((0, 0), (0, LANES - 48)))
    blank = jnp.zeros_like(vec_lanes)
    vec_lanes = jnp.concatenate(
        [
            jnp.where(tensor_rank == 0, vec_lanes, blank),
            jnp.where(tensor_rank == 0, blank, vec_lanes),
        ],
        axis=0,
    )
    low_qkv = w_qkv.astype(LOW)
    shard_one = jnp.concatenate(
        [low_qkv[0], low_qkv[1], vec_lanes, low_qkv[2], w_out.T.astype(LOW)], axis=1
    )
    a_width = 2 * part + LANES
    rank = tensor_rank.astype(jnp.int32).reshape(1)
    scalar = pl.BlockSpec(memory_space=pltpu.SMEM)
    vmem = pl.BlockSpec(memory_space=pltpu.VMEM)

    tokens_far = swap_tensor(tokens)
    one_high = gather_high(shard_one)
    one = join_high(one_high, a_width)
    one_far = swap_tensor(one[0]), swap_dp(one[1], 2)
    shard_pair = run(
        cast_kernel,
        [shape_of(shard_rows, full_inner, LOW)],
        [w_in, w_back.T],
        0,
        after=one[:1],
    )[0]
    pair_high = gather_high(shard_pair)

    order = relative_order(width)
    permute = (jnp.arange(width, dtype=jnp.int32)[:, None] == order[None, :]).astype(LOW)
    rows_all = jnp.concatenate([dot(tokens, permute), dot(tokens_far, permute)]).astype(LOW)
    cot = dot(cotangent, permute)

    one = join_plane(*one, *one_far, after=[rows_all])
    one_far = swap_dp(one[0], 2), swap_tensor(one[1])
    unit = 2 * own_rows * width * width
    pair = join_high(pair_high, hidden_half, 400 * unit)
    one = join_plane(one[1], one[0], one_far[1], one_far[0], after=pair[:1])[::-1]
    a_own, b_own = one
    a_far, b_far = swap_dp(a_own, 1), swap_dp(b_own, 1)
    pair_far = swap_tensor(pair[0]), swap_dp(pair[1], 2)

    vec, bias_query, bias_value, bias_inner = run(
        vectors_kernel,
        [
            shape_of(6, width, F32),
            shape_of(1, width, F32),
            shape_of(1, width, F32),
            shape_of(1, full_inner, F32),
        ],
        [rank, permute, a_own, a_far],
        1,
        in_specs=[scalar, vmem, vmem, vmem],
    )

    seq_ends = jnp.cumsum(lengths[0])
    local = jnp.arange(own_rows, dtype=jnp.int32)
    own_positions = tensor_rank * own_rows + local
    key_positions = jnp.concatenate([own_positions, (1 - tensor_rank) * own_rows + local])

    def segments(positions):
        return jnp.sum((positions[:, None] >= seq_ends[None, :]).astype(jnp.int32), axis=1)

    seg_own, seg_keys = segments(own_positions)[None, :], segments(key_positions)[:, None]
    valid = (own_positions < seq_ends[-1]).astype(F32)[:, None]

    wide_low = shape_of(own_rows, width, LOW)
    wide = shape_of(own_rows, width, F32)
    group_low = shape_of(group_rows, width, LOW)
    sums_shape = shape_of(8, width, F32)
    queries, key_rows, value_rows = run(
        project_kernel,
        [wide_low, group_low, group_low],
        [rows_all, a_own, a_far, b_own, b_far, bias_query, bias_value],
        5 * unit,
    )
    pair = join_plane(*pair, *pair_far, after=[queries])
    pair_far = swap_dp(pair[0], 2), swap_tensor(pair[1])
    pairs = width // LANES
    own_block = pl.BlockSpec((own_rows, LANES), lambda i: (0, i))
    all_block = pl.BlockSpec((group_rows, LANES), lambda i: (0, i))

    def fixed(shape):
        return pl.BlockSpec(shape, lambda i: (0, 0))

    attended = run(
        attend_kernel,
        [wide_low],
        [seg_own, seg_keys, queries, key_rows, value_rows],
        3 * unit,
        after=pair[:1],
        grid=(pairs,),
        in_specs=[fixed((1, own_rows)), fixed((group_rows, 1)), own_block, all_block, all_block],
        out_specs=[own_block],
    )[0]
    first_norm, first_low, normed_one, inv_one = run(
        out_norm_kernel,
        [wide, wide_low, wide, shape_of(own_rows, 1, F32)],
        [attended, rows_all, b_own, b_far, vec],
        2 * unit,
    )
    pair = join_plane(pair[1], pair[0], pair_far[1], pair_far[0], after=[first_low])[::-1]
    c_own, d_own = pair
    c_far, d_far = swap_dp(c_own, 1), swap_dp(d_own, 1)
    activation, slope = run(
        hidden_kernel,
        [shape_of(own_rows, full_inner, LOW), shape_of(own_rows, full_inner, F32)],
        [first_low, c_own, c_far, bias_inner],
        8 * unit,
    )
    mixed_rel, grad_two, grad_two_low, sums_two = run(
        out_back_kernel,
        [wide_low, wide, wide_low, sums_shape],
        [activation, d_own, d_far, first_norm, cot, valid, vec],
        5 * unit,
    )
    mixed = dot_nt(mixed_rel, permute).astype(LOW)

    def weight_grad(left, right):
        send = dot_tn(left[:, half:], right).astype(LOW)
        return dot_tn(left[:, :half], right).astype(LOW), swap_dp(send, 1)

    outer = weight_grad(grad_two_low, activation)
    grad_pre, sums_inner = run(
        hidden_back_kernel,
        [shape_of(own_rows, full_inner, LOW), shape_of(1, full_inner, F32)],
        [grad_two_low, d_own, d_far, slope],
        6 * unit,
    )
    inner = weight_grad(first_low, grad_pre)
    b_keep, b_send = split_columns(*outer, 400 * unit, after=[grad_pre])
    a_keep, a_send = split_rows(*inner, after=[b_keep])
    pair = a_keep, swap_dp(a_send, 2), b_keep, swap_tensor(b_send)
    grad_one, grad_one_low, grad_attn, sums_one = run(
        norm_back_kernel,
        [wide, wide_low, wide_low, sums_shape],
        [grad_pre, c_own, c_far, grad_two, normed_one, inv_one, vec, b_own, b_far],
        6 * unit,
        after=[a_keep],
    )
    grad_q, grad_k, grad_v = run(
        attend_back_kernel,
        [wide_low, group_low, group_low],
        [seg_own, seg_keys, queries, key_rows, value_rows, grad_attn],
        5 * unit,
        grid=(pairs,),
        in_specs=[fixed((1, own_rows)), fixed((group_rows, 1))]
        + [own_block, all_block, all_block, own_block],
        out_specs=[own_block, all_block, all_block],
    )
    a_shape, b_shape = shape_of(half, 2 * a_width, LOW), shape_of(half, 4 * part, LOW)
    a_send, b_send, one_a, one_b = run(
        functools.partial(first_grads_kernel, a_width),
        [a_shape, b_shape, a_shape, b_shape],
        [rank, permute, rows_all, grad_q, grad_k, grad_v, grad_one_low, attended]
        + [sums_one, sums_two, sums_inner],
        6 * unit,
        in_specs=[scalar] + [vmem] * 10,
        scratch=[pltpu.VMEM((16, width), F32), pltpu.VMEM((LANES, width), F32)],
    )
    one = one_a, swap_dp(a_send, 1), one_b, swap_dp(b_send, 1)
    a_keep, a_send, b_keep, b_send = split_plane(*pair, after=[one_a, mixed])
    pair = a_keep, swap_tensor(a_send), b_keep, swap_dp(b_send, 2)
    grad_own, grad_away = run(
        rows_back_kernel,
        [wide, wide_low],
        [grad_q, grad_k, grad_v, a_own, a_far, b_own, b_far, grad_one],
        400 * unit,
        after=[a_keep],
    )
    a_keep, a_send, b_keep, b_send = split_core(*one, after=[grad_own])
    one = a_keep, swap_dp(a_send, 2), b_keep, swap_tensor(b_send)
    pair = send_high(split_high(*pair, after=[a_keep]))
    a_keep, a_send, b_keep, b_send = split_plane(*one, after=pair[:1])
    one = a_keep, swap_tensor(a_send), b_keep, swap_dp(b_send, 2)
    pair = sum_parts(pair, 400 * unit, after=[a_keep])
    one = send_high(split_high(*one, after=pair))
    input_grad = run(
        rows_out_kernel,
        [wide],
        [grad_own, swap_tensor(grad_away), permute],
        3 * unit,
        after=one[:1],
    )[0]
    sum_pair = reduce_rest(pair[0])
    summed_in, summed_back = sum_pair[:, :hidden_half], sum_pair[:, hidden_half:].T
    sum_one = reduce_rest(sum(part.astype(F32) for part in one))

    summed_vectors = lax.dynamic_slice_in_dim(
        sum_one[:, 2 * part : a_width], tensor_rank * shard_width, shard_width, axis=0
    )[:, :count].T
    summed_qkv = jnp.stack(
        [
            sum_one[:, :part],
            sum_one[:, part : 2 * part],
            sum_one[:, a_width : a_width + part],
        ]
    )
    summed_out = sum_one[:, a_width + part :].T
    new_qkv, moment_qkv, square_qkv = adamw(
        w_qkv, m_qkv, v_qkv, summed_qkv, float(width) ** (-0.5), WEIGHT_DECAY
    )
    new_out, moment_out, square_out = adamw(
        w_out, m_out, v_out, summed_out, (4.0 * width / group_rows) ** (-0.5), WEIGHT_DECAY
    )
    new_in, moment_in, square_in = adamw(
        w_in, m_in, v_in, summed_in, float(width) ** (-0.5), WEIGHT_DECAY
    )
    new_back, moment_back, square_back = adamw(
        w_back, m_back, v_back, summed_back, float(full_inner) ** (-0.5), WEIGHT_DECAY
    )
    new_vectors, moment_vectors, square_vectors = adamw(
        vectors, m_vectors, v_vectors, summed_vectors, 0.1, 0.0
    )
    return (
        mixed,
        input_grad,
        new_qkv,
        moment_qkv,
        square_qkv,
        new_out,
        moment_out,
        square_out,
        new_in,
        moment_in,
        square_in,
        new_back,
        moment_back,
        square_back,
        new_vectors,
        moment_vectors,
        square_vectors,
    )


def solution(mesh):
    placed = (
        P(("dp", "tensor"), None),
        P(("dp", "tensor"), None),
        P("dp", None),
        P(None, "dp", "tensor"),
        P(None, "dp", "tensor"),
        P(None, "dp", "tensor"),
        P("tensor", "dp"),
        P("tensor", "dp"),
        P("tensor", "dp"),
        P("dp", "tensor"),
        P("dp", "tensor"),
        P("dp", "tensor"),
        P("tensor", "dp"),
        P("tensor", "dp"),
        P("tensor", "dp"),
        P(None, ("dp", "tensor")),
        P(None, ("dp", "tensor")),
        P(None, ("dp", "tensor")),
    )
    return jax.shard_map(
        on_device,
        mesh=mesh,
        in_specs=placed,
        out_specs=(
            P(("dp", "tensor"), None),
            P(("dp", "tensor"), None),
            P(None, "dp", "tensor"),
            P(None, "dp", "tensor"),
            P(None, "dp", "tensor"),
            P("tensor", "dp"),
            P("tensor", "dp"),
            P("tensor", "dp"),
            P("dp", "tensor"),
            P("dp", "tensor"),
            P("dp", "tensor"),
            P("tensor", "dp"),
            P("tensor", "dp"),
            P("tensor", "dp"),
            P(None, ("dp", "tensor")),
            P(None, ("dp", "tensor")),
            P(None, ("dp", "tensor")),
        ),
        check_vma=False,
    )
```

```python
import functools

import numpy as np

import jax
import jax.numpy as jnp
from jax import lax
from jax.experimental import pallas as pl
from jax.experimental.pallas import tpu as pltpu
from jax.sharding import PartitionSpec as P

HEAD_DIM = 64
LANES = 128
STEP = 10


EPS_NORM = 1e-05
BETA_ONE = 0.9
BETA_TWO = 0.999
EPS_ADAM = 1e-08
WEIGHT_DECAY = 0.01
NEG_FILL = -1000000000.0
LOW = jnp.bfloat16
F32 = jnp.float32


def normalize_fwd(values, gain_row, shift_row):
    row_mean = jnp.mean(values, axis=-1, keepdims=True)
    centered = values - row_mean
    variance = jnp.mean(centered * centered, axis=-1, keepdims=True)
    inv_std = lax.rsqrt(variance + EPS_NORM)
    normed = centered * inv_std
    return (normed * gain_row + shift_row, normed, inv_std)


def normalize_back(gradient, normed, inv_std, gain_row):
    grad_norm = gradient * gain_row
    grad_in = inv_std * (
        grad_norm
        - jnp.mean(grad_norm, axis=-1, keepdims=True)
        - normed * jnp.mean(grad_norm * normed, axis=-1, keepdims=True)
    )
    return (grad_in, jnp.sum(gradient * normed, axis=0), jnp.sum(gradient, axis=0))


def adamw(weight, moment, square, gradient, step_rate, decay_rate):
    moment = BETA_ONE * moment + (1.0 - BETA_ONE) * gradient
    square = BETA_TWO * square + (1.0 - BETA_TWO) * gradient * gradient
    direction = (
        moment / (1.0 - BETA_ONE**STEP) / (jnp.sqrt(square / (1.0 - BETA_TWO**STEP)) + EPS_ADAM)
    )
    return (weight - step_rate * (direction + decay_rate * weight), moment, square)


def swap_dp(values, mask):
    size = lax.axis_size("dp")
    return lax.ppermute(values, "dp", [(i, i ^ mask) for i in range(size)])


def swap_tensor(values):
    return lax.ppermute(values, "tensor", [(0, 1), (1, 0)])


def high_bits():
    return list(range(2, lax.axis_size("dp").bit_length() - 1))


def high_groups():
    bits = high_bits()
    return [[1 << bit for bit in bits[i : i + 2]] for i in range(0, len(bits), 2)]


def group_masks(group):
    return [0] + group + ([group[0] ^ group[1]] if len(group) == 2 else [])


def gather_high(shard):
    groups = high_groups()
    for place, group in enumerate(groups):
        pieces = [shard if mask == 0 else swap_dp(shard, mask) for mask in group_masks(group)]
        if place < len(groups) - 1:
            shard = jnp.concatenate(pieces, axis=0)
    return pieces


def send_high(parts):
    masks = group_masks(high_groups()[-1])
    return [parts[0]] + [swap_dp(part, mask) for part, mask in zip(parts[1:], masks[1:])]


def reduce_rest(total):
    for group in reversed(high_groups()[:-1]):
        masks = group_masks(group)
        rows = total.shape[0] // len(masks)
        low = total.astype(LOW)
        total = total[:rows]
        for place, mask in enumerate(masks[1:], 1):
            total = total + swap_dp(low[place * rows : (place + 1) * rows], mask).astype(F32)
    return total


def relative_order(width):
    size = lax.axis_size("dp")
    rows = width // size
    inner_first = high_bits() + [1, 0]
    masks = np.zeros((size,), np.int32)
    for block in range(size):
        for place, bit in enumerate(inner_first):
            if (block >> place) & 1:
                masks[block] |= 1 << bit
    block_mask = jnp.asarray(np.repeat(masks, rows))
    offsets = jnp.asarray(np.tile(np.arange(rows, dtype=np.int32), size))
    return (lax.axis_index("dp") ^ block_mask) * rows + offsets


def dot(left, right):
    return jnp.dot(left, right, preferred_element_type=F32)


def dot_nt(left, right):
    return lax.dot_general(left, right, (((1,), (1,)), ((), ())), preferred_element_type=F32)


def dot_tn(left, right):
    return lax.dot_general(left, right, (((0,), (0,)), ((), ())), preferred_element_type=F32)


def shape_of(rows, columns, kind):
    return jax.ShapeDtypeStruct((rows, columns), kind)


def run(kernel, outs, operands, flops, after=(), grid=(), in_specs=None, out_specs=None, scratch=()):
    count = len(operands)

    def body(*refs):
        kernel(*refs[:count], *refs[count + len(after) :])

    whole = pl.BlockSpec(memory_space=pltpu.VMEM)
    in_specs = in_specs or [whole] * count
    size = sum(v.size * v.dtype.itemsize for v in list(operands) + list(outs))
    return pl.pallas_call(
        body,
        grid=grid,
        out_shape=list(outs),
        in_specs=list(in_specs) + [pl.BlockSpec(memory_space=pl.ANY)] * len(after),
        out_specs=list(out_specs or [whole] * len(outs)),
        scratch_shapes=list(scratch),
        compiler_params=pltpu.CompilerParams(
            vmem_limit_bytes=min(size + ((12 if flops else 4) << 20), 44 << 20)
        ),
        cost_estimate=pl.CostEstimate(flops=flops, bytes_accessed=size, transcendentals=0),
    )(*operands, *after)


def gate(values, after):
    anywhere = pl.BlockSpec(memory_space=pl.ANY)
    return pl.pallas_call(
        lambda *refs: None,
        out_shape=[shape_of(*value.shape, value.dtype) for value in values],
        in_specs=[anywhere] * (len(values) + len(after)),
        out_specs=[anywhere] * len(values),
        input_output_aliases={place: place for place in range(len(values))},
        cost_estimate=pl.CostEstimate(flops=0, bytes_accessed=0, transcendentals=0),
    )(*values, *after)


def join_high_kernel(count, *refs):
    pieces, (first, second) = refs[:count], refs[count:]
    cut = first.shape[1]
    rows = pieces[0].shape[0]
    for place, piece in enumerate(pieces):
        to = slice(place * rows, (place + 1) * rows)
        first[to, :] = piece[:, :cut]
        second[to, :] = piece[:, cut:]


def join_high(pieces, cut, flops=0, after=()):
    rows, columns = pieces[0].shape
    rows = rows * len(pieces)
    return run(
        functools.partial(join_high_kernel, len(pieces)),
        [shape_of(rows, cut, LOW), shape_of(rows, columns - cut, LOW)],
        pieces,
        flops,
        after,
    )


def join_plane_kernel(across, down, across_far, down_far, across_all, down_all):
    columns, rows = across.shape[1], down.shape[0]
    across_all[:, :columns] = across[...]
    across_all[:, columns:] = across_far[...]
    down_all[:rows, :] = down[...]
    down_all[rows:, :] = down_far[...]


def join_plane(across, down, across_far, down_far, after=()):
    return run(
        join_plane_kernel,
        [
            shape_of(across.shape[0], 2 * across.shape[1], LOW),
            shape_of(2 * down.shape[0], down.shape[1], LOW),
        ],
        [across, down, across_far, down_far],
        0,
        after,
    )


def added(left, right, rows, columns):
    return (left[rows, columns].astype(F32) + right[rows, columns].astype(F32)).astype(LOW)


def split_rows_kernel(array, far, keep, send):
    rows = keep.shape[0]
    keep[...] = added(array, far, slice(0, rows), slice(None))
    send[...] = added(array, far, slice(rows, 2 * rows), slice(None))


def split_columns_kernel(array, far, keep, send):
    columns = keep.shape[1]
    keep[...] = added(array, far, slice(None), slice(0, columns))
    send[...] = added(array, far, slice(None), slice(columns, 2 * columns))


def split_rows(array, far, flops=0, after=()):
    part = shape_of(array.shape[0] // 2, array.shape[1], LOW)
    return run(split_rows_kernel, [part, part], [array, far], flops, after)


def split_columns(array, far, flops=0, after=()):
    part = shape_of(array.shape[0], array.shape[1] // 2, LOW)
    return run(split_columns_kernel, [part, part], [array, far], flops, after)


def split_core_kernel(a, a_far, b, b_far, a_keep, a_send, b_keep, b_send):
    split_rows_kernel(a, a_far, a_keep, a_send)
    split_columns_kernel(b, b_far, b_keep, b_send)


def split_core(a, a_far, b, b_far, after=()):
    a_shape = shape_of(a.shape[0] // 2, a.shape[1], LOW)
    b_shape = shape_of(b.shape[0], b.shape[1] // 2, LOW)
    return run(
        split_core_kernel, [a_shape, a_shape, b_shape, b_shape], [a, a_far, b, b_far], 0, after
    )


def sum_kernel(*refs):
    total = refs[0][...].astype(F32)
    for ref in refs[1:-1]:
        total = total + ref[...].astype(F32)
    refs[-1][...] = total


def sum_parts(parts, flops, after=()):
    return run(sum_kernel, [shape_of(*parts[0].shape, F32)], parts, flops, after)


def split_plane_kernel(a, a_far, b, b_far, a_keep, a_send, b_keep, b_send):
    half, rows = a_keep.shape[1], b_keep.shape[0]
    every = slice(None)
    a_keep[...] = added(a, a_far, every, slice(0, half))
    a_send[...] = added(a, a_far, every, slice(half, 2 * half))
    b_keep[...] = added(b, b_far, slice(0, rows), every)
    b_send[...] = added(b, b_far, slice(rows, 2 * rows), every)


def split_plane(a, a_far, b, b_far, after=()):
    a_shape = shape_of(a.shape[0], a.shape[1] // 2, LOW)
    b_shape = shape_of(b.shape[0] // 2, b.shape[1], LOW)
    return run(
        split_plane_kernel, [a_shape, a_shape, b_shape, b_shape], [a, a_far, b, b_far], 0, after
    )


def split_high_kernel(a, a_far, b, b_far, *parts):
    cut = a.shape[1]
    rows = parts[0].shape[0]
    for place, part in enumerate(parts):
        at = slice(place * rows, (place + 1) * rows)
        part[:, :cut] = added(a, a_far, at, slice(None))
        part[:, cut:] = added(b, b_far, at, slice(None))


def split_high(a, a_far, b, b_far, after=()):
    count = len(group_masks(high_groups()[-1]))
    part = shape_of(a.shape[0] // count, a.shape[1] + b.shape[1], LOW)
    return run(split_high_kernel, [part] * count, [a, a_far, b, b_far], 0, after)


def flip(rank, first, second):
    return jnp.where(rank == 0, first, second)


def vectors_kernel(rank_ref, permute, a_own, a_far, relative, bias_q, bias_v, bias_inner):
    rank = rank_ref[0]
    side = a_own.shape[1] // 2
    width = relative.shape[1]
    half = width // 2
    spread = jnp.concatenate(
        [
            (ref[:, side - LANES : side].astype(F32) + ref[:, 2 * side - LANES :].astype(F32))
            for ref in (a_own, a_far)
        ],
        axis=0,
    )
    parts = jnp.transpose(spread)
    parts = [parts[16 * i : 16 * (i + 1)] for i in range(3)]
    relative[...] = ((parts[0] + parts[1]) + parts[2])[2:8]
    natural = [dot_nt(part.astype(LOW), permute[...]) for part in parts]
    natural = (natural[0] + natural[1]) + natural[2]
    for row, target in ((0, bias_q), (1, bias_v)):
        first, second = natural[row : row + 1, :half], natural[row : row + 1, half:]
        target[:, :half] = flip(rank, first, second)
        target[:, half:] = flip(rank, second, first)
    for place in range(2):
        for cut in range(2):
            near, far = 8 + 2 * place + cut, 8 + 2 * (1 - place) + cut
            at = (2 * place + cut) * width
            bias_inner[:, at : at + width] = flip(
                rank, natural[near : near + 1], natural[far : far + 1]
            )


def vector_lanes(rank, permute, grad_q, grad_v, sums_one, sums_two, sums_inner, natural, relative):
    width = natural.shape[1]
    half = width // 2
    natural[...] = jnp.zeros_like(natural)
    relative[...] = jnp.zeros_like(relative)
    for row, source in ((0, grad_q), (1, grad_v)):
        total = jnp.sum(source[...].astype(F32), axis=0, keepdims=True)
        first, second = total[:, :half], total[:, half:]
        natural[row : row + 1, :half] = flip(rank, first, second)
        natural[row : row + 1, half:] = flip(rank, second, first)
    for place in range(2):
        for cut in range(2):
            near, far = (2 * place + cut) * width, (2 * (1 - place) + cut) * width
            row = 8 + 2 * place + cut
            natural[row : row + 1, :] = flip(
                rank, sums_inner[:, near : near + width], sums_inner[:, far : far + width]
            )
    relative[:16, :] = dot(natural[...].astype(LOW), permute[...])
    relative[2:5, :] = sums_one[:3, :]
    relative[5:8, :] = sums_two[:3, :]
    return jnp.transpose(relative[...]).astype(LOW)


def cast_kernel(first, second, target):
    columns = first.shape[1]
    target[:, :columns] = first[...].astype(LOW)
    target[:, columns:] = second[...].astype(LOW)


def project_kernel(rows, a_own, a_far, b_own, b_far, bias_q, bias_v, q, k, v):
    half = a_own.shape[0]
    own_rows, width = q.shape
    part = width // 2
    low, high = rows[:, :half], rows[:, half:]
    a_half, b_half = a_own.shape[1] // 2, b_own.shape[1] // 2
    for side in range(2):
        cols = slice(side * part, (side + 1) * part)
        at = slice(side * a_half, side * a_half + part)
        q[:, cols] = (
            dot(low[:own_rows], a_own[:, at]) + dot(high[:own_rows], a_far[:, at]) + bias_q[:, cols]
        ).astype(LOW)
        at = slice(side * a_half + part, side * a_half + 2 * part)
        k[:, cols] = (dot(low, a_own[:, at]) + dot(high, a_far[:, at])).astype(LOW)
        at = slice(side * b_half, side * b_half + part)
        v[:, cols] = (dot(low, b_own[:, at]) + dot(high, b_far[:, at]) + bias_v[:, cols]).astype(
            LOW
        )


def softmax_down(seg_q, seg_k, key_rows, queries):
    scores = dot_nt(key_rows, queries) * 0.125
    scores = jnp.where(seg_k[...] == seg_q[...], scores, NEG_FILL)
    exp_scores = jnp.exp(scores - jnp.max(scores, axis=0, keepdims=True))
    return exp_scores * (1.0 / jnp.sum(exp_scores, axis=0, keepdims=True))


def two_heads(out):
    joined = jnp.concatenate([out[0][:HEAD_DIM], out[1][HEAD_DIM:]], axis=0)
    return jnp.transpose(joined).astype(LOW)


def attend_kernel(seg_q, seg_k, q, k, v, attended):
    queries, key_rows, value_rows = q[...], k[...], v[...]
    first = lax.broadcasted_iota(jnp.int32, queries.shape, 1) < HEAD_DIM
    out = []
    for mine in (first, jnp.logical_not(first)):
        prob = softmax_down(
            seg_q, seg_k, key_rows, jnp.where(mine, queries, jnp.zeros_like(queries))
        )
        out.append(dot_tn(value_rows, prob.astype(LOW)))
    attended[...] = two_heads(out)


def attend_back_kernel(seg_q, seg_k, q, k, v, grad, grad_q, grad_k, grad_v):
    queries, key_rows, value_rows, grad_rows = q[...], k[...], v[...], grad[...]
    first = lax.broadcasted_iota(jnp.int32, queries.shape, 1) < HEAD_DIM
    first_all = lax.broadcasted_iota(jnp.int32, key_rows.shape, 1) < HEAD_DIM
    blank = jnp.zeros_like(queries)
    out_q, out_k, out_v = [], [], []
    for mine in (first, jnp.logical_not(first)):
        prob = softmax_down(seg_q, seg_k, key_rows, jnp.where(mine, queries, blank))
        grad_prob = dot_nt(value_rows, jnp.where(mine, grad_rows, blank))
        delta = jnp.sum(grad_prob * prob, axis=0, keepdims=True)
        grad_score = (prob * (grad_prob - delta)).astype(LOW)
        out_q.append(dot_tn(key_rows, grad_score) * 0.125)
        out_k.append(dot(grad_score, queries) * 0.125)
        out_v.append(dot(prob.astype(LOW), grad_rows))
    grad_q[...] = two_heads(out_q)
    grad_k[...] = jnp.where(first_all, out_k[0], out_k[1]).astype(LOW)
    grad_v[...] = jnp.where(first_all, out_v[0], out_v[1]).astype(LOW)


def out_norm_kernel(attended, rows, b_own, b_far, vec, y, y_low, normed, inv):
    half = b_own.shape[0]
    own_rows, width = y.shape
    part = width // 2
    b_half = b_own.shape[1] // 2
    near, far = attended[:, :part], attended[:, part:]
    out = []
    for weights in (b_own, b_far):
        out.append(
            dot_nt(near, weights[:, part : 2 * part])
            + dot_nt(far, weights[:, b_half + part : b_half + 2 * part])
        )
    total = rows[:own_rows, :].astype(F32) + jnp.concatenate(out, axis=1) + vec[0:1]
    y_new, normed[...], inv[...] = normalize_fwd(total, vec[1:2], vec[2:3])
    y[...] = y_new
    y_low[...] = y_new.astype(LOW)


def stacked(pieces, at=slice(None)):
    return jnp.concatenate([piece[:, at] for piece in pieces], axis=0)


def hidden_kernel(y_low, *refs):
    pieces, (bias, activation, slope) = refs[:4], refs[4:]
    rows = y_low[...]
    columns = pieces[0].shape[1]
    step = columns // 8
    for start in range(0, columns, step):
        at = slice(start, start + step)
        pre = dot(rows, stacked(pieces, at)) + bias[:, at]
        cdf = 0.5 + 0.5 * lax.erf(pre * (0.5**0.5))
        activation[:, at] = (pre * cdf).astype(LOW)
        slope[:, at] = cdf + pre * jnp.exp(-0.5 * pre * pre) * ((2.0 * np.pi) ** -0.5)


def out_back_kernel(
    activation, own, own_side, far, far_side, y, cot, valid, vec, mixed, grad, grad_low, sums
):
    columns = own.shape[1]
    near, side = activation[:, :columns], activation[:, columns:]
    out = [
        dot_nt(near, first[...]) + dot_nt(side, second[...])
        for first, second in ((own, own_side), (far, far_side))
    ]
    total = y[...] + jnp.concatenate(out, axis=1) + vec[3:4]
    result, normed, inv_std = normalize_fwd(total, vec[4:5], vec[5:6])
    mixed[...] = result.astype(LOW)
    grad_in, gain_sum, shift_sum = normalize_back(
        cot[...] * valid[...], normed, inv_std, vec[4:5]
    )
    grad[...] = grad_in
    grad_low[...] = grad_in.astype(LOW)
    sums[0:1] = jnp.sum(grad_in, axis=0, keepdims=True)
    sums[1:2] = gain_sum[None]
    sums[2:3] = shift_sum[None]


def hidden_back_kernel(grad_low, own, own_side, far, far_side, slope, grad_pre, sums):
    rows = grad_low[...]
    columns = own.shape[1]
    step = columns // 4
    for place, pieces in enumerate(((own, far), (own_side, far_side))):
        for start in range(0, columns, step):
            to = slice(place * columns + start, place * columns + start + step)
            grad_act = dot(rows, stacked(pieces, slice(start, start + step)))
            value = (grad_act * slope[:, to]).astype(LOW)
            grad_pre[:, to] = value
            sums[:, to] = jnp.sum(value.astype(F32), axis=0, keepdims=True)


def norm_back_kernel(
    grad_pre, own, own_side, far, far_side, grad_two, normed, inv, vec, o_own, o_far,
    grad, grad_low, grad_attn, sums,
):
    out = [
        dot_nt(grad_pre[...], stacked(pieces)) for pieces in ((own, own_side), (far, far_side))
    ]
    grad_in, gain_sum, shift_sum = normalize_back(
        grad_two[...] + jnp.concatenate(out, axis=1), normed[...], inv[...], vec[1:2]
    )
    grad[...] = grad_in
    low = grad_in.astype(LOW)
    grad_low[...] = low
    sums[0:1] = jnp.sum(grad_in, axis=0, keepdims=True)
    sums[1:2] = gain_sum[None]
    sums[2:3] = shift_sum[None]
    half = o_own.shape[0]
    part = grad.shape[1] // 2
    o_half = o_own.shape[1] // 2
    for side in range(2):
        at = slice(side * o_half + part, side * o_half + 2 * part)
        grad_attn[:, side * part : (side + 1) * part] = (
            dot(low[:, :half], o_own[:, at]) + dot(low[:, half:], o_far[:, at])
        ).astype(LOW)


def rows_back_kernel(grad_q, grad_k, grad_v, a_own, a_far, b_own, b_far, grad_one, own, away):
    own_rows, width = own.shape
    part = width // 2
    a_half, b_half = a_own.shape[1] // 2, b_own.shape[1] // 2
    half = a_own.shape[0]
    for place, (wa, wb) in enumerate(((a_own, b_own), (a_far, b_far))):
        to = slice(place * half, (place + 1) * half)
        both = jnp.zeros((2 * own_rows, half), F32)
        mine = grad_one[:, to]
        for side in range(2):
            cols = slice(side * part, (side + 1) * part)
            at = side * a_half
            mine = mine + dot_nt(grad_q[:, cols], wa[:, at : at + part])
            both = both + dot_nt(grad_k[:, cols], wa[:, at + part : at + 2 * part])
            at = side * b_half
            both = both + dot_nt(grad_v[:, cols], wb[:, at : at + part])
        own[:, to] = mine + both[:own_rows]
        away[:, to] = both[own_rows:].astype(LOW)


def rows_out_kernel(own, away, permute, out):
    rest = own[...] + away[...].astype(F32)
    total = None
    for _ in range(3):
        part = rest.astype(LOW)
        rest = rest - part.astype(F32)
        moved = dot_nt(part, permute[...])
        total = moved if total is None else total + moved
    out[...] = total


def first_grads_kernel(
    a_half, rank_ref, permute, rows, grad_q, grad_k, grad_v, grad_low, attended,
    sums_one, sums_two, sums_inner, a_send, b_send, a_keep, b_keep, natural, relative,
):
    half = a_keep.shape[0]
    own_rows, width = grad_q.shape
    part = width // 2
    extra = vector_lanes(
        rank_ref[0], permute, grad_q, grad_v, sums_one, sums_two, sums_inner, natural, relative
    )
    for place, to, to_b in ((1, a_send, b_send), (0, a_keep, b_keep)):
        at = slice(place * half, (place + 1) * half)
        both = rows[:, at]
        mine = rows[:own_rows, at]
        low = grad_low[:, at]
        for side in range(2):
            cols = slice(side * part, (side + 1) * part)
            base = side * a_half
            to[:, base : base + part] = dot_tn(mine, grad_q[:, cols]).astype(LOW)
            to[:, base + part : base + 2 * part] = dot_tn(both, grad_k[:, cols]).astype(LOW)
            to[:, base + 2 * part : base + a_half] = extra[at, :]
            base = side * 2 * part
            to_b[:, base : base + part] = dot_tn(both, grad_v[:, cols]).astype(LOW)
            to_b[:, base + part : base + 2 * part] = dot_tn(low, attended[:, cols]).astype(LOW)


def close_kernel(rates, rank_ref, *refs):
    inputs, parts = refs[:9], refs[9:-10]
    outs, turned = refs[-10:-1], refs[-1]
    total = parts[0][...].astype(F32)
    for part in parts[1:]:
        total = total + part[...].astype(F32)
    columns = outs[3].shape[1]
    count, shard_width = outs[6].shape
    a_width = 2 * columns + LANES
    for place, start in enumerate((0, columns, a_width)):
        values = adamw(
            *[ref[place] for ref in inputs[:3]],
            total[:, start : start + columns],
            rates[0],
            WEIGHT_DECAY,
        )
        for out, value in zip(outs[:3], values):
            out[place] = value
    values = adamw(
        *[ref[...] for ref in inputs[3:6]],
        total[:, a_width + columns :],
        rates[1],
        WEIGHT_DECAY,
    )
    for out, value in zip(outs[3:6], values):
        out[...] = value
    lanes = total[:, 2 * columns : a_width]
    turned[...] = jnp.zeros_like(turned)
    turned[:shard_width, :] = flip(
        rank_ref[0], lanes[:shard_width], lanes[shard_width : 2 * shard_width]
    )
    gradient = jnp.transpose(turned[...])[:count, :shard_width]
    values = adamw(*[ref[...] for ref in inputs[6:]], gradient, 0.1, 0.0)
    for out, value in zip(outs[6:], values):
        out[...] = value


def on_device(
    tokens,
    cotangent,
    lengths,
    w_qkv,
    m_qkv,
    v_qkv,
    w_out,
    m_out,
    v_out,
    w_in,
    m_in,
    v_in,
    w_back,
    m_back,
    v_back,
    vectors,
    m_vectors,
    v_vectors,
):
    own_rows, width = tokens.shape
    tensor_rank = lax.axis_index("tensor")
    group_rows = 2 * own_rows
    shard_rows = w_qkv.shape[1]
    part = w_qkv.shape[2]
    hidden_half = w_in.shape[1]
    full_inner = 2 * hidden_half
    half = width // 2
    count = vectors.shape[0]
    shard_width = vectors.shape[1]

    rest = vectors.T
    vec_parts = []
    for _ in range(3):
        vec_parts.append(jnp.pad(rest.astype(LOW), ((0, 0), (0, 16 - count))))
        rest = rest - rest.astype(LOW).astype(F32)
    vec_lanes = jnp.pad(jnp.concatenate(vec_parts, axis=1), ((0, 0), (0, LANES - 48)))
    blank = jnp.zeros_like(vec_lanes)
    vec_lanes = jnp.concatenate(
        [
            jnp.where(tensor_rank == 0, vec_lanes, blank),
            jnp.where(tensor_rank == 0, blank, vec_lanes),
        ],
        axis=0,
    )
    low_qkv = w_qkv.astype(LOW)
    shard_one = jnp.concatenate(
        [low_qkv[0], low_qkv[1], vec_lanes, low_qkv[2], w_out.T.astype(LOW)], axis=1
    )
    a_width = 2 * part + LANES
    rank = tensor_rank.astype(jnp.int32).reshape(1)
    scalar = pl.BlockSpec(memory_space=pltpu.SMEM)
    vmem = pl.BlockSpec(memory_space=pltpu.VMEM)

    tokens_far = swap_tensor(tokens)
    one_high = gather_high(shard_one)
    one = join_high(one_high, a_width)
    one_far = swap_tensor(one[0]), swap_dp(one[1], 2)
    shard_pair = run(
        cast_kernel,
        [shape_of(shard_rows, full_inner, LOW)],
        [w_in, w_back.T],
        0,
        after=one[:1],
    )[0]
    pair_high = gather_high(shard_pair)

    order = relative_order(width)
    permute = (jnp.arange(width, dtype=jnp.int32)[:, None] == order[None, :]).astype(LOW)
    rows_all = jnp.concatenate([dot(tokens, permute), dot(tokens_far, permute)]).astype(LOW)
    cot = dot(cotangent, permute)

    one = join_plane(*one, *one_far, after=[rows_all])
    one_far = swap_dp(one[0], 2), swap_tensor(one[1])
    unit = 2 * own_rows * width * width
    pair = join_high(pair_high, hidden_half, 400 * unit)
    one = join_plane(one[1], one[0], one_far[1], one_far[0], after=pair[:1])[::-1]
    a_own, b_own = one
    a_far, b_far = swap_dp(a_own, 1), swap_dp(b_own, 1)
    pair_far = swap_tensor(pair[0]), swap_dp(pair[1], 2)

    vec, bias_query, bias_value, bias_inner = run(
        vectors_kernel,
        [
            shape_of(6, width, F32),
            shape_of(1, width, F32),
            shape_of(1, width, F32),
            shape_of(1, full_inner, F32),
        ],
        [rank, permute, a_own, a_far],
        1,
        in_specs=[scalar, vmem, vmem, vmem],
    )

    seq_ends = jnp.cumsum(lengths[0])
    local = jnp.arange(own_rows, dtype=jnp.int32)
    own_positions = tensor_rank * own_rows + local
    key_positions = jnp.concatenate([own_positions, (1 - tensor_rank) * own_rows + local])

    def segments(positions):
        return jnp.sum((positions[:, None] >= seq_ends[None, :]).astype(jnp.int32), axis=1)

    seg_own, seg_keys = segments(own_positions)[None, :], segments(key_positions)[:, None]
    valid = (own_positions < seq_ends[-1]).astype(F32)[:, None]

    wide_low = shape_of(own_rows, width, LOW)
    wide = shape_of(own_rows, width, F32)
    group_low = shape_of(group_rows, width, LOW)
    sums_shape = shape_of(8, width, F32)
    queries, key_rows, value_rows = run(
        project_kernel,
        [wide_low, group_low, group_low],
        [rows_all, a_own, a_far, b_own, b_far, bias_query, bias_value],
        5 * unit,
    )
    pair = join_plane(*pair, *pair_far, after=[queries])
    in_near, in_side = pair[0], swap_dp(pair[0], 2)
    back_near, back_side = pair[1], swap_tensor(pair[1])
    in_far, back_far = swap_dp(in_near, 1), swap_dp(back_near, 1)
    pairs = width // LANES
    own_block = pl.BlockSpec((own_rows, LANES), lambda i: (0, i))
    all_block = pl.BlockSpec((group_rows, LANES), lambda i: (0, i))

    def fixed(shape):
        return pl.BlockSpec(shape, lambda i: (0, 0))

    attended = run(
        attend_kernel,
        [wide_low],
        [seg_own, seg_keys, queries, key_rows, value_rows],
        3 * unit,
        after=pair[:1],
        grid=(pairs,),
        in_specs=[fixed((1, own_rows)), fixed((group_rows, 1)), own_block, all_block, all_block],
        out_specs=[own_block],
    )[0]
    first_norm, first_low, normed_one, inv_one = run(
        out_norm_kernel,
        [wide, wide_low, wide, shape_of(own_rows, 1, F32)],
        [attended, rows_all, b_own, b_far, vec],
        2 * unit,
        after=[in_far, back_far],
    )
    in_side, back_side = gate([in_side, back_side], [first_low])
    pieces_in = [in_near, in_side, in_far, swap_dp(in_side, 1)]
    pieces_back = [back_near, back_side, back_far, swap_dp(back_side, 1)]
    activation, slope = run(
        hidden_kernel,
        [shape_of(own_rows, full_inner, LOW), shape_of(own_rows, full_inner, F32)],
        [first_low, *pieces_in, bias_inner],
        8 * unit,
    )
    mixed_rel, grad_two, grad_two_low, sums_two = run(
        out_back_kernel,
        [wide_low, wide, wide_low, sums_shape],
        [activation, *pieces_back, first_norm, cot, valid, vec],
        5 * unit,
    )
    mixed = dot_nt(mixed_rel, permute).astype(LOW)

    def weight_grad(left, right):
        send = dot_tn(left[:, half:], right).astype(LOW)
        return dot_tn(left[:, :half], right).astype(LOW), swap_dp(send, 1)

    outer = weight_grad(grad_two_low, activation)
    grad_pre, sums_inner = run(
        hidden_back_kernel,
        [shape_of(own_rows, full_inner, LOW), shape_of(1, full_inner, F32)],
        [grad_two_low, *pieces_back, slope],
        6 * unit,
    )
    inner = weight_grad(first_low, grad_pre)
    b_keep, b_send = split_columns(*outer, 400 * unit, after=[grad_pre])
    a_keep, a_send = split_rows(*inner, after=[b_keep])
    pair = a_keep, swap_dp(a_send, 2), b_keep, swap_tensor(b_send)
    grad_one, grad_one_low, grad_attn, sums_one = run(
        norm_back_kernel,
        [wide, wide_low, wide_low, sums_shape],
        [grad_pre, *pieces_in, grad_two, normed_one, inv_one, vec, b_own, b_far],
        6 * unit,
        after=[a_keep],
    )
    grad_q, grad_k, grad_v = run(
        attend_back_kernel,
        [wide_low, group_low, group_low],
        [seg_own, seg_keys, queries, key_rows, value_rows, grad_attn],
        5 * unit,
        grid=(pairs,),
        in_specs=[fixed((1, own_rows)), fixed((group_rows, 1))]
        + [own_block, all_block, all_block, own_block],
        out_specs=[own_block, all_block, all_block],
    )
    a_shape, b_shape = shape_of(half, 2 * a_width, LOW), shape_of(half, 4 * part, LOW)
    a_send, b_send, one_a, one_b = run(
        functools.partial(first_grads_kernel, a_width),
        [a_shape, b_shape, a_shape, b_shape],
        [rank, permute, rows_all, grad_q, grad_k, grad_v, grad_one_low, attended]
        + [sums_one, sums_two, sums_inner],
        6 * unit,
        in_specs=[scalar] + [vmem] * 10,
        scratch=[pltpu.VMEM((16, width), F32), pltpu.VMEM((LANES, width), F32)],
    )
    one = one_a, swap_dp(a_send, 1), one_b, swap_dp(b_send, 1)
    a_keep, a_send, b_keep, b_send = split_plane(*pair, after=[one_a, mixed])
    pair = a_keep, swap_tensor(a_send), b_keep, swap_dp(b_send, 2)
    grad_own, grad_away = run(
        rows_back_kernel,
        [wide, wide_low],
        [grad_q, grad_k, grad_v, a_own, a_far, b_own, b_far, grad_one],
        400 * unit,
        after=[a_keep],
    )
    a_keep, a_send, b_keep, b_send = split_core(*one, after=[grad_own])
    one = a_keep, swap_dp(a_send, 2), b_keep, swap_tensor(b_send)
    pair = send_high(split_high(*pair, after=[a_keep]))
    a_keep, a_send, b_keep, b_send = split_plane(*one, after=pair[:1])
    one = a_keep, swap_tensor(a_send), b_keep, swap_dp(b_send, 2)
    pair = sum_parts(pair, 400 * unit, after=[a_keep])
    one = send_high(split_high(*one, after=pair))
    input_grad = run(
        rows_out_kernel,
        [wide],
        [grad_own, swap_tensor(grad_away), permute],
        3 * unit,
        after=one[:1],
    )[0]
    sum_pair = reduce_rest(pair[0])
    summed_in, summed_back = sum_pair[:, :hidden_half], sum_pair[:, hidden_half:].T
    if len(high_groups()) > 1:
        one = [reduce_rest(sum(piece.astype(F32) for piece in one))]
    qkv_shape = jax.ShapeDtypeStruct(w_qkv.shape, F32)
    out_shape = shape_of(shard_rows, part, F32)
    vec_shape = shape_of(count, shard_width, F32)
    done = run(
        functools.partial(
            close_kernel,
            (float(width) ** (-0.5), (4.0 * width / group_rows) ** (-0.5)),
        ),
        [qkv_shape] * 3 + [out_shape] * 3 + [vec_shape] * 3,
        [rank, w_qkv, m_qkv, v_qkv, w_out.T, m_out.T, v_out.T]
        + [vectors, m_vectors, v_vectors, *one],
        unit,
        in_specs=[scalar] + [vmem] * (9 + len(one)),
        scratch=[pltpu.VMEM((LANES, LANES), F32)],
    )
    new_qkv, moment_qkv, square_qkv = done[:3]
    new_out, moment_out, square_out = [value.T for value in done[3:6]]
    new_vectors, moment_vectors, square_vectors = done[6:]
    new_in, moment_in, square_in = adamw(
        w_in, m_in, v_in, summed_in, float(width) ** (-0.5), WEIGHT_DECAY
    )
    new_back, moment_back, square_back = adamw(
        w_back, m_back, v_back, summed_back, float(full_inner) ** (-0.5), WEIGHT_DECAY
    )
    return (
        mixed,
        input_grad,
        new_qkv,
        moment_qkv,
        square_qkv,
        new_out,
        moment_out,
        square_out,
        new_in,
        moment_in,
        square_in,
        new_back,
        moment_back,
        square_back,
        new_vectors,
        moment_vectors,
        square_vectors,
    )


def solution(mesh):
    placed = (
        P(("dp", "tensor"), None),
        P(("dp", "tensor"), None),
        P("dp", None),
        P(None, "dp", "tensor"),
        P(None, "dp", "tensor"),
        P(None, "dp", "tensor"),
        P("tensor", "dp"),
        P("tensor", "dp"),
        P("tensor", "dp"),
        P("dp", "tensor"),
        P("dp", "tensor"),
        P("dp", "tensor"),
        P("tensor", "dp"),
        P("tensor", "dp"),
        P("tensor", "dp"),
        P(None, ("dp", "tensor")),
        P(None, ("dp", "tensor")),
        P(None, ("dp", "tensor")),
    )
    return jax.shard_map(
        on_device,
        mesh=mesh,
        in_specs=placed,
        out_specs=(
            P(("dp", "tensor"), None),
            P(("dp", "tensor"), None),
            P(None, "dp", "tensor"),
            P(None, "dp", "tensor"),
            P(None, "dp", "tensor"),
            P("tensor", "dp"),
            P("tensor", "dp"),
            P("tensor", "dp"),
            P("dp", "tensor"),
            P("dp", "tensor"),
            P("dp", "tensor"),
            P("tensor", "dp"),
            P("tensor", "dp"),
            P("tensor", "dp"),
            P(None, ("dp", "tensor")),
            P(None, ("dp", "tensor")),
            P(None, ("dp", "tensor")),
        ),
        check_vma=False,
    )
```

```python
import functools

import numpy as np

import jax
import jax.numpy as jnp
from jax import lax
from jax.experimental import pallas as pl
from jax.experimental.pallas import tpu as pltpu
from jax.sharding import PartitionSpec as P

HEAD_DIM = 64
LANES = 128
STEP = 10


EPS_NORM = 1e-05
BETA_ONE = 0.9
BETA_TWO = 0.999
EPS_ADAM = 1e-08
WEIGHT_DECAY = 0.01
NEG_FILL = -1000000000.0
LOW = jnp.bfloat16
F32 = jnp.float32


def normalize_fwd(values, gain_row, shift_row):
    row_mean = jnp.mean(values, axis=-1, keepdims=True)
    centered = values - row_mean
    variance = jnp.mean(centered * centered, axis=-1, keepdims=True)
    inv_std = lax.rsqrt(variance + EPS_NORM)
    normed = centered * inv_std
    return (normed * gain_row + shift_row, normed, inv_std)


def normalize_back(gradient, normed, inv_std, gain_row):
    grad_norm = gradient * gain_row
    grad_in = inv_std * (
        grad_norm
        - jnp.mean(grad_norm, axis=-1, keepdims=True)
        - normed * jnp.mean(grad_norm * normed, axis=-1, keepdims=True)
    )
    return (grad_in, jnp.sum(gradient * normed, axis=0), jnp.sum(gradient, axis=0))


def adamw(weight, moment, square, gradient, step_rate, decay_rate):
    moment = BETA_ONE * moment + (1.0 - BETA_ONE) * gradient
    square = BETA_TWO * square + (1.0 - BETA_TWO) * gradient * gradient
    direction = (
        moment / (1.0 - BETA_ONE**STEP) / (jnp.sqrt(square / (1.0 - BETA_TWO**STEP)) + EPS_ADAM)
    )
    return (weight - step_rate * (direction + decay_rate * weight), moment, square)


def swap_dp(values, mask):
    size = lax.axis_size("dp")
    return lax.ppermute(values, "dp", [(i, i ^ mask) for i in range(size)])


def swap_tensor(values):
    return lax.ppermute(values, "tensor", [(0, 1), (1, 0)])


def high_bits():
    return list(range(2, lax.axis_size("dp").bit_length() - 1))


def high_groups():
    bits = high_bits()
    return [[1 << bit for bit in bits[i : i + 2]] for i in range(0, len(bits), 2)]


def group_masks(group):
    return [0] + group + ([group[0] ^ group[1]] if len(group) == 2 else [])


def gather_high(shard):
    groups = high_groups()
    for place, group in enumerate(groups):
        pieces = [shard if mask == 0 else swap_dp(shard, mask) for mask in group_masks(group)]
        if place < len(groups) - 1:
            shard = jnp.concatenate(pieces, axis=0)
    return pieces


def send_high(parts):
    masks = group_masks(high_groups()[-1])
    return [parts[0]] + [swap_dp(part, mask) for part, mask in zip(parts[1:], masks[1:])]


def reduce_rest(total):
    for group in reversed(high_groups()[:-1]):
        masks = group_masks(group)
        rows = total.shape[0] // len(masks)
        low = total.astype(LOW)
        total = total[:rows]
        for place, mask in enumerate(masks[1:], 1):
            total = total + swap_dp(low[place * rows : (place + 1) * rows], mask).astype(F32)
    return total


def relative_order(width):
    size = lax.axis_size("dp")
    rows = width // size
    inner_first = high_bits() + [1, 0]
    masks = np.zeros((size,), np.int32)
    for block in range(size):
        for place, bit in enumerate(inner_first):
            if (block >> place) & 1:
                masks[block] |= 1 << bit
    block_mask = jnp.asarray(np.repeat(masks, rows))
    offsets = jnp.asarray(np.tile(np.arange(rows, dtype=np.int32), size))
    return (lax.axis_index("dp") ^ block_mask) * rows + offsets


def dot(left, right):
    return jnp.dot(left, right, preferred_element_type=F32)


def dot_nt(left, right):
    return lax.dot_general(left, right, (((1,), (1,)), ((), ())), preferred_element_type=F32)


def dot_tn(left, right):
    return lax.dot_general(left, right, (((0,), (0,)), ((), ())), preferred_element_type=F32)


def shape_of(rows, columns, kind):
    return jax.ShapeDtypeStruct((rows, columns), kind)


def run(kernel, outs, operands, flops, after=(), grid=(), in_specs=None, out_specs=None, scratch=()):
    count = len(operands)

    def body(*refs):
        kernel(*refs[:count], *refs[count + len(after) :])

    whole = pl.BlockSpec(memory_space=pltpu.VMEM)
    in_specs = in_specs or [whole] * count
    size = sum(v.size * v.dtype.itemsize for v in list(operands) + list(outs))
    grant = 10 << 20 if grid else size + ((8 if flops else 2) << 20)
    return pl.pallas_call(
        body,
        grid=grid,
        out_shape=list(outs),
        in_specs=list(in_specs) + [pl.BlockSpec(memory_space=pl.ANY)] * len(after),
        out_specs=list(out_specs or [whole] * len(outs)),
        scratch_shapes=list(scratch),
        compiler_params=pltpu.CompilerParams(vmem_limit_bytes=grant),
        cost_estimate=pl.CostEstimate(flops=flops, bytes_accessed=size, transcendentals=0),
    )(*operands, *after)


def gate(values, after):
    anywhere = pl.BlockSpec(memory_space=pl.ANY)
    return pl.pallas_call(
        lambda *refs: None,
        out_shape=[shape_of(*value.shape, value.dtype) for value in values],
        in_specs=[anywhere] * (len(values) + len(after)),
        out_specs=[anywhere] * len(values),
        input_output_aliases={place: place for place in range(len(values))},
        compiler_params=pltpu.CompilerParams(vmem_limit_bytes=1 << 20),
        cost_estimate=pl.CostEstimate(flops=0, bytes_accessed=0, transcendentals=0),
    )(*values, *after)


def join_high_kernel(count, *refs):
    pieces, (first, second) = refs[:count], refs[count:]
    cut = first.shape[1]
    rows = pieces[0].shape[0]
    for place, piece in enumerate(pieces):
        to = slice(place * rows, (place + 1) * rows)
        first[to, :] = piece[:, :cut]
        second[to, :] = piece[:, cut:]


def join_high(pieces, cut, flops=0, after=()):
    rows, columns = pieces[0].shape
    rows = rows * len(pieces)
    return run(
        functools.partial(join_high_kernel, len(pieces)),
        [shape_of(rows, cut, LOW), shape_of(rows, columns - cut, LOW)],
        pieces,
        flops,
        after,
    )


def join_plane_kernel(across, down, across_far, down_far, across_all, down_all):
    columns, rows = across.shape[1], down.shape[0]
    across_all[:, :columns] = across[...]
    across_all[:, columns:] = across_far[...]
    down_all[:rows, :] = down[...]
    down_all[rows:, :] = down_far[...]


def join_plane(across, down, across_far, down_far, after=()):
    return run(
        join_plane_kernel,
        [
            shape_of(across.shape[0], 2 * across.shape[1], LOW),
            shape_of(2 * down.shape[0], down.shape[1], LOW),
        ],
        [across, down, across_far, down_far],
        0,
        after,
    )


def added(left, right, rows, columns):
    return (left[rows, columns].astype(F32) + right[rows, columns].astype(F32)).astype(LOW)


def split_rows_kernel(array, far, keep, send):
    rows = keep.shape[0]
    keep[...] = added(array, far, slice(0, rows), slice(None))
    send[...] = added(array, far, slice(rows, 2 * rows), slice(None))


def split_columns_kernel(array, far, keep, send):
    columns = keep.shape[1]
    keep[...] = added(array, far, slice(None), slice(0, columns))
    send[...] = added(array, far, slice(None), slice(columns, 2 * columns))


def split_rows(array, far, flops=0, after=()):
    part = shape_of(array.shape[0] // 2, array.shape[1], LOW)
    return run(split_rows_kernel, [part, part], [array, far], flops, after)


def split_columns(array, far, flops=0, after=()):
    part = shape_of(array.shape[0], array.shape[1] // 2, LOW)
    return run(split_columns_kernel, [part, part], [array, far], flops, after)


def split_core_kernel(a, a_far, b, b_far, a_keep, a_send, b_keep, b_send):
    split_rows_kernel(a, a_far, a_keep, a_send)
    split_columns_kernel(b, b_far, b_keep, b_send)


def split_core(a, a_far, b, b_far, after=()):
    a_shape = shape_of(a.shape[0] // 2, a.shape[1], LOW)
    b_shape = shape_of(b.shape[0], b.shape[1] // 2, LOW)
    return run(
        split_core_kernel, [a_shape, a_shape, b_shape, b_shape], [a, a_far, b, b_far], 0, after
    )


def sum_kernel(*refs):
    total = refs[0][...].astype(F32)
    for ref in refs[1:-1]:
        total = total + ref[...].astype(F32)
    refs[-1][...] = total


def sum_parts(parts, flops, after=()):
    return run(sum_kernel, [shape_of(*parts[0].shape, F32)], parts, flops, after)


def split_plane_kernel(a, a_far, b, b_far, a_keep, a_send, b_keep, b_send):
    half, rows = a_keep.shape[1], b_keep.shape[0]
    every = slice(None)
    a_keep[...] = added(a, a_far, every, slice(0, half))
    a_send[...] = added(a, a_far, every, slice(half, 2 * half))
    b_keep[...] = added(b, b_far, slice(0, rows), every)
    b_send[...] = added(b, b_far, slice(rows, 2 * rows), every)


def split_plane(a, a_far, b, b_far, after=()):
    a_shape = shape_of(a.shape[0], a.shape[1] // 2, LOW)
    b_shape = shape_of(b.shape[0] // 2, b.shape[1], LOW)
    return run(
        split_plane_kernel, [a_shape, a_shape, b_shape, b_shape], [a, a_far, b, b_far], 0, after
    )


def split_high_kernel(a, a_far, b, b_far, *parts):
    cut = a.shape[1]
    rows = parts[0].shape[0]
    for place, part in enumerate(parts):
        at = slice(place * rows, (place + 1) * rows)
        part[:, :cut] = added(a, a_far, at, slice(None))
        part[:, cut:] = added(b, b_far, at, slice(None))


def split_high(a, a_far, b, b_far, after=()):
    count = len(group_masks(high_groups()[-1]))
    part = shape_of(a.shape[0] // count, a.shape[1] + b.shape[1], LOW)
    return run(split_high_kernel, [part] * count, [a, a_far, b, b_far], 0, after)


def flip(rank, first, second):
    return jnp.where(rank == 0, first, second)


def vectors_kernel(rank_ref, permute, a_own, a_far, relative, bias_q, bias_v, bias_inner):
    rank = rank_ref[0]
    side = a_own.shape[1] // 2
    width = relative.shape[1]
    half = width // 2
    spread = jnp.concatenate(
        [
            (ref[:, side - LANES : side].astype(F32) + ref[:, 2 * side - LANES :].astype(F32))
            for ref in (a_own, a_far)
        ],
        axis=0,
    )
    parts = jnp.transpose(spread)
    parts = [parts[16 * i : 16 * (i + 1)] for i in range(3)]
    relative[...] = ((parts[0] + parts[1]) + parts[2])[2:8]
    natural = [dot_nt(part.astype(LOW), permute[...]) for part in parts]
    natural = (natural[0] + natural[1]) + natural[2]
    for row, target in ((0, bias_q), (1, bias_v)):
        first, second = natural[row : row + 1, :half], natural[row : row + 1, half:]
        target[:, :half] = flip(rank, first, second)
        target[:, half:] = flip(rank, second, first)
    for place in range(2):
        for cut in range(2):
            near, far = 8 + 2 * place + cut, 8 + 2 * (1 - place) + cut
            at = (2 * place + cut) * width
            bias_inner[:, at : at + width] = flip(
                rank, natural[near : near + 1], natural[far : far + 1]
            )


def vector_lanes(rank, permute, grad_q, grad_v, sums_one, sums_two, sums_inner, natural, relative):
    width = natural.shape[1]
    half = width // 2
    natural[...] = jnp.zeros_like(natural)
    relative[...] = jnp.zeros_like(relative)
    for row, source in ((0, grad_q), (1, grad_v)):
        total = jnp.sum(source[...].astype(F32), axis=0, keepdims=True)
        first, second = total[:, :half], total[:, half:]
        natural[row : row + 1, :half] = flip(rank, first, second)
        natural[row : row + 1, half:] = flip(rank, second, first)
    for place in range(2):
        for cut in range(2):
            near, far = (2 * place + cut) * width, (2 * (1 - place) + cut) * width
            row = 8 + 2 * place + cut
            natural[row : row + 1, :] = flip(
                rank, sums_inner[:, near : near + width], sums_inner[:, far : far + width]
            )
    relative[:16, :] = dot(natural[...].astype(LOW), permute[...])
    relative[2:5, :] = sums_one[:3, :]
    relative[5:8, :] = sums_two[:3, :]
    return jnp.transpose(relative[...]).astype(LOW)


def cast_kernel(first, second, target):
    columns = first.shape[1]
    target[:, :columns] = first[...].astype(LOW)
    target[:, columns:] = second[...].astype(LOW)


def project_kernel(rows, a_own, a_far, b_own, b_far, bias_q, bias_v, q, k, v):
    half = a_own.shape[0]
    own_rows, width = q.shape
    part = width // 2
    low, high = rows[:, :half], rows[:, half:]
    a_half, b_half = a_own.shape[1] // 2, b_own.shape[1] // 2
    for side in range(2):
        cols = slice(side * part, (side + 1) * part)
        at = slice(side * a_half, side * a_half + part)
        q[:, cols] = (
            dot(low[:own_rows], a_own[:, at]) + dot(high[:own_rows], a_far[:, at]) + bias_q[:, cols]
        ).astype(LOW)
        at = slice(side * a_half + part, side * a_half + 2 * part)
        k[:, cols] = (dot(low, a_own[:, at]) + dot(high, a_far[:, at])).astype(LOW)
        at = slice(side * b_half, side * b_half + part)
        v[:, cols] = (dot(low, b_own[:, at]) + dot(high, b_far[:, at]) + bias_v[:, cols]).astype(
            LOW
        )


def softmax_down(seg_q, seg_k, key_rows, queries):
    scores = dot_nt(key_rows, queries) * 0.125
    scores = jnp.where(seg_k[...] == seg_q[...], scores, NEG_FILL)
    exp_scores = jnp.exp(scores - jnp.max(scores, axis=0, keepdims=True))
    return exp_scores * (1.0 / jnp.sum(exp_scores, axis=0, keepdims=True))


def two_heads(out):
    joined = jnp.concatenate([out[0][:HEAD_DIM], out[1][HEAD_DIM:]], axis=0)
    return jnp.transpose(joined).astype(LOW)


def attend_kernel(seg_q, seg_k, q, k, v, attended):
    queries, key_rows, value_rows = q[...], k[...], v[...]
    first = lax.broadcasted_iota(jnp.int32, queries.shape, 1) < HEAD_DIM
    out = []
    for mine in (first, jnp.logical_not(first)):
        prob = softmax_down(
            seg_q, seg_k, key_rows, jnp.where(mine, queries, jnp.zeros_like(queries))
        )
        out.append(dot_tn(value_rows, prob.astype(LOW)))
    attended[...] = two_heads(out)


def attend_back_kernel(seg_q, seg_k, q, k, v, grad, grad_q, grad_k, grad_v):
    queries, key_rows, value_rows, grad_rows = q[...], k[...], v[...], grad[...]
    first = lax.broadcasted_iota(jnp.int32, queries.shape, 1) < HEAD_DIM
    first_all = lax.broadcasted_iota(jnp.int32, key_rows.shape, 1) < HEAD_DIM
    blank = jnp.zeros_like(queries)
    out_q, out_k, out_v = [], [], []
    for mine in (first, jnp.logical_not(first)):
        prob = softmax_down(seg_q, seg_k, key_rows, jnp.where(mine, queries, blank))
        grad_prob = dot_nt(value_rows, jnp.where(mine, grad_rows, blank))
        delta = jnp.sum(grad_prob * prob, axis=0, keepdims=True)
        grad_score = (prob * (grad_prob - delta)).astype(LOW)
        out_q.append(dot_tn(key_rows, grad_score) * 0.125)
        out_k.append(dot(grad_score, queries) * 0.125)
        out_v.append(dot(prob.astype(LOW), grad_rows))
    grad_q[...] = two_heads(out_q)
    grad_k[...] = jnp.where(first_all, out_k[0], out_k[1]).astype(LOW)
    grad_v[...] = jnp.where(first_all, out_v[0], out_v[1]).astype(LOW)


def out_norm_kernel(attended, rows, b_own, b_far, vec, y, y_low, normed, inv):
    half = b_own.shape[0]
    own_rows, width = y.shape
    part = width // 2
    b_half = b_own.shape[1] // 2
    near, far = attended[:, :part], attended[:, part:]
    out = []
    for weights in (b_own, b_far):
        out.append(
            dot_nt(near, weights[:, part : 2 * part])
            + dot_nt(far, weights[:, b_half + part : b_half + 2 * part])
        )
    total = rows[:own_rows, :].astype(F32) + jnp.concatenate(out, axis=1) + vec[0:1]
    y_new, normed[...], inv[...] = normalize_fwd(total, vec[1:2], vec[2:3])
    y[...] = y_new
    y_low[...] = y_new.astype(LOW)


def stacked(pieces, at=slice(None)):
    return jnp.concatenate([piece[:, at] for piece in pieces], axis=0)


def hidden_kernel(y_low, *refs):
    pieces, (bias, activation, slope) = refs[:4], refs[4:]
    rows = y_low[...]
    columns = pieces[0].shape[1]
    step = columns // 8
    for start in range(0, columns, step):
        at = slice(start, start + step)
        pre = dot(rows, stacked(pieces, at)) + bias[:, at]
        cdf = 0.5 + 0.5 * lax.erf(pre * (0.5**0.5))
        activation[:, at] = (pre * cdf).astype(LOW)
        slope[:, at] = cdf + pre * jnp.exp(-0.5 * pre * pre) * ((2.0 * np.pi) ** -0.5)


def out_back_kernel(
    activation, own, own_side, far, far_side, y, cot, valid, vec, mixed, grad, grad_low, sums
):
    columns = own.shape[1]
    near, side = activation[:, :columns], activation[:, columns:]
    out = [
        dot_nt(near, first[...]) + dot_nt(side, second[...])
        for first, second in ((own, own_side), (far, far_side))
    ]
    total = y[...] + jnp.concatenate(out, axis=1) + vec[3:4]
    result, normed, inv_std = normalize_fwd(total, vec[4:5], vec[5:6])
    mixed[...] = result.astype(LOW)
    grad_in, gain_sum, shift_sum = normalize_back(
        cot[...] * valid[...], normed, inv_std, vec[4:5]
    )
    grad[...] = grad_in
    grad_low[...] = grad_in.astype(LOW)
    sums[0:1] = jnp.sum(grad_in, axis=0, keepdims=True)
    sums[1:2] = gain_sum[None]
    sums[2:3] = shift_sum[None]


def hidden_back_kernel(grad_low, own, own_side, far, far_side, slope, grad_pre, sums):
    rows = grad_low[...]
    columns = own.shape[1]
    step = columns // 4
    for place, pieces in enumerate(((own, far), (own_side, far_side))):
        for start in range(0, columns, step):
            to = slice(place * columns + start, place * columns + start + step)
            grad_act = dot(rows, stacked(pieces, slice(start, start + step)))
            value = (grad_act * slope[:, to]).astype(LOW)
            grad_pre[:, to] = value
            sums[:, to] = jnp.sum(value.astype(F32), axis=0, keepdims=True)


def norm_back_kernel(
    grad_pre, own, own_side, far, far_side, grad_two, normed, inv, vec, o_own, o_far,
    grad, grad_low, grad_attn, sums,
):
    out = [
        dot_nt(grad_pre[...], stacked(pieces)) for pieces in ((own, own_side), (far, far_side))
    ]
    grad_in, gain_sum, shift_sum = normalize_back(
        grad_two[...] + jnp.concatenate(out, axis=1), normed[...], inv[...], vec[1:2]
    )
    grad[...] = grad_in
    low = grad_in.astype(LOW)
    grad_low[...] = low
    sums[0:1] = jnp.sum(grad_in, axis=0, keepdims=True)
    sums[1:2] = gain_sum[None]
    sums[2:3] = shift_sum[None]
    half = o_own.shape[0]
    part = grad.shape[1] // 2
    o_half = o_own.shape[1] // 2
    for side in range(2):
        at = slice(side * o_half + part, side * o_half + 2 * part)
        grad_attn[:, side * part : (side + 1) * part] = (
            dot(low[:, :half], o_own[:, at]) + dot(low[:, half:], o_far[:, at])
        ).astype(LOW)


def rows_back_kernel(grad_q, grad_k, grad_v, a_own, a_far, b_own, b_far, grad_one, own, away):
    own_rows, width = own.shape
    part = width // 2
    a_half, b_half = a_own.shape[1] // 2, b_own.shape[1] // 2
    half = a_own.shape[0]
    for place, (wa, wb) in enumerate(((a_own, b_own), (a_far, b_far))):
        to = slice(place * half, (place + 1) * half)
        both = jnp.zeros((2 * own_rows, half), F32)
        mine = grad_one[:, to]
        for side in range(2):
            cols = slice(side * part, (side + 1) * part)
            at = side * a_half
            mine = mine + dot_nt(grad_q[:, cols], wa[:, at : at + part])
            both = both + dot_nt(grad_k[:, cols], wa[:, at + part : at + 2 * part])
            at = side * b_half
            both = both + dot_nt(grad_v[:, cols], wb[:, at : at + part])
        own[:, to] = mine + both[:own_rows]
        away[:, to] = both[own_rows:].astype(LOW)


def rows_out_kernel(own, away, permute, out):
    rest = own[...] + away[...].astype(F32)
    total = None
    for _ in range(3):
        part = rest.astype(LOW)
        rest = rest - part.astype(F32)
        moved = dot_nt(part, permute[...])
        total = moved if total is None else total + moved
    out[...] = total


def first_grads_kernel(
    a_half, rank_ref, permute, rows, grad_q, grad_k, grad_v, grad_low, attended,
    sums_one, sums_two, sums_inner, a_send, b_send, a_keep, b_keep, natural, relative,
):
    half = a_keep.shape[0]
    own_rows, width = grad_q.shape
    part = width // 2
    extra = vector_lanes(
        rank_ref[0], permute, grad_q, grad_v, sums_one, sums_two, sums_inner, natural, relative
    )
    for place, to, to_b in ((1, a_send, b_send), (0, a_keep, b_keep)):
        at = slice(place * half, (place + 1) * half)
        both = rows[:, at]
        mine = rows[:own_rows, at]
        low = grad_low[:, at]
        for side in range(2):
            cols = slice(side * part, (side + 1) * part)
            base = side * a_half
            to[:, base : base + part] = dot_tn(mine, grad_q[:, cols]).astype(LOW)
            to[:, base + part : base + 2 * part] = dot_tn(both, grad_k[:, cols]).astype(LOW)
            to[:, base + 2 * part : base + a_half] = extra[at, :]
            base = side * 2 * part
            to_b[:, base : base + part] = dot_tn(both, grad_v[:, cols]).astype(LOW)
            to_b[:, base + part : base + 2 * part] = dot_tn(low, attended[:, cols]).astype(LOW)


def close_kernel(rates, rank_ref, *refs):
    inputs, parts = refs[:9], refs[9:-10]
    outs, turned = refs[-10:-1], refs[-1]
    total = parts[0][...].astype(F32)
    for part in parts[1:]:
        total = total + part[...].astype(F32)
    columns = outs[3].shape[1]
    count, shard_width = outs[6].shape
    a_width = 2 * columns + LANES
    for place, start in enumerate((0, columns, a_width)):
        values = adamw(
            *[ref[place] for ref in inputs[:3]],
            total[:, start : start + columns],
            rates[0],
            WEIGHT_DECAY,
        )
        for out, value in zip(outs[:3], values):
            out[place] = value
    values = adamw(
        *[ref[...] for ref in inputs[3:6]],
        total[:, a_width + columns :],
        rates[1],
        WEIGHT_DECAY,
    )
    for out, value in zip(outs[3:6], values):
        out[...] = value
    lanes = total[:, 2 * columns : a_width]
    turned[...] = jnp.zeros_like(turned)
    turned[:shard_width, :] = flip(
        rank_ref[0], lanes[:shard_width], lanes[shard_width : 2 * shard_width]
    )
    gradient = jnp.transpose(turned[...])[:count, :shard_width]
    values = adamw(*[ref[...] for ref in inputs[6:]], gradient, 0.1, 0.0)
    for out, value in zip(outs[6:], values):
        out[...] = value


def on_device(
    tokens,
    cotangent,
    lengths,
    w_qkv,
    m_qkv,
    v_qkv,
    w_out,
    m_out,
    v_out,
    w_in,
    m_in,
    v_in,
    w_back,
    m_back,
    v_back,
    vectors,
    m_vectors,
    v_vectors,
):
    own_rows, width = tokens.shape
    tensor_rank = lax.axis_index("tensor")
    group_rows = 2 * own_rows
    shard_rows = w_qkv.shape[1]
    part = w_qkv.shape[2]
    hidden_half = w_in.shape[1]
    full_inner = 2 * hidden_half
    half = width // 2
    count = vectors.shape[0]
    shard_width = vectors.shape[1]

    rest = vectors.T
    vec_parts = []
    for _ in range(3):
        vec_parts.append(jnp.pad(rest.astype(LOW), ((0, 0), (0, 16 - count))))
        rest = rest - rest.astype(LOW).astype(F32)
    vec_lanes = jnp.pad(jnp.concatenate(vec_parts, axis=1), ((0, 0), (0, LANES - 48)))
    blank = jnp.zeros_like(vec_lanes)
    vec_lanes = jnp.concatenate(
        [
            jnp.where(tensor_rank == 0, vec_lanes, blank),
            jnp.where(tensor_rank == 0, blank, vec_lanes),
        ],
        axis=0,
    )
    low_qkv = w_qkv.astype(LOW)
    shard_one = jnp.concatenate(
        [low_qkv[0], low_qkv[1], vec_lanes, low_qkv[2], w_out.T.astype(LOW)], axis=1
    )
    a_width = 2 * part + LANES
    rank = tensor_rank.astype(jnp.int32).reshape(1)
    scalar = pl.BlockSpec(memory_space=pltpu.SMEM)
    vmem = pl.BlockSpec(memory_space=pltpu.VMEM)

    tokens_far = swap_tensor(tokens)
    one_high = gather_high(shard_one)
    one = join_high(one_high, a_width)
    one_far = swap_tensor(one[0]), swap_dp(one[1], 2)
    shard_pair = run(
        cast_kernel,
        [shape_of(shard_rows, full_inner, LOW)],
        [w_in, w_back.T],
        0,
        after=one[:1],
    )[0]
    pair_high = gather_high(shard_pair)

    order = relative_order(width)
    permute = (jnp.arange(width, dtype=jnp.int32)[:, None] == order[None, :]).astype(LOW)
    rows_all = jnp.concatenate([dot(tokens, permute), dot(tokens_far, permute)]).astype(LOW)
    cot = dot(cotangent, permute)

    one = join_plane(*one, *one_far, after=[rows_all])
    one_far = swap_dp(one[0], 2), swap_tensor(one[1])
    unit = 2 * own_rows * width * width
    pair = join_high(pair_high, hidden_half, 400 * unit)
    one = join_plane(one[1], one[0], one_far[1], one_far[0], after=pair[:1])[::-1]
    a_own, b_own = one
    a_far, b_far = swap_dp(a_own, 1), swap_dp(b_own, 1)
    pair_far = swap_tensor(pair[0]), swap_dp(pair[1], 2)

    vec, bias_query, bias_value, bias_inner = run(
        vectors_kernel,
        [
            shape_of(6, width, F32),
            shape_of(1, width, F32),
            shape_of(1, width, F32),
            shape_of(1, full_inner, F32),
        ],
        [rank, permute, a_own, a_far],
        1,
        in_specs=[scalar, vmem, vmem, vmem],
    )

    seq_ends = jnp.cumsum(lengths[0])
    local = jnp.arange(own_rows, dtype=jnp.int32)
    own_positions = tensor_rank * own_rows + local
    key_positions = jnp.concatenate([own_positions, (1 - tensor_rank) * own_rows + local])

    def segments(positions):
        return jnp.sum((positions[:, None] >= seq_ends[None, :]).astype(jnp.int32), axis=1)

    seg_own, seg_keys = segments(own_positions)[None, :], segments(key_positions)[:, None]
    valid = (own_positions < seq_ends[-1]).astype(F32)[:, None]

    wide_low = shape_of(own_rows, width, LOW)
    wide = shape_of(own_rows, width, F32)
    group_low = shape_of(group_rows, width, LOW)
    sums_shape = shape_of(8, width, F32)
    queries, key_rows, value_rows = run(
        project_kernel,
        [wide_low, group_low, group_low],
        [rows_all, a_own, a_far, b_own, b_far, bias_query, bias_value],
        5 * unit,
    )
    pair = join_plane(*pair, *pair_far, after=[queries])
    in_near, in_side = pair[0], swap_dp(pair[0], 2)
    back_near, back_side = pair[1], swap_tensor(pair[1])
    in_far, back_far = swap_dp(in_near, 1), swap_dp(back_near, 1)
    pairs = width // LANES
    own_block = pl.BlockSpec((own_rows, LANES), lambda i: (0, i))
    all_block = pl.BlockSpec((group_rows, LANES), lambda i: (0, i))

    def fixed(shape):
        return pl.BlockSpec(shape, lambda i: (0, 0))

    attended = run(
        attend_kernel,
        [wide_low],
        [seg_own, seg_keys, queries, key_rows, value_rows],
        3 * unit,
        after=pair[:1],
        grid=(pairs,),
        in_specs=[fixed((1, own_rows)), fixed((group_rows, 1)), own_block, all_block, all_block],
        out_specs=[own_block],
    )[0]
    first_norm, first_low, normed_one, inv_one = run(
        out_norm_kernel,
        [wide, wide_low, wide, shape_of(own_rows, 1, F32)],
        [attended, rows_all, b_own, b_far, vec],
        2 * unit,
        after=[in_far, back_far],
    )
    in_side, back_side = gate([in_side, back_side], [first_low])
    pieces_in = [in_near, in_side, in_far, swap_dp(in_side, 1)]
    pieces_back = [back_near, back_side, back_far, swap_dp(back_side, 1)]
    activation, slope = run(
        hidden_kernel,
        [shape_of(own_rows, full_inner, LOW), shape_of(own_rows, full_inner, F32)],
        [first_low, *pieces_in, bias_inner],
        8 * unit,
    )
    mixed_rel, grad_two, grad_two_low, sums_two = run(
        out_back_kernel,
        [wide_low, wide, wide_low, sums_shape],
        [activation, *pieces_back, first_norm, cot, valid, vec],
        5 * unit,
    )
    mixed = dot_nt(mixed_rel, permute).astype(LOW)

    def weight_grad(left, right):
        send = dot_tn(left[:, half:], right).astype(LOW)
        return dot_tn(left[:, :half], right).astype(LOW), swap_dp(send, 1)

    outer = weight_grad(grad_two_low, activation)
    grad_pre, sums_inner = run(
        hidden_back_kernel,
        [shape_of(own_rows, full_inner, LOW), shape_of(1, full_inner, F32)],
        [grad_two_low, *pieces_back, slope],
        6 * unit,
    )
    inner = weight_grad(first_low, grad_pre)
    b_keep, b_send = split_columns(*outer, 400 * unit, after=[grad_pre])
    a_keep, a_send = split_rows(*inner, after=[b_keep])
    pair = a_keep, swap_dp(a_send, 2), b_keep, swap_tensor(b_send)
    grad_one, grad_one_low, grad_attn, sums_one = run(
        norm_back_kernel,
        [wide, wide_low, wide_low, sums_shape],
        [grad_pre, *pieces_in, grad_two, normed_one, inv_one, vec, b_own, b_far],
        6 * unit,
        after=[a_keep],
    )
    grad_q, grad_k, grad_v = run(
        attend_back_kernel,
        [wide_low, group_low, group_low],
        [seg_own, seg_keys, queries, key_rows, value_rows, grad_attn],
        5 * unit,
        grid=(pairs,),
        in_specs=[fixed((1, own_rows)), fixed((group_rows, 1))]
        + [own_block, all_block, all_block, own_block],
        out_specs=[own_block, all_block, all_block],
    )
    a_shape, b_shape = shape_of(half, 2 * a_width, LOW), shape_of(half, 4 * part, LOW)
    a_send, b_send, one_a, one_b = run(
        functools.partial(first_grads_kernel, a_width),
        [a_shape, b_shape, a_shape, b_shape],
        [rank, permute, rows_all, grad_q, grad_k, grad_v, grad_one_low, attended]
        + [sums_one, sums_two, sums_inner],
        6 * unit,
        in_specs=[scalar] + [vmem] * 10,
        scratch=[pltpu.VMEM((16, width), F32), pltpu.VMEM((LANES, width), F32)],
    )
    one = one_a, swap_dp(a_send, 1), one_b, swap_dp(b_send, 1)
    a_keep, a_send, b_keep, b_send = split_plane(*pair, after=[one_a, mixed])
    pair = a_keep, swap_tensor(a_send), b_keep, swap_dp(b_send, 2)
    grad_own, grad_away = run(
        rows_back_kernel,
        [wide, wide_low],
        [grad_q, grad_k, grad_v, a_own, a_far, b_own, b_far, grad_one],
        400 * unit,
        after=[a_keep],
    )
    a_keep, a_send, b_keep, b_send = split_core(*one, after=[grad_own])
    one = a_keep, swap_dp(a_send, 2), b_keep, swap_tensor(b_send)
    pair = send_high(split_high(*pair, after=[a_keep]))
    a_keep, a_send, b_keep, b_send = split_plane(*one, after=pair[:1])
    one = a_keep, swap_tensor(a_send), b_keep, swap_dp(b_send, 2)
    pair = sum_parts(pair, 400 * unit, after=[a_keep])
    one = send_high(split_high(*one, after=pair))
    input_grad = run(
        rows_out_kernel,
        [wide],
        [grad_own, swap_tensor(gate([grad_away], one[:1])[0]), permute],
        3 * unit,
        after=one[:1],
    )[0]
    sum_pair = reduce_rest(pair[0])
    summed_in, summed_back = sum_pair[:, :hidden_half], sum_pair[:, hidden_half:].T
    if len(high_groups()) > 1:
        one = [reduce_rest(sum(piece.astype(F32) for piece in one))]
    qkv_shape = jax.ShapeDtypeStruct(w_qkv.shape, F32)
    out_shape = shape_of(shard_rows, part, F32)
    vec_shape = shape_of(count, shard_width, F32)
    done = run(
        functools.partial(
            close_kernel,
            (float(width) ** (-0.5), (4.0 * width / group_rows) ** (-0.5)),
        ),
        [qkv_shape] * 3 + [out_shape] * 3 + [vec_shape] * 3,
        [rank, w_qkv, m_qkv, v_qkv, w_out.T, m_out.T, v_out.T]
        + [vectors, m_vectors, v_vectors, *one],
        unit,
        after=[input_grad],
        in_specs=[scalar] + [vmem] * (9 + len(one)),
        scratch=[pltpu.VMEM((LANES, LANES), F32)],
    )
    new_qkv, moment_qkv, square_qkv = done[:3]
    new_out, moment_out, square_out = [value.T for value in done[3:6]]
    new_vectors, moment_vectors, square_vectors = done[6:]
    new_in, moment_in, square_in = adamw(
        w_in, m_in, v_in, summed_in, float(width) ** (-0.5), WEIGHT_DECAY
    )
    new_back, moment_back, square_back = adamw(
        w_back, m_back, v_back, summed_back, float(full_inner) ** (-0.5), WEIGHT_DECAY
    )
    return (
        mixed,
        input_grad,
        new_qkv,
        moment_qkv,
        square_qkv,
        new_out,
        moment_out,
        square_out,
        new_in,
        moment_in,
        square_in,
        new_back,
        moment_back,
        square_back,
        new_vectors,
        moment_vectors,
        square_vectors,
    )


def solution(mesh):
    placed = (
        P(("dp", "tensor"), None),
        P(("dp", "tensor"), None),
        P("dp", None),
        P(None, "dp", "tensor"),
        P(None, "dp", "tensor"),
        P(None, "dp", "tensor"),
        P("tensor", "dp"),
        P("tensor", "dp"),
        P("tensor", "dp"),
        P("dp", "tensor"),
        P("dp", "tensor"),
        P("dp", "tensor"),
        P("tensor", "dp"),
        P("tensor", "dp"),
        P("tensor", "dp"),
        P(None, ("dp", "tensor")),
        P(None, ("dp", "tensor")),
        P(None, ("dp", "tensor")),
    )
    return jax.shard_map(
        on_device,
        mesh=mesh,
        in_specs=placed,
        out_specs=(
            P(("dp", "tensor"), None),
            P(("dp", "tensor"), None),
            P(None, "dp", "tensor"),
            P(None, "dp", "tensor"),
            P(None, "dp", "tensor"),
            P("tensor", "dp"),
            P("tensor", "dp"),
            P("tensor", "dp"),
            P("dp", "tensor"),
            P("dp", "tensor"),
            P("dp", "tensor"),
            P("tensor", "dp"),
            P("tensor", "dp"),
            P("tensor", "dp"),
            P(None, ("dp", "tensor")),
            P(None, ("dp", "tensor")),
            P(None, ("dp", "tensor")),
        ),
        check_vma=False,
    )
```

```python
import functools

import numpy as np

import jax
import jax.numpy as jnp
from jax import lax
from jax.experimental import pallas as pl
from jax.experimental.pallas import tpu as pltpu
from jax.sharding import PartitionSpec as P

HEAD_DIM = 64
LANES = 128
STEP = 10


EPS_NORM = 1e-05
BETA_ONE = 0.9
BETA_TWO = 0.999
EPS_ADAM = 1e-08
WEIGHT_DECAY = 0.01
NEG_FILL = -1000000000.0
LOW = jnp.bfloat16
F32 = jnp.float32


def normalize_fwd(values, gain_row, shift_row):
    row_mean = jnp.mean(values, axis=-1, keepdims=True)
    centered = values - row_mean
    variance = jnp.mean(centered * centered, axis=-1, keepdims=True)
    inv_std = lax.rsqrt(variance + EPS_NORM)
    normed = centered * inv_std
    return (normed * gain_row + shift_row, normed, inv_std)


def normalize_back(gradient, normed, inv_std, gain_row):
    grad_norm = gradient * gain_row
    grad_in = inv_std * (
        grad_norm
        - jnp.mean(grad_norm, axis=-1, keepdims=True)
        - normed * jnp.mean(grad_norm * normed, axis=-1, keepdims=True)
    )
    return (grad_in, jnp.sum(gradient * normed, axis=0), jnp.sum(gradient, axis=0))


def adamw(weight, moment, square, gradient, step_rate, decay_rate):
    moment = BETA_ONE * moment + (1.0 - BETA_ONE) * gradient
    square = BETA_TWO * square + (1.0 - BETA_TWO) * gradient * gradient
    direction = (
        moment / (1.0 - BETA_ONE**STEP) / (jnp.sqrt(square / (1.0 - BETA_TWO**STEP)) + EPS_ADAM)
    )
    return (weight - step_rate * (direction + decay_rate * weight), moment, square)


def swap_dp(values, mask):
    size = lax.axis_size("dp")
    return lax.ppermute(values, "dp", [(i, i ^ mask) for i in range(size)])


def swap_tensor(values):
    return lax.ppermute(values, "tensor", [(0, 1), (1, 0)])


def high_bits():
    return list(range(2, lax.axis_size("dp").bit_length() - 1))


def high_groups():
    bits = high_bits()
    return [[1 << bit for bit in bits[i : i + 2]] for i in range(0, len(bits), 2)]


def group_masks(group):
    return [0] + group + ([group[0] ^ group[1]] if len(group) == 2 else [])


def gather_high(shard):
    groups = high_groups()
    for place, group in enumerate(groups):
        pieces = [shard if mask == 0 else swap_dp(shard, mask) for mask in group_masks(group)]
        if place < len(groups) - 1:
            shard = jnp.concatenate(pieces, axis=0)
    return pieces


def send_high(parts):
    masks = group_masks(high_groups()[-1])
    return [parts[0]] + [swap_dp(part, mask) for part, mask in zip(parts[1:], masks[1:])]


def reduce_rest(total):
    for group in reversed(high_groups()[:-1]):
        masks = group_masks(group)
        rows = total.shape[0] // len(masks)
        low = total.astype(LOW)
        total = total[:rows]
        for place, mask in enumerate(masks[1:], 1):
            total = total + swap_dp(low[place * rows : (place + 1) * rows], mask).astype(F32)
    return total


def relative_order(width):
    size = lax.axis_size("dp")
    rows = width // size
    inner_first = high_bits() + [1, 0]
    masks = np.zeros((size,), np.int32)
    for block in range(size):
        for place, bit in enumerate(inner_first):
            if (block >> place) & 1:
                masks[block] |= 1 << bit
    block_mask = jnp.asarray(np.repeat(masks, rows))
    offsets = jnp.asarray(np.tile(np.arange(rows, dtype=np.int32), size))
    return (lax.axis_index("dp") ^ block_mask) * rows + offsets


def dot(left, right):
    return jnp.dot(left, right, preferred_element_type=F32)


def dot_nt(left, right):
    return lax.dot_general(left, right, (((1,), (1,)), ((), ())), preferred_element_type=F32)


def dot_tn(left, right):
    return lax.dot_general(left, right, (((0,), (0,)), ((), ())), preferred_element_type=F32)


def shape_of(rows, columns, kind):
    return jax.ShapeDtypeStruct((rows, columns), kind)


def run(kernel, outs, operands, flops, after=(), grid=(), in_specs=None, out_specs=None, scratch=()):
    count = len(operands)

    def body(*refs):
        kernel(*refs[:count], *refs[count + len(after) :])

    whole = pl.BlockSpec(memory_space=pltpu.VMEM)
    in_specs = in_specs or [whole] * count
    size = sum(v.size * v.dtype.itemsize for v in list(operands) + list(outs))
    grant = 10 << 20 if grid else size + ((8 if flops else 2) << 20)
    return pl.pallas_call(
        body,
        grid=grid,
        out_shape=list(outs),
        in_specs=list(in_specs) + [pl.BlockSpec(memory_space=pl.ANY)] * len(after),
        out_specs=list(out_specs or [whole] * len(outs)),
        scratch_shapes=list(scratch),
        compiler_params=pltpu.CompilerParams(vmem_limit_bytes=grant),
        cost_estimate=pl.CostEstimate(flops=flops, bytes_accessed=size, transcendentals=0),
    )(*operands, *after)


def gate(values, after):
    anywhere = pl.BlockSpec(memory_space=pl.ANY)
    return pl.pallas_call(
        lambda *refs: None,
        out_shape=[shape_of(*value.shape, value.dtype) for value in values],
        in_specs=[anywhere] * (len(values) + len(after)),
        out_specs=[anywhere] * len(values),
        input_output_aliases={place: place for place in range(len(values))},
        compiler_params=pltpu.CompilerParams(vmem_limit_bytes=1 << 20),
        cost_estimate=pl.CostEstimate(flops=0, bytes_accessed=0, transcendentals=0),
    )(*values, *after)


def join_high_kernel(count, *refs):
    pieces, (first, second) = refs[:count], refs[count:]
    cut = first.shape[1]
    rows = pieces[0].shape[0]
    for place, piece in enumerate(pieces):
        to = slice(place * rows, (place + 1) * rows)
        first[to, :] = piece[:, :cut]
        second[to, :] = piece[:, cut:]


def join_high(pieces, cut, flops=0, after=()):
    rows, columns = pieces[0].shape
    rows = rows * len(pieces)
    return run(
        functools.partial(join_high_kernel, len(pieces)),
        [shape_of(rows, cut, LOW), shape_of(rows, columns - cut, LOW)],
        pieces,
        flops,
        after,
    )


def join_plane_kernel(across, down, across_far, down_far, across_all, down_all):
    columns, rows = across.shape[1], down.shape[0]
    across_all[:, :columns] = across[...]
    across_all[:, columns:] = across_far[...]
    down_all[:rows, :] = down[...]
    down_all[rows:, :] = down_far[...]


def join_plane(across, down, across_far, down_far, after=()):
    return run(
        join_plane_kernel,
        [
            shape_of(across.shape[0], 2 * across.shape[1], LOW),
            shape_of(2 * down.shape[0], down.shape[1], LOW),
        ],
        [across, down, across_far, down_far],
        0,
        after,
    )


def added(left, right, rows, columns):
    return (left[rows, columns].astype(F32) + right[rows, columns].astype(F32)).astype(LOW)


def split_rows_kernel(array, far, keep, send):
    rows = keep.shape[0]
    keep[...] = added(array, far, slice(0, rows), slice(None))
    send[...] = added(array, far, slice(rows, 2 * rows), slice(None))


def split_columns_kernel(array, far, keep, send):
    columns = keep.shape[1]
    keep[...] = added(array, far, slice(None), slice(0, columns))
    send[...] = added(array, far, slice(None), slice(columns, 2 * columns))


def split_rows(array, far, flops=0, after=()):
    part = shape_of(array.shape[0] // 2, array.shape[1], LOW)
    return run(split_rows_kernel, [part, part], [array, far], flops, after)


def split_columns(array, far, flops=0, after=()):
    part = shape_of(array.shape[0], array.shape[1] // 2, LOW)
    return run(split_columns_kernel, [part, part], [array, far], flops, after)


def split_core_kernel(a, a_far, b, b_far, a_keep, a_send, b_keep, b_send):
    split_rows_kernel(a, a_far, a_keep, a_send)
    split_columns_kernel(b, b_far, b_keep, b_send)


def split_core(a, a_far, b, b_far, after=()):
    a_shape = shape_of(a.shape[0] // 2, a.shape[1], LOW)
    b_shape = shape_of(b.shape[0], b.shape[1] // 2, LOW)
    return run(
        split_core_kernel, [a_shape, a_shape, b_shape, b_shape], [a, a_far, b, b_far], 0, after
    )


def sum_kernel(*refs):
    total = refs[0][...].astype(F32)
    for ref in refs[1:-1]:
        total = total + ref[...].astype(F32)
    refs[-1][...] = total


def sum_parts(parts, flops, after=()):
    return run(sum_kernel, [shape_of(*parts[0].shape, F32)], parts, flops, after)


def split_plane_kernel(a, a_far, b, b_far, a_keep, a_send, b_keep, b_send):
    half, rows = a_keep.shape[1], b_keep.shape[0]
    every = slice(None)
    a_keep[...] = added(a, a_far, every, slice(0, half))
    a_send[...] = added(a, a_far, every, slice(half, 2 * half))
    b_keep[...] = added(b, b_far, slice(0, rows), every)
    b_send[...] = added(b, b_far, slice(rows, 2 * rows), every)


def split_plane(a, a_far, b, b_far, after=()):
    a_shape = shape_of(a.shape[0], a.shape[1] // 2, LOW)
    b_shape = shape_of(b.shape[0] // 2, b.shape[1], LOW)
    return run(
        split_plane_kernel, [a_shape, a_shape, b_shape, b_shape], [a, a_far, b, b_far], 0, after
    )


def split_high_kernel(a, a_far, b, b_far, *parts):
    cut = a.shape[1]
    rows = parts[0].shape[0]
    for place, part in enumerate(parts):
        at = slice(place * rows, (place + 1) * rows)
        part[:, :cut] = added(a, a_far, at, slice(None))
        part[:, cut:] = added(b, b_far, at, slice(None))


def split_high(a, a_far, b, b_far, after=()):
    count = len(group_masks(high_groups()[-1]))
    part = shape_of(a.shape[0] // count, a.shape[1] + b.shape[1], LOW)
    return run(split_high_kernel, [part] * count, [a, a_far, b, b_far], 0, after)


def flip(rank, first, second):
    return jnp.where(rank == 0, first, second)


def vectors_kernel(rank_ref, permute, a_own, a_far, relative, bias_q, bias_v, bias_inner):
    rank = rank_ref[0]
    side = a_own.shape[1] // 2
    width = relative.shape[1]
    half = width // 2
    spread = jnp.concatenate(
        [
            (ref[:, side - LANES : side].astype(F32) + ref[:, 2 * side - LANES :].astype(F32))
            for ref in (a_own, a_far)
        ],
        axis=0,
    )
    parts = jnp.transpose(spread)
    parts = [parts[16 * i : 16 * (i + 1)] for i in range(3)]
    relative[...] = ((parts[0] + parts[1]) + parts[2])[2:8]
    natural = [dot_nt(part.astype(LOW), permute[...]) for part in parts]
    natural = (natural[0] + natural[1]) + natural[2]
    for row, target in ((0, bias_q), (1, bias_v)):
        first, second = natural[row : row + 1, :half], natural[row : row + 1, half:]
        target[:, :half] = flip(rank, first, second)
        target[:, half:] = flip(rank, second, first)
    for place in range(2):
        for cut in range(2):
            near, far = 8 + 2 * place + cut, 8 + 2 * (1 - place) + cut
            at = (2 * place + cut) * width
            bias_inner[:, at : at + width] = flip(
                rank, natural[near : near + 1], natural[far : far + 1]
            )


def vector_lanes(rank, permute, grad_q, grad_v, sums_one, sums_two, sums_inner, natural, relative):
    width = natural.shape[1]
    half = width // 2
    natural[...] = jnp.zeros_like(natural)
    relative[...] = jnp.zeros_like(relative)
    for row, source in ((0, grad_q), (1, grad_v)):
        total = jnp.sum(source[...].astype(F32), axis=0, keepdims=True)
        first, second = total[:, :half], total[:, half:]
        natural[row : row + 1, :half] = flip(rank, first, second)
        natural[row : row + 1, half:] = flip(rank, second, first)
    for place in range(2):
        for cut in range(2):
            near, far = (2 * place + cut) * width, (2 * (1 - place) + cut) * width
            row = 8 + 2 * place + cut
            natural[row : row + 1, :] = flip(
                rank, sums_inner[:, near : near + width], sums_inner[:, far : far + width]
            )
    relative[:16, :] = dot(natural[...].astype(LOW), permute[...])
    relative[2:5, :] = sums_one[:3, :]
    relative[5:8, :] = sums_two[:3, :]
    return jnp.transpose(relative[...]).astype(LOW)


def cast_kernel(first, second, target):
    columns = first.shape[1]
    target[:, :columns] = first[...].astype(LOW)
    target[:, columns:] = second[...].astype(LOW)


def project_kernel(rows, a_own, a_far, b_own, b_far, bias_q, bias_v, q, k, v):
    half = a_own.shape[0]
    own_rows, width = q.shape
    part = width // 2
    low, high = rows[:, :half], rows[:, half:]
    a_half, b_half = a_own.shape[1] // 2, b_own.shape[1] // 2
    for side in range(2):
        cols = slice(side * part, (side + 1) * part)
        at = slice(side * a_half, side * a_half + part)
        q[:, cols] = (
            dot(low[:own_rows], a_own[:, at]) + dot(high[:own_rows], a_far[:, at]) + bias_q[:, cols]
        ).astype(LOW)
        at = slice(side * a_half + part, side * a_half + 2 * part)
        k[:, cols] = (dot(low, a_own[:, at]) + dot(high, a_far[:, at])).astype(LOW)
        at = slice(side * b_half, side * b_half + part)
        v[:, cols] = (dot(low, b_own[:, at]) + dot(high, b_far[:, at]) + bias_v[:, cols]).astype(
            LOW
        )


def segment(lengths, positions):
    end, total = 0, jnp.zeros_like(positions)
    for place in range(lengths.shape[1]):
        end = end + lengths[0, place]
        total = total + (positions >= end).astype(jnp.int32)
    return total


def same_segment(rank, lengths, keys, queries):
    own = lax.broadcasted_iota(jnp.int32, (1, queries), 1) + rank * queries
    rows = lax.broadcasted_iota(jnp.int32, (keys, 1), 0)
    rows = jnp.where(rows < queries, rows + rank * queries, rows - rank * queries)
    return segment(lengths, rows) == segment(lengths, own)


def softmax_down(same, key_rows, queries):
    scores = dot_nt(key_rows, queries) * 0.125
    scores = jnp.where(same, scores, NEG_FILL)
    exp_scores = jnp.exp(scores - jnp.max(scores, axis=0, keepdims=True))
    return exp_scores * (1.0 / jnp.sum(exp_scores, axis=0, keepdims=True))


def two_heads(out):
    joined = jnp.concatenate([out[0][:HEAD_DIM], out[1][HEAD_DIM:]], axis=0)
    return jnp.transpose(joined).astype(LOW)


def attend_kernel(rank_ref, lengths, q, k, v, attended):
    queries, key_rows, value_rows = q[...], k[...], v[...]
    same = same_segment(rank_ref[0], lengths, k.shape[0], q.shape[0])
    first = lax.broadcasted_iota(jnp.int32, queries.shape, 1) < HEAD_DIM
    out = []
    for mine in (first, jnp.logical_not(first)):
        prob = softmax_down(same, key_rows, jnp.where(mine, queries, jnp.zeros_like(queries)))
        out.append(dot_tn(value_rows, prob.astype(LOW)))
    attended[...] = two_heads(out)


def attend_back_kernel(rank_ref, lengths, q, k, v, grad, grad_q, grad_k, grad_v):
    queries, key_rows, value_rows, grad_rows = q[...], k[...], v[...], grad[...]
    same = same_segment(rank_ref[0], lengths, k.shape[0], q.shape[0])
    first = lax.broadcasted_iota(jnp.int32, queries.shape, 1) < HEAD_DIM
    first_all = lax.broadcasted_iota(jnp.int32, key_rows.shape, 1) < HEAD_DIM
    blank = jnp.zeros_like(queries)
    out_q, out_k, out_v = [], [], []
    for mine in (first, jnp.logical_not(first)):
        prob = softmax_down(same, key_rows, jnp.where(mine, queries, blank))
        grad_prob = dot_nt(value_rows, jnp.where(mine, grad_rows, blank))
        delta = jnp.sum(grad_prob * prob, axis=0, keepdims=True)
        grad_score = (prob * (grad_prob - delta)).astype(LOW)
        out_q.append(dot_tn(key_rows, grad_score) * 0.125)
        out_k.append(dot(grad_score, queries) * 0.125)
        out_v.append(dot(prob.astype(LOW), grad_rows))
    grad_q[...] = two_heads(out_q)
    grad_k[...] = jnp.where(first_all, out_k[0], out_k[1]).astype(LOW)
    grad_v[...] = jnp.where(first_all, out_v[0], out_v[1]).astype(LOW)


def out_norm_kernel(attended, rows, b_own, b_far, vec, y, y_low, normed, inv):
    half = b_own.shape[0]
    own_rows, width = y.shape
    part = width // 2
    b_half = b_own.shape[1] // 2
    near, far = attended[:, :part], attended[:, part:]
    out = []
    for weights in (b_own, b_far):
        out.append(
            dot_nt(near, weights[:, part : 2 * part])
            + dot_nt(far, weights[:, b_half + part : b_half + 2 * part])
        )
    total = rows[:own_rows, :].astype(F32) + jnp.concatenate(out, axis=1) + vec[0:1]
    y_new, normed[...], inv[...] = normalize_fwd(total, vec[1:2], vec[2:3])
    y[...] = y_new
    y_low[...] = y_new.astype(LOW)


def stacked(pieces, at=slice(None)):
    return jnp.concatenate([piece[:, at] for piece in pieces], axis=0)


def hidden_kernel(y_low, *refs):
    pieces, (bias, activation, slope) = refs[:4], refs[4:]
    rows = y_low[...]
    columns = pieces[0].shape[1]
    step = columns // 8
    for start in range(0, columns, step):
        at = slice(start, start + step)
        pre = dot(rows, stacked(pieces, at)) + bias[:, at]
        cdf = 0.5 + 0.5 * lax.erf(pre * (0.5**0.5))
        activation[:, at] = (pre * cdf).astype(LOW)
        slope[:, at] = cdf + pre * jnp.exp(-0.5 * pre * pre) * ((2.0 * np.pi) ** -0.5)


def out_back_kernel(
    rank_ref, lengths, activation, own, own_side, far, far_side, y, cot, vec,
    mixed, grad, grad_low, sums,
):
    columns = own.shape[1]
    near, side = activation[:, :columns], activation[:, columns:]
    out = [
        dot_nt(near, first[...]) + dot_nt(side, second[...])
        for first, second in ((own, own_side), (far, far_side))
    ]
    total = y[...] + jnp.concatenate(out, axis=1) + vec[3:4]
    result, normed, inv_std = normalize_fwd(total, vec[4:5], vec[5:6])
    mixed[...] = result.astype(LOW)
    rows = lax.broadcasted_iota(jnp.int32, (y.shape[0], 1), 0) + rank_ref[0] * y.shape[0]
    valid = (segment(lengths, rows) < lengths.shape[1]).astype(F32)
    grad_in, gain_sum, shift_sum = normalize_back(cot[...] * valid, normed, inv_std, vec[4:5])
    grad[...] = grad_in
    grad_low[...] = grad_in.astype(LOW)
    sums[0:1] = jnp.sum(grad_in, axis=0, keepdims=True)
    sums[1:2] = gain_sum[None]
    sums[2:3] = shift_sum[None]


def hidden_back_kernel(grad_low, own, own_side, far, far_side, slope, grad_pre, sums):
    rows = grad_low[...]
    columns = own.shape[1]
    step = columns // 4
    for place, pieces in enumerate(((own, far), (own_side, far_side))):
        for start in range(0, columns, step):
            to = slice(place * columns + start, place * columns + start + step)
            grad_act = dot(rows, stacked(pieces, slice(start, start + step)))
            value = (grad_act * slope[:, to]).astype(LOW)
            grad_pre[:, to] = value
            sums[:, to] = jnp.sum(value.astype(F32), axis=0, keepdims=True)


def norm_back_kernel(
    grad_pre, own, own_side, far, far_side, grad_two, normed, inv, vec, o_own, o_far,
    grad, grad_low, grad_attn, sums,
):
    out = [
        dot_nt(grad_pre[...], stacked(pieces)) for pieces in ((own, own_side), (far, far_side))
    ]
    grad_in, gain_sum, shift_sum = normalize_back(
        grad_two[...] + jnp.concatenate(out, axis=1), normed[...], inv[...], vec[1:2]
    )
    grad[...] = grad_in
    low = grad_in.astype(LOW)
    grad_low[...] = low
    sums[0:1] = jnp.sum(grad_in, axis=0, keepdims=True)
    sums[1:2] = gain_sum[None]
    sums[2:3] = shift_sum[None]
    half = o_own.shape[0]
    part = grad.shape[1] // 2
    o_half = o_own.shape[1] // 2
    for side in range(2):
        at = slice(side * o_half + part, side * o_half + 2 * part)
        grad_attn[:, side * part : (side + 1) * part] = (
            dot(low[:, :half], o_own[:, at]) + dot(low[:, half:], o_far[:, at])
        ).astype(LOW)


def rows_back_kernel(grad_q, grad_k, grad_v, a_own, a_far, b_own, b_far, grad_one, own, away):
    own_rows, width = own.shape
    part = width // 2
    a_half, b_half = a_own.shape[1] // 2, b_own.shape[1] // 2
    half = a_own.shape[0]
    for place, (wa, wb) in enumerate(((a_own, b_own), (a_far, b_far))):
        to = slice(place * half, (place + 1) * half)
        both = jnp.zeros((2 * own_rows, half), F32)
        mine = grad_one[:, to]
        for side in range(2):
            cols = slice(side * part, (side + 1) * part)
            at = side * a_half
            mine = mine + dot_nt(grad_q[:, cols], wa[:, at : at + part])
            both = both + dot_nt(grad_k[:, cols], wa[:, at + part : at + 2 * part])
            at = side * b_half
            both = both + dot_nt(grad_v[:, cols], wb[:, at : at + part])
        own[:, to] = mine + both[:own_rows]
        away[:, to] = both[own_rows:].astype(LOW)


def rows_out_kernel(own, away, permute, out):
    rest = own[...] + away[...].astype(F32)
    total = None
    for _ in range(3):
        part = rest.astype(LOW)
        rest = rest - part.astype(F32)
        moved = dot_nt(part, permute[...])
        total = moved if total is None else total + moved
    out[...] = total


def first_grads_kernel(
    a_half, rank_ref, permute, rows, grad_q, grad_k, grad_v, grad_low, attended,
    sums_one, sums_two, sums_inner, a_send, b_send, a_keep, b_keep, natural, relative,
):
    half = a_keep.shape[0]
    own_rows, width = grad_q.shape
    part = width // 2
    extra = vector_lanes(
        rank_ref[0], permute, grad_q, grad_v, sums_one, sums_two, sums_inner, natural, relative
    )
    for place, to, to_b in ((1, a_send, b_send), (0, a_keep, b_keep)):
        at = slice(place * half, (place + 1) * half)
        both = rows[:, at]
        mine = rows[:own_rows, at]
        low = grad_low[:, at]
        for side in range(2):
            cols = slice(side * part, (side + 1) * part)
            base = side * a_half
            to[:, base : base + part] = dot_tn(mine, grad_q[:, cols]).astype(LOW)
            to[:, base + part : base + 2 * part] = dot_tn(both, grad_k[:, cols]).astype(LOW)
            to[:, base + 2 * part : base + a_half] = extra[at, :]
            base = side * 2 * part
            to_b[:, base : base + part] = dot_tn(both, grad_v[:, cols]).astype(LOW)
            to_b[:, base + part : base + 2 * part] = dot_tn(low, attended[:, cols]).astype(LOW)


def close_kernel(rates, rank_ref, *refs):
    inputs, parts = refs[:9], refs[9:-10]
    outs, turned = refs[-10:-1], refs[-1]
    total = parts[0][...].astype(F32)
    for part in parts[1:]:
        total = total + part[...].astype(F32)
    columns = outs[3].shape[1]
    count, shard_width = outs[6].shape
    a_width = 2 * columns + LANES
    for place, start in enumerate((0, columns, a_width)):
        values = adamw(
            *[ref[place] for ref in inputs[:3]],
            total[:, start : start + columns],
            rates[0],
            WEIGHT_DECAY,
        )
        for out, value in zip(outs[:3], values):
            out[place] = value
    values = adamw(
        *[ref[...] for ref in inputs[3:6]],
        total[:, a_width + columns :],
        rates[1],
        WEIGHT_DECAY,
    )
    for out, value in zip(outs[3:6], values):
        out[...] = value
    lanes = total[:, 2 * columns : a_width]
    turned[...] = jnp.zeros_like(turned)
    turned[:shard_width, :] = flip(
        rank_ref[0], lanes[:shard_width], lanes[shard_width : 2 * shard_width]
    )
    gradient = jnp.transpose(turned[...])[:count, :shard_width]
    values = adamw(*[ref[...] for ref in inputs[6:]], gradient, 0.1, 0.0)
    for out, value in zip(outs[6:], values):
        out[...] = value


def on_device(
    tokens,
    cotangent,
    lengths,
    w_qkv,
    m_qkv,
    v_qkv,
    w_out,
    m_out,
    v_out,
    w_in,
    m_in,
    v_in,
    w_back,
    m_back,
    v_back,
    vectors,
    m_vectors,
    v_vectors,
):
    own_rows, width = tokens.shape
    tensor_rank = lax.axis_index("tensor")
    group_rows = 2 * own_rows
    shard_rows = w_qkv.shape[1]
    part = w_qkv.shape[2]
    hidden_half = w_in.shape[1]
    full_inner = 2 * hidden_half
    half = width // 2
    count = vectors.shape[0]
    shard_width = vectors.shape[1]

    rest = vectors.T
    vec_parts = []
    for _ in range(3):
        vec_parts.append(jnp.pad(rest.astype(LOW), ((0, 0), (0, 16 - count))))
        rest = rest - rest.astype(LOW).astype(F32)
    vec_lanes = jnp.pad(jnp.concatenate(vec_parts, axis=1), ((0, 0), (0, LANES - 48)))
    blank = jnp.zeros_like(vec_lanes)
    vec_lanes = jnp.concatenate(
        [
            jnp.where(tensor_rank == 0, vec_lanes, blank),
            jnp.where(tensor_rank == 0, blank, vec_lanes),
        ],
        axis=0,
    )
    low_qkv = w_qkv.astype(LOW)
    shard_one = jnp.concatenate(
        [low_qkv[0], low_qkv[1], vec_lanes, low_qkv[2], w_out.T.astype(LOW)], axis=1
    )
    a_width = 2 * part + LANES
    rank = tensor_rank.astype(jnp.int32).reshape(1)
    scalar = pl.BlockSpec(memory_space=pltpu.SMEM)
    vmem = pl.BlockSpec(memory_space=pltpu.VMEM)

    tokens_far = swap_tensor(tokens)
    one_high = gather_high(shard_one)
    one = join_high(one_high, a_width)
    one_far = swap_tensor(one[0]), swap_dp(one[1], 2)
    shard_pair = run(
        cast_kernel,
        [shape_of(shard_rows, full_inner, LOW)],
        [w_in, w_back.T],
        0,
        after=one[:1],
    )[0]
    pair_high = gather_high(shard_pair)

    order = relative_order(width)
    permute = (jnp.arange(width, dtype=jnp.int32)[:, None] == order[None, :]).astype(LOW)
    rows_all = jnp.concatenate([dot(tokens, permute), dot(tokens_far, permute)]).astype(LOW)
    cot = dot(cotangent, permute)

    one = join_plane(*one, *one_far, after=[rows_all])
    one_far = swap_dp(one[0], 2), swap_tensor(one[1])
    unit = 2 * own_rows * width * width
    pair = join_high(pair_high, hidden_half, 400 * unit)
    one = join_plane(one[1], one[0], one_far[1], one_far[0], after=pair[:1])[::-1]
    a_own, b_own = one
    a_far, b_far = swap_dp(a_own, 1), swap_dp(b_own, 1)
    pair_far = swap_tensor(pair[0]), swap_dp(pair[1], 2)

    vec, bias_query, bias_value, bias_inner = run(
        vectors_kernel,
        [
            shape_of(6, width, F32),
            shape_of(1, width, F32),
            shape_of(1, width, F32),
            shape_of(1, full_inner, F32),
        ],
        [rank, permute, a_own, a_far],
        1,
        in_specs=[scalar, vmem, vmem, vmem],
    )

    wide_low = shape_of(own_rows, width, LOW)
    wide = shape_of(own_rows, width, F32)
    group_low = shape_of(group_rows, width, LOW)
    sums_shape = shape_of(8, width, F32)
    queries, key_rows, value_rows = run(
        project_kernel,
        [wide_low, group_low, group_low],
        [rows_all, a_own, a_far, b_own, b_far, bias_query, bias_value],
        5 * unit,
    )
    pair = join_plane(*pair, *pair_far, after=[queries])
    in_near, in_side = pair[0], swap_dp(pair[0], 2)
    back_near, back_side = pair[1], swap_tensor(pair[1])
    in_far, back_far = swap_dp(in_near, 1), swap_dp(back_near, 1)
    pairs = width // LANES
    own_block = pl.BlockSpec((own_rows, LANES), lambda i: (0, i))
    all_block = pl.BlockSpec((group_rows, LANES), lambda i: (0, i))

    attended = run(
        attend_kernel,
        [wide_low],
        [rank, lengths, queries, key_rows, value_rows],
        3 * unit,
        after=pair[:1],
        grid=(pairs,),
        in_specs=[scalar, scalar, own_block, all_block, all_block],
        out_specs=[own_block],
    )[0]
    first_norm, first_low, normed_one, inv_one = run(
        out_norm_kernel,
        [wide, wide_low, wide, shape_of(own_rows, 1, F32)],
        [attended, rows_all, b_own, b_far, vec],
        2 * unit,
        after=[in_far, back_far],
    )
    in_side, back_side = gate([in_side, back_side], [first_low])
    pieces_in = [in_near, in_side, in_far, swap_dp(in_side, 1)]
    pieces_back = [back_near, back_side, back_far, swap_dp(back_side, 1)]
    activation, slope = run(
        hidden_kernel,
        [shape_of(own_rows, full_inner, LOW), shape_of(own_rows, full_inner, F32)],
        [first_low, *pieces_in, bias_inner],
        8 * unit,
    )
    mixed_rel, grad_two, grad_two_low, sums_two = run(
        out_back_kernel,
        [wide_low, wide, wide_low, sums_shape],
        [rank, lengths, activation, *pieces_back, first_norm, cot, vec],
        5 * unit,
        in_specs=[scalar, scalar] + [vmem] * 8,
    )
    mixed = dot_nt(mixed_rel, permute).astype(LOW)

    def weight_grad(left, right):
        send = dot_tn(left[:, half:], right).astype(LOW)
        return dot_tn(left[:, :half], right).astype(LOW), swap_dp(send, 1)

    outer = weight_grad(grad_two_low, activation)
    grad_pre, sums_inner = run(
        hidden_back_kernel,
        [shape_of(own_rows, full_inner, LOW), shape_of(1, full_inner, F32)],
        [grad_two_low, *pieces_back, slope],
        6 * unit,
    )
    inner = weight_grad(first_low, grad_pre)
    b_keep, b_send = split_columns(*outer, 400 * unit, after=[grad_pre])
    a_keep, a_send = split_rows(*inner, after=[b_keep])
    pair = a_keep, swap_dp(a_send, 2), b_keep, swap_tensor(b_send)
    grad_one, grad_one_low, grad_attn, sums_one = run(
        norm_back_kernel,
        [wide, wide_low, wide_low, sums_shape],
        [grad_pre, *pieces_in, grad_two, normed_one, inv_one, vec, b_own, b_far],
        6 * unit,
        after=[a_keep],
    )
    grad_q, grad_k, grad_v = run(
        attend_back_kernel,
        [wide_low, group_low, group_low],
        [rank, lengths, queries, key_rows, value_rows, grad_attn],
        5 * unit,
        grid=(pairs,),
        in_specs=[scalar, scalar, own_block, all_block, all_block, own_block],
        out_specs=[own_block, all_block, all_block],
    )
    a_shape, b_shape = shape_of(half, 2 * a_width, LOW), shape_of(half, 4 * part, LOW)
    a_send, b_send, one_a, one_b = run(
        functools.partial(first_grads_kernel, a_width),
        [a_shape, b_shape, a_shape, b_shape],
        [rank, permute, rows_all, grad_q, grad_k, grad_v, grad_one_low, attended]
        + [sums_one, sums_two, sums_inner],
        6 * unit,
        in_specs=[scalar] + [vmem] * 10,
        scratch=[pltpu.VMEM((16, width), F32), pltpu.VMEM((LANES, width), F32)],
    )
    one = one_a, swap_dp(a_send, 1), one_b, swap_dp(b_send, 1)
    a_keep, a_send, b_keep, b_send = split_plane(*pair, after=[one_a, mixed])
    pair = a_keep, swap_tensor(a_send), b_keep, swap_dp(b_send, 2)
    grad_own, grad_away = run(
        rows_back_kernel,
        [wide, wide_low],
        [grad_q, grad_k, grad_v, a_own, a_far, b_own, b_far, grad_one],
        400 * unit,
        after=[a_keep],
    )
    a_keep, a_send, b_keep, b_send = split_core(*one, after=[grad_own])
    one = a_keep, swap_dp(a_send, 2), b_keep, swap_tensor(b_send)
    pair = send_high(split_high(*pair, after=[a_keep]))
    a_keep, a_send, b_keep, b_send = split_plane(*one, after=pair[:1])
    one = a_keep, swap_tensor(a_send), b_keep, swap_dp(b_send, 2)
    pair = sum_parts(pair, 400 * unit, after=[a_keep])
    one = send_high(split_high(*one, after=pair))
    input_grad = run(
        rows_out_kernel,
        [wide],
        [grad_own, swap_tensor(gate([grad_away], one[:1])[0]), permute],
        3 * unit,
        after=one[:1],
    )[0]
    sum_pair = reduce_rest(pair[0])
    summed_in, summed_back = sum_pair[:, :hidden_half], sum_pair[:, hidden_half:].T
    if len(high_groups()) > 1:
        one = [reduce_rest(sum(piece.astype(F32) for piece in one))]
    qkv_shape = jax.ShapeDtypeStruct(w_qkv.shape, F32)
    out_shape = shape_of(shard_rows, part, F32)
    vec_shape = shape_of(count, shard_width, F32)
    done = run(
        functools.partial(
            close_kernel,
            (float(width) ** (-0.5), (4.0 * width / group_rows) ** (-0.5)),
        ),
        [qkv_shape] * 3 + [out_shape] * 3 + [vec_shape] * 3,
        [rank, w_qkv, m_qkv, v_qkv, w_out.T, m_out.T, v_out.T]
        + [vectors, m_vectors, v_vectors, *one],
        unit,
        after=[input_grad],
        in_specs=[scalar] + [vmem] * (9 + len(one)),
        scratch=[pltpu.VMEM((LANES, LANES), F32)],
    )
    new_qkv, moment_qkv, square_qkv = done[:3]
    new_out, moment_out, square_out = [value.T for value in done[3:6]]
    new_vectors, moment_vectors, square_vectors = done[6:]
    new_in, moment_in, square_in = adamw(
        w_in, m_in, v_in, summed_in, float(width) ** (-0.5), WEIGHT_DECAY
    )
    new_back, moment_back, square_back = adamw(
        w_back, m_back, v_back, summed_back, float(full_inner) ** (-0.5), WEIGHT_DECAY
    )
    return (
        mixed,
        input_grad,
        new_qkv,
        moment_qkv,
        square_qkv,
        new_out,
        moment_out,
        square_out,
        new_in,
        moment_in,
        square_in,
        new_back,
        moment_back,
        square_back,
        new_vectors,
        moment_vectors,
        square_vectors,
    )


def solution(mesh):
    placed = (
        P(("dp", "tensor"), None),
        P(("dp", "tensor"), None),
        P("dp", None),
        P(None, "dp", "tensor"),
        P(None, "dp", "tensor"),
        P(None, "dp", "tensor"),
        P("tensor", "dp"),
        P("tensor", "dp"),
        P("tensor", "dp"),
        P("dp", "tensor"),
        P("dp", "tensor"),
        P("dp", "tensor"),
        P("tensor", "dp"),
        P("tensor", "dp"),
        P("tensor", "dp"),
        P(None, ("dp", "tensor")),
        P(None, ("dp", "tensor")),
        P(None, ("dp", "tensor")),
    )
    return jax.shard_map(
        on_device,
        mesh=mesh,
        in_specs=placed,
        out_specs=(
            P(("dp", "tensor"), None),
            P(("dp", "tensor"), None),
            P(None, "dp", "tensor"),
            P(None, "dp", "tensor"),
            P(None, "dp", "tensor"),
            P("tensor", "dp"),
            P("tensor", "dp"),
            P("tensor", "dp"),
            P("dp", "tensor"),
            P("dp", "tensor"),
            P("dp", "tensor"),
            P("tensor", "dp"),
            P("tensor", "dp"),
            P("tensor", "dp"),
            P(None, ("dp", "tensor")),
            P(None, ("dp", "tensor")),
            P(None, ("dp", "tensor")),
        ),
        check_vma=False,
    )
```

```python
import functools

import numpy as np

import jax
import jax.numpy as jnp
from jax import lax
from jax.experimental import pallas as pl
from jax.experimental.pallas import tpu as pltpu
from jax.sharding import PartitionSpec as P

HEAD_DIM = 64
LANES = 128
STEP = 10


EPS_NORM = 1e-05
BETA_ONE = 0.9
BETA_TWO = 0.999
EPS_ADAM = 1e-08
WEIGHT_DECAY = 0.01
NEG_FILL = -1000000000.0
LOW = jnp.bfloat16
F32 = jnp.float32


def normalize_fwd(values, gain_row, shift_row):
    row_mean = jnp.mean(values, axis=-1, keepdims=True)
    centered = values - row_mean
    variance = jnp.mean(centered * centered, axis=-1, keepdims=True)
    inv_std = lax.rsqrt(variance + EPS_NORM)
    normed = centered * inv_std
    return (normed * gain_row + shift_row, normed, inv_std)


def normalize_back(gradient, normed, inv_std, gain_row):
    grad_norm = gradient * gain_row
    grad_in = inv_std * (
        grad_norm
        - jnp.mean(grad_norm, axis=-1, keepdims=True)
        - normed * jnp.mean(grad_norm * normed, axis=-1, keepdims=True)
    )
    return (grad_in, jnp.sum(gradient * normed, axis=0), jnp.sum(gradient, axis=0))


def adamw(weight, moment, square, gradient, step_rate, decay_rate):
    moment = BETA_ONE * moment + (1.0 - BETA_ONE) * gradient
    square = BETA_TWO * square + (1.0 - BETA_TWO) * gradient * gradient
    direction = (
        moment / (1.0 - BETA_ONE**STEP) / (jnp.sqrt(square / (1.0 - BETA_TWO**STEP)) + EPS_ADAM)
    )
    return (weight - step_rate * (direction + decay_rate * weight), moment, square)


def swap_dp(values, mask):
    size = lax.axis_size("dp")
    return lax.ppermute(values, "dp", [(i, i ^ mask) for i in range(size)])


def swap_tensor(values):
    return lax.ppermute(values, "tensor", [(0, 1), (1, 0)])


def high_bits():
    return list(range(2, lax.axis_size("dp").bit_length() - 1))


def high_groups():
    bits = high_bits()
    return [[1 << bit for bit in bits[i : i + 2]] for i in range(0, len(bits), 2)]


def group_masks(group):
    return [0] + group + ([group[0] ^ group[1]] if len(group) == 2 else [])


def gather_high(shard):
    groups = high_groups()
    for place, group in enumerate(groups):
        pieces = [shard if mask == 0 else swap_dp(shard, mask) for mask in group_masks(group)]
        if place < len(groups) - 1:
            shard = jnp.concatenate(pieces, axis=0)
    return pieces


def send_high(parts):
    masks = group_masks(high_groups()[-1])
    return [parts[0]] + [swap_dp(part, mask) for part, mask in zip(parts[1:], masks[1:])]


def reduce_rest(total):
    for group in reversed(high_groups()[:-1]):
        masks = group_masks(group)
        rows = total.shape[0] // len(masks)
        low = total.astype(LOW)
        total = total[:rows]
        for place, mask in enumerate(masks[1:], 1):
            total = total + swap_dp(low[place * rows : (place + 1) * rows], mask).astype(F32)
    return total


def relative_order(width):
    size = lax.axis_size("dp")
    rows = width // size
    inner_first = high_bits() + [1, 0]
    masks = np.zeros((size,), np.int32)
    for block in range(size):
        for place, bit in enumerate(inner_first):
            if (block >> place) & 1:
                masks[block] |= 1 << bit
    block_mask = jnp.asarray(np.repeat(masks, rows))
    offsets = jnp.asarray(np.tile(np.arange(rows, dtype=np.int32), size))
    return (lax.axis_index("dp") ^ block_mask) * rows + offsets


def dot(left, right):
    return jnp.dot(left, right, preferred_element_type=F32)


def dot_nt(left, right):
    return lax.dot_general(left, right, (((1,), (1,)), ((), ())), preferred_element_type=F32)


def dot_tn(left, right):
    return lax.dot_general(left, right, (((0,), (0,)), ((), ())), preferred_element_type=F32)


def shape_of(rows, columns, kind):
    return jax.ShapeDtypeStruct((rows, columns), kind)


def run(kernel, outs, operands, flops, after=(), grid=(), in_specs=None, out_specs=None, scratch=()):
    count = len(operands)

    def body(*refs):
        kernel(*refs[:count], *refs[count + len(after) :])

    whole = pl.BlockSpec(memory_space=pltpu.VMEM)
    in_specs = in_specs or [whole] * count
    size = sum(v.size * v.dtype.itemsize for v in list(operands) + list(outs))
    grant = 10 << 20 if grid else size + ((8 if flops else 2) << 20)
    return pl.pallas_call(
        body,
        grid=grid,
        out_shape=list(outs),
        in_specs=list(in_specs) + [pl.BlockSpec(memory_space=pl.ANY)] * len(after),
        out_specs=list(out_specs or [whole] * len(outs)),
        scratch_shapes=list(scratch),
        compiler_params=pltpu.CompilerParams(vmem_limit_bytes=grant),
        cost_estimate=pl.CostEstimate(flops=flops, bytes_accessed=size, transcendentals=0),
    )(*operands, *after)


def gate(values, after):
    anywhere = pl.BlockSpec(memory_space=pl.ANY)
    return pl.pallas_call(
        lambda *refs: None,
        out_shape=[shape_of(*value.shape, value.dtype) for value in values],
        in_specs=[anywhere] * (len(values) + len(after)),
        out_specs=[anywhere] * len(values),
        input_output_aliases={place: place for place in range(len(values))},
        compiler_params=pltpu.CompilerParams(vmem_limit_bytes=1 << 20),
        cost_estimate=pl.CostEstimate(flops=0, bytes_accessed=0, transcendentals=0),
    )(*values, *after)


def join_high_kernel(count, *refs):
    pieces, (first, second) = refs[:count], refs[count:]
    cut = first.shape[1]
    rows = pieces[0].shape[0]
    for place, piece in enumerate(pieces):
        to = slice(place * rows, (place + 1) * rows)
        first[to, :] = piece[:, :cut]
        second[to, :] = piece[:, cut:]


def join_high(pieces, cut, flops=0, after=()):
    rows, columns = pieces[0].shape
    rows = rows * len(pieces)
    return run(
        functools.partial(join_high_kernel, len(pieces)),
        [shape_of(rows, cut, LOW), shape_of(rows, columns - cut, LOW)],
        pieces,
        flops,
        after,
    )


def join_plane_kernel(across, down, across_far, down_far, across_all, down_all):
    columns, rows = across.shape[1], down.shape[0]
    across_all[:, :columns] = across[...]
    across_all[:, columns:] = across_far[...]
    down_all[:rows, :] = down[...]
    down_all[rows:, :] = down_far[...]


def join_plane(across, down, across_far, down_far, after=()):
    return run(
        join_plane_kernel,
        [
            shape_of(across.shape[0], 2 * across.shape[1], LOW),
            shape_of(2 * down.shape[0], down.shape[1], LOW),
        ],
        [across, down, across_far, down_far],
        0,
        after,
    )


def added(left, right, rows, columns):
    return (left[rows, columns].astype(F32) + right[rows, columns].astype(F32)).astype(LOW)


def split_rows_kernel(array, far, keep, send):
    rows = keep.shape[0]
    keep[...] = added(array, far, slice(0, rows), slice(None))
    send[...] = added(array, far, slice(rows, 2 * rows), slice(None))


def split_columns_kernel(array, far, keep, send):
    columns = keep.shape[1]
    keep[...] = added(array, far, slice(None), slice(0, columns))
    send[...] = added(array, far, slice(None), slice(columns, 2 * columns))


def split_rows(array, far, flops=0, after=()):
    part = shape_of(array.shape[0] // 2, array.shape[1], LOW)
    return run(split_rows_kernel, [part, part], [array, far], flops, after)


def split_columns(array, far, flops=0, after=()):
    part = shape_of(array.shape[0], array.shape[1] // 2, LOW)
    return run(split_columns_kernel, [part, part], [array, far], flops, after)


def split_core_kernel(a, a_far, b, b_far, a_keep, a_send, b_keep, b_send):
    split_rows_kernel(a, a_far, a_keep, a_send)
    split_columns_kernel(b, b_far, b_keep, b_send)


def split_core(a, a_far, b, b_far, after=()):
    a_shape = shape_of(a.shape[0] // 2, a.shape[1], LOW)
    b_shape = shape_of(b.shape[0], b.shape[1] // 2, LOW)
    return run(
        split_core_kernel, [a_shape, a_shape, b_shape, b_shape], [a, a_far, b, b_far], 0, after
    )


def sum_kernel(*refs):
    total = refs[0][...].astype(F32)
    for ref in refs[1:-1]:
        total = total + ref[...].astype(F32)
    refs[-1][...] = total


def sum_parts(parts, flops, after=()):
    return run(sum_kernel, [shape_of(*parts[0].shape, F32)], parts, flops, after)


def split_plane_kernel(a, a_far, b, b_far, a_keep, a_send, b_keep, b_send):
    half, rows = a_keep.shape[1], b_keep.shape[0]
    every = slice(None)
    a_keep[...] = added(a, a_far, every, slice(0, half))
    a_send[...] = added(a, a_far, every, slice(half, 2 * half))
    b_keep[...] = added(b, b_far, slice(0, rows), every)
    b_send[...] = added(b, b_far, slice(rows, 2 * rows), every)


def split_plane(a, a_far, b, b_far, after=()):
    a_shape = shape_of(a.shape[0], a.shape[1] // 2, LOW)
    b_shape = shape_of(b.shape[0] // 2, b.shape[1], LOW)
    return run(
        split_plane_kernel, [a_shape, a_shape, b_shape, b_shape], [a, a_far, b, b_far], 0, after
    )


def split_high_kernel(a, a_far, b, b_far, *parts):
    cut = a.shape[1]
    rows = parts[0].shape[0]
    for place, part in enumerate(parts):
        at = slice(place * rows, (place + 1) * rows)
        part[:, :cut] = added(a, a_far, at, slice(None))
        part[:, cut:] = added(b, b_far, at, slice(None))


def split_high(a, a_far, b, b_far, after=()):
    count = len(group_masks(high_groups()[-1]))
    part = shape_of(a.shape[0] // count, a.shape[1] + b.shape[1], LOW)
    return run(split_high_kernel, [part] * count, [a, a_far, b, b_far], 0, after)


def flip(rank, first, second):
    return jnp.where(rank == 0, first, second)


def vectors_kernel(rank_ref, permute, a_own, a_far, relative, bias_q, bias_v, bias_inner):
    rank = rank_ref[0]
    side = a_own.shape[1] // 2
    width = relative.shape[1]
    half = width // 2
    spread = jnp.concatenate(
        [
            (ref[:, side - LANES : side].astype(F32) + ref[:, 2 * side - LANES :].astype(F32))
            for ref in (a_own, a_far)
        ],
        axis=0,
    )
    parts = jnp.transpose(spread)
    parts = [parts[16 * i : 16 * (i + 1)] for i in range(3)]
    relative[...] = ((parts[0] + parts[1]) + parts[2])[2:8]
    natural = [dot_nt(part.astype(LOW), permute[...]) for part in parts]
    natural = (natural[0] + natural[1]) + natural[2]
    for row, target in ((0, bias_q), (1, bias_v)):
        first, second = natural[row : row + 1, :half], natural[row : row + 1, half:]
        target[:, :half] = flip(rank, first, second)
        target[:, half:] = flip(rank, second, first)
    for place in range(2):
        for cut in range(2):
            near, far = 8 + 2 * place + cut, 8 + 2 * (1 - place) + cut
            at = (2 * place + cut) * width
            bias_inner[:, at : at + width] = flip(
                rank, natural[near : near + 1], natural[far : far + 1]
            )


def vector_lanes(rank, permute, grad_q, grad_v, sums_one, sums_two, sums_inner, natural, relative):
    width = natural.shape[1]
    half = width // 2
    natural[...] = jnp.zeros_like(natural)
    relative[...] = jnp.zeros_like(relative)
    for row, source in ((0, grad_q), (1, grad_v)):
        total = jnp.sum(source[...].astype(F32), axis=0, keepdims=True)
        first, second = total[:, :half], total[:, half:]
        natural[row : row + 1, :half] = flip(rank, first, second)
        natural[row : row + 1, half:] = flip(rank, second, first)
    for place in range(2):
        for cut in range(2):
            near, far = (2 * place + cut) * width, (2 * (1 - place) + cut) * width
            row = 8 + 2 * place + cut
            natural[row : row + 1, :] = flip(
                rank, sums_inner[:, near : near + width], sums_inner[:, far : far + width]
            )
    relative[:16, :] = dot(natural[...].astype(LOW), permute[...])
    relative[2:5, :] = sums_one[:3, :]
    relative[5:8, :] = sums_two[:3, :]
    return jnp.transpose(relative[...]).astype(LOW)


def pack_kernel(rank_ref, w_qkv, w_out, vectors, target, turned):
    columns = w_out.shape[1]
    count, shard_width = vectors.shape
    a_width = 2 * columns + LANES
    turned[...] = jnp.zeros_like(turned)
    for place in range(3):
        turned[16 * place : 16 * place + count, :shard_width] = vectors[...]
    values = jnp.transpose(turned[...])
    lane = lax.broadcasted_iota(jnp.int32, values.shape, 1)
    first = values.astype(LOW).astype(F32)
    second = (values - first).astype(LOW).astype(F32)
    third = values - first - second
    values = jnp.where(lane < 16, first, jnp.where(lane < 32, second, third))[:shard_width]
    blank = jnp.zeros_like(values)
    values = jnp.concatenate(
        [flip(rank_ref[0], values, blank), flip(rank_ref[0], blank, values)], axis=0
    )
    target[:, :columns] = w_qkv[0].astype(LOW)
    target[:, columns : 2 * columns] = w_qkv[1].astype(LOW)
    target[:, 2 * columns : a_width] = values.astype(LOW)
    target[:, a_width : a_width + columns] = w_qkv[2].astype(LOW)
    target[:, a_width + columns :] = w_out[...].astype(LOW)


def cast_kernel(first, second, target):
    columns = first.shape[1]
    target[:, :columns] = first[...].astype(LOW)
    target[:, columns:] = second[...].astype(LOW)


def project_kernel(rows, a_own, a_far, b_own, b_far, bias_q, bias_v, q, k, v):
    half = a_own.shape[0]
    own_rows, width = q.shape
    part = width // 2
    low, high = rows[:, :half], rows[:, half:]
    a_half, b_half = a_own.shape[1] // 2, b_own.shape[1] // 2
    for side in range(2):
        cols = slice(side * part, (side + 1) * part)
        at = slice(side * a_half, side * a_half + part)
        q[:, cols] = (
            dot(low[:own_rows], a_own[:, at]) + dot(high[:own_rows], a_far[:, at]) + bias_q[:, cols]
        ).astype(LOW)
        at = slice(side * a_half + part, side * a_half + 2 * part)
        k[:, cols] = (dot(low, a_own[:, at]) + dot(high, a_far[:, at])).astype(LOW)
        at = slice(side * b_half, side * b_half + part)
        v[:, cols] = (dot(low, b_own[:, at]) + dot(high, b_far[:, at]) + bias_v[:, cols]).astype(
            LOW
        )


def segment(lengths, positions):
    end, total = 0, jnp.zeros_like(positions)
    for place in range(lengths.shape[1]):
        end = end + lengths[0, place]
        total = total + (positions >= end).astype(jnp.int32)
    return total


def same_segment(rank, lengths, keys, queries):
    own = lax.broadcasted_iota(jnp.int32, (1, queries), 1) + rank * queries
    rows = lax.broadcasted_iota(jnp.int32, (keys, 1), 0)
    rows = jnp.where(rows < queries, rows + rank * queries, rows - rank * queries)
    return segment(lengths, rows) == segment(lengths, own)


def softmax_down(same, key_rows, queries):
    scores = dot_nt(key_rows, queries) * 0.125
    scores = jnp.where(same, scores, NEG_FILL)
    exp_scores = jnp.exp(scores - jnp.max(scores, axis=0, keepdims=True))
    return exp_scores * (1.0 / jnp.sum(exp_scores, axis=0, keepdims=True))


def two_heads(out):
    joined = jnp.concatenate([out[0][:HEAD_DIM], out[1][HEAD_DIM:]], axis=0)
    return jnp.transpose(joined).astype(LOW)


def attend_kernel(rank_ref, lengths, q, k, v, attended):
    queries, key_rows, value_rows = q[...], k[...], v[...]
    same = same_segment(rank_ref[0], lengths, k.shape[0], q.shape[0])
    first = lax.broadcasted_iota(jnp.int32, queries.shape, 1) < HEAD_DIM
    out = []
    for mine in (first, jnp.logical_not(first)):
        prob = softmax_down(same, key_rows, jnp.where(mine, queries, jnp.zeros_like(queries)))
        out.append(dot_tn(value_rows, prob.astype(LOW)))
    attended[...] = two_heads(out)


def attend_back_kernel(rank_ref, lengths, q, k, v, grad, grad_q, grad_k, grad_v):
    queries, key_rows, value_rows, grad_rows = q[...], k[...], v[...], grad[...]
    same = same_segment(rank_ref[0], lengths, k.shape[0], q.shape[0])
    first = lax.broadcasted_iota(jnp.int32, queries.shape, 1) < HEAD_DIM
    first_all = lax.broadcasted_iota(jnp.int32, key_rows.shape, 1) < HEAD_DIM
    blank = jnp.zeros_like(queries)
    out_q, out_k, out_v = [], [], []
    for mine in (first, jnp.logical_not(first)):
        prob = softmax_down(same, key_rows, jnp.where(mine, queries, blank))
        grad_prob = dot_nt(value_rows, jnp.where(mine, grad_rows, blank))
        delta = jnp.sum(grad_prob * prob, axis=0, keepdims=True)
        grad_score = (prob * (grad_prob - delta)).astype(LOW)
        out_q.append(dot_tn(key_rows, grad_score) * 0.125)
        out_k.append(dot(grad_score, queries) * 0.125)
        out_v.append(dot(prob.astype(LOW), grad_rows))
    grad_q[...] = two_heads(out_q)
    grad_k[...] = jnp.where(first_all, out_k[0], out_k[1]).astype(LOW)
    grad_v[...] = jnp.where(first_all, out_v[0], out_v[1]).astype(LOW)


def out_norm_kernel(attended, rows, b_own, b_far, vec, y, y_low, normed, inv):
    half = b_own.shape[0]
    own_rows, width = y.shape
    part = width // 2
    b_half = b_own.shape[1] // 2
    near, far = attended[:, :part], attended[:, part:]
    out = []
    for weights in (b_own, b_far):
        out.append(
            dot_nt(near, weights[:, part : 2 * part])
            + dot_nt(far, weights[:, b_half + part : b_half + 2 * part])
        )
    total = rows[:own_rows, :].astype(F32) + jnp.concatenate(out, axis=1) + vec[0:1]
    y_new, normed[...], inv[...] = normalize_fwd(total, vec[1:2], vec[2:3])
    y[...] = y_new
    y_low[...] = y_new.astype(LOW)


def stacked(pieces, at=slice(None)):
    return jnp.concatenate([piece[:, at] for piece in pieces], axis=0)


def hidden_kernel(y_low, *refs):
    pieces, (bias, activation, slope) = refs[:4], refs[4:]
    rows = y_low[...]
    columns = pieces[0].shape[1]
    step = columns // 8
    for start in range(0, columns, step):
        at = slice(start, start + step)
        pre = dot(rows, stacked(pieces, at)) + bias[:, at]
        cdf = 0.5 + 0.5 * lax.erf(pre * (0.5**0.5))
        activation[:, at] = (pre * cdf).astype(LOW)
        slope[:, at] = cdf + pre * jnp.exp(-0.5 * pre * pre) * ((2.0 * np.pi) ** -0.5)


def out_back_kernel(
    rank_ref, lengths, activation, own, own_side, far, far_side, y, cot, vec,
    mixed, grad, grad_low, sums,
):
    columns = own.shape[1]
    near, side = activation[:, :columns], activation[:, columns:]
    out = [
        dot_nt(near, first[...]) + dot_nt(side, second[...])
        for first, second in ((own, own_side), (far, far_side))
    ]
    total = y[...] + jnp.concatenate(out, axis=1) + vec[3:4]
    result, normed, inv_std = normalize_fwd(total, vec[4:5], vec[5:6])
    mixed[...] = result.astype(LOW)
    rows = lax.broadcasted_iota(jnp.int32, (y.shape[0], 1), 0) + rank_ref[0] * y.shape[0]
    valid = (segment(lengths, rows) < lengths.shape[1]).astype(F32)
    grad_in, gain_sum, shift_sum = normalize_back(cot[...] * valid, normed, inv_std, vec[4:5])
    grad[...] = grad_in
    grad_low[...] = grad_in.astype(LOW)
    sums[0:1] = jnp.sum(grad_in, axis=0, keepdims=True)
    sums[1:2] = gain_sum[None]
    sums[2:3] = shift_sum[None]


def hidden_back_kernel(grad_low, own, own_side, far, far_side, slope, grad_pre, sums):
    rows = grad_low[...]
    columns = own.shape[1]
    step = columns // 4
    for place, pieces in enumerate(((own, far), (own_side, far_side))):
        for start in range(0, columns, step):
            to = slice(place * columns + start, place * columns + start + step)
            grad_act = dot(rows, stacked(pieces, slice(start, start + step)))
            value = (grad_act * slope[:, to]).astype(LOW)
            grad_pre[:, to] = value
            sums[:, to] = jnp.sum(value.astype(F32), axis=0, keepdims=True)


def norm_back_kernel(
    grad_pre, own, own_side, far, far_side, grad_two, normed, inv, vec, o_own, o_far,
    grad, grad_low, grad_attn, sums,
):
    out = [
        dot_nt(grad_pre[...], stacked(pieces)) for pieces in ((own, own_side), (far, far_side))
    ]
    grad_in, gain_sum, shift_sum = normalize_back(
        grad_two[...] + jnp.concatenate(out, axis=1), normed[...], inv[...], vec[1:2]
    )
    grad[...] = grad_in
    low = grad_in.astype(LOW)
    grad_low[...] = low
    sums[0:1] = jnp.sum(grad_in, axis=0, keepdims=True)
    sums[1:2] = gain_sum[None]
    sums[2:3] = shift_sum[None]
    half = o_own.shape[0]
    part = grad.shape[1] // 2
    o_half = o_own.shape[1] // 2
    for side in range(2):
        at = slice(side * o_half + part, side * o_half + 2 * part)
        grad_attn[:, side * part : (side + 1) * part] = (
            dot(low[:, :half], o_own[:, at]) + dot(low[:, half:], o_far[:, at])
        ).astype(LOW)


def rows_back_kernel(grad_q, grad_k, grad_v, a_own, a_far, b_own, b_far, grad_one, own, away):
    own_rows, width = own.shape
    part = width // 2
    a_half, b_half = a_own.shape[1] // 2, b_own.shape[1] // 2
    half = a_own.shape[0]
    for place, (wa, wb) in enumerate(((a_own, b_own), (a_far, b_far))):
        to = slice(place * half, (place + 1) * half)
        both = jnp.zeros((2 * own_rows, half), F32)
        mine = grad_one[:, to]
        for side in range(2):
            cols = slice(side * part, (side + 1) * part)
            at = side * a_half
            mine = mine + dot_nt(grad_q[:, cols], wa[:, at : at + part])
            both = both + dot_nt(grad_k[:, cols], wa[:, at + part : at + 2 * part])
            at = side * b_half
            both = both + dot_nt(grad_v[:, cols], wb[:, at : at + part])
        own[:, to] = mine + both[:own_rows]
        away[:, to] = both[own_rows:].astype(LOW)


def rows_out_kernel(own, away, permute, out):
    rest = own[...] + away[...].astype(F32)
    total = None
    for _ in range(3):
        part = rest.astype(LOW)
        rest = rest - part.astype(F32)
        moved = dot_nt(part, permute[...])
        total = moved if total is None else total + moved
    out[...] = total


def first_grads_kernel(
    a_half, rank_ref, permute, rows, grad_q, grad_k, grad_v, grad_low, attended,
    sums_one, sums_two, sums_inner, a_send, b_send, a_keep, b_keep, natural, relative,
):
    half = a_keep.shape[0]
    own_rows, width = grad_q.shape
    part = width // 2
    extra = vector_lanes(
        rank_ref[0], permute, grad_q, grad_v, sums_one, sums_two, sums_inner, natural, relative
    )
    for place, to, to_b in ((1, a_send, b_send), (0, a_keep, b_keep)):
        at = slice(place * half, (place + 1) * half)
        both = rows[:, at]
        mine = rows[:own_rows, at]
        low = grad_low[:, at]
        for side in range(2):
            cols = slice(side * part, (side + 1) * part)
            base = side * a_half
            to[:, base : base + part] = dot_tn(mine, grad_q[:, cols]).astype(LOW)
            to[:, base + part : base + 2 * part] = dot_tn(both, grad_k[:, cols]).astype(LOW)
            to[:, base + 2 * part : base + a_half] = extra[at, :]
            base = side * 2 * part
            to_b[:, base : base + part] = dot_tn(both, grad_v[:, cols]).astype(LOW)
            to_b[:, base + part : base + 2 * part] = dot_tn(low, attended[:, cols]).astype(LOW)


def close_kernel(rates, rank_ref, *refs):
    inputs, parts = refs[:9], refs[9:-10]
    outs, turned = refs[-10:-1], refs[-1]
    total = parts[0][...].astype(F32)
    for part in parts[1:]:
        total = total + part[...].astype(F32)
    columns = outs[3].shape[1]
    count, shard_width = outs[6].shape
    a_width = 2 * columns + LANES
    for place, start in enumerate((0, columns, a_width)):
        values = adamw(
            *[ref[place] for ref in inputs[:3]],
            total[:, start : start + columns],
            rates[0],
            WEIGHT_DECAY,
        )
        for out, value in zip(outs[:3], values):
            out[place] = value
    values = adamw(
        *[ref[...] for ref in inputs[3:6]],
        total[:, a_width + columns :],
        rates[1],
        WEIGHT_DECAY,
    )
    for out, value in zip(outs[3:6], values):
        out[...] = value
    lanes = total[:, 2 * columns : a_width]
    turned[...] = jnp.zeros_like(turned)
    turned[:shard_width, :] = flip(
        rank_ref[0], lanes[:shard_width], lanes[shard_width : 2 * shard_width]
    )
    gradient = jnp.transpose(turned[...])[:count, :shard_width]
    values = adamw(*[ref[...] for ref in inputs[6:]], gradient, 0.1, 0.0)
    for out, value in zip(outs[6:], values):
        out[...] = value


def on_device(
    tokens,
    cotangent,
    lengths,
    w_qkv,
    m_qkv,
    v_qkv,
    w_out,
    m_out,
    v_out,
    w_in,
    m_in,
    v_in,
    w_back,
    m_back,
    v_back,
    vectors,
    m_vectors,
    v_vectors,
):
    own_rows, width = tokens.shape
    tensor_rank = lax.axis_index("tensor")
    group_rows = 2 * own_rows
    shard_rows = w_qkv.shape[1]
    part = w_qkv.shape[2]
    hidden_half = w_in.shape[1]
    full_inner = 2 * hidden_half
    half = width // 2
    count = vectors.shape[0]
    shard_width = vectors.shape[1]

    a_width = 2 * part + LANES
    rank = tensor_rank.astype(jnp.int32).reshape(1)
    scalar = pl.BlockSpec(memory_space=pltpu.SMEM)
    vmem = pl.BlockSpec(memory_space=pltpu.VMEM)
    shard_one = run(
        pack_kernel,
        [shape_of(shard_rows, a_width + 2 * part, LOW)],
        [rank, w_qkv, w_out.T, vectors],
        0,
        in_specs=[scalar] + [vmem] * 3,
        scratch=[pltpu.VMEM((LANES, LANES), F32)],
    )[0]

    tokens_far = swap_tensor(tokens)
    one_high = gather_high(shard_one)
    one = join_high(one_high, a_width)
    one_far = swap_tensor(one[0]), swap_dp(one[1], 2)
    shard_pair = run(
        cast_kernel,
        [shape_of(shard_rows, full_inner, LOW)],
        [w_in, w_back.T],
        0,
        after=one_high[1:2],
    )[0]
    pair_high = gather_high(shard_pair)

    order = relative_order(width)
    permute = (jnp.arange(width, dtype=jnp.int32)[:, None] == order[None, :]).astype(LOW)
    rows_all = jnp.concatenate([dot(tokens, permute), dot(tokens_far, permute)]).astype(LOW)
    cot = dot(cotangent, permute)

    one = join_plane(*one, *one_far, after=[rows_all])
    one_far = swap_dp(one[0], 2), swap_tensor(one[1])
    unit = 2 * own_rows * width * width
    pair = join_high(pair_high, hidden_half, 400 * unit)
    one = join_plane(one[1], one[0], one_far[1], one_far[0], after=pair[:1])[::-1]
    a_own, b_own = one
    a_far, b_far = swap_dp(a_own, 1), swap_dp(b_own, 1)
    pair_far = swap_tensor(pair[0]), swap_dp(pair[1], 2)

    vec, bias_query, bias_value, bias_inner = run(
        vectors_kernel,
        [
            shape_of(6, width, F32),
            shape_of(1, width, F32),
            shape_of(1, width, F32),
            shape_of(1, full_inner, F32),
        ],
        [rank, permute, a_own, a_far],
        1,
        in_specs=[scalar, vmem, vmem, vmem],
    )

    wide_low = shape_of(own_rows, width, LOW)
    wide = shape_of(own_rows, width, F32)
    group_low = shape_of(group_rows, width, LOW)
    sums_shape = shape_of(8, width, F32)
    queries, key_rows, value_rows = run(
        project_kernel,
        [wide_low, group_low, group_low],
        [rows_all, a_own, a_far, b_own, b_far, bias_query, bias_value],
        5 * unit,
    )
    pair = join_plane(*pair, *pair_far, after=[queries])
    in_near, in_side = pair[0], swap_dp(pair[0], 2)
    back_near, back_side = pair[1], swap_tensor(pair[1])
    in_far, back_far = swap_dp(in_near, 1), swap_dp(back_near, 1)
    pairs = width // LANES
    own_block = pl.BlockSpec((own_rows, LANES), lambda i: (0, i))
    all_block = pl.BlockSpec((group_rows, LANES), lambda i: (0, i))

    attended = run(
        attend_kernel,
        [wide_low],
        [rank, lengths, queries, key_rows, value_rows],
        3 * unit,
        after=pair[:1],
        grid=(pairs,),
        in_specs=[scalar, scalar, own_block, all_block, all_block],
        out_specs=[own_block],
    )[0]
    first_norm, first_low, normed_one, inv_one = run(
        out_norm_kernel,
        [wide, wide_low, wide, shape_of(own_rows, 1, F32)],
        [attended, rows_all, b_own, b_far, vec],
        2 * unit,
        after=[in_far, back_far],
    )
    in_side, back_side = gate([in_side, back_side], [first_low])
    pieces_in = [in_near, in_side, in_far, swap_dp(in_side, 1)]
    pieces_back = [back_near, back_side, back_far, swap_dp(back_side, 1)]
    activation, slope = run(
        hidden_kernel,
        [shape_of(own_rows, full_inner, LOW), shape_of(own_rows, full_inner, F32)],
        [first_low, *pieces_in, bias_inner],
        8 * unit,
    )
    mixed_rel, grad_two, grad_two_low, sums_two = run(
        out_back_kernel,
        [wide_low, wide, wide_low, sums_shape],
        [rank, lengths, activation, *pieces_back, first_norm, cot, vec],
        5 * unit,
        in_specs=[scalar, scalar] + [vmem] * 8,
    )
    mixed = dot_nt(mixed_rel, permute).astype(LOW)

    def weight_grad(left, right):
        send = dot_tn(left[:, half:], right).astype(LOW)
        return dot_tn(left[:, :half], right).astype(LOW), swap_dp(send, 1)

    outer = weight_grad(grad_two_low, activation)
    grad_pre, sums_inner = run(
        hidden_back_kernel,
        [shape_of(own_rows, full_inner, LOW), shape_of(1, full_inner, F32)],
        [grad_two_low, *pieces_back, slope],
        6 * unit,
    )
    inner = weight_grad(first_low, grad_pre)
    b_keep, b_send = split_columns(*outer, 400 * unit, after=[grad_pre])
    a_keep, a_send = split_rows(*inner, after=[b_keep])
    pair = a_keep, swap_dp(a_send, 2), b_keep, swap_tensor(b_send)
    grad_one, grad_one_low, grad_attn, sums_one = run(
        norm_back_kernel,
        [wide, wide_low, wide_low, sums_shape],
        [grad_pre, *pieces_in, grad_two, normed_one, inv_one, vec, b_own, b_far],
        6 * unit,
        after=[a_keep],
    )
    grad_q, grad_k, grad_v = run(
        attend_back_kernel,
        [wide_low, group_low, group_low],
        [rank, lengths, queries, key_rows, value_rows, grad_attn],
        5 * unit,
        grid=(pairs,),
        in_specs=[scalar, scalar, own_block, all_block, all_block, own_block],
        out_specs=[own_block, all_block, all_block],
    )
    a_shape, b_shape = shape_of(half, 2 * a_width, LOW), shape_of(half, 4 * part, LOW)
    a_send, b_send, one_a, one_b = run(
        functools.partial(first_grads_kernel, a_width),
        [a_shape, b_shape, a_shape, b_shape],
        [rank, permute, rows_all, grad_q, grad_k, grad_v, grad_one_low, attended]
        + [sums_one, sums_two, sums_inner],
        6 * unit,
        in_specs=[scalar] + [vmem] * 10,
        scratch=[pltpu.VMEM((16, width), F32), pltpu.VMEM((LANES, width), F32)],
    )
    one = one_a, swap_dp(a_send, 1), one_b, swap_dp(b_send, 1)
    a_keep, a_send, b_keep, b_send = split_plane(*pair, after=[one_a, mixed])
    pair = a_keep, swap_tensor(a_send), b_keep, swap_dp(b_send, 2)
    grad_own, grad_away = run(
        rows_back_kernel,
        [wide, wide_low],
        [grad_q, grad_k, grad_v, a_own, a_far, b_own, b_far, grad_one],
        400 * unit,
        after=[a_keep],
    )
    a_keep, a_send, b_keep, b_send = split_core(*one, after=[grad_own])
    one = a_keep, swap_dp(a_send, 2), b_keep, swap_tensor(b_send)
    pair = send_high(split_high(*pair, after=[a_keep]))
    a_keep, a_send, b_keep, b_send = split_plane(*one, after=pair[:1])
    one = a_keep, swap_tensor(a_send), b_keep, swap_dp(b_send, 2)
    pair = sum_parts(pair, 400 * unit, after=[a_keep])
    one = send_high(split_high(*one, after=pair))
    input_grad = run(
        rows_out_kernel,
        [wide],
        [grad_own, swap_tensor(gate([grad_away], pair)[0]), permute],
        3 * unit,
        after=one[:1],
    )[0]
    sum_pair = reduce_rest(gate(pair, one[:1])[0])
    summed_in, summed_back = sum_pair[:, :hidden_half], sum_pair[:, hidden_half:].T
    if len(high_groups()) > 1:
        one = [reduce_rest(sum(piece.astype(F32) for piece in one))]
    qkv_shape = jax.ShapeDtypeStruct(w_qkv.shape, F32)
    out_shape = shape_of(shard_rows, part, F32)
    vec_shape = shape_of(count, shard_width, F32)
    done = run(
        functools.partial(
            close_kernel,
            (float(width) ** (-0.5), (4.0 * width / group_rows) ** (-0.5)),
        ),
        [qkv_shape] * 3 + [out_shape] * 3 + [vec_shape] * 3,
        [rank, w_qkv, m_qkv, v_qkv, w_out.T, m_out.T, v_out.T]
        + [vectors, m_vectors, v_vectors, *one],
        unit,
        after=[input_grad],
        in_specs=[scalar] + [vmem] * (9 + len(one)),
        scratch=[pltpu.VMEM((LANES, LANES), F32)],
    )
    new_qkv, moment_qkv, square_qkv = done[:3]
    new_out, moment_out, square_out = [value.T for value in done[3:6]]
    new_vectors, moment_vectors, square_vectors = done[6:]
    new_in, moment_in, square_in = adamw(
        w_in, m_in, v_in, summed_in, float(width) ** (-0.5), WEIGHT_DECAY
    )
    new_back, moment_back, square_back = adamw(
        w_back, m_back, v_back, summed_back, float(full_inner) ** (-0.5), WEIGHT_DECAY
    )
    return (
        mixed,
        input_grad,
        new_qkv,
        moment_qkv,
        square_qkv,
        new_out,
        moment_out,
        square_out,
        new_in,
        moment_in,
        square_in,
        new_back,
        moment_back,
        square_back,
        new_vectors,
        moment_vectors,
        square_vectors,
    )


def solution(mesh):
    placed = (
        P(("dp", "tensor"), None),
        P(("dp", "tensor"), None),
        P("dp", None),
        P(None, "dp", "tensor"),
        P(None, "dp", "tensor"),
        P(None, "dp", "tensor"),
        P("tensor", "dp"),
        P("tensor", "dp"),
        P("tensor", "dp"),
        P("dp", "tensor"),
        P("dp", "tensor"),
        P("dp", "tensor"),
        P("tensor", "dp"),
        P("tensor", "dp"),
        P("tensor", "dp"),
        P(None, ("dp", "tensor")),
        P(None, ("dp", "tensor")),
        P(None, ("dp", "tensor")),
    )
    return jax.shard_map(
        on_device,
        mesh=mesh,
        in_specs=placed,
        out_specs=(
            P(("dp", "tensor"), None),
            P(("dp", "tensor"), None),
            P(None, "dp", "tensor"),
            P(None, "dp", "tensor"),
            P(None, "dp", "tensor"),
            P("tensor", "dp"),
            P("tensor", "dp"),
            P("tensor", "dp"),
            P("dp", "tensor"),
            P("dp", "tensor"),
            P("dp", "tensor"),
            P("tensor", "dp"),
            P("tensor", "dp"),
            P("tensor", "dp"),
            P(None, ("dp", "tensor")),
            P(None, ("dp", "tensor")),
            P(None, ("dp", "tensor")),
        ),
        check_vma=False,
    )
```

```python
import functools

import numpy as np

import jax
import jax.numpy as jnp
from jax import lax
from jax.experimental import pallas as pl
from jax.experimental.pallas import tpu as pltpu
from jax.sharding import PartitionSpec as P

HEAD_DIM = 64
LANES = 128
STEP = 10


EPS_NORM = 1e-05
BETA_ONE = 0.9
BETA_TWO = 0.999
EPS_ADAM = 1e-08
WEIGHT_DECAY = 0.01
NEG_FILL = -1000000000.0
LOW = jnp.bfloat16
F32 = jnp.float32


def normalize_fwd(values, gain_row, shift_row):
    row_mean = jnp.mean(values, axis=-1, keepdims=True)
    centered = values - row_mean
    variance = jnp.mean(centered * centered, axis=-1, keepdims=True)
    inv_std = lax.rsqrt(variance + EPS_NORM)
    normed = centered * inv_std
    return (normed * gain_row + shift_row, normed, inv_std)


def normalize_back(gradient, normed, inv_std, gain_row):
    grad_norm = gradient * gain_row
    grad_in = inv_std * (
        grad_norm
        - jnp.mean(grad_norm, axis=-1, keepdims=True)
        - normed * jnp.mean(grad_norm * normed, axis=-1, keepdims=True)
    )
    return (grad_in, jnp.sum(gradient * normed, axis=0), jnp.sum(gradient, axis=0))


def adamw(weight, moment, square, gradient, step_rate, decay_rate):
    moment = BETA_ONE * moment + (1.0 - BETA_ONE) * gradient
    square = BETA_TWO * square + (1.0 - BETA_TWO) * gradient * gradient
    direction = (
        moment / (1.0 - BETA_ONE**STEP) / (jnp.sqrt(square / (1.0 - BETA_TWO**STEP)) + EPS_ADAM)
    )
    return (weight - step_rate * (direction + decay_rate * weight), moment, square)


def swap_dp(values, mask):
    size = lax.axis_size("dp")
    return lax.ppermute(values, "dp", [(i, i ^ mask) for i in range(size)])


def swap_tensor(values):
    return lax.ppermute(values, "tensor", [(0, 1), (1, 0)])


def high_bits():
    return list(range(2, lax.axis_size("dp").bit_length() - 1))


def high_groups():
    bits = high_bits()
    return [[1 << bit for bit in bits[i : i + 2]] for i in range(0, len(bits), 2)]


def group_masks(group):
    return [0] + group + ([group[0] ^ group[1]] if len(group) == 2 else [])


def gather_high(shard):
    groups = high_groups()
    for place, group in enumerate(groups):
        pieces = [shard if mask == 0 else swap_dp(shard, mask) for mask in group_masks(group)]
        if place < len(groups) - 1:
            shard = jnp.concatenate(pieces, axis=0)
    return pieces


def send_high(parts):
    masks = group_masks(high_groups()[-1])
    return [parts[0]] + [swap_dp(part, mask) for part, mask in zip(parts[1:], masks[1:])]


def reduce_rest(total):
    for group in reversed(high_groups()[:-1]):
        masks = group_masks(group)
        rows = total.shape[0] // len(masks)
        low = total.astype(LOW)
        total = total[:rows]
        for place, mask in enumerate(masks[1:], 1):
            total = total + swap_dp(low[place * rows : (place + 1) * rows], mask).astype(F32)
    return total


def relative_order(width):
    size = lax.axis_size("dp")
    rows = width // size
    inner_first = high_bits() + [1, 0]
    masks = np.zeros((size,), np.int32)
    for block in range(size):
        for place, bit in enumerate(inner_first):
            if (block >> place) & 1:
                masks[block] |= 1 << bit
    block_mask = jnp.asarray(np.repeat(masks, rows))
    offsets = jnp.asarray(np.tile(np.arange(rows, dtype=np.int32), size))
    return (lax.axis_index("dp") ^ block_mask) * rows + offsets


def dot(left, right):
    return jnp.dot(left, right, preferred_element_type=F32)


def dot_nt(left, right):
    return lax.dot_general(left, right, (((1,), (1,)), ((), ())), preferred_element_type=F32)


def dot_tn(left, right):
    return lax.dot_general(left, right, (((0,), (0,)), ((), ())), preferred_element_type=F32)


def shape_of(rows, columns, kind):
    return jax.ShapeDtypeStruct((rows, columns), kind)


def run(kernel, outs, operands, flops, after=(), grid=(), in_specs=None, out_specs=None, scratch=()):
    count = len(operands)

    def body(*refs):
        kernel(*refs[:count], *refs[count + len(after) :])

    whole = pl.BlockSpec(memory_space=pltpu.VMEM)
    in_specs = in_specs or [whole] * count
    size = sum(v.size * v.dtype.itemsize for v in list(operands) + list(outs))
    grant = 10 << 20 if grid else size + ((8 if flops else 2) << 20)
    return pl.pallas_call(
        body,
        grid=grid,
        out_shape=list(outs),
        in_specs=list(in_specs) + [pl.BlockSpec(memory_space=pl.ANY)] * len(after),
        out_specs=list(out_specs or [whole] * len(outs)),
        scratch_shapes=list(scratch),
        compiler_params=pltpu.CompilerParams(vmem_limit_bytes=grant),
        cost_estimate=pl.CostEstimate(flops=flops, bytes_accessed=size, transcendentals=0),
    )(*operands, *after)


def gate(values, after):
    anywhere = pl.BlockSpec(memory_space=pl.ANY)
    return pl.pallas_call(
        lambda *refs: None,
        out_shape=[shape_of(*value.shape, value.dtype) for value in values],
        in_specs=[anywhere] * (len(values) + len(after)),
        out_specs=[anywhere] * len(values),
        input_output_aliases={place: place for place in range(len(values))},
        compiler_params=pltpu.CompilerParams(vmem_limit_bytes=1 << 20),
        cost_estimate=pl.CostEstimate(flops=0, bytes_accessed=0, transcendentals=0),
    )(*values, *after)


def join_high_kernel(count, *refs):
    pieces, (first, second) = refs[:count], refs[count:]
    cut = first.shape[1]
    rows = pieces[0].shape[0]
    for place, piece in enumerate(pieces):
        to = slice(place * rows, (place + 1) * rows)
        first[to, :] = piece[:, :cut]
        second[to, :] = piece[:, cut:]


def join_high(pieces, cut, flops=0, after=()):
    rows, columns = pieces[0].shape
    rows = rows * len(pieces)
    return run(
        functools.partial(join_high_kernel, len(pieces)),
        [shape_of(rows, cut, LOW), shape_of(rows, columns - cut, LOW)],
        pieces,
        flops,
        after,
    )


def join_plane_kernel(across, down, across_far, down_far, across_all, down_all):
    columns, rows = across.shape[1], down.shape[0]
    across_all[:, :columns] = across[...]
    across_all[:, columns:] = across_far[...]
    down_all[:rows, :] = down[...]
    down_all[rows:, :] = down_far[...]


def join_plane(across, down, across_far, down_far, after=()):
    return run(
        join_plane_kernel,
        [
            shape_of(across.shape[0], 2 * across.shape[1], LOW),
            shape_of(2 * down.shape[0], down.shape[1], LOW),
        ],
        [across, down, across_far, down_far],
        0,
        after,
    )


def added(left, right, rows, columns):
    return (left[rows, columns].astype(F32) + right[rows, columns].astype(F32)).astype(LOW)


def split_rows_kernel(array, far, keep, send):
    rows = keep.shape[0]
    keep[...] = added(array, far, slice(0, rows), slice(None))
    send[...] = added(array, far, slice(rows, 2 * rows), slice(None))


def split_columns_kernel(array, far, keep, send):
    columns = keep.shape[1]
    keep[...] = added(array, far, slice(None), slice(0, columns))
    send[...] = added(array, far, slice(None), slice(columns, 2 * columns))


def split_rows(array, far, flops=0, after=()):
    part = shape_of(array.shape[0] // 2, array.shape[1], LOW)
    return run(split_rows_kernel, [part, part], [array, far], flops, after)


def split_columns(array, far, flops=0, after=()):
    part = shape_of(array.shape[0], array.shape[1] // 2, LOW)
    return run(split_columns_kernel, [part, part], [array, far], flops, after)


def split_core_kernel(a, a_far, b, b_far, a_keep, a_send, b_keep, b_send):
    split_rows_kernel(a, a_far, a_keep, a_send)
    split_columns_kernel(b, b_far, b_keep, b_send)


def split_core(a, a_far, b, b_far, after=()):
    a_shape = shape_of(a.shape[0] // 2, a.shape[1], LOW)
    b_shape = shape_of(b.shape[0], b.shape[1] // 2, LOW)
    return run(
        split_core_kernel, [a_shape, a_shape, b_shape, b_shape], [a, a_far, b, b_far], 0, after
    )


def sum_kernel(*refs):
    total = refs[0][...].astype(F32)
    for ref in refs[1:-1]:
        total = total + ref[...].astype(F32)
    refs[-1][...] = total


def sum_parts(parts, flops, after=()):
    return run(sum_kernel, [shape_of(*parts[0].shape, F32)], parts, flops, after)


def split_plane_kernel(a, a_far, b, b_far, a_keep, a_send, b_keep, b_send):
    half, rows = a_keep.shape[1], b_keep.shape[0]
    every = slice(None)
    a_keep[...] = added(a, a_far, every, slice(0, half))
    a_send[...] = added(a, a_far, every, slice(half, 2 * half))
    b_keep[...] = added(b, b_far, slice(0, rows), every)
    b_send[...] = added(b, b_far, slice(rows, 2 * rows), every)


def split_plane(a, a_far, b, b_far, after=()):
    a_shape = shape_of(a.shape[0], a.shape[1] // 2, LOW)
    b_shape = shape_of(b.shape[0] // 2, b.shape[1], LOW)
    return run(
        split_plane_kernel, [a_shape, a_shape, b_shape, b_shape], [a, a_far, b, b_far], 0, after
    )


def split_high_kernel(a, a_far, b, b_far, *parts):
    cut = a.shape[1]
    rows = parts[0].shape[0]
    for place, part in enumerate(parts):
        at = slice(place * rows, (place + 1) * rows)
        part[:, :cut] = added(a, a_far, at, slice(None))
        part[:, cut:] = added(b, b_far, at, slice(None))


def split_high(a, a_far, b, b_far, after=()):
    count = len(group_masks(high_groups()[-1]))
    part = shape_of(a.shape[0] // count, a.shape[1] + b.shape[1], LOW)
    return run(split_high_kernel, [part] * count, [a, a_far, b, b_far], 0, after)


def flip(rank, first, second):
    return jnp.where(rank == 0, first, second)


def vectors_kernel(rank_ref, permute, a_own, a_far, relative, bias_q, bias_v, bias_inner):
    rank = rank_ref[0]
    side = a_own.shape[1] // 2
    width = relative.shape[1]
    half = width // 2
    spread = jnp.concatenate(
        [
            (ref[:, side - LANES : side].astype(F32) + ref[:, 2 * side - LANES :].astype(F32))
            for ref in (a_own, a_far)
        ],
        axis=0,
    )
    parts = jnp.transpose(spread)
    parts = [parts[16 * i : 16 * (i + 1)] for i in range(3)]
    relative[...] = ((parts[0] + parts[1]) + parts[2])[2:8]
    natural = [dot_nt(part.astype(LOW), permute[...]) for part in parts]
    natural = (natural[0] + natural[1]) + natural[2]
    for row, target in ((0, bias_q), (1, bias_v)):
        first, second = natural[row : row + 1, :half], natural[row : row + 1, half:]
        target[:, :half] = flip(rank, first, second)
        target[:, half:] = flip(rank, second, first)
    for place in range(2):
        for cut in range(2):
            near, far = 8 + 2 * place + cut, 8 + 2 * (1 - place) + cut
            at = (2 * place + cut) * width
            bias_inner[:, at : at + width] = flip(
                rank, natural[near : near + 1], natural[far : far + 1]
            )


def vector_lanes(rank, permute, grad_q, grad_v, sums_one, sums_two, sums_inner, natural, relative):
    width = natural.shape[1]
    half = width // 2
    natural[...] = jnp.zeros_like(natural)
    relative[...] = jnp.zeros_like(relative)
    for row, source in ((0, grad_q), (1, grad_v)):
        total = jnp.sum(source[...].astype(F32), axis=0, keepdims=True)
        first, second = total[:, :half], total[:, half:]
        natural[row : row + 1, :half] = flip(rank, first, second)
        natural[row : row + 1, half:] = flip(rank, second, first)
    for place in range(2):
        for cut in range(2):
            near, far = (2 * place + cut) * width, (2 * (1 - place) + cut) * width
            row = 8 + 2 * place + cut
            natural[row : row + 1, :] = flip(
                rank, sums_inner[:, near : near + width], sums_inner[:, far : far + width]
            )
    relative[:16, :] = dot(natural[...].astype(LOW), permute[...])
    relative[2:5, :] = sums_one[:3, :]
    relative[5:8, :] = sums_two[:3, :]
    return jnp.transpose(relative[...]).astype(LOW)


def pack_kernel(rank_ref, w_qkv, w_out, vectors, target, turned):
    columns = w_out.shape[1]
    count, shard_width = vectors.shape
    a_width = 2 * columns + LANES
    turned[...] = jnp.zeros_like(turned)
    for place in range(3):
        turned[16 * place : 16 * place + count, :shard_width] = vectors[...]
    values = jnp.transpose(turned[...])
    lane = lax.broadcasted_iota(jnp.int32, values.shape, 1)
    first = values.astype(LOW).astype(F32)
    second = (values - first).astype(LOW).astype(F32)
    third = values - first - second
    values = jnp.where(lane < 16, first, jnp.where(lane < 32, second, third))[:shard_width]
    blank = jnp.zeros_like(values)
    values = jnp.concatenate(
        [flip(rank_ref[0], values, blank), flip(rank_ref[0], blank, values)], axis=0
    )
    target[:, :columns] = w_qkv[0].astype(LOW)
    target[:, columns : 2 * columns] = w_qkv[1].astype(LOW)
    target[:, 2 * columns : a_width] = values.astype(LOW)
    target[:, a_width : a_width + columns] = w_qkv[2].astype(LOW)
    target[:, a_width + columns :] = w_out[...].astype(LOW)


def cast_kernel(first, second, target):
    columns = first.shape[1]
    target[:, :columns] = first[...].astype(LOW)
    target[:, columns:] = second[...].astype(LOW)


def project_kernel(rows, a_own, a_far, b_own, b_far, bias_q, bias_v, q, k, v):
    half = a_own.shape[0]
    own_rows, width = q.shape
    part = width // 2
    low, high = rows[:, :half], rows[:, half:]
    a_half, b_half = a_own.shape[1] // 2, b_own.shape[1] // 2
    for side in range(2):
        cols = slice(side * part, (side + 1) * part)
        at = slice(side * a_half, side * a_half + part)
        q[:, cols] = (
            dot(low[:own_rows], a_own[:, at]) + dot(high[:own_rows], a_far[:, at]) + bias_q[:, cols]
        ).astype(LOW)
        at = slice(side * a_half + part, side * a_half + 2 * part)
        k[:, cols] = (dot(low, a_own[:, at]) + dot(high, a_far[:, at])).astype(LOW)
        at = slice(side * b_half, side * b_half + part)
        v[:, cols] = (dot(low, b_own[:, at]) + dot(high, b_far[:, at]) + bias_v[:, cols]).astype(
            LOW
        )


def segment(lengths, positions):
    end, total = 0, jnp.zeros_like(positions)
    for place in range(lengths.shape[1]):
        end = end + lengths[0, place]
        total = total + (positions >= end).astype(jnp.int32)
    return total


def same_segment(rank, lengths, keys, queries):
    own = lax.broadcasted_iota(jnp.int32, (1, queries), 1) + rank * queries
    rows = lax.broadcasted_iota(jnp.int32, (keys, 1), 0)
    rows = jnp.where(rows < queries, rows + rank * queries, rows - rank * queries)
    return segment(lengths, rows) == segment(lengths, own)


def softmax_down(same, key_rows, queries):
    scores = dot_nt(key_rows, queries) * 0.125
    scores = jnp.where(same, scores, NEG_FILL)
    exp_scores = jnp.exp(scores - jnp.max(scores, axis=0, keepdims=True))
    return exp_scores * (1.0 / jnp.sum(exp_scores, axis=0, keepdims=True))


def two_heads(out):
    joined = jnp.concatenate([out[0][:HEAD_DIM], out[1][HEAD_DIM:]], axis=0)
    return jnp.transpose(joined).astype(LOW)


def attend_kernel(rank_ref, lengths, q, k, v, attended):
    queries, key_rows, value_rows = q[...], k[...], v[...]
    same = same_segment(rank_ref[0], lengths, k.shape[0], q.shape[0])
    first = lax.broadcasted_iota(jnp.int32, queries.shape, 1) < HEAD_DIM
    out = []
    for mine in (first, jnp.logical_not(first)):
        prob = softmax_down(same, key_rows, jnp.where(mine, queries, jnp.zeros_like(queries)))
        out.append(dot_tn(value_rows, prob.astype(LOW)))
    attended[...] = two_heads(out)


def attend_back_kernel(rank_ref, lengths, q, k, v, grad, grad_q, grad_k, grad_v):
    queries, key_rows, value_rows, grad_rows = q[...], k[...], v[...], grad[...]
    same = same_segment(rank_ref[0], lengths, k.shape[0], q.shape[0])
    first = lax.broadcasted_iota(jnp.int32, queries.shape, 1) < HEAD_DIM
    first_all = lax.broadcasted_iota(jnp.int32, key_rows.shape, 1) < HEAD_DIM
    blank = jnp.zeros_like(queries)
    out_q, out_k, out_v = [], [], []
    for mine in (first, jnp.logical_not(first)):
        prob = softmax_down(same, key_rows, jnp.where(mine, queries, blank))
        grad_prob = dot_nt(value_rows, jnp.where(mine, grad_rows, blank))
        delta = jnp.sum(grad_prob * prob, axis=0, keepdims=True)
        grad_score = (prob * (grad_prob - delta)).astype(LOW)
        out_q.append(dot_tn(key_rows, grad_score) * 0.125)
        out_k.append(dot(grad_score, queries) * 0.125)
        out_v.append(dot(prob.astype(LOW), grad_rows))
    grad_q[...] = two_heads(out_q)
    grad_k[...] = jnp.where(first_all, out_k[0], out_k[1]).astype(LOW)
    grad_v[...] = jnp.where(first_all, out_v[0], out_v[1]).astype(LOW)


def out_norm_kernel(attended, rows, b_own, b_far, vec, y, y_low, normed, inv):
    half = b_own.shape[0]
    own_rows, width = y.shape
    part = width // 2
    b_half = b_own.shape[1] // 2
    near, far = attended[:, :part], attended[:, part:]
    out = []
    for weights in (b_own, b_far):
        out.append(
            dot_nt(near, weights[:, part : 2 * part])
            + dot_nt(far, weights[:, b_half + part : b_half + 2 * part])
        )
    total = rows[:own_rows, :].astype(F32) + jnp.concatenate(out, axis=1) + vec[0:1]
    y_new, normed[...], inv[...] = normalize_fwd(total, vec[1:2], vec[2:3])
    y[...] = y_new
    y_low[...] = y_new.astype(LOW)


def stacked(pieces, at=slice(None)):
    return jnp.concatenate([piece[:, at] for piece in pieces], axis=0)


def hidden_kernel(y_low, *refs):
    pieces, (bias, activation, slope) = refs[:4], refs[4:]
    rows = y_low[...]
    columns = pieces[0].shape[1]
    step = columns // 8
    for start in range(0, columns, step):
        at = slice(start, start + step)
        pre = dot(rows, stacked(pieces, at)) + bias[:, at]
        cdf = 0.5 + 0.5 * lax.erf(pre * (0.5**0.5))
        activation[:, at] = (pre * cdf).astype(LOW)
        slope[:, at] = cdf + pre * jnp.exp(-0.5 * pre * pre) * ((2.0 * np.pi) ** -0.5)


def out_back_kernel(
    rank_ref, lengths, activation, own, own_side, far, far_side, y, cot, vec,
    mixed, grad, grad_low, sums,
):
    columns = own.shape[1]
    near, side = activation[:, :columns], activation[:, columns:]
    out = [
        dot_nt(near, first[...]) + dot_nt(side, second[...])
        for first, second in ((own, own_side), (far, far_side))
    ]
    total = y[...] + jnp.concatenate(out, axis=1) + vec[3:4]
    result, normed, inv_std = normalize_fwd(total, vec[4:5], vec[5:6])
    mixed[...] = result.astype(LOW)
    rows = lax.broadcasted_iota(jnp.int32, (y.shape[0], 1), 0) + rank_ref[0] * y.shape[0]
    valid = (segment(lengths, rows) < lengths.shape[1]).astype(F32)
    grad_in, gain_sum, shift_sum = normalize_back(cot[...] * valid, normed, inv_std, vec[4:5])
    grad[...] = grad_in
    grad_low[...] = grad_in.astype(LOW)
    sums[0:1] = jnp.sum(grad_in, axis=0, keepdims=True)
    sums[1:2] = gain_sum[None]
    sums[2:3] = shift_sum[None]


def hidden_back_kernel(grad_low, own, own_side, far, far_side, slope, grad_pre, sums):
    rows = grad_low[...]
    columns = own.shape[1]
    step = columns // 4
    for place, pieces in enumerate(((own, far), (own_side, far_side))):
        for start in range(0, columns, step):
            to = slice(place * columns + start, place * columns + start + step)
            grad_act = dot(rows, stacked(pieces, slice(start, start + step)))
            value = (grad_act * slope[:, to]).astype(LOW)
            grad_pre[:, to] = value
            sums[:, to] = jnp.sum(value.astype(F32), axis=0, keepdims=True)


def norm_back_kernel(
    grad_pre, own, own_side, far, far_side, grad_two, normed, inv, vec, o_own, o_far,
    grad, grad_low, grad_attn, sums,
):
    out = [
        dot_nt(grad_pre[...], stacked(pieces)) for pieces in ((own, own_side), (far, far_side))
    ]
    grad_in, gain_sum, shift_sum = normalize_back(
        grad_two[...] + jnp.concatenate(out, axis=1), normed[...], inv[...], vec[1:2]
    )
    grad[...] = grad_in
    low = grad_in.astype(LOW)
    grad_low[...] = low
    sums[0:1] = jnp.sum(grad_in, axis=0, keepdims=True)
    sums[1:2] = gain_sum[None]
    sums[2:3] = shift_sum[None]
    half = o_own.shape[0]
    part = grad.shape[1] // 2
    o_half = o_own.shape[1] // 2
    for side in range(2):
        at = slice(side * o_half + part, side * o_half + 2 * part)
        grad_attn[:, side * part : (side + 1) * part] = (
            dot(low[:, :half], o_own[:, at]) + dot(low[:, half:], o_far[:, at])
        ).astype(LOW)


def rows_back_kernel(grad_q, grad_k, grad_v, a_own, a_far, b_own, b_far, grad_one, own, away):
    own_rows, width = own.shape
    part = width // 2
    a_half, b_half = a_own.shape[1] // 2, b_own.shape[1] // 2
    half = a_own.shape[0]
    for place, (wa, wb) in enumerate(((a_own, b_own), (a_far, b_far))):
        to = slice(place * half, (place + 1) * half)
        both = jnp.zeros((2 * own_rows, half), F32)
        mine = grad_one[:, to]
        for side in range(2):
            cols = slice(side * part, (side + 1) * part)
            at = side * a_half
            mine = mine + dot_nt(grad_q[:, cols], wa[:, at : at + part])
            both = both + dot_nt(grad_k[:, cols], wa[:, at + part : at + 2 * part])
            at = side * b_half
            both = both + dot_nt(grad_v[:, cols], wb[:, at : at + part])
        own[:, to] = mine + both[:own_rows]
        away[:, to] = both[own_rows:].astype(LOW)


def rows_out_kernel(own, away, permute, out):
    rest = own[...] + away[...].astype(F32)
    total = None
    for _ in range(3):
        part = rest.astype(LOW)
        rest = rest - part.astype(F32)
        moved = dot_nt(part, permute[...])
        total = moved if total is None else total + moved
    out[...] = total


def first_grads_kernel(
    a_half, rank_ref, permute, rows, grad_q, grad_k, grad_v, grad_low, attended,
    sums_one, sums_two, sums_inner, a_send, b_send, a_keep, b_keep, natural, relative,
):
    half = a_keep.shape[0]
    own_rows, width = grad_q.shape
    part = width // 2
    extra = vector_lanes(
        rank_ref[0], permute, grad_q, grad_v, sums_one, sums_two, sums_inner, natural, relative
    )
    for place, to, to_b in ((1, a_send, b_send), (0, a_keep, b_keep)):
        at = slice(place * half, (place + 1) * half)
        both = rows[:, at]
        mine = rows[:own_rows, at]
        low = grad_low[:, at]
        for side in range(2):
            cols = slice(side * part, (side + 1) * part)
            base = side * a_half
            to[:, base : base + part] = dot_tn(mine, grad_q[:, cols]).astype(LOW)
            to[:, base + part : base + 2 * part] = dot_tn(both, grad_k[:, cols]).astype(LOW)
            to[:, base + 2 * part : base + a_half] = extra[at, :]
            base = side * 2 * part
            to_b[:, base : base + part] = dot_tn(both, grad_v[:, cols]).astype(LOW)
            to_b[:, base + part : base + 2 * part] = dot_tn(low, attended[:, cols]).astype(LOW)


def close_kernel(rates, rank_ref, *refs):
    inputs, parts = refs[:9], refs[9:-10]
    outs, turned = refs[-10:-1], refs[-1]
    total = parts[0][...].astype(F32)
    for part in parts[1:]:
        total = total + part[...].astype(F32)
    columns = outs[3].shape[1]
    count, shard_width = outs[6].shape
    a_width = 2 * columns + LANES
    for place, start in enumerate((0, columns, a_width)):
        values = adamw(
            *[ref[place] for ref in inputs[:3]],
            total[:, start : start + columns],
            rates[0],
            WEIGHT_DECAY,
        )
        for out, value in zip(outs[:3], values):
            out[place] = value
    values = adamw(
        *[ref[...] for ref in inputs[3:6]],
        total[:, a_width + columns :],
        rates[1],
        WEIGHT_DECAY,
    )
    for out, value in zip(outs[3:6], values):
        out[...] = value
    lanes = total[:, 2 * columns : a_width]
    turned[...] = jnp.zeros_like(turned)
    turned[:shard_width, :] = flip(
        rank_ref[0], lanes[:shard_width], lanes[shard_width : 2 * shard_width]
    )
    gradient = jnp.transpose(turned[...])[:count, :shard_width]
    values = adamw(*[ref[...] for ref in inputs[6:]], gradient, 0.1, 0.0)
    for out, value in zip(outs[6:], values):
        out[...] = value


def on_device(
    tokens,
    cotangent,
    lengths,
    w_qkv,
    m_qkv,
    v_qkv,
    w_out,
    m_out,
    v_out,
    w_in,
    m_in,
    v_in,
    w_back,
    m_back,
    v_back,
    vectors,
    m_vectors,
    v_vectors,
):
    own_rows, width = tokens.shape
    tensor_rank = lax.axis_index("tensor")
    group_rows = 2 * own_rows
    shard_rows = w_qkv.shape[1]
    part = w_qkv.shape[2]
    hidden_half = w_in.shape[1]
    full_inner = 2 * hidden_half
    half = width // 2
    count = vectors.shape[0]
    shard_width = vectors.shape[1]

    a_width = 2 * part + LANES
    rank = tensor_rank.astype(jnp.int32).reshape(1)
    scalar = pl.BlockSpec(memory_space=pltpu.SMEM)
    vmem = pl.BlockSpec(memory_space=pltpu.VMEM)
    shard_one = run(
        pack_kernel,
        [shape_of(shard_rows, a_width + 2 * part, LOW)],
        [rank, w_qkv, w_out.T, vectors],
        0,
        in_specs=[scalar] + [vmem] * 3,
        scratch=[pltpu.VMEM((LANES, LANES), F32)],
    )[0]

    tokens_far = swap_tensor(tokens)
    one_high = gather_high(shard_one)
    one = join_high(one_high, a_width)
    one_far = swap_tensor(one[0]), swap_dp(one[1], 2)
    shard_pair = run(
        cast_kernel,
        [shape_of(shard_rows, full_inner, LOW)],
        [w_in, w_back.T],
        0,
        after=one[:1],
    )[0]
    pair_high = gather_high(shard_pair)

    order = relative_order(width)
    permute = (jnp.arange(width, dtype=jnp.int32)[:, None] == order[None, :]).astype(LOW)
    rows_all = jnp.concatenate([dot(tokens, permute), dot(tokens_far, permute)]).astype(LOW)
    cot = dot(cotangent, permute)

    one = join_plane(*one, *one_far, after=[rows_all])
    one_far = swap_dp(one[0], 2), swap_tensor(one[1])
    unit = 2 * own_rows * width * width
    pair = join_high(pair_high, hidden_half, 400 * unit)
    one = join_plane(one[1], one[0], one_far[1], one_far[0], after=pair[:1])[::-1]
    a_own, b_own = one
    a_far, b_far = swap_dp(a_own, 1), swap_dp(b_own, 1)
    pair_far = swap_tensor(pair[0]), swap_dp(pair[1], 2)

    vec, bias_query, bias_value, bias_inner = run(
        vectors_kernel,
        [
            shape_of(6, width, F32),
            shape_of(1, width, F32),
            shape_of(1, width, F32),
            shape_of(1, full_inner, F32),
        ],
        [rank, permute, a_own, a_far],
        1,
        in_specs=[scalar, vmem, vmem, vmem],
    )

    wide_low = shape_of(own_rows, width, LOW)
    wide = shape_of(own_rows, width, F32)
    group_low = shape_of(group_rows, width, LOW)
    sums_shape = shape_of(8, width, F32)
    queries, key_rows, value_rows = run(
        project_kernel,
        [wide_low, group_low, group_low],
        [rows_all, a_own, a_far, b_own, b_far, bias_query, bias_value],
        5 * unit,
    )
    pair = join_plane(*pair, *pair_far, after=[queries])
    in_near, in_side = pair[0], swap_dp(pair[0], 2)
    back_near, back_side = pair[1], swap_tensor(pair[1])
    in_far, back_far = swap_dp(in_near, 1), swap_dp(back_near, 1)
    pairs = width // LANES
    own_block = pl.BlockSpec((own_rows, LANES), lambda i: (0, i))
    all_block = pl.BlockSpec((group_rows, LANES), lambda i: (0, i))

    attended = run(
        attend_kernel,
        [wide_low],
        [rank, lengths, queries, key_rows, value_rows],
        3 * unit,
        after=pair[:1],
        grid=(pairs,),
        in_specs=[scalar, scalar, own_block, all_block, all_block],
        out_specs=[own_block],
    )[0]
    first_norm, first_low, normed_one, inv_one = run(
        out_norm_kernel,
        [wide, wide_low, wide, shape_of(own_rows, 1, F32)],
        [attended, rows_all, b_own, b_far, vec],
        2 * unit,
        after=[in_far, back_far],
    )
    in_side, back_side = gate([in_side, back_side], [first_low])
    pieces_in = [in_near, in_side, in_far, swap_dp(in_side, 1)]
    pieces_back = [back_near, back_side, back_far, swap_dp(back_side, 1)]
    activation, slope = run(
        hidden_kernel,
        [shape_of(own_rows, full_inner, LOW), shape_of(own_rows, full_inner, F32)],
        [first_low, *pieces_in, bias_inner],
        8 * unit,
    )
    mixed_rel, grad_two, grad_two_low, sums_two = run(
        out_back_kernel,
        [wide_low, wide, wide_low, sums_shape],
        [rank, lengths, activation, *pieces_back, first_norm, cot, vec],
        5 * unit,
        in_specs=[scalar, scalar] + [vmem] * 8,
    )
    mixed = dot_nt(mixed_rel, permute).astype(LOW)

    def weight_grad(left, right):
        send = dot_tn(left[:, half:], right).astype(LOW)
        return dot_tn(left[:, :half], right).astype(LOW), swap_dp(send, 1)

    outer = weight_grad(grad_two_low, activation)
    grad_pre, sums_inner = run(
        hidden_back_kernel,
        [shape_of(own_rows, full_inner, LOW), shape_of(1, full_inner, F32)],
        [grad_two_low, *pieces_back, slope],
        6 * unit,
    )
    inner = weight_grad(first_low, grad_pre)
    b_keep, b_send = split_columns(*outer, 400 * unit, after=[grad_pre])
    a_keep, a_send = split_rows(*inner, after=[b_keep])
    pair = a_keep, swap_dp(a_send, 2), b_keep, swap_tensor(b_send)
    grad_one, grad_one_low, grad_attn, sums_one = run(
        norm_back_kernel,
        [wide, wide_low, wide_low, sums_shape],
        [grad_pre, *pieces_in, grad_two, normed_one, inv_one, vec, b_own, b_far],
        6 * unit,
        after=[a_keep],
    )
    grad_q, grad_k, grad_v = run(
        attend_back_kernel,
        [wide_low, group_low, group_low],
        [rank, lengths, queries, key_rows, value_rows, grad_attn],
        5 * unit,
        grid=(pairs,),
        in_specs=[scalar, scalar, own_block, all_block, all_block, own_block],
        out_specs=[own_block, all_block, all_block],
    )
    a_shape, b_shape = shape_of(half, 2 * a_width, LOW), shape_of(half, 4 * part, LOW)
    a_send, b_send, one_a, one_b = run(
        functools.partial(first_grads_kernel, a_width),
        [a_shape, b_shape, a_shape, b_shape],
        [rank, permute, rows_all, grad_q, grad_k, grad_v, grad_one_low, attended]
        + [sums_one, sums_two, sums_inner],
        6 * unit,
        in_specs=[scalar] + [vmem] * 10,
        scratch=[pltpu.VMEM((16, width), F32), pltpu.VMEM((LANES, width), F32)],
    )
    one = one_a, swap_dp(a_send, 1), one_b, swap_dp(b_send, 1)
    a_keep, a_send, b_keep, b_send = split_plane(*pair, after=[one_a, mixed])
    pair = a_keep, swap_tensor(a_send), b_keep, swap_dp(b_send, 2)
    grad_own, grad_away = run(
        rows_back_kernel,
        [wide, wide_low],
        [grad_q, grad_k, grad_v, a_own, a_far, b_own, b_far, grad_one],
        400 * unit,
        after=[a_keep],
    )
    a_keep, a_send, b_keep, b_send = split_core(*one, after=[grad_own, pair[1], pair[3]])
    one = a_keep, swap_dp(a_send, 2), b_keep, swap_tensor(b_send)
    pair = send_high(split_high(*pair, after=[a_keep]))
    a_keep, a_send, b_keep, b_send = split_plane(*one, after=pair[:1])
    one = a_keep, swap_tensor(a_send), b_keep, swap_dp(b_send, 2)
    pair = sum_parts(pair, 400 * unit, after=[a_keep])
    one = send_high(split_high(*one, after=pair))
    input_grad = run(
        rows_out_kernel,
        [wide],
        [grad_own, swap_tensor(gate([grad_away], pair)[0]), permute],
        3 * unit,
        after=one[:1],
    )[0]
    sum_pair = reduce_rest(gate(pair, one[:1])[0])
    summed_in, summed_back = sum_pair[:, :hidden_half], sum_pair[:, hidden_half:].T
    if len(high_groups()) > 1:
        one = [reduce_rest(sum(piece.astype(F32) for piece in one))]
    qkv_shape = jax.ShapeDtypeStruct(w_qkv.shape, F32)
    out_shape = shape_of(shard_rows, part, F32)
    vec_shape = shape_of(count, shard_width, F32)
    done = run(
        functools.partial(
            close_kernel,
            (float(width) ** (-0.5), (4.0 * width / group_rows) ** (-0.5)),
        ),
        [qkv_shape] * 3 + [out_shape] * 3 + [vec_shape] * 3,
        [rank, w_qkv, m_qkv, v_qkv, w_out.T, m_out.T, v_out.T]
        + [vectors, m_vectors, v_vectors, *one],
        unit,
        after=[input_grad],
        in_specs=[scalar] + [vmem] * (9 + len(one)),
        scratch=[pltpu.VMEM((LANES, LANES), F32)],
    )
    new_qkv, moment_qkv, square_qkv = done[:3]
    new_out, moment_out, square_out = [value.T for value in done[3:6]]
    new_vectors, moment_vectors, square_vectors = done[6:]
    new_in, moment_in, square_in = adamw(
        w_in, m_in, v_in, summed_in, float(width) ** (-0.5), WEIGHT_DECAY
    )
    new_back, moment_back, square_back = adamw(
        w_back, m_back, v_back, summed_back, float(full_inner) ** (-0.5), WEIGHT_DECAY
    )
    return (
        mixed,
        input_grad,
        new_qkv,
        moment_qkv,
        square_qkv,
        new_out,
        moment_out,
        square_out,
        new_in,
        moment_in,
        square_in,
        new_back,
        moment_back,
        square_back,
        new_vectors,
        moment_vectors,
        square_vectors,
    )


def solution(mesh):
    placed = (
        P(("dp", "tensor"), None),
        P(("dp", "tensor"), None),
        P("dp", None),
        P(None, "dp", "tensor"),
        P(None, "dp", "tensor"),
        P(None, "dp", "tensor"),
        P("tensor", "dp"),
        P("tensor", "dp"),
        P("tensor", "dp"),
        P("dp", "tensor"),
        P("dp", "tensor"),
        P("dp", "tensor"),
        P("tensor", "dp"),
        P("tensor", "dp"),
        P("tensor", "dp"),
        P(None, ("dp", "tensor")),
        P(None, ("dp", "tensor")),
        P(None, ("dp", "tensor")),
    )
    return jax.shard_map(
        on_device,
        mesh=mesh,
        in_specs=placed,
        out_specs=(
            P(("dp", "tensor"), None),
            P(("dp", "tensor"), None),
            P(None, "dp", "tensor"),
            P(None, "dp", "tensor"),
            P(None, "dp", "tensor"),
            P("tensor", "dp"),
            P("tensor", "dp"),
            P("tensor", "dp"),
            P("dp", "tensor"),
            P("dp", "tensor"),
            P("dp", "tensor"),
            P("tensor", "dp"),
            P("tensor", "dp"),
            P("tensor", "dp"),
            P(None, ("dp", "tensor")),
            P(None, ("dp", "tensor")),
            P(None, ("dp", "tensor")),
        ),
        check_vma=False,
    )
```

```python
import functools

import numpy as np

import jax
import jax.numpy as jnp
from jax import lax
from jax.experimental import pallas as pl
from jax.experimental.pallas import tpu as pltpu
from jax.sharding import PartitionSpec as P

HEAD_DIM = 64
LANES = 128
STEP = 10


EPS_NORM = 1e-05
BETA_ONE = 0.9
BETA_TWO = 0.999
EPS_ADAM = 1e-08
WEIGHT_DECAY = 0.01
NEG_FILL = -1000000000.0
LOW = jnp.bfloat16
F32 = jnp.float32


def normalize_fwd(values, gain_row, shift_row):
    row_mean = jnp.mean(values, axis=-1, keepdims=True)
    centered = values - row_mean
    variance = jnp.mean(centered * centered, axis=-1, keepdims=True)
    inv_std = lax.rsqrt(variance + EPS_NORM)
    normed = centered * inv_std
    return (normed * gain_row + shift_row, normed, inv_std)


def normalize_back(gradient, normed, inv_std, gain_row):
    grad_norm = gradient * gain_row
    grad_in = inv_std * (
        grad_norm
        - jnp.mean(grad_norm, axis=-1, keepdims=True)
        - normed * jnp.mean(grad_norm * normed, axis=-1, keepdims=True)
    )
    return (grad_in, jnp.sum(gradient * normed, axis=0), jnp.sum(gradient, axis=0))


def adamw(weight, moment, square, gradient, step_rate, decay_rate):
    moment = BETA_ONE * moment + (1.0 - BETA_ONE) * gradient
    square = BETA_TWO * square + (1.0 - BETA_TWO) * gradient * gradient
    direction = (
        moment / (1.0 - BETA_ONE**STEP) / (jnp.sqrt(square / (1.0 - BETA_TWO**STEP)) + EPS_ADAM)
    )
    return (weight - step_rate * (direction + decay_rate * weight), moment, square)


def swap_dp(values, mask):
    size = lax.axis_size("dp")
    return lax.ppermute(values, "dp", [(i, i ^ mask) for i in range(size)])


def swap_tensor(values):
    return lax.ppermute(values, "tensor", [(0, 1), (1, 0)])


def high_bits():
    return list(range(2, lax.axis_size("dp").bit_length() - 1))


def high_groups():
    bits = high_bits()
    return [[1 << bit for bit in bits[i : i + 2]] for i in range(0, len(bits), 2)]


def group_masks(group):
    return [0] + group + ([group[0] ^ group[1]] if len(group) == 2 else [])


def gather_high(shard):
    groups = high_groups()
    for place, group in enumerate(groups):
        pieces = [shard if mask == 0 else swap_dp(shard, mask) for mask in group_masks(group)]
        if place < len(groups) - 1:
            shard = jnp.concatenate(pieces, axis=0)
    return pieces


def send_high(parts):
    masks = group_masks(high_groups()[-1])
    return [parts[0]] + [swap_dp(part, mask) for part, mask in zip(parts[1:], masks[1:])]


def reduce_rest(total):
    for group in reversed(high_groups()[:-1]):
        masks = group_masks(group)
        rows = total.shape[0] // len(masks)
        low = total.astype(LOW)
        total = total[:rows]
        for place, mask in enumerate(masks[1:], 1):
            total = total + swap_dp(low[place * rows : (place + 1) * rows], mask).astype(F32)
    return total


def relative_order(width):
    size = lax.axis_size("dp")
    rows = width // size
    inner_first = high_bits() + [1, 0]
    masks = np.zeros((size,), np.int32)
    for block in range(size):
        for place, bit in enumerate(inner_first):
            if (block >> place) & 1:
                masks[block] |= 1 << bit
    block_mask = jnp.asarray(np.repeat(masks, rows))
    offsets = jnp.asarray(np.tile(np.arange(rows, dtype=np.int32), size))
    return (lax.axis_index("dp") ^ block_mask) * rows + offsets


def dot(left, right):
    return jnp.dot(left, right, preferred_element_type=F32)


def dot_nt(left, right):
    return lax.dot_general(left, right, (((1,), (1,)), ((), ())), preferred_element_type=F32)


def dot_tn(left, right):
    return lax.dot_general(left, right, (((0,), (0,)), ((), ())), preferred_element_type=F32)


def shape_of(rows, columns, kind):
    return jax.ShapeDtypeStruct((rows, columns), kind)


def run(kernel, outs, operands, flops, after=(), grid=(), in_specs=None, out_specs=None, scratch=()):
    count = len(operands)

    def body(*refs):
        kernel(*refs[:count], *refs[count + len(after) :])

    whole = pl.BlockSpec(memory_space=pltpu.VMEM)
    in_specs = in_specs or [whole] * count
    size = sum(v.size * v.dtype.itemsize for v in list(operands) + list(outs))
    grant = 10 << 20 if grid else size + ((8 if flops else 2) << 20)
    return pl.pallas_call(
        body,
        grid=grid,
        out_shape=list(outs),
        in_specs=list(in_specs) + [pl.BlockSpec(memory_space=pl.ANY)] * len(after),
        out_specs=list(out_specs or [whole] * len(outs)),
        scratch_shapes=list(scratch),
        compiler_params=pltpu.CompilerParams(vmem_limit_bytes=grant),
        cost_estimate=pl.CostEstimate(flops=flops, bytes_accessed=size, transcendentals=0),
    )(*operands, *after)


def gate(values, after):
    anywhere = pl.BlockSpec(memory_space=pl.ANY)
    return pl.pallas_call(
        lambda *refs: None,
        out_shape=[shape_of(*value.shape, value.dtype) for value in values],
        in_specs=[anywhere] * (len(values) + len(after)),
        out_specs=[anywhere] * len(values),
        input_output_aliases={place: place for place in range(len(values))},
        compiler_params=pltpu.CompilerParams(vmem_limit_bytes=1 << 20),
        cost_estimate=pl.CostEstimate(flops=0, bytes_accessed=0, transcendentals=0),
    )(*values, *after)


def join_high_kernel(count, *refs):
    pieces, (first, second) = refs[:count], refs[count:]
    cut = first.shape[1]
    rows = pieces[0].shape[0]
    for place, piece in enumerate(pieces):
        to = slice(place * rows, (place + 1) * rows)
        first[to, :] = piece[:, :cut]
        second[to, :] = piece[:, cut:]


def join_high(pieces, cut, flops=0, after=()):
    rows, columns = pieces[0].shape
    rows = rows * len(pieces)
    return run(
        functools.partial(join_high_kernel, len(pieces)),
        [shape_of(rows, cut, LOW), shape_of(rows, columns - cut, LOW)],
        pieces,
        flops,
        after,
    )


def join_plane_kernel(across, down, across_far, down_far, across_all, down_all):
    columns, rows = across.shape[1], down.shape[0]
    across_all[:, :columns] = across[...]
    across_all[:, columns:] = across_far[...]
    down_all[:rows, :] = down[...]
    down_all[rows:, :] = down_far[...]


def join_plane(across, down, across_far, down_far, after=()):
    return run(
        join_plane_kernel,
        [
            shape_of(across.shape[0], 2 * across.shape[1], LOW),
            shape_of(2 * down.shape[0], down.shape[1], LOW),
        ],
        [across, down, across_far, down_far],
        0,
        after,
    )


def added(left, right, rows, columns):
    return (left[rows, columns].astype(F32) + right[rows, columns].astype(F32)).astype(LOW)


def add_kernel(array, far, total):
    total[...] = added(array, far, slice(None), slice(None))


def add_parts(array, far, flops=0, after=()):
    return run(add_kernel, [shape_of(*array.shape, LOW)], [array, far], flops, after)[0]


def split_rows_kernel(array, far, keep, send):
    rows = keep.shape[0]
    keep[...] = added(array, far, slice(0, rows), slice(None))
    send[...] = added(array, far, slice(rows, 2 * rows), slice(None))


def split_columns_kernel(array, far, keep, send):
    columns = keep.shape[1]
    keep[...] = added(array, far, slice(None), slice(0, columns))
    send[...] = added(array, far, slice(None), slice(columns, 2 * columns))


def split_core_kernel(a, a_far, b, b_far, a_keep, a_send, b_keep, b_send):
    split_rows_kernel(a, a_far, a_keep, a_send)
    split_columns_kernel(b, b_far, b_keep, b_send)


def split_core(a, a_far, b, b_far, after=()):
    a_shape = shape_of(a.shape[0] // 2, a.shape[1], LOW)
    b_shape = shape_of(b.shape[0], b.shape[1] // 2, LOW)
    return run(
        split_core_kernel, [a_shape, a_shape, b_shape, b_shape], [a, a_far, b, b_far], 0, after
    )


def sum_kernel(*refs):
    total = refs[0][...].astype(F32)
    for ref in refs[1:-1]:
        total = total + ref[...].astype(F32)
    refs[-1][...] = total


def sum_parts(parts, flops, after=()):
    return run(sum_kernel, [shape_of(*parts[0].shape, F32)], parts, flops, after)


def split_plane_kernel(a, a_far, b, b_far, a_keep, a_send, b_keep, b_send):
    half, rows = a_keep.shape[1], b_keep.shape[0]
    every = slice(None)
    a_keep[...] = added(a, a_far, every, slice(0, half))
    a_send[...] = added(a, a_far, every, slice(half, 2 * half))
    b_keep[...] = added(b, b_far, slice(0, rows), every)
    b_send[...] = added(b, b_far, slice(rows, 2 * rows), every)


def split_plane(a, a_far, b, b_far, after=()):
    a_shape = shape_of(a.shape[0], a.shape[1] // 2, LOW)
    b_shape = shape_of(b.shape[0] // 2, b.shape[1], LOW)
    return run(
        split_plane_kernel, [a_shape, a_shape, b_shape, b_shape], [a, a_far, b, b_far], 0, after
    )


def split_high_kernel(a, a_far, b, b_far, *parts):
    cut = a.shape[1]
    rows = parts[0].shape[0]
    for place, part in enumerate(parts):
        at = slice(place * rows, (place + 1) * rows)
        part[:, :cut] = added(a, a_far, at, slice(None))
        part[:, cut:] = added(b, b_far, at, slice(None))


def split_high(a, a_far, b, b_far, after=()):
    count = len(group_masks(high_groups()[-1]))
    part = shape_of(a.shape[0] // count, a.shape[1] + b.shape[1], LOW)
    return run(split_high_kernel, [part] * count, [a, a_far, b, b_far], 0, after)


def flip(rank, first, second):
    return jnp.where(rank == 0, first, second)


def vectors_kernel(rank_ref, permute, a_own, a_far, relative, bias_q, bias_v, bias_inner):
    rank = rank_ref[0]
    side = a_own.shape[1] // 2
    width = relative.shape[1]
    half = width // 2
    spread = jnp.concatenate(
        [
            (ref[:, side - LANES : side].astype(F32) + ref[:, 2 * side - LANES :].astype(F32))
            for ref in (a_own, a_far)
        ],
        axis=0,
    )
    parts = jnp.transpose(spread)
    parts = [parts[16 * i : 16 * (i + 1)] for i in range(3)]
    relative[...] = ((parts[0] + parts[1]) + parts[2])[2:8]
    natural = [dot_nt(part.astype(LOW), permute[...]) for part in parts]
    natural = (natural[0] + natural[1]) + natural[2]
    for row, target in ((0, bias_q), (1, bias_v)):
        first, second = natural[row : row + 1, :half], natural[row : row + 1, half:]
        target[:, :half] = flip(rank, first, second)
        target[:, half:] = flip(rank, second, first)
    for place in range(2):
        for cut in range(2):
            near, far = 8 + 2 * place + cut, 8 + 2 * (1 - place) + cut
            at = (2 * place + cut) * width
            bias_inner[:, at : at + width] = flip(
                rank, natural[near : near + 1], natural[far : far + 1]
            )


def vector_lanes(rank, permute, grad_q, grad_v, sums_one, sums_two, sums_inner, natural, relative):
    width = natural.shape[1]
    half = width // 2
    natural[...] = jnp.zeros_like(natural)
    relative[...] = jnp.zeros_like(relative)
    for row, source in ((0, grad_q), (1, grad_v)):
        total = jnp.sum(source[...].astype(F32), axis=0, keepdims=True)
        first, second = total[:, :half], total[:, half:]
        natural[row : row + 1, :half] = flip(rank, first, second)
        natural[row : row + 1, half:] = flip(rank, second, first)
    for place in range(2):
        for cut in range(2):
            near, far = (2 * place + cut) * width, (2 * (1 - place) + cut) * width
            row = 8 + 2 * place + cut
            natural[row : row + 1, :] = flip(
                rank, sums_inner[:, near : near + width], sums_inner[:, far : far + width]
            )
    relative[:16, :] = dot(natural[...].astype(LOW), permute[...])
    relative[2:5, :] = sums_one[:3, :]
    relative[5:8, :] = sums_two[:3, :]
    return jnp.transpose(relative[...]).astype(LOW)


def pack_kernel(rank_ref, w_qkv, w_out, vectors, target, turned):
    columns = w_out.shape[1]
    count, shard_width = vectors.shape
    a_width = 2 * columns + LANES
    turned[...] = jnp.zeros_like(turned)
    for place in range(3):
        turned[16 * place : 16 * place + count, :shard_width] = vectors[...]
    values = jnp.transpose(turned[...])
    lane = lax.broadcasted_iota(jnp.int32, values.shape, 1)
    first = values.astype(LOW).astype(F32)
    second = (values - first).astype(LOW).astype(F32)
    third = values - first - second
    values = jnp.where(lane < 16, first, jnp.where(lane < 32, second, third))[:shard_width]
    blank = jnp.zeros_like(values)
    values = jnp.concatenate(
        [flip(rank_ref[0], values, blank), flip(rank_ref[0], blank, values)], axis=0
    )
    target[:, :columns] = w_qkv[0].astype(LOW)
    target[:, columns : 2 * columns] = w_qkv[1].astype(LOW)
    target[:, 2 * columns : a_width] = values.astype(LOW)
    target[:, a_width : a_width + columns] = w_qkv[2].astype(LOW)
    target[:, a_width + columns :] = w_out[...].astype(LOW)


def cast_kernel(first, second, target):
    columns = first.shape[1]
    target[:, :columns] = first[...].astype(LOW)
    target[:, columns:] = second[...].astype(LOW)


def project_kernel(rows, a_own, a_far, b_own, b_far, bias_q, bias_v, q, k, v):
    half = a_own.shape[0]
    own_rows, width = q.shape
    part = width // 2
    low, high = rows[:, :half], rows[:, half:]
    a_half, b_half = a_own.shape[1] // 2, b_own.shape[1] // 2
    for side in range(2):
        cols = slice(side * part, (side + 1) * part)
        at = slice(side * a_half, side * a_half + part)
        q[:, cols] = (
            dot(low[:own_rows], a_own[:, at]) + dot(high[:own_rows], a_far[:, at]) + bias_q[:, cols]
        ).astype(LOW)
        at = slice(side * a_half + part, side * a_half + 2 * part)
        k[:, cols] = (dot(low, a_own[:, at]) + dot(high, a_far[:, at])).astype(LOW)
        at = slice(side * b_half, side * b_half + part)
        v[:, cols] = (dot(low, b_own[:, at]) + dot(high, b_far[:, at]) + bias_v[:, cols]).astype(
            LOW
        )


def segment(lengths, positions):
    end, total = 0, jnp.zeros_like(positions)
    for place in range(lengths.shape[1]):
        end = end + lengths[0, place]
        total = total + (positions >= end).astype(jnp.int32)
    return total


def same_segment(rank, lengths, keys, queries):
    own = lax.broadcasted_iota(jnp.int32, (1, queries), 1) + rank * queries
    rows = lax.broadcasted_iota(jnp.int32, (keys, 1), 0)
    rows = jnp.where(rows < queries, rows + rank * queries, rows - rank * queries)
    return segment(lengths, rows) == segment(lengths, own)


def softmax_down(same, key_rows, queries):
    scores = dot_nt(key_rows, queries) * 0.125
    scores = jnp.where(same, scores, NEG_FILL)
    exp_scores = jnp.exp(scores - jnp.max(scores, axis=0, keepdims=True))
    return exp_scores * (1.0 / jnp.sum(exp_scores, axis=0, keepdims=True))


def two_heads(out):
    joined = jnp.concatenate([out[0][:HEAD_DIM], out[1][HEAD_DIM:]], axis=0)
    return jnp.transpose(joined).astype(LOW)


def attend_kernel(rank_ref, lengths, q, k, v, attended):
    queries, key_rows, value_rows = q[...], k[...], v[...]
    same = same_segment(rank_ref[0], lengths, k.shape[0], q.shape[0])
    first = lax.broadcasted_iota(jnp.int32, queries.shape, 1) < HEAD_DIM
    out = []
    for mine in (first, jnp.logical_not(first)):
        prob = softmax_down(same, key_rows, jnp.where(mine, queries, jnp.zeros_like(queries)))
        out.append(dot_tn(value_rows, prob.astype(LOW)))
    attended[...] = two_heads(out)


def attend_back_kernel(rank_ref, lengths, q, k, v, grad, grad_q, grad_k, grad_v):
    queries, key_rows, value_rows, grad_rows = q[...], k[...], v[...], grad[...]
    same = same_segment(rank_ref[0], lengths, k.shape[0], q.shape[0])
    first = lax.broadcasted_iota(jnp.int32, queries.shape, 1) < HEAD_DIM
    first_all = lax.broadcasted_iota(jnp.int32, key_rows.shape, 1) < HEAD_DIM
    blank = jnp.zeros_like(queries)
    out_q, out_k, out_v = [], [], []
    for mine in (first, jnp.logical_not(first)):
        prob = softmax_down(same, key_rows, jnp.where(mine, queries, blank))
        grad_prob = dot_nt(value_rows, jnp.where(mine, grad_rows, blank))
        delta = jnp.sum(grad_prob * prob, axis=0, keepdims=True)
        grad_score = (prob * (grad_prob - delta)).astype(LOW)
        out_q.append(dot_tn(key_rows, grad_score) * 0.125)
        out_k.append(dot(grad_score, queries) * 0.125)
        out_v.append(dot(prob.astype(LOW), grad_rows))
    grad_q[...] = two_heads(out_q)
    grad_k[...] = jnp.where(first_all, out_k[0], out_k[1]).astype(LOW)
    grad_v[...] = jnp.where(first_all, out_v[0], out_v[1]).astype(LOW)


def out_norm_kernel(attended, rows, b_own, b_far, vec, y, y_low, normed, inv):
    half = b_own.shape[0]
    own_rows, width = y.shape
    part = width // 2
    b_half = b_own.shape[1] // 2
    near, far = attended[:, :part], attended[:, part:]
    out = []
    for weights in (b_own, b_far):
        out.append(
            dot_nt(near, weights[:, part : 2 * part])
            + dot_nt(far, weights[:, b_half + part : b_half + 2 * part])
        )
    total = rows[:own_rows, :].astype(F32) + jnp.concatenate(out, axis=1) + vec[0:1]
    y_new, normed[...], inv[...] = normalize_fwd(total, vec[1:2], vec[2:3])
    y[...] = y_new
    y_low[...] = y_new.astype(LOW)


def stacked(pieces, at=slice(None)):
    return jnp.concatenate([piece[:, at] for piece in pieces], axis=0)


def hidden_kernel(y_low, *refs):
    pieces, (bias, activation, slope) = refs[:4], refs[4:]
    rows = y_low[...]
    columns = pieces[0].shape[1]
    step = columns // 8
    for start in range(0, columns, step):
        at = slice(start, start + step)
        pre = dot(rows, stacked(pieces, at)) + bias[:, at]
        cdf = 0.5 + 0.5 * lax.erf(pre * (0.5**0.5))
        activation[:, at] = (pre * cdf).astype(LOW)
        slope[:, at] = cdf + pre * jnp.exp(-0.5 * pre * pre) * ((2.0 * np.pi) ** -0.5)


def out_back_kernel(
    rank_ref, lengths, activation, own, own_side, far, far_side, y, cot, vec,
    mixed, grad, grad_low, sums,
):
    columns = own.shape[1]
    near, side = activation[:, :columns], activation[:, columns:]
    out = [
        dot_nt(near, first[...]) + dot_nt(side, second[...])
        for first, second in ((own, own_side), (far, far_side))
    ]
    total = y[...] + jnp.concatenate(out, axis=1) + vec[3:4]
    result, normed, inv_std = normalize_fwd(total, vec[4:5], vec[5:6])
    mixed[...] = result.astype(LOW)
    rows = lax.broadcasted_iota(jnp.int32, (y.shape[0], 1), 0) + rank_ref[0] * y.shape[0]
    valid = (segment(lengths, rows) < lengths.shape[1]).astype(F32)
    grad_in, gain_sum, shift_sum = normalize_back(cot[...] * valid, normed, inv_std, vec[4:5])
    grad[...] = grad_in
    grad_low[...] = grad_in.astype(LOW)
    sums[0:1] = jnp.sum(grad_in, axis=0, keepdims=True)
    sums[1:2] = gain_sum[None]
    sums[2:3] = shift_sum[None]


def hidden_back_kernel(grad_low, own, own_side, far, far_side, slope, grad_pre, sums):
    rows = grad_low[...]
    columns = own.shape[1]
    step = columns // 4
    for place, pieces in enumerate(((own, far), (own_side, far_side))):
        for start in range(0, columns, step):
            to = slice(place * columns + start, place * columns + start + step)
            grad_act = dot(rows, stacked(pieces, slice(start, start + step)))
            value = (grad_act * slope[:, to]).astype(LOW)
            grad_pre[:, to] = value
            sums[:, to] = jnp.sum(value.astype(F32), axis=0, keepdims=True)


def norm_back_kernel(
    grad_pre, own, own_side, far, far_side, grad_two, normed, inv, vec, o_own, o_far,
    grad, grad_low, grad_attn, sums,
):
    out = [
        dot_nt(grad_pre[...], stacked(pieces)) for pieces in ((own, own_side), (far, far_side))
    ]
    grad_in, gain_sum, shift_sum = normalize_back(
        grad_two[...] + jnp.concatenate(out, axis=1), normed[...], inv[...], vec[1:2]
    )
    grad[...] = grad_in
    low = grad_in.astype(LOW)
    grad_low[...] = low
    sums[0:1] = jnp.sum(grad_in, axis=0, keepdims=True)
    sums[1:2] = gain_sum[None]
    sums[2:3] = shift_sum[None]
    half = o_own.shape[0]
    part = grad.shape[1] // 2
    o_half = o_own.shape[1] // 2
    for side in range(2):
        at = slice(side * o_half + part, side * o_half + 2 * part)
        grad_attn[:, side * part : (side + 1) * part] = (
            dot(low[:, :half], o_own[:, at]) + dot(low[:, half:], o_far[:, at])
        ).astype(LOW)


def rows_back_kernel(grad_q, grad_k, grad_v, a_own, a_far, b_own, b_far, grad_one, own, away):
    own_rows, width = own.shape
    part = width // 2
    a_half, b_half = a_own.shape[1] // 2, b_own.shape[1] // 2
    half = a_own.shape[0]
    for place, (wa, wb) in enumerate(((a_own, b_own), (a_far, b_far))):
        to = slice(place * half, (place + 1) * half)
        both = jnp.zeros((2 * own_rows, half), F32)
        mine = grad_one[:, to]
        for side in range(2):
            cols = slice(side * part, (side + 1) * part)
            at = side * a_half
            mine = mine + dot_nt(grad_q[:, cols], wa[:, at : at + part])
            both = both + dot_nt(grad_k[:, cols], wa[:, at + part : at + 2 * part])
            at = side * b_half
            both = both + dot_nt(grad_v[:, cols], wb[:, at : at + part])
        own[:, to] = mine + both[:own_rows]
        away[:, to] = both[own_rows:].astype(LOW)


def rows_out_kernel(own, away, permute, out):
    rest = own[...] + away[...].astype(F32)
    total = None
    for _ in range(3):
        part = rest.astype(LOW)
        rest = rest - part.astype(F32)
        moved = dot_nt(part, permute[...])
        total = moved if total is None else total + moved
    out[...] = total


def first_grads_kernel(
    a_half, rank_ref, permute, rows, grad_q, grad_k, grad_v, grad_low, attended,
    sums_one, sums_two, sums_inner, a_send, b_send, a_keep, b_keep, natural, relative,
):
    half = a_keep.shape[0]
    own_rows, width = grad_q.shape
    part = width // 2
    extra = vector_lanes(
        rank_ref[0], permute, grad_q, grad_v, sums_one, sums_two, sums_inner, natural, relative
    )
    for place, to, to_b in ((1, a_send, b_send), (0, a_keep, b_keep)):
        at = slice(place * half, (place + 1) * half)
        both = rows[:, at]
        mine = rows[:own_rows, at]
        low = grad_low[:, at]
        for side in range(2):
            cols = slice(side * part, (side + 1) * part)
            base = side * a_half
            to[:, base : base + part] = dot_tn(mine, grad_q[:, cols]).astype(LOW)
            to[:, base + part : base + 2 * part] = dot_tn(both, grad_k[:, cols]).astype(LOW)
            to[:, base + 2 * part : base + a_half] = extra[at, :]
            base = side * 2 * part
            to_b[:, base : base + part] = dot_tn(both, grad_v[:, cols]).astype(LOW)
            to_b[:, base + part : base + 2 * part] = dot_tn(low, attended[:, cols]).astype(LOW)


def close_kernel(rates, rank_ref, *refs):
    inputs, parts = refs[:9], refs[9:-10]
    outs, turned = refs[-10:-1], refs[-1]
    total = parts[0][...].astype(F32)
    for part in parts[1:]:
        total = total + part[...].astype(F32)
    columns = outs[3].shape[1]
    count, shard_width = outs[6].shape
    a_width = 2 * columns + LANES
    for place, start in enumerate((0, columns, a_width)):
        values = adamw(
            *[ref[place] for ref in inputs[:3]],
            total[:, start : start + columns],
            rates[0],
            WEIGHT_DECAY,
        )
        for out, value in zip(outs[:3], values):
            out[place] = value
    values = adamw(
        *[ref[...] for ref in inputs[3:6]],
        total[:, a_width + columns :],
        rates[1],
        WEIGHT_DECAY,
    )
    for out, value in zip(outs[3:6], values):
        out[...] = value
    lanes = total[:, 2 * columns : a_width]
    turned[...] = jnp.zeros_like(turned)
    turned[:shard_width, :] = flip(
        rank_ref[0], lanes[:shard_width], lanes[shard_width : 2 * shard_width]
    )
    gradient = jnp.transpose(turned[...])[:count, :shard_width]
    values = adamw(*[ref[...] for ref in inputs[6:]], gradient, 0.1, 0.0)
    for out, value in zip(outs[6:], values):
        out[...] = value


def on_device(
    tokens,
    cotangent,
    lengths,
    w_qkv,
    m_qkv,
    v_qkv,
    w_out,
    m_out,
    v_out,
    w_in,
    m_in,
    v_in,
    w_back,
    m_back,
    v_back,
    vectors,
    m_vectors,
    v_vectors,
):
    own_rows, width = tokens.shape
    tensor_rank = lax.axis_index("tensor")
    group_rows = 2 * own_rows
    shard_rows = w_qkv.shape[1]
    part = w_qkv.shape[2]
    hidden_half = w_in.shape[1]
    full_inner = 2 * hidden_half
    half = width // 2
    count = vectors.shape[0]
    shard_width = vectors.shape[1]

    a_width = 2 * part + LANES
    rank = tensor_rank.astype(jnp.int32).reshape(1)
    scalar = pl.BlockSpec(memory_space=pltpu.SMEM)
    vmem = pl.BlockSpec(memory_space=pltpu.VMEM)
    shard_one = run(
        pack_kernel,
        [shape_of(shard_rows, a_width + 2 * part, LOW)],
        [rank, w_qkv, w_out.T, vectors],
        0,
        in_specs=[scalar] + [vmem] * 3,
        scratch=[pltpu.VMEM((LANES, LANES), F32)],
    )[0]

    tokens_far = swap_tensor(tokens)
    one_high = gather_high(shard_one)
    one = join_high(one_high, a_width)
    one_far = swap_tensor(one[0]), swap_dp(one[1], 2)
    shard_pair = run(
        cast_kernel,
        [shape_of(shard_rows, full_inner, LOW)],
        [w_in, w_back.T],
        0,
        after=one[:1],
    )[0]
    pair_high = gather_high(shard_pair)

    order = relative_order(width)
    permute = (jnp.arange(width, dtype=jnp.int32)[:, None] == order[None, :]).astype(LOW)
    rows_all = jnp.concatenate([dot(tokens, permute), dot(tokens_far, permute)]).astype(LOW)
    cot = dot(cotangent, permute)

    one = join_plane(*one, *one_far, after=[rows_all])
    one_far = swap_dp(one[0], 2), swap_tensor(one[1])
    unit = 2 * own_rows * width * width
    pair = join_high(pair_high, hidden_half, 400 * unit)
    one = join_plane(one[1], one[0], one_far[1], one_far[0], after=pair[:1])[::-1]
    a_own, b_own = one
    a_far, b_far = swap_dp(a_own, 1), swap_dp(b_own, 1)
    pair_far = swap_tensor(pair[0]), swap_dp(pair[1], 2)

    vec, bias_query, bias_value, bias_inner = run(
        vectors_kernel,
        [
            shape_of(6, width, F32),
            shape_of(1, width, F32),
            shape_of(1, width, F32),
            shape_of(1, full_inner, F32),
        ],
        [rank, permute, a_own, a_far],
        1,
        in_specs=[scalar, vmem, vmem, vmem],
    )

    wide_low = shape_of(own_rows, width, LOW)
    wide = shape_of(own_rows, width, F32)
    group_low = shape_of(group_rows, width, LOW)
    sums_shape = shape_of(8, width, F32)
    queries, key_rows, value_rows = run(
        project_kernel,
        [wide_low, group_low, group_low],
        [rows_all, a_own, a_far, b_own, b_far, bias_query, bias_value],
        5 * unit,
    )
    pair = join_plane(*pair, *pair_far, after=[queries])
    in_near, in_side = pair[0], swap_dp(pair[0], 2)
    back_near, back_side = pair[1], swap_tensor(pair[1])
    in_far, back_far = swap_dp(in_near, 1), swap_dp(back_near, 1)
    pairs = width // LANES
    own_block = pl.BlockSpec((own_rows, LANES), lambda i: (0, i))
    all_block = pl.BlockSpec((group_rows, LANES), lambda i: (0, i))

    attended = run(
        attend_kernel,
        [wide_low],
        [rank, lengths, queries, key_rows, value_rows],
        3 * unit,
        after=pair[:1],
        grid=(pairs,),
        in_specs=[scalar, scalar, own_block, all_block, all_block],
        out_specs=[own_block],
    )[0]
    first_norm, first_low, normed_one, inv_one = run(
        out_norm_kernel,
        [wide, wide_low, wide, shape_of(own_rows, 1, F32)],
        [attended, rows_all, b_own, b_far, vec],
        2 * unit,
        after=[in_far, back_far],
    )
    in_side, back_side = gate([in_side, back_side], [first_low])
    pieces_in = [in_near, in_side, in_far, swap_dp(in_side, 1)]
    pieces_back = [back_near, back_side, back_far, swap_dp(back_side, 1)]
    activation, slope = run(
        hidden_kernel,
        [shape_of(own_rows, full_inner, LOW), shape_of(own_rows, full_inner, F32)],
        [first_low, *pieces_in, bias_inner],
        8 * unit,
    )
    mixed_rel, grad_two, grad_two_low, sums_two = run(
        out_back_kernel,
        [wide_low, wide, wide_low, sums_shape],
        [rank, lengths, activation, *pieces_back, first_norm, cot, vec],
        5 * unit,
        in_specs=[scalar, scalar] + [vmem] * 8,
    )
    mixed = dot_nt(mixed_rel, permute).astype(LOW)

    def gradient(left, right):
        return dot_tn(left, right).astype(LOW)

    back_parts = []
    for columns in (activation[:, hidden_half:], activation[:, :hidden_half]):
        sent = swap_dp(gradient(grad_two_low[:, half:], columns), 1)
        back_parts.append((gradient(grad_two_low[:, :half], columns), sent))
    grad_pre, sums_inner = run(
        hidden_back_kernel,
        [shape_of(own_rows, full_inner, LOW), shape_of(1, full_inner, F32)],
        [grad_two_low, *pieces_back, slope],
        6 * unit,
    )
    quarter = half // 2
    in_parts = []
    for start in (quarter, 0):
        rows = slice(half + start, half + start + quarter)
        sent = swap_dp(gradient(first_low[:, rows], grad_pre), 1)
        in_parts.append((gradient(first_low[:, start : start + quarter], grad_pre), sent))
    b_send = add_parts(*back_parts[0], 400 * unit, after=[grad_pre])
    a_send = add_parts(*in_parts[0], after=[b_send])
    a_far_sum, b_far_sum = swap_dp(a_send, 2), swap_tensor(b_send)
    grad_one, grad_one_low, grad_attn, sums_one = run(
        norm_back_kernel,
        [wide, wide_low, wide_low, sums_shape],
        [grad_pre, *pieces_in, grad_two, normed_one, inv_one, vec, b_own, b_far],
        6 * unit,
        after=[a_send],
    )
    b_keep = add_parts(*back_parts[1], after=[grad_one_low])
    a_keep = add_parts(*in_parts[1], after=[b_keep])
    pair = a_keep, a_far_sum, b_keep, b_far_sum
    grad_q, grad_k, grad_v = run(
        attend_back_kernel,
        [wide_low, group_low, group_low],
        [rank, lengths, queries, key_rows, value_rows, grad_attn],
        5 * unit,
        grid=(pairs,),
        in_specs=[scalar, scalar, own_block, all_block, all_block, own_block],
        out_specs=[own_block, all_block, all_block],
    )
    a_shape, b_shape = shape_of(half, 2 * a_width, LOW), shape_of(half, 4 * part, LOW)
    a_send, b_send, one_a, one_b = run(
        functools.partial(first_grads_kernel, a_width),
        [a_shape, b_shape, a_shape, b_shape],
        [rank, permute, rows_all, grad_q, grad_k, grad_v, grad_one_low, attended]
        + [sums_one, sums_two, sums_inner],
        6 * unit,
        in_specs=[scalar] + [vmem] * 10,
        scratch=[pltpu.VMEM((16, width), F32), pltpu.VMEM((LANES, width), F32)],
    )
    one = one_a, swap_dp(a_send, 1), one_b, swap_dp(b_send, 1)
    a_keep, a_send, b_keep, b_send = split_plane(*pair, after=[one_a, mixed])
    pair = a_keep, swap_tensor(a_send), b_keep, swap_dp(b_send, 2)
    grad_own, grad_away = run(
        rows_back_kernel,
        [wide, wide_low],
        [grad_q, grad_k, grad_v, a_own, a_far, b_own, b_far, grad_one],
        400 * unit,
        after=[a_keep],
    )
    a_keep, a_send, b_keep, b_send = split_core(*one, after=[grad_own])
    one = a_keep, swap_dp(a_send, 2), b_keep, swap_tensor(b_send)
    pair = send_high(split_high(*pair, after=[a_keep]))
    a_keep, a_send, b_keep, b_send = split_plane(*one, after=pair[:1])
    one = a_keep, swap_tensor(a_send), b_keep, swap_dp(b_send, 2)
    pair = sum_parts(pair, 400 * unit, after=[a_keep])
    one = send_high(split_high(*one, after=pair))
    input_grad = run(
        rows_out_kernel,
        [wide],
        [grad_own, swap_tensor(gate([grad_away], pair)[0]), permute],
        3 * unit,
        after=one[:1],
    )[0]
    sum_pair = reduce_rest(gate(pair, one[:1])[0])
    summed_in, summed_back = sum_pair[:, :hidden_half], sum_pair[:, hidden_half:].T
    if len(high_groups()) > 1:
        one = [reduce_rest(sum(piece.astype(F32) for piece in one))]
    qkv_shape = jax.ShapeDtypeStruct(w_qkv.shape, F32)
    out_shape = shape_of(shard_rows, part, F32)
    vec_shape = shape_of(count, shard_width, F32)
    done = run(
        functools.partial(
            close_kernel,
            (float(width) ** (-0.5), (4.0 * width / group_rows) ** (-0.5)),
        ),
        [qkv_shape] * 3 + [out_shape] * 3 + [vec_shape] * 3,
        [rank, w_qkv, m_qkv, v_qkv, w_out.T, m_out.T, v_out.T]
        + [vectors, m_vectors, v_vectors, *one],
        unit,
        after=[input_grad],
        in_specs=[scalar] + [vmem] * (9 + len(one)),
        scratch=[pltpu.VMEM((LANES, LANES), F32)],
    )
    new_qkv, moment_qkv, square_qkv = done[:3]
    new_out, moment_out, square_out = [value.T for value in done[3:6]]
    new_vectors, moment_vectors, square_vectors = done[6:]
    new_in, moment_in, square_in = adamw(
        w_in, m_in, v_in, summed_in, float(width) ** (-0.5), WEIGHT_DECAY
    )
    new_back, moment_back, square_back = adamw(
        w_back, m_back, v_back, summed_back, float(full_inner) ** (-0.5), WEIGHT_DECAY
    )
    return (
        mixed,
        input_grad,
        new_qkv,
        moment_qkv,
        square_qkv,
        new_out,
        moment_out,
        square_out,
        new_in,
        moment_in,
        square_in,
        new_back,
        moment_back,
        square_back,
        new_vectors,
        moment_vectors,
        square_vectors,
    )


def solution(mesh):
    placed = (
        P(("dp", "tensor"), None),
        P(("dp", "tensor"), None),
        P("dp", None),
        P(None, "dp", "tensor"),
        P(None, "dp", "tensor"),
        P(None, "dp", "tensor"),
        P("tensor", "dp"),
        P("tensor", "dp"),
        P("tensor", "dp"),
        P("dp", "tensor"),
        P("dp", "tensor"),
        P("dp", "tensor"),
        P("tensor", "dp"),
        P("tensor", "dp"),
        P("tensor", "dp"),
        P(None, ("dp", "tensor")),
        P(None, ("dp", "tensor")),
        P(None, ("dp", "tensor")),
    )
    return jax.shard_map(
        on_device,
        mesh=mesh,
        in_specs=placed,
        out_specs=(
            P(("dp", "tensor"), None),
            P(("dp", "tensor"), None),
            P(None, "dp", "tensor"),
            P(None, "dp", "tensor"),
            P(None, "dp", "tensor"),
            P("tensor", "dp"),
            P("tensor", "dp"),
            P("tensor", "dp"),
            P("dp", "tensor"),
            P("dp", "tensor"),
            P("dp", "tensor"),
            P("tensor", "dp"),
            P("tensor", "dp"),
            P("tensor", "dp"),
            P(None, ("dp", "tensor")),
            P(None, ("dp", "tensor")),
            P(None, ("dp", "tensor")),
        ),
        check_vma=False,
    )
```

```python
import functools

import numpy as np

import jax
import jax.numpy as jnp
from jax import lax
from jax.experimental import pallas as pl
from jax.experimental.pallas import tpu as pltpu
from jax.sharding import PartitionSpec as P

HEAD_DIM = 64
LANES = 128
STEP = 10


EPS_NORM = 1e-05
BETA_ONE = 0.9
BETA_TWO = 0.999
EPS_ADAM = 1e-08
WEIGHT_DECAY = 0.01
NEG_FILL = -1000000000.0
LOW = jnp.bfloat16
F32 = jnp.float32


def normalize_fwd(values, gain_row, shift_row):
    row_mean = jnp.mean(values, axis=-1, keepdims=True)
    centered = values - row_mean
    variance = jnp.mean(centered * centered, axis=-1, keepdims=True)
    inv_std = lax.rsqrt(variance + EPS_NORM)
    normed = centered * inv_std
    return (normed * gain_row + shift_row, normed, inv_std)


def normalize_back(gradient, normed, inv_std, gain_row):
    grad_norm = gradient * gain_row
    grad_in = inv_std * (
        grad_norm
        - jnp.mean(grad_norm, axis=-1, keepdims=True)
        - normed * jnp.mean(grad_norm * normed, axis=-1, keepdims=True)
    )
    return (grad_in, jnp.sum(gradient * normed, axis=0), jnp.sum(gradient, axis=0))


def adamw(weight, moment, square, gradient, step_rate, decay_rate):
    moment = BETA_ONE * moment + (1.0 - BETA_ONE) * gradient
    square = BETA_TWO * square + (1.0 - BETA_TWO) * gradient * gradient
    direction = (
        moment / (1.0 - BETA_ONE**STEP) / (jnp.sqrt(square / (1.0 - BETA_TWO**STEP)) + EPS_ADAM)
    )
    return (weight - step_rate * (direction + decay_rate * weight), moment, square)


def swap_dp(values, mask):
    size = lax.axis_size("dp")
    return lax.ppermute(values, "dp", [(i, i ^ mask) for i in range(size)])


def swap_tensor(values):
    return lax.ppermute(values, "tensor", [(0, 1), (1, 0)])


def high_bits():
    return list(range(2, lax.axis_size("dp").bit_length() - 1))


def high_groups():
    bits = high_bits()
    return [[1 << bit for bit in bits[i : i + 2]] for i in range(0, len(bits), 2)]


def group_masks(group):
    return [0] + group + ([group[0] ^ group[1]] if len(group) == 2 else [])


def gather_high(shard):
    groups = high_groups()
    for place, group in enumerate(groups):
        pieces = [shard if mask == 0 else swap_dp(shard, mask) for mask in group_masks(group)]
        if place < len(groups) - 1:
            shard = jnp.concatenate(pieces, axis=0)
    return pieces


def send_high(parts):
    masks = group_masks(high_groups()[-1])
    return [parts[0]] + [swap_dp(part, mask) for part, mask in zip(parts[1:], masks[1:])]


def reduce_rest(total):
    for group in reversed(high_groups()[:-1]):
        masks = group_masks(group)
        rows = total.shape[0] // len(masks)
        low = total.astype(LOW)
        total = total[:rows]
        for place, mask in enumerate(masks[1:], 1):
            total = total + swap_dp(low[place * rows : (place + 1) * rows], mask).astype(F32)
    return total


def relative_order(width):
    size = lax.axis_size("dp")
    rows = width // size
    inner_first = high_bits() + [1, 0]
    masks = np.zeros((size,), np.int32)
    for block in range(size):
        for place, bit in enumerate(inner_first):
            if (block >> place) & 1:
                masks[block] |= 1 << bit
    block_mask = jnp.asarray(np.repeat(masks, rows))
    offsets = jnp.asarray(np.tile(np.arange(rows, dtype=np.int32), size))
    return (lax.axis_index("dp") ^ block_mask) * rows + offsets


def dot(left, right):
    return jnp.dot(left, right, preferred_element_type=F32)


def dot_nt(left, right):
    return lax.dot_general(left, right, (((1,), (1,)), ((), ())), preferred_element_type=F32)


def dot_tn(left, right):
    return lax.dot_general(left, right, (((0,), (0,)), ((), ())), preferred_element_type=F32)


def shape_of(rows, columns, kind):
    return jax.ShapeDtypeStruct((rows, columns), kind)


def run(kernel, outs, operands, flops, after=(), grid=(), in_specs=None, out_specs=None, scratch=()):
    count = len(operands)

    def body(*refs):
        kernel(*refs[:count], *refs[count + len(after) :])

    whole = pl.BlockSpec(memory_space=pltpu.VMEM)
    in_specs = in_specs or [whole] * count
    size = sum(v.size * v.dtype.itemsize for v in list(operands) + list(outs))
    grant = 10 << 20 if grid else size + ((8 if flops else 2) << 20)
    return pl.pallas_call(
        body,
        grid=grid,
        out_shape=list(outs),
        in_specs=list(in_specs) + [pl.BlockSpec(memory_space=pl.ANY)] * len(after),
        out_specs=list(out_specs or [whole] * len(outs)),
        scratch_shapes=list(scratch),
        compiler_params=pltpu.CompilerParams(vmem_limit_bytes=grant),
        cost_estimate=pl.CostEstimate(flops=flops, bytes_accessed=size, transcendentals=0),
    )(*operands, *after)


def gate(values, after):
    anywhere = pl.BlockSpec(memory_space=pl.ANY)
    return pl.pallas_call(
        lambda *refs: None,
        out_shape=[shape_of(*value.shape, value.dtype) for value in values],
        in_specs=[anywhere] * (len(values) + len(after)),
        out_specs=[anywhere] * len(values),
        input_output_aliases={place: place for place in range(len(values))},
        compiler_params=pltpu.CompilerParams(vmem_limit_bytes=1 << 20),
        cost_estimate=pl.CostEstimate(flops=0, bytes_accessed=0, transcendentals=0),
    )(*values, *after)


def join_high_kernel(count, *refs):
    pieces, (first, second) = refs[:count], refs[count:]
    cut = first.shape[1]
    rows = pieces[0].shape[0]
    for place, piece in enumerate(pieces):
        to = slice(place * rows, (place + 1) * rows)
        first[to, :] = piece[:, :cut]
        second[to, :] = piece[:, cut:]


def join_high(pieces, cut, flops=0, after=()):
    rows, columns = pieces[0].shape
    rows = rows * len(pieces)
    return run(
        functools.partial(join_high_kernel, len(pieces)),
        [shape_of(rows, cut, LOW), shape_of(rows, columns - cut, LOW)],
        pieces,
        flops,
        after,
    )


def join_plane_kernel(across, down, across_far, down_far, across_all, down_all):
    columns, rows = across.shape[1], down.shape[0]
    across_all[:, :columns] = across[...]
    across_all[:, columns:] = across_far[...]
    down_all[:rows, :] = down[...]
    down_all[rows:, :] = down_far[...]


def join_plane(across, down, across_far, down_far, after=()):
    return run(
        join_plane_kernel,
        [
            shape_of(across.shape[0], 2 * across.shape[1], LOW),
            shape_of(2 * down.shape[0], down.shape[1], LOW),
        ],
        [across, down, across_far, down_far],
        0,
        after,
    )


def added(left, right, rows, columns):
    return (left[rows, columns].astype(F32) + right[rows, columns].astype(F32)).astype(LOW)


def add_kernel(array, far, total):
    total[...] = added(array, far, slice(None), slice(None))


def add_parts(array, far, flops=0, after=()):
    return run(add_kernel, [shape_of(*array.shape, LOW)], [array, far], flops, after)[0]


def split_rows_kernel(array, far, keep, send):
    rows = keep.shape[0]
    keep[...] = added(array, far, slice(0, rows), slice(None))
    send[...] = added(array, far, slice(rows, 2 * rows), slice(None))


def split_columns_kernel(array, far, keep, send):
    columns = keep.shape[1]
    keep[...] = added(array, far, slice(None), slice(0, columns))
    send[...] = added(array, far, slice(None), slice(columns, 2 * columns))


def split_core_kernel(a, a_far, b, b_far, a_keep, a_send, b_keep, b_send):
    split_rows_kernel(a, a_far, a_keep, a_send)
    split_columns_kernel(b, b_far, b_keep, b_send)


def split_core(a, a_far, b, b_far, after=()):
    a_shape = shape_of(a.shape[0] // 2, a.shape[1], LOW)
    b_shape = shape_of(b.shape[0], b.shape[1] // 2, LOW)
    return run(
        split_core_kernel, [a_shape, a_shape, b_shape, b_shape], [a, a_far, b, b_far], 0, after
    )


def sum_kernel(*refs):
    total = refs[0][...].astype(F32)
    for ref in refs[1:-1]:
        total = total + ref[...].astype(F32)
    refs[-1][...] = total


def sum_parts(parts, flops, after=()):
    return run(sum_kernel, [shape_of(*parts[0].shape, F32)], parts, flops, after)


def split_plane_kernel(a, a_far, b, b_far, a_keep, a_send, b_keep, b_send):
    half, rows = a_keep.shape[1], b_keep.shape[0]
    every = slice(None)
    a_keep[...] = added(a, a_far, every, slice(0, half))
    a_send[...] = added(a, a_far, every, slice(half, 2 * half))
    b_keep[...] = added(b, b_far, slice(0, rows), every)
    b_send[...] = added(b, b_far, slice(rows, 2 * rows), every)


def split_plane(a, a_far, b, b_far, after=()):
    a_shape = shape_of(a.shape[0], a.shape[1] // 2, LOW)
    b_shape = shape_of(b.shape[0] // 2, b.shape[1], LOW)
    return run(
        split_plane_kernel, [a_shape, a_shape, b_shape, b_shape], [a, a_far, b, b_far], 0, after
    )


def split_high_kernel(a, a_far, b, b_far, *parts):
    cut = a.shape[1]
    rows = parts[0].shape[0]
    for place, part in enumerate(parts):
        at = slice(place * rows, (place + 1) * rows)
        part[:, :cut] = added(a, a_far, at, slice(None))
        part[:, cut:] = added(b, b_far, at, slice(None))


def split_high(a, a_far, b, b_far, after=()):
    count = len(group_masks(high_groups()[-1]))
    part = shape_of(a.shape[0] // count, a.shape[1] + b.shape[1], LOW)
    return run(split_high_kernel, [part] * count, [a, a_far, b, b_far], 0, after)


def flip(rank, first, second):
    return jnp.where(rank == 0, first, second)


def vectors_kernel(rank_ref, permute, a_own, a_far, relative, bias_q, bias_v, bias_inner):
    rank = rank_ref[0]
    side = a_own.shape[1] // 2
    width = relative.shape[1]
    half = width // 2
    spread = jnp.concatenate(
        [
            (ref[:, side - LANES : side].astype(F32) + ref[:, 2 * side - LANES :].astype(F32))
            for ref in (a_own, a_far)
        ],
        axis=0,
    )
    parts = jnp.transpose(spread)
    parts = [parts[16 * i : 16 * (i + 1)] for i in range(3)]
    relative[...] = ((parts[0] + parts[1]) + parts[2])[2:8]
    natural = [dot_nt(part.astype(LOW), permute[...]) for part in parts]
    natural = (natural[0] + natural[1]) + natural[2]
    for row, target in ((0, bias_q), (1, bias_v)):
        first, second = natural[row : row + 1, :half], natural[row : row + 1, half:]
        target[:, :half] = flip(rank, first, second)
        target[:, half:] = flip(rank, second, first)
    for place in range(2):
        for cut in range(2):
            near, far = 8 + 2 * place + cut, 8 + 2 * (1 - place) + cut
            at = (2 * place + cut) * width
            bias_inner[:, at : at + width] = flip(
                rank, natural[near : near + 1], natural[far : far + 1]
            )


def vector_lanes(rank, permute, grad_q, grad_v, sums_one, sums_two, sums_inner, natural, relative):
    width = natural.shape[1]
    half = width // 2
    natural[...] = jnp.zeros_like(natural)
    relative[...] = jnp.zeros_like(relative)
    for row, source in ((0, grad_q), (1, grad_v)):
        total = jnp.sum(source[...].astype(F32), axis=0, keepdims=True)
        first, second = total[:, :half], total[:, half:]
        natural[row : row + 1, :half] = flip(rank, first, second)
        natural[row : row + 1, half:] = flip(rank, second, first)
    for place in range(2):
        for cut in range(2):
            near, far = (2 * place + cut) * width, (2 * (1 - place) + cut) * width
            row = 8 + 2 * place + cut
            natural[row : row + 1, :] = flip(
                rank, sums_inner[:, near : near + width], sums_inner[:, far : far + width]
            )
    relative[:16, :] = dot(natural[...].astype(LOW), permute[...])
    relative[2:5, :] = sums_one[:3, :]
    relative[5:8, :] = sums_two[:3, :]
    return jnp.transpose(relative[...]).astype(LOW)


def pack_kernel(rank_ref, w_qkv, w_out, vectors, target, turned):
    columns = w_out.shape[1]
    count, shard_width = vectors.shape
    a_width = 2 * columns + LANES
    turned[...] = jnp.zeros_like(turned)
    for place in range(3):
        turned[16 * place : 16 * place + count, :shard_width] = vectors[...]
    values = jnp.transpose(turned[...])
    lane = lax.broadcasted_iota(jnp.int32, values.shape, 1)
    first = values.astype(LOW).astype(F32)
    second = (values - first).astype(LOW).astype(F32)
    third = values - first - second
    values = jnp.where(lane < 16, first, jnp.where(lane < 32, second, third))[:shard_width]
    blank = jnp.zeros_like(values)
    values = jnp.concatenate(
        [flip(rank_ref[0], values, blank), flip(rank_ref[0], blank, values)], axis=0
    )
    target[:, :columns] = w_qkv[0].astype(LOW)
    target[:, columns : 2 * columns] = w_qkv[1].astype(LOW)
    target[:, 2 * columns : a_width] = values.astype(LOW)
    target[:, a_width : a_width + columns] = w_qkv[2].astype(LOW)
    target[:, a_width + columns :] = w_out[...].astype(LOW)


def cast_kernel(first, second, target):
    columns = first.shape[1]
    target[:, :columns] = first[...].astype(LOW)
    target[:, columns:] = second[...].astype(LOW)


def project_kernel(rows, a_own, a_far, b_own, b_far, bias_q, bias_v, q, k, v):
    half = a_own.shape[0]
    own_rows, width = q.shape
    part = width // 2
    low, high = rows[:, :half], rows[:, half:]
    a_half, b_half = a_own.shape[1] // 2, b_own.shape[1] // 2
    for side in range(2):
        cols = slice(side * part, (side + 1) * part)
        at = slice(side * a_half, side * a_half + part)
        q[:, cols] = (
            dot(low[:own_rows], a_own[:, at]) + dot(high[:own_rows], a_far[:, at]) + bias_q[:, cols]
        ).astype(LOW)
        at = slice(side * a_half + part, side * a_half + 2 * part)
        k[:, cols] = (dot(low, a_own[:, at]) + dot(high, a_far[:, at])).astype(LOW)
        at = slice(side * b_half, side * b_half + part)
        v[:, cols] = (dot(low, b_own[:, at]) + dot(high, b_far[:, at]) + bias_v[:, cols]).astype(
            LOW
        )


def segment(lengths, positions):
    end, total = 0, jnp.zeros_like(positions)
    for place in range(lengths.shape[1]):
        end = end + lengths[0, place]
        total = total + (positions >= end).astype(jnp.int32)
    return total


def same_segment(rank, lengths, keys, queries):
    own = lax.broadcasted_iota(jnp.int32, (1, queries), 1) + rank * queries
    rows = lax.broadcasted_iota(jnp.int32, (keys, 1), 0)
    rows = jnp.where(rows < queries, rows + rank * queries, rows - rank * queries)
    return segment(lengths, rows) == segment(lengths, own)


def softmax_down(same, key_rows, queries):
    scores = dot_nt(key_rows, queries) * 0.125
    scores = jnp.where(same, scores, NEG_FILL)
    exp_scores = jnp.exp(scores - jnp.max(scores, axis=0, keepdims=True))
    return exp_scores * (1.0 / jnp.sum(exp_scores, axis=0, keepdims=True))


def two_heads(out):
    joined = jnp.concatenate([out[0][:HEAD_DIM], out[1][HEAD_DIM:]], axis=0)
    return jnp.transpose(joined).astype(LOW)


def attend_kernel(rank_ref, lengths, q, k, v, attended):
    queries, key_rows, value_rows = q[...], k[...], v[...]
    same = same_segment(rank_ref[0], lengths, k.shape[0], q.shape[0])
    first = lax.broadcasted_iota(jnp.int32, queries.shape, 1) < HEAD_DIM
    out = []
    for mine in (first, jnp.logical_not(first)):
        prob = softmax_down(same, key_rows, jnp.where(mine, queries, jnp.zeros_like(queries)))
        out.append(dot_tn(value_rows, prob.astype(LOW)))
    attended[...] = two_heads(out)


def attend_back_kernel(rank_ref, lengths, q, k, v, grad, grad_q, grad_k, grad_v):
    queries, key_rows, value_rows, grad_rows = q[...], k[...], v[...], grad[...]
    same = same_segment(rank_ref[0], lengths, k.shape[0], q.shape[0])
    first = lax.broadcasted_iota(jnp.int32, queries.shape, 1) < HEAD_DIM
    first_all = lax.broadcasted_iota(jnp.int32, key_rows.shape, 1) < HEAD_DIM
    blank = jnp.zeros_like(queries)
    out_q, out_k, out_v = [], [], []
    for mine in (first, jnp.logical_not(first)):
        prob = softmax_down(same, key_rows, jnp.where(mine, queries, blank))
        grad_prob = dot_nt(value_rows, jnp.where(mine, grad_rows, blank))
        delta = jnp.sum(grad_prob * prob, axis=0, keepdims=True)
        grad_score = (prob * (grad_prob - delta)).astype(LOW)
        out_q.append(dot_tn(key_rows, grad_score) * 0.125)
        out_k.append(dot(grad_score, queries) * 0.125)
        out_v.append(dot(prob.astype(LOW), grad_rows))
    grad_q[...] = two_heads(out_q)
    grad_k[...] = jnp.where(first_all, out_k[0], out_k[1]).astype(LOW)
    grad_v[...] = jnp.where(first_all, out_v[0], out_v[1]).astype(LOW)


def out_norm_kernel(attended, rows, b_own, b_far, vec, y, y_low, normed, inv):
    half = b_own.shape[0]
    own_rows, width = y.shape
    part = width // 2
    b_half = b_own.shape[1] // 2
    near, far = attended[:, :part], attended[:, part:]
    out = []
    for weights in (b_own, b_far):
        out.append(
            dot_nt(near, weights[:, part : 2 * part])
            + dot_nt(far, weights[:, b_half + part : b_half + 2 * part])
        )
    total = rows[:own_rows, :].astype(F32) + jnp.concatenate(out, axis=1) + vec[0:1]
    y_new, normed[...], inv[...] = normalize_fwd(total, vec[1:2], vec[2:3])
    y[...] = y_new
    y_low[...] = y_new.astype(LOW)


def stacked(pieces, at=slice(None)):
    return jnp.concatenate([piece[:, at] for piece in pieces], axis=0)


def hidden_kernel(y_low, *refs):
    pieces, (bias, activation, slope) = refs[:4], refs[4:]
    rows = y_low[...]
    columns = pieces[0].shape[1]
    step = columns // 8

    @pl.loop(0, 8)
    def _(place):
        at = pl.ds(pl.multiple_of(place * step, LANES), step)
        pre = dot(rows, stacked(pieces, at)) + bias[:, at]
        cdf = 0.5 + 0.5 * lax.erf(pre * (0.5**0.5))
        activation[:, at] = (pre * cdf).astype(LOW)
        slope[:, at] = cdf + pre * jnp.exp(-0.5 * pre * pre) * ((2.0 * np.pi) ** -0.5)


def out_back_kernel(
    rank_ref, lengths, activation, own, own_side, far, far_side, y, cot, vec,
    mixed, grad, grad_low, sums,
):
    columns = own.shape[1]
    near, side = activation[:, :columns], activation[:, columns:]
    out = [
        dot_nt(near, first[...]) + dot_nt(side, second[...])
        for first, second in ((own, own_side), (far, far_side))
    ]
    total = y[...] + jnp.concatenate(out, axis=1) + vec[3:4]
    result, normed, inv_std = normalize_fwd(total, vec[4:5], vec[5:6])
    mixed[...] = result.astype(LOW)
    rows = lax.broadcasted_iota(jnp.int32, (y.shape[0], 1), 0) + rank_ref[0] * y.shape[0]
    valid = (segment(lengths, rows) < lengths.shape[1]).astype(F32)
    grad_in, gain_sum, shift_sum = normalize_back(cot[...] * valid, normed, inv_std, vec[4:5])
    grad[...] = grad_in
    grad_low[...] = grad_in.astype(LOW)
    sums[0:1] = jnp.sum(grad_in, axis=0, keepdims=True)
    sums[1:2] = gain_sum[None]
    sums[2:3] = shift_sum[None]


def hidden_back_kernel(grad_low, own, own_side, far, far_side, slope, grad_pre, sums):
    rows = grad_low[...]
    columns = own.shape[1]
    step = columns // 4
    for side, pieces in enumerate(((own, far), (own_side, far_side))):

        @pl.loop(0, 4)
        def _(place, side=side, pieces=pieces):
            to = pl.ds(pl.multiple_of(side * columns + place * step, LANES), step)
            at = pl.ds(pl.multiple_of(place * step, LANES), step)
            grad_act = dot(rows, stacked(pieces, at))
            value = (grad_act * slope[:, to]).astype(LOW)
            grad_pre[:, to] = value
            sums[:, to] = jnp.sum(value.astype(F32), axis=0, keepdims=True)


def norm_back_kernel(
    grad_pre, own, own_side, far, far_side, grad_two, normed, inv, vec, o_own, o_far,
    grad, grad_low, grad_attn, sums,
):
    out = [
        dot_nt(grad_pre[...], stacked(pieces)) for pieces in ((own, own_side), (far, far_side))
    ]
    grad_in, gain_sum, shift_sum = normalize_back(
        grad_two[...] + jnp.concatenate(out, axis=1), normed[...], inv[...], vec[1:2]
    )
    grad[...] = grad_in
    low = grad_in.astype(LOW)
    grad_low[...] = low
    sums[0:1] = jnp.sum(grad_in, axis=0, keepdims=True)
    sums[1:2] = gain_sum[None]
    sums[2:3] = shift_sum[None]
    half = o_own.shape[0]
    part = grad.shape[1] // 2
    o_half = o_own.shape[1] // 2
    for side in range(2):
        at = slice(side * o_half + part, side * o_half + 2 * part)
        grad_attn[:, side * part : (side + 1) * part] = (
            dot(low[:, :half], o_own[:, at]) + dot(low[:, half:], o_far[:, at])
        ).astype(LOW)


def rows_back_kernel(grad_q, grad_k, grad_v, a_own, a_far, b_own, b_far, grad_one, own, away):
    own_rows, width = own.shape
    part = width // 2
    a_half, b_half = a_own.shape[1] // 2, b_own.shape[1] // 2
    half = a_own.shape[0]
    for place, (wa, wb) in enumerate(((a_own, b_own), (a_far, b_far))):
        to = slice(place * half, (place + 1) * half)
        both = jnp.zeros((2 * own_rows, half), F32)
        mine = grad_one[:, to]
        for side in range(2):
            cols = slice(side * part, (side + 1) * part)
            at = side * a_half
            mine = mine + dot_nt(grad_q[:, cols], wa[:, at : at + part])
            both = both + dot_nt(grad_k[:, cols], wa[:, at + part : at + 2 * part])
            at = side * b_half
            both = both + dot_nt(grad_v[:, cols], wb[:, at : at + part])
        own[:, to] = mine + both[:own_rows]
        away[:, to] = both[own_rows:].astype(LOW)


def rows_out_kernel(own, away, permute, out):
    rest = own[...] + away[...].astype(F32)
    total = None
    for _ in range(3):
        part = rest.astype(LOW)
        rest = rest - part.astype(F32)
        moved = dot_nt(part, permute[...])
        total = moved if total is None else total + moved
    out[...] = total


def first_grads_kernel(
    a_half, rank_ref, permute, rows, grad_q, grad_k, grad_v, grad_low, attended,
    sums_one, sums_two, sums_inner, a_send, b_send, a_keep, b_keep, natural, relative,
):
    half = a_keep.shape[0]
    own_rows, width = grad_q.shape
    part = width // 2
    extra = vector_lanes(
        rank_ref[0], permute, grad_q, grad_v, sums_one, sums_two, sums_inner, natural, relative
    )
    for place, to, to_b in ((1, a_send, b_send), (0, a_keep, b_keep)):
        at = slice(place * half, (place + 1) * half)
        both = rows[:, at]
        mine = rows[:own_rows, at]
        low = grad_low[:, at]
        for side in range(2):
            cols = slice(side * part, (side + 1) * part)
            base = side * a_half
            to[:, base : base + part] = dot_tn(mine, grad_q[:, cols]).astype(LOW)
            to[:, base + part : base + 2 * part] = dot_tn(both, grad_k[:, cols]).astype(LOW)
            to[:, base + 2 * part : base + a_half] = extra[at, :]
            base = side * 2 * part
            to_b[:, base : base + part] = dot_tn(both, grad_v[:, cols]).astype(LOW)
            to_b[:, base + part : base + 2 * part] = dot_tn(low, attended[:, cols]).astype(LOW)


def close_kernel(rates, rank_ref, *refs):
    inputs, parts = refs[:9], refs[9:-10]
    outs, turned = refs[-10:-1], refs[-1]
    total = parts[0][...].astype(F32)
    for part in parts[1:]:
        total = total + part[...].astype(F32)
    columns = outs[3].shape[1]
    count, shard_width = outs[6].shape
    a_width = 2 * columns + LANES
    for place, start in enumerate((0, columns, a_width)):
        values = adamw(
            *[ref[place] for ref in inputs[:3]],
            total[:, start : start + columns],
            rates[0],
            WEIGHT_DECAY,
        )
        for out, value in zip(outs[:3], values):
            out[place] = value
    values = adamw(
        *[ref[...] for ref in inputs[3:6]],
        total[:, a_width + columns :],
        rates[1],
        WEIGHT_DECAY,
    )
    for out, value in zip(outs[3:6], values):
        out[...] = value
    lanes = total[:, 2 * columns : a_width]
    turned[...] = jnp.zeros_like(turned)
    turned[:shard_width, :] = flip(
        rank_ref[0], lanes[:shard_width], lanes[shard_width : 2 * shard_width]
    )
    gradient = jnp.transpose(turned[...])[:count, :shard_width]
    values = adamw(*[ref[...] for ref in inputs[6:]], gradient, 0.1, 0.0)
    for out, value in zip(outs[6:], values):
        out[...] = value


def on_device(
    tokens,
    cotangent,
    lengths,
    w_qkv,
    m_qkv,
    v_qkv,
    w_out,
    m_out,
    v_out,
    w_in,
    m_in,
    v_in,
    w_back,
    m_back,
    v_back,
    vectors,
    m_vectors,
    v_vectors,
):
    own_rows, width = tokens.shape
    tensor_rank = lax.axis_index("tensor")
    group_rows = 2 * own_rows
    shard_rows = w_qkv.shape[1]
    part = w_qkv.shape[2]
    hidden_half = w_in.shape[1]
    full_inner = 2 * hidden_half
    half = width // 2
    count = vectors.shape[0]
    shard_width = vectors.shape[1]

    a_width = 2 * part + LANES
    rank = tensor_rank.astype(jnp.int32).reshape(1)
    scalar = pl.BlockSpec(memory_space=pltpu.SMEM)
    vmem = pl.BlockSpec(memory_space=pltpu.VMEM)
    shard_one = run(
        pack_kernel,
        [shape_of(shard_rows, a_width + 2 * part, LOW)],
        [rank, w_qkv, w_out.T, vectors],
        0,
        in_specs=[scalar] + [vmem] * 3,
        scratch=[pltpu.VMEM((LANES, LANES), F32)],
    )[0]

    tokens_far = swap_tensor(tokens)
    one_high = gather_high(shard_one)
    one = join_high(one_high, a_width)
    one_far = swap_tensor(one[0]), swap_dp(one[1], 2)
    shard_pair = run(
        cast_kernel,
        [shape_of(shard_rows, full_inner, LOW)],
        [w_in, w_back.T],
        0,
        after=one[:1],
    )[0]
    pair_high = gather_high(shard_pair)

    order = relative_order(width)
    permute = (jnp.arange(width, dtype=jnp.int32)[:, None] == order[None, :]).astype(LOW)
    rows_all = jnp.concatenate([dot(tokens, permute), dot(tokens_far, permute)]).astype(LOW)
    cot = dot(cotangent, permute)

    one = join_plane(*one, *one_far, after=[rows_all])
    one_far = swap_dp(one[0], 2), swap_tensor(one[1])
    unit = 2 * own_rows * width * width
    pair = join_high(pair_high, hidden_half, 400 * unit)
    one = join_plane(one[1], one[0], one_far[1], one_far[0], after=pair[:1])[::-1]
    a_own, b_own = one
    a_far, b_far = swap_dp(a_own, 1), swap_dp(b_own, 1)
    pair_far = swap_tensor(pair[0]), swap_dp(pair[1], 2)

    vec, bias_query, bias_value, bias_inner = run(
        vectors_kernel,
        [
            shape_of(6, width, F32),
            shape_of(1, width, F32),
            shape_of(1, width, F32),
            shape_of(1, full_inner, F32),
        ],
        [rank, permute, a_own, a_far],
        1,
        in_specs=[scalar, vmem, vmem, vmem],
    )

    wide_low = shape_of(own_rows, width, LOW)
    wide = shape_of(own_rows, width, F32)
    group_low = shape_of(group_rows, width, LOW)
    sums_shape = shape_of(8, width, F32)
    queries, key_rows, value_rows = run(
        project_kernel,
        [wide_low, group_low, group_low],
        [rows_all, a_own, a_far, b_own, b_far, bias_query, bias_value],
        5 * unit,
    )
    pair = join_plane(*pair, *pair_far, after=[queries])
    in_near, in_side = pair[0], swap_dp(pair[0], 2)
    back_near, back_side = pair[1], swap_tensor(pair[1])
    in_far, back_far = swap_dp(in_near, 1), swap_dp(back_near, 1)
    pairs = width // LANES
    own_block = pl.BlockSpec((own_rows, LANES), lambda i: (0, i))
    all_block = pl.BlockSpec((group_rows, LANES), lambda i: (0, i))

    attended = run(
        attend_kernel,
        [wide_low],
        [rank, lengths, queries, key_rows, value_rows],
        3 * unit,
        after=pair[:1],
        grid=(pairs,),
        in_specs=[scalar, scalar, own_block, all_block, all_block],
        out_specs=[own_block],
    )[0]
    first_norm, first_low, normed_one, inv_one = run(
        out_norm_kernel,
        [wide, wide_low, wide, shape_of(own_rows, 1, F32)],
        [attended, rows_all, b_own, b_far, vec],
        2 * unit,
        after=[in_far, back_far],
    )
    in_side, back_side = gate([in_side, back_side], [first_low])
    pieces_in = [in_near, in_side, in_far, swap_dp(in_side, 1)]
    pieces_back = [back_near, back_side, back_far, swap_dp(back_side, 1)]
    activation, slope = run(
        hidden_kernel,
        [shape_of(own_rows, full_inner, LOW), shape_of(own_rows, full_inner, F32)],
        [first_low, *pieces_in, bias_inner],
        8 * unit,
    )
    mixed_rel, grad_two, grad_two_low, sums_two = run(
        out_back_kernel,
        [wide_low, wide, wide_low, sums_shape],
        [rank, lengths, activation, *pieces_back, first_norm, cot, vec],
        5 * unit,
        in_specs=[scalar, scalar] + [vmem] * 8,
    )
    mixed = dot_nt(mixed_rel, permute).astype(LOW)

    def gradient(left, right):
        return dot_tn(left, right).astype(LOW)

    back_parts = []
    for columns in (activation[:, hidden_half:], activation[:, :hidden_half]):
        sent = swap_dp(gradient(grad_two_low[:, half:], columns), 1)
        back_parts.append((gradient(grad_two_low[:, :half], columns), sent))
    grad_pre, sums_inner = run(
        hidden_back_kernel,
        [shape_of(own_rows, full_inner, LOW), shape_of(1, full_inner, F32)],
        [grad_two_low, *pieces_back, slope],
        6 * unit,
    )
    quarter = half // 2
    in_parts = []
    for start in (quarter, 0):
        rows = slice(half + start, half + start + quarter)
        sent = swap_dp(gradient(first_low[:, rows], grad_pre), 1)
        in_parts.append((gradient(first_low[:, start : start + quarter], grad_pre), sent))
    b_send = add_parts(*back_parts[0], 400 * unit, after=[grad_pre])
    a_send = add_parts(*in_parts[0], after=[b_send])
    a_far_sum, b_far_sum = swap_dp(a_send, 2), swap_tensor(b_send)
    grad_one, grad_one_low, grad_attn, sums_one = run(
        norm_back_kernel,
        [wide, wide_low, wide_low, sums_shape],
        [grad_pre, *pieces_in, grad_two, normed_one, inv_one, vec, b_own, b_far],
        6 * unit,
        after=[a_send],
    )
    b_keep = add_parts(*back_parts[1], after=[grad_one_low])
    a_keep = add_parts(*in_parts[1], after=[b_keep])
    pair = a_keep, a_far_sum, b_keep, b_far_sum
    grad_q, grad_k, grad_v = run(
        attend_back_kernel,
        [wide_low, group_low, group_low],
        [rank, lengths, queries, key_rows, value_rows, grad_attn],
        5 * unit,
        grid=(pairs,),
        in_specs=[scalar, scalar, own_block, all_block, all_block, own_block],
        out_specs=[own_block, all_block, all_block],
    )
    a_shape, b_shape = shape_of(half, 2 * a_width, LOW), shape_of(half, 4 * part, LOW)
    a_send, b_send, one_a, one_b = run(
        functools.partial(first_grads_kernel, a_width),
        [a_shape, b_shape, a_shape, b_shape],
        [rank, permute, rows_all, grad_q, grad_k, grad_v, grad_one_low, attended]
        + [sums_one, sums_two, sums_inner],
        6 * unit,
        in_specs=[scalar] + [vmem] * 10,
        scratch=[pltpu.VMEM((16, width), F32), pltpu.VMEM((LANES, width), F32)],
    )
    one = one_a, swap_dp(a_send, 1), one_b, swap_dp(b_send, 1)
    a_keep, a_send, b_keep, b_send = split_plane(*pair, after=[one_a, mixed])
    pair = a_keep, swap_tensor(a_send), b_keep, swap_dp(b_send, 2)
    grad_own, grad_away = run(
        rows_back_kernel,
        [wide, wide_low],
        [grad_q, grad_k, grad_v, a_own, a_far, b_own, b_far, grad_one],
        400 * unit,
        after=[a_keep],
    )
    a_keep, a_send, b_keep, b_send = split_core(*one, after=[grad_own])
    one = a_keep, swap_dp(a_send, 2), b_keep, swap_tensor(b_send)
    pair = send_high(split_high(*pair, after=[a_keep]))
    a_keep, a_send, b_keep, b_send = split_plane(*one, after=pair[:1])
    one = a_keep, swap_tensor(a_send), b_keep, swap_dp(b_send, 2)
    pair = sum_parts(pair, 400 * unit, after=[a_keep])
    one = send_high(split_high(*one, after=pair))
    input_grad = run(
        rows_out_kernel,
        [wide],
        [grad_own, swap_tensor(gate([grad_away], pair)[0]), permute],
        3 * unit,
        after=one[:1],
    )[0]
    sum_pair = reduce_rest(gate(pair, one[:1])[0])
    summed_in, summed_back = sum_pair[:, :hidden_half], sum_pair[:, hidden_half:].T
    if len(high_groups()) > 1:
        one = [reduce_rest(sum(piece.astype(F32) for piece in one))]
    qkv_shape = jax.ShapeDtypeStruct(w_qkv.shape, F32)
    out_shape = shape_of(shard_rows, part, F32)
    vec_shape = shape_of(count, shard_width, F32)
    done = run(
        functools.partial(
            close_kernel,
            (float(width) ** (-0.5), (4.0 * width / group_rows) ** (-0.5)),
        ),
        [qkv_shape] * 3 + [out_shape] * 3 + [vec_shape] * 3,
        [rank, w_qkv, m_qkv, v_qkv, w_out.T, m_out.T, v_out.T]
        + [vectors, m_vectors, v_vectors, *one],
        unit,
        after=[input_grad],
        in_specs=[scalar] + [vmem] * (9 + len(one)),
        scratch=[pltpu.VMEM((LANES, LANES), F32)],
    )
    new_qkv, moment_qkv, square_qkv = done[:3]
    new_out, moment_out, square_out = [value.T for value in done[3:6]]
    new_vectors, moment_vectors, square_vectors = done[6:]
    new_in, moment_in, square_in = adamw(
        w_in, m_in, v_in, summed_in, float(width) ** (-0.5), WEIGHT_DECAY
    )
    new_back, moment_back, square_back = adamw(
        w_back, m_back, v_back, summed_back, float(full_inner) ** (-0.5), WEIGHT_DECAY
    )
    return (
        mixed,
        input_grad,
        new_qkv,
        moment_qkv,
        square_qkv,
        new_out,
        moment_out,
        square_out,
        new_in,
        moment_in,
        square_in,
        new_back,
        moment_back,
        square_back,
        new_vectors,
        moment_vectors,
        square_vectors,
    )


def solution(mesh):
    placed = (
        P(("dp", "tensor"), None),
        P(("dp", "tensor"), None),
        P("dp", None),
        P(None, "dp", "tensor"),
        P(None, "dp", "tensor"),
        P(None, "dp", "tensor"),
        P("tensor", "dp"),
        P("tensor", "dp"),
        P("tensor", "dp"),
        P("dp", "tensor"),
        P("dp", "tensor"),
        P("dp", "tensor"),
        P("tensor", "dp"),
        P("tensor", "dp"),
        P("tensor", "dp"),
        P(None, ("dp", "tensor")),
        P(None, ("dp", "tensor")),
        P(None, ("dp", "tensor")),
    )
    return jax.shard_map(
        on_device,
        mesh=mesh,
        in_specs=placed,
        out_specs=(
            P(("dp", "tensor"), None),
            P(("dp", "tensor"), None),
            P(None, "dp", "tensor"),
            P(None, "dp", "tensor"),
            P(None, "dp", "tensor"),
            P("tensor", "dp"),
            P("tensor", "dp"),
            P("tensor", "dp"),
            P("dp", "tensor"),
            P("dp", "tensor"),
            P("dp", "tensor"),
            P("tensor", "dp"),
            P("tensor", "dp"),
            P("tensor", "dp"),
            P(None, ("dp", "tensor")),
            P(None, ("dp", "tensor")),
            P(None, ("dp", "tensor")),
        ),
        check_vma=False,
    )
```

```python
import functools

import numpy as np

import jax
import jax.numpy as jnp
from jax import lax
from jax.experimental import pallas as pl
from jax.experimental.pallas import tpu as pltpu
from jax.sharding import PartitionSpec as P

HEAD_DIM = 64
LANES = 128
STEP = 10


EPS_NORM = 1e-05
BETA_ONE = 0.9
BETA_TWO = 0.999
EPS_ADAM = 1e-08
WEIGHT_DECAY = 0.01
NEG_FILL = -1000000000.0
LOW = jnp.bfloat16
F32 = jnp.float32


def normalize_fwd(values, gain_row, shift_row):
    row_mean = jnp.mean(values, axis=-1, keepdims=True)
    centered = values - row_mean
    variance = jnp.mean(centered * centered, axis=-1, keepdims=True)
    inv_std = lax.rsqrt(variance + EPS_NORM)
    normed = centered * inv_std
    return (normed * gain_row + shift_row, normed, inv_std)


def normalize_back(gradient, normed, inv_std, gain_row):
    grad_norm = gradient * gain_row
    grad_in = inv_std * (
        grad_norm
        - jnp.mean(grad_norm, axis=-1, keepdims=True)
        - normed * jnp.mean(grad_norm * normed, axis=-1, keepdims=True)
    )
    return (grad_in, jnp.sum(gradient * normed, axis=0), jnp.sum(gradient, axis=0))


def adamw(weight, moment, square, gradient, step_rate, decay_rate):
    moment = BETA_ONE * moment + (1.0 - BETA_ONE) * gradient
    square = BETA_TWO * square + (1.0 - BETA_TWO) * gradient * gradient
    direction = (
        moment / (1.0 - BETA_ONE**STEP) / (jnp.sqrt(square / (1.0 - BETA_TWO**STEP)) + EPS_ADAM)
    )
    return (weight - step_rate * (direction + decay_rate * weight), moment, square)


def swap_dp(values, mask):
    size = lax.axis_size("dp")
    return lax.ppermute(values, "dp", [(i, i ^ mask) for i in range(size)])


def swap_tensor(values):
    return lax.ppermute(values, "tensor", [(0, 1), (1, 0)])


def high_bits():
    return list(range(2, lax.axis_size("dp").bit_length() - 1))


def high_groups():
    bits = high_bits()
    return [[1 << bit for bit in bits[i : i + 2]] for i in range(0, len(bits), 2)]


def group_masks(group):
    return [0] + group + ([group[0] ^ group[1]] if len(group) == 2 else [])


def gather_high(shard):
    groups = high_groups()
    for place, group in enumerate(groups):
        pieces = [shard if mask == 0 else swap_dp(shard, mask) for mask in group_masks(group)]
        if place < len(groups) - 1:
            shard = jnp.concatenate(pieces, axis=0)
    return pieces


def send_high(parts):
    masks = group_masks(high_groups()[-1])
    return [parts[0]] + [swap_dp(part, mask) for part, mask in zip(parts[1:], masks[1:])]


def reduce_rest(total):
    for group in reversed(high_groups()[:-1]):
        masks = group_masks(group)
        rows = total.shape[0] // len(masks)
        low = total.astype(LOW)
        total = total[:rows]
        for place, mask in enumerate(masks[1:], 1):
            total = total + swap_dp(low[place * rows : (place + 1) * rows], mask).astype(F32)
    return total


def relative_order(width):
    size = lax.axis_size("dp")
    rows = width // size
    inner_first = high_bits() + [1, 0]
    masks = np.zeros((size,), np.int32)
    for block in range(size):
        for place, bit in enumerate(inner_first):
            if (block >> place) & 1:
                masks[block] |= 1 << bit
    block_mask = jnp.asarray(np.repeat(masks, rows))
    offsets = jnp.asarray(np.tile(np.arange(rows, dtype=np.int32), size))
    return (lax.axis_index("dp") ^ block_mask) * rows + offsets


def dot(left, right):
    return jnp.dot(left, right, preferred_element_type=F32)


def dot_nt(left, right):
    return lax.dot_general(left, right, (((1,), (1,)), ((), ())), preferred_element_type=F32)


def dot_tn(left, right):
    return lax.dot_general(left, right, (((0,), (0,)), ((), ())), preferred_element_type=F32)


def shape_of(rows, columns, kind):
    return jax.ShapeDtypeStruct((rows, columns), kind)


def run(kernel, outs, operands, flops, after=(), grid=(), in_specs=None, out_specs=None, scratch=()):
    count = len(operands)

    def body(*refs):
        kernel(*refs[:count], *refs[count + len(after) :])

    whole = pl.BlockSpec(memory_space=pltpu.VMEM)
    in_specs = in_specs or [whole] * count
    size = sum(v.size * v.dtype.itemsize for v in list(operands) + list(outs))
    grant = 10 << 20 if grid else size + ((8 if flops else 2) << 20)
    return pl.pallas_call(
        body,
        grid=grid,
        out_shape=list(outs),
        in_specs=list(in_specs) + [pl.BlockSpec(memory_space=pl.ANY)] * len(after),
        out_specs=list(out_specs or [whole] * len(outs)),
        scratch_shapes=list(scratch),
        compiler_params=pltpu.CompilerParams(vmem_limit_bytes=grant),
        cost_estimate=pl.CostEstimate(flops=flops, bytes_accessed=size, transcendentals=0),
    )(*operands, *after)


def gate(values, after):
    anywhere = pl.BlockSpec(memory_space=pl.ANY)
    return pl.pallas_call(
        lambda *refs: None,
        out_shape=[shape_of(*value.shape, value.dtype) for value in values],
        in_specs=[anywhere] * (len(values) + len(after)),
        out_specs=[anywhere] * len(values),
        input_output_aliases={place: place for place in range(len(values))},
        compiler_params=pltpu.CompilerParams(vmem_limit_bytes=1 << 20),
        cost_estimate=pl.CostEstimate(flops=0, bytes_accessed=0, transcendentals=0),
    )(*values, *after)


def join_high_kernel(count, *refs):
    pieces, (first, second) = refs[:count], refs[count:]
    cut = first.shape[1]
    rows = pieces[0].shape[0]
    for place, piece in enumerate(pieces):
        to = slice(place * rows, (place + 1) * rows)
        first[to, :] = piece[:, :cut]
        second[to, :] = piece[:, cut:]


def join_high(pieces, cut, flops=0, after=()):
    rows, columns = pieces[0].shape
    rows = rows * len(pieces)
    return run(
        functools.partial(join_high_kernel, len(pieces)),
        [shape_of(rows, cut, LOW), shape_of(rows, columns - cut, LOW)],
        pieces,
        flops,
        after,
    )


def join_plane_kernel(across, down, across_far, down_far, across_all, down_all):
    columns, rows = across.shape[1], down.shape[0]
    across_all[:, :columns] = across[...]
    across_all[:, columns:] = across_far[...]
    down_all[:rows, :] = down[...]
    down_all[rows:, :] = down_far[...]


def join_plane(across, down, across_far, down_far, after=()):
    return run(
        join_plane_kernel,
        [
            shape_of(across.shape[0], 2 * across.shape[1], LOW),
            shape_of(2 * down.shape[0], down.shape[1], LOW),
        ],
        [across, down, across_far, down_far],
        0,
        after,
    )


def added(left, right, rows, columns):
    return (left[rows, columns].astype(F32) + right[rows, columns].astype(F32)).astype(LOW)


def add_kernel(array, far, total):
    total[...] = added(array, far, slice(None), slice(None))


def add_parts(array, far, flops=0, after=()):
    return run(add_kernel, [shape_of(*array.shape, LOW)], [array, far], flops, after)[0]


def split_rows_kernel(array, far, keep, send):
    rows = keep.shape[0]
    keep[...] = added(array, far, slice(0, rows), slice(None))
    send[...] = added(array, far, slice(rows, 2 * rows), slice(None))


def split_columns_kernel(array, far, keep, send):
    columns = keep.shape[1]
    keep[...] = added(array, far, slice(None), slice(0, columns))
    send[...] = added(array, far, slice(None), slice(columns, 2 * columns))


def split_core_kernel(a, a_far, b, b_far, a_keep, a_send, b_keep, b_send):
    split_rows_kernel(a, a_far, a_keep, a_send)
    split_columns_kernel(b, b_far, b_keep, b_send)


def split_core(a, a_far, b, b_far, after=()):
    a_shape = shape_of(a.shape[0] // 2, a.shape[1], LOW)
    b_shape = shape_of(b.shape[0], b.shape[1] // 2, LOW)
    return run(
        split_core_kernel, [a_shape, a_shape, b_shape, b_shape], [a, a_far, b, b_far], 0, after
    )


def sum_kernel(*refs):
    total = refs[0][...].astype(F32)
    for ref in refs[1:-1]:
        total = total + ref[...].astype(F32)
    refs[-1][...] = total


def sum_parts(parts, flops, after=()):
    return run(sum_kernel, [shape_of(*parts[0].shape, F32)], parts, flops, after)


def split_plane_kernel(a, a_far, b, b_far, a_keep, a_send, b_keep, b_send):
    half, rows = a_keep.shape[1], b_keep.shape[0]
    every = slice(None)
    a_keep[...] = added(a, a_far, every, slice(0, half))
    a_send[...] = added(a, a_far, every, slice(half, 2 * half))
    b_keep[...] = added(b, b_far, slice(0, rows), every)
    b_send[...] = added(b, b_far, slice(rows, 2 * rows), every)


def split_plane(a, a_far, b, b_far, after=()):
    a_shape = shape_of(a.shape[0], a.shape[1] // 2, LOW)
    b_shape = shape_of(b.shape[0] // 2, b.shape[1], LOW)
    return run(
        split_plane_kernel, [a_shape, a_shape, b_shape, b_shape], [a, a_far, b, b_far], 0, after
    )


def split_high_kernel(a, a_far, b, b_far, *parts):
    cut = a.shape[1]
    rows = parts[0].shape[0]
    for place, part in enumerate(parts):
        at = slice(place * rows, (place + 1) * rows)
        part[:, :cut] = added(a, a_far, at, slice(None))
        part[:, cut:] = added(b, b_far, at, slice(None))


def split_high(a, a_far, b, b_far, after=()):
    count = len(group_masks(high_groups()[-1]))
    part = shape_of(a.shape[0] // count, a.shape[1] + b.shape[1], LOW)
    return run(split_high_kernel, [part] * count, [a, a_far, b, b_far], 0, after)


def flip(rank, first, second):
    return jnp.where(rank == 0, first, second)


def vectors_kernel(rank_ref, permute, a_own, a_far, relative, bias_q, bias_v, bias_inner):
    rank = rank_ref[0]
    side = a_own.shape[1] // 2
    width = relative.shape[1]
    half = width // 2
    spread = jnp.concatenate(
        [
            (ref[:, side - LANES : side].astype(F32) + ref[:, 2 * side - LANES :].astype(F32))
            for ref in (a_own, a_far)
        ],
        axis=0,
    )
    parts = jnp.transpose(spread)
    parts = [parts[16 * i : 16 * (i + 1)] for i in range(3)]
    relative[...] = ((parts[0] + parts[1]) + parts[2])[2:8]
    natural = [dot_nt(part.astype(LOW), permute[...]) for part in parts]
    natural = (natural[0] + natural[1]) + natural[2]
    for row, target in ((0, bias_q), (1, bias_v)):
        first, second = natural[row : row + 1, :half], natural[row : row + 1, half:]
        target[:, :half] = flip(rank, first, second)
        target[:, half:] = flip(rank, second, first)
    for place in range(2):
        for cut in range(2):
            near, far = 8 + 2 * place + cut, 8 + 2 * (1 - place) + cut
            at = (2 * place + cut) * width
            bias_inner[:, at : at + width] = flip(
                rank, natural[near : near + 1], natural[far : far + 1]
            )


def vector_lanes(rank, permute, grad_q, grad_v, sums_one, sums_two, sums_inner, natural, relative):
    width = natural.shape[1]
    half = width // 2
    natural[...] = jnp.zeros_like(natural)
    relative[...] = jnp.zeros_like(relative)
    for row, source in ((0, grad_q), (1, grad_v)):
        total = jnp.sum(source[...].astype(F32), axis=0, keepdims=True)
        first, second = total[:, :half], total[:, half:]
        natural[row : row + 1, :half] = flip(rank, first, second)
        natural[row : row + 1, half:] = flip(rank, second, first)
    for place in range(2):
        for cut in range(2):
            near, far = (2 * place + cut) * width, (2 * (1 - place) + cut) * width
            row = 8 + 2 * place + cut
            natural[row : row + 1, :] = flip(
                rank, sums_inner[:, near : near + width], sums_inner[:, far : far + width]
            )
    relative[:16, :] = dot(natural[...].astype(LOW), permute[...])
    relative[2:5, :] = sums_one[:3, :]
    relative[5:8, :] = sums_two[:3, :]
    return jnp.transpose(relative[...]).astype(LOW)


def pack_kernel(rank_ref, w_qkv, w_out, vectors, target, turned):
    columns = w_out.shape[1]
    count, shard_width = vectors.shape
    a_width = 2 * columns + LANES
    turned[...] = jnp.zeros_like(turned)
    for place in range(3):
        turned[16 * place : 16 * place + count, :shard_width] = vectors[...]
    values = jnp.transpose(turned[...])
    lane = lax.broadcasted_iota(jnp.int32, values.shape, 1)
    first = values.astype(LOW).astype(F32)
    second = (values - first).astype(LOW).astype(F32)
    third = values - first - second
    values = jnp.where(lane < 16, first, jnp.where(lane < 32, second, third))[:shard_width]
    blank = jnp.zeros_like(values)
    values = jnp.concatenate(
        [flip(rank_ref[0], values, blank), flip(rank_ref[0], blank, values)], axis=0
    )
    target[:, :columns] = w_qkv[0].astype(LOW)
    target[:, columns : 2 * columns] = w_qkv[1].astype(LOW)
    target[:, 2 * columns : a_width] = values.astype(LOW)
    target[:, a_width : a_width + columns] = w_qkv[2].astype(LOW)
    target[:, a_width + columns :] = w_out[...].astype(LOW)


def cast_kernel(first, second, target):
    columns = first.shape[1]
    target[:, :columns] = first[...].astype(LOW)
    target[:, columns:] = second[...].astype(LOW)


def project_kernel(rows, a_own, a_far, b_own, b_far, bias_q, bias_v, q, k, v):
    half = a_own.shape[0]
    own_rows, width = q.shape
    part = width // 2
    low, high = rows[:, :half], rows[:, half:]
    a_half, b_half = a_own.shape[1] // 2, b_own.shape[1] // 2

    def block(start):
        return pl.ds(pl.multiple_of(start, LANES), part)

    @pl.loop(0, 2)
    def _(side):
        cols = block(side * part)
        at = block(side * a_half)
        q[:, cols] = (
            dot(low[:own_rows], a_own[:, at]) + dot(high[:own_rows], a_far[:, at]) + bias_q[:, cols]
        ).astype(LOW)
        at = block(side * a_half + part)
        k[:, cols] = (dot(low, a_own[:, at]) + dot(high, a_far[:, at])).astype(LOW)
        at = block(side * b_half)
        v[:, cols] = (dot(low, b_own[:, at]) + dot(high, b_far[:, at]) + bias_v[:, cols]).astype(
            LOW
        )


def segment(lengths, positions):
    end, total = 0, jnp.zeros_like(positions)
    for place in range(lengths.shape[1]):
        end = end + lengths[0, place]
        total = total + (positions >= end).astype(jnp.int32)
    return total


def same_segment(rank, lengths, keys, queries):
    own = lax.broadcasted_iota(jnp.int32, (1, queries), 1) + rank * queries
    rows = lax.broadcasted_iota(jnp.int32, (keys, 1), 0)
    rows = jnp.where(rows < queries, rows + rank * queries, rows - rank * queries)
    return segment(lengths, rows) == segment(lengths, own)


def softmax_down(same, key_rows, queries):
    scores = dot_nt(key_rows, queries) * 0.125
    scores = jnp.where(same, scores, NEG_FILL)
    exp_scores = jnp.exp(scores - jnp.max(scores, axis=0, keepdims=True))
    return exp_scores * (1.0 / jnp.sum(exp_scores, axis=0, keepdims=True))


def two_heads(out):
    joined = jnp.concatenate([out[0][:HEAD_DIM], out[1][HEAD_DIM:]], axis=0)
    return jnp.transpose(joined).astype(LOW)


def attend_kernel(rank_ref, lengths, q, k, v, attended):
    queries, key_rows, value_rows = q[...], k[...], v[...]
    same = same_segment(rank_ref[0], lengths, k.shape[0], q.shape[0])
    first = lax.broadcasted_iota(jnp.int32, queries.shape, 1) < HEAD_DIM
    out = []
    for mine in (first, jnp.logical_not(first)):
        prob = softmax_down(same, key_rows, jnp.where(mine, queries, jnp.zeros_like(queries)))
        out.append(dot_tn(value_rows, prob.astype(LOW)))
    attended[...] = two_heads(out)


def attend_back_kernel(rank_ref, lengths, q, k, v, grad, grad_q, grad_k, grad_v):
    queries, key_rows, value_rows, grad_rows = q[...], k[...], v[...], grad[...]
    same = same_segment(rank_ref[0], lengths, k.shape[0], q.shape[0])
    first = lax.broadcasted_iota(jnp.int32, queries.shape, 1) < HEAD_DIM
    first_all = lax.broadcasted_iota(jnp.int32, key_rows.shape, 1) < HEAD_DIM
    blank = jnp.zeros_like(queries)
    out_q, out_k, out_v = [], [], []
    for mine in (first, jnp.logical_not(first)):
        prob = softmax_down(same, key_rows, jnp.where(mine, queries, blank))
        grad_prob = dot_nt(value_rows, jnp.where(mine, grad_rows, blank))
        delta = jnp.sum(grad_prob * prob, axis=0, keepdims=True)
        grad_score = (prob * (grad_prob - delta)).astype(LOW)
        out_q.append(dot_tn(key_rows, grad_score) * 0.125)
        out_k.append(dot(grad_score, queries) * 0.125)
        out_v.append(dot(prob.astype(LOW), grad_rows))
    grad_q[...] = two_heads(out_q)
    grad_k[...] = jnp.where(first_all, out_k[0], out_k[1]).astype(LOW)
    grad_v[...] = jnp.where(first_all, out_v[0], out_v[1]).astype(LOW)


def out_norm_kernel(attended, rows, b_own, b_far, vec, y, y_low, normed, inv):
    half = b_own.shape[0]
    own_rows, width = y.shape
    part = width // 2
    b_half = b_own.shape[1] // 2
    near, far = attended[:, :part], attended[:, part:]
    out = []
    for weights in (b_own, b_far):
        out.append(
            dot_nt(near, weights[:, part : 2 * part])
            + dot_nt(far, weights[:, b_half + part : b_half + 2 * part])
        )
    total = rows[:own_rows, :].astype(F32) + jnp.concatenate(out, axis=1) + vec[0:1]
    y_new, normed[...], inv[...] = normalize_fwd(total, vec[1:2], vec[2:3])
    y[...] = y_new
    y_low[...] = y_new.astype(LOW)


def stacked(pieces, at=slice(None)):
    return jnp.concatenate([piece[:, at] for piece in pieces], axis=0)


def hidden_kernel(y_low, *refs):
    pieces, (bias, activation, slope) = refs[:4], refs[4:]
    rows = y_low[...]
    columns = pieces[0].shape[1]
    step = columns // 8
    for start in range(0, columns, step):
        at = slice(start, start + step)
        pre = dot(rows, stacked(pieces, at)) + bias[:, at]
        cdf = 0.5 + 0.5 * lax.erf(pre * (0.5**0.5))
        activation[:, at] = (pre * cdf).astype(LOW)
        slope[:, at] = cdf + pre * jnp.exp(-0.5 * pre * pre) * ((2.0 * np.pi) ** -0.5)


def out_back_kernel(
    rank_ref, lengths, activation, own, own_side, far, far_side, y, cot, vec,
    mixed, grad, grad_low, sums,
):
    columns = own.shape[1]
    near, side = activation[:, :columns], activation[:, columns:]
    out = [
        dot_nt(near, first[...]) + dot_nt(side, second[...])
        for first, second in ((own, own_side), (far, far_side))
    ]
    total = y[...] + jnp.concatenate(out, axis=1) + vec[3:4]
    result, normed, inv_std = normalize_fwd(total, vec[4:5], vec[5:6])
    mixed[...] = result.astype(LOW)
    rows = lax.broadcasted_iota(jnp.int32, (y.shape[0], 1), 0) + rank_ref[0] * y.shape[0]
    valid = (segment(lengths, rows) < lengths.shape[1]).astype(F32)
    grad_in, gain_sum, shift_sum = normalize_back(cot[...] * valid, normed, inv_std, vec[4:5])
    grad[...] = grad_in
    grad_low[...] = grad_in.astype(LOW)
    sums[0:1] = jnp.sum(grad_in, axis=0, keepdims=True)
    sums[1:2] = gain_sum[None]
    sums[2:3] = shift_sum[None]


def hidden_back_kernel(grad_low, own, own_side, far, far_side, slope, grad_pre, sums):
    rows = grad_low[...]
    columns = own.shape[1]
    step = columns // 4
    for place, pieces in enumerate(((own, far), (own_side, far_side))):
        for start in range(0, columns, step):
            to = slice(place * columns + start, place * columns + start + step)
            grad_act = dot(rows, stacked(pieces, slice(start, start + step)))
            value = (grad_act * slope[:, to]).astype(LOW)
            grad_pre[:, to] = value
            sums[:, to] = jnp.sum(value.astype(F32), axis=0, keepdims=True)


def norm_back_kernel(
    grad_pre, own, own_side, far, far_side, grad_two, normed, inv, vec, o_own, o_far,
    grad, grad_low, grad_attn, sums,
):
    out = [
        dot_nt(grad_pre[...], stacked(pieces)) for pieces in ((own, own_side), (far, far_side))
    ]
    grad_in, gain_sum, shift_sum = normalize_back(
        grad_two[...] + jnp.concatenate(out, axis=1), normed[...], inv[...], vec[1:2]
    )
    grad[...] = grad_in
    low = grad_in.astype(LOW)
    grad_low[...] = low
    sums[0:1] = jnp.sum(grad_in, axis=0, keepdims=True)
    sums[1:2] = gain_sum[None]
    sums[2:3] = shift_sum[None]
    half = o_own.shape[0]
    part = grad.shape[1] // 2
    o_half = o_own.shape[1] // 2
    for side in range(2):
        at = slice(side * o_half + part, side * o_half + 2 * part)
        grad_attn[:, side * part : (side + 1) * part] = (
            dot(low[:, :half], o_own[:, at]) + dot(low[:, half:], o_far[:, at])
        ).astype(LOW)


def rows_back_kernel(grad_q, grad_k, grad_v, a_own, a_far, b_own, b_far, grad_one, own, away):
    own_rows, width = own.shape
    part = width // 2
    a_half, b_half = a_own.shape[1] // 2, b_own.shape[1] // 2
    half = a_own.shape[0]
    for place, (wa, wb) in enumerate(((a_own, b_own), (a_far, b_far))):
        to = slice(place * half, (place + 1) * half)
        both = jnp.zeros((2 * own_rows, half), F32)
        mine = grad_one[:, to]
        for side in range(2):
            cols = slice(side * part, (side + 1) * part)
            at = side * a_half
            mine = mine + dot_nt(grad_q[:, cols], wa[:, at : at + part])
            both = both + dot_nt(grad_k[:, cols], wa[:, at + part : at + 2 * part])
            at = side * b_half
            both = both + dot_nt(grad_v[:, cols], wb[:, at : at + part])
        own[:, to] = mine + both[:own_rows]
        away[:, to] = both[own_rows:].astype(LOW)


def rows_out_kernel(own, away, permute, out):
    rest = own[...] + away[...].astype(F32)
    total = None
    for _ in range(3):
        part = rest.astype(LOW)
        rest = rest - part.astype(F32)
        moved = dot_nt(part, permute[...])
        total = moved if total is None else total + moved
    out[...] = total


def first_grads_kernel(
    a_half, rank_ref, permute, rows, grad_q, grad_k, grad_v, grad_low, attended,
    sums_one, sums_two, sums_inner, a_send, b_send, a_keep, b_keep, natural, relative,
):
    half = a_keep.shape[0]
    own_rows, width = grad_q.shape
    part = width // 2
    extra = vector_lanes(
        rank_ref[0], permute, grad_q, grad_v, sums_one, sums_two, sums_inner, natural, relative
    )
    for place, to, to_b in ((1, a_send, b_send), (0, a_keep, b_keep)):
        at = slice(place * half, (place + 1) * half)
        both = rows[:, at]
        mine = rows[:own_rows, at]
        low = grad_low[:, at]
        lanes = extra[at, :]

        @pl.loop(0, 2)
        def _(side, to=to, to_b=to_b, both=both, mine=mine, low=low, lanes=lanes):
            def block(start, size=part):
                return pl.ds(pl.multiple_of(start, LANES), size)

            cols = block(side * part)
            base = side * a_half
            to[:, block(base)] = dot_tn(mine, grad_q[:, cols]).astype(LOW)
            to[:, block(base + part)] = dot_tn(both, grad_k[:, cols]).astype(LOW)
            to[:, block(base + 2 * part, LANES)] = lanes
            base = side * 2 * part
            to_b[:, block(base)] = dot_tn(both, grad_v[:, cols]).astype(LOW)
            to_b[:, block(base + part)] = dot_tn(low, attended[:, cols]).astype(LOW)


def close_kernel(rates, rank_ref, *refs):
    inputs, parts = refs[:9], refs[9:-10]
    outs, turned = refs[-10:-1], refs[-1]
    total = parts[0][...].astype(F32)
    for part in parts[1:]:
        total = total + part[...].astype(F32)
    columns = outs[3].shape[1]
    count, shard_width = outs[6].shape
    a_width = 2 * columns + LANES
    for place, start in enumerate((0, columns, a_width)):
        values = adamw(
            *[ref[place] for ref in inputs[:3]],
            total[:, start : start + columns],
            rates[0],
            WEIGHT_DECAY,
        )
        for out, value in zip(outs[:3], values):
            out[place] = value
    values = adamw(
        *[ref[...] for ref in inputs[3:6]],
        total[:, a_width + columns :],
        rates[1],
        WEIGHT_DECAY,
    )
    for out, value in zip(outs[3:6], values):
        out[...] = value
    lanes = total[:, 2 * columns : a_width]
    turned[...] = jnp.zeros_like(turned)
    turned[:shard_width, :] = flip(
        rank_ref[0], lanes[:shard_width], lanes[shard_width : 2 * shard_width]
    )
    gradient = jnp.transpose(turned[...])[:count, :shard_width]
    values = adamw(*[ref[...] for ref in inputs[6:]], gradient, 0.1, 0.0)
    for out, value in zip(outs[6:], values):
        out[...] = value


def on_device(
    tokens,
    cotangent,
    lengths,
    w_qkv,
    m_qkv,
    v_qkv,
    w_out,
    m_out,
    v_out,
    w_in,
    m_in,
    v_in,
    w_back,
    m_back,
    v_back,
    vectors,
    m_vectors,
    v_vectors,
):
    own_rows, width = tokens.shape
    tensor_rank = lax.axis_index("tensor")
    group_rows = 2 * own_rows
    shard_rows = w_qkv.shape[1]
    part = w_qkv.shape[2]
    hidden_half = w_in.shape[1]
    full_inner = 2 * hidden_half
    half = width // 2
    count = vectors.shape[0]
    shard_width = vectors.shape[1]

    a_width = 2 * part + LANES
    rank = tensor_rank.astype(jnp.int32).reshape(1)
    scalar = pl.BlockSpec(memory_space=pltpu.SMEM)
    vmem = pl.BlockSpec(memory_space=pltpu.VMEM)
    shard_one = run(
        pack_kernel,
        [shape_of(shard_rows, a_width + 2 * part, LOW)],
        [rank, w_qkv, w_out.T, vectors],
        0,
        in_specs=[scalar] + [vmem] * 3,
        scratch=[pltpu.VMEM((LANES, LANES), F32)],
    )[0]

    tokens_far = swap_tensor(tokens)
    one_high = gather_high(shard_one)
    one = join_high(one_high, a_width)
    one_far = swap_tensor(one[0]), swap_dp(one[1], 2)
    shard_pair = run(
        cast_kernel,
        [shape_of(shard_rows, full_inner, LOW)],
        [w_in, w_back.T],
        0,
        after=one[:1],
    )[0]
    pair_high = gather_high(shard_pair)

    order = relative_order(width)
    permute = (jnp.arange(width, dtype=jnp.int32)[:, None] == order[None, :]).astype(LOW)
    rows_all = jnp.concatenate([dot(tokens, permute), dot(tokens_far, permute)]).astype(LOW)
    cot = dot(cotangent, permute)

    one = join_plane(*one, *one_far, after=[rows_all])
    one_far = swap_dp(one[0], 2), swap_tensor(one[1])
    unit = 2 * own_rows * width * width
    pair = join_high(pair_high, hidden_half, 400 * unit)
    one = join_plane(one[1], one[0], one_far[1], one_far[0], after=pair[:1])[::-1]
    a_own, b_own = one
    a_far, b_far = swap_dp(a_own, 1), swap_dp(b_own, 1)
    pair_far = swap_tensor(pair[0]), swap_dp(pair[1], 2)

    vec, bias_query, bias_value, bias_inner = run(
        vectors_kernel,
        [
            shape_of(6, width, F32),
            shape_of(1, width, F32),
            shape_of(1, width, F32),
            shape_of(1, full_inner, F32),
        ],
        [rank, permute, a_own, a_far],
        1,
        in_specs=[scalar, vmem, vmem, vmem],
    )

    wide_low = shape_of(own_rows, width, LOW)
    wide = shape_of(own_rows, width, F32)
    group_low = shape_of(group_rows, width, LOW)
    sums_shape = shape_of(8, width, F32)
    queries, key_rows, value_rows = run(
        project_kernel,
        [wide_low, group_low, group_low],
        [rows_all, a_own, a_far, b_own, b_far, bias_query, bias_value],
        5 * unit,
    )
    pair = join_plane(*pair, *pair_far, after=[queries])
    in_near, in_side = pair[0], swap_dp(pair[0], 2)
    back_near, back_side = pair[1], swap_tensor(pair[1])
    in_far, back_far = swap_dp(in_near, 1), swap_dp(back_near, 1)
    pairs = width // LANES
    own_block = pl.BlockSpec((own_rows, LANES), lambda i: (0, i))
    all_block = pl.BlockSpec((group_rows, LANES), lambda i: (0, i))

    attended = run(
        attend_kernel,
        [wide_low],
        [rank, lengths, queries, key_rows, value_rows],
        3 * unit,
        after=pair[:1],
        grid=(pairs,),
        in_specs=[scalar, scalar, own_block, all_block, all_block],
        out_specs=[own_block],
    )[0]
    first_norm, first_low, normed_one, inv_one = run(
        out_norm_kernel,
        [wide, wide_low, wide, shape_of(own_rows, 1, F32)],
        [attended, rows_all, b_own, b_far, vec],
        2 * unit,
        after=[in_far, back_far],
    )
    in_side, back_side = gate([in_side, back_side], [first_low])
    pieces_in = [in_near, in_side, in_far, swap_dp(in_side, 1)]
    pieces_back = [back_near, back_side, back_far, swap_dp(back_side, 1)]
    activation, slope = run(
        hidden_kernel,
        [shape_of(own_rows, full_inner, LOW), shape_of(own_rows, full_inner, F32)],
        [first_low, *pieces_in, bias_inner],
        8 * unit,
    )
    mixed_rel, grad_two, grad_two_low, sums_two = run(
        out_back_kernel,
        [wide_low, wide, wide_low, sums_shape],
        [rank, lengths, activation, *pieces_back, first_norm, cot, vec],
        5 * unit,
        in_specs=[scalar, scalar] + [vmem] * 8,
    )
    mixed = dot_nt(mixed_rel, permute).astype(LOW)

    def gradient(left, right):
        return dot_tn(left, right).astype(LOW)

    back_parts = []
    for columns in (activation[:, hidden_half:], activation[:, :hidden_half]):
        sent = swap_dp(gradient(grad_two_low[:, half:], columns), 1)
        back_parts.append((gradient(grad_two_low[:, :half], columns), sent))
    grad_pre, sums_inner = run(
        hidden_back_kernel,
        [shape_of(own_rows, full_inner, LOW), shape_of(1, full_inner, F32)],
        [grad_two_low, *pieces_back, slope],
        6 * unit,
    )
    quarter = half // 2
    in_parts = []
    for start in (quarter, 0):
        rows = slice(half + start, half + start + quarter)
        sent = swap_dp(gradient(first_low[:, rows], grad_pre), 1)
        in_parts.append((gradient(first_low[:, start : start + quarter], grad_pre), sent))
    b_send = add_parts(*back_parts[0], 400 * unit, after=[grad_pre])
    a_send = add_parts(*in_parts[0], after=[b_send])
    a_far_sum, b_far_sum = swap_dp(a_send, 2), swap_tensor(b_send)
    grad_one, grad_one_low, grad_attn, sums_one = run(
        norm_back_kernel,
        [wide, wide_low, wide_low, sums_shape],
        [grad_pre, *pieces_in, grad_two, normed_one, inv_one, vec, b_own, b_far],
        6 * unit,
        after=[a_send],
    )
    b_keep = add_parts(*back_parts[1], after=[grad_one_low])
    a_keep = add_parts(*in_parts[1], after=[b_keep])
    pair = a_keep, a_far_sum, b_keep, b_far_sum
    grad_q, grad_k, grad_v = run(
        attend_back_kernel,
        [wide_low, group_low, group_low],
        [rank, lengths, queries, key_rows, value_rows, grad_attn],
        5 * unit,
        grid=(pairs,),
        in_specs=[scalar, scalar, own_block, all_block, all_block, own_block],
        out_specs=[own_block, all_block, all_block],
    )
    a_shape, b_shape = shape_of(half, 2 * a_width, LOW), shape_of(half, 4 * part, LOW)
    a_send, b_send, one_a, one_b = run(
        functools.partial(first_grads_kernel, a_width),
        [a_shape, b_shape, a_shape, b_shape],
        [rank, permute, rows_all, grad_q, grad_k, grad_v, grad_one_low, attended]
        + [sums_one, sums_two, sums_inner],
        6 * unit,
        in_specs=[scalar] + [vmem] * 10,
        scratch=[pltpu.VMEM((16, width), F32), pltpu.VMEM((LANES, width), F32)],
    )
    one = one_a, swap_dp(a_send, 1), one_b, swap_dp(b_send, 1)
    a_keep, a_send, b_keep, b_send = split_plane(*pair, after=[one_a, mixed])
    pair = a_keep, swap_tensor(a_send), b_keep, swap_dp(b_send, 2)
    grad_own, grad_away = run(
        rows_back_kernel,
        [wide, wide_low],
        [grad_q, grad_k, grad_v, a_own, a_far, b_own, b_far, grad_one],
        400 * unit,
        after=[a_keep],
    )
    a_keep, a_send, b_keep, b_send = split_core(*one, after=[grad_own])
    one = a_keep, swap_dp(a_send, 2), b_keep, swap_tensor(b_send)
    pair = send_high(split_high(*pair, after=[a_keep]))
    a_keep, a_send, b_keep, b_send = split_plane(*one, after=pair[:1])
    one = a_keep, swap_tensor(a_send), b_keep, swap_dp(b_send, 2)
    pair = sum_parts(pair, 400 * unit, after=[a_keep])
    one = send_high(split_high(*one, after=pair))
    input_grad = run(
        rows_out_kernel,
        [wide],
        [grad_own, swap_tensor(gate([grad_away], pair)[0]), permute],
        3 * unit,
        after=one[:1],
    )[0]
    sum_pair = reduce_rest(gate(pair, one[:1])[0])
    summed_in, summed_back = sum_pair[:, :hidden_half], sum_pair[:, hidden_half:].T
    if len(high_groups()) > 1:
        one = [reduce_rest(sum(piece.astype(F32) for piece in one))]
    qkv_shape = jax.ShapeDtypeStruct(w_qkv.shape, F32)
    out_shape = shape_of(shard_rows, part, F32)
    vec_shape = shape_of(count, shard_width, F32)
    done = run(
        functools.partial(
            close_kernel,
            (float(width) ** (-0.5), (4.0 * width / group_rows) ** (-0.5)),
        ),
        [qkv_shape] * 3 + [out_shape] * 3 + [vec_shape] * 3,
        [rank, w_qkv, m_qkv, v_qkv, w_out.T, m_out.T, v_out.T]
        + [vectors, m_vectors, v_vectors, *one],
        unit,
        after=[input_grad],
        in_specs=[scalar] + [vmem] * (9 + len(one)),
        scratch=[pltpu.VMEM((LANES, LANES), F32)],
    )
    new_qkv, moment_qkv, square_qkv = done[:3]
    new_out, moment_out, square_out = [value.T for value in done[3:6]]
    new_vectors, moment_vectors, square_vectors = done[6:]
    new_in, moment_in, square_in = adamw(
        w_in, m_in, v_in, summed_in, float(width) ** (-0.5), WEIGHT_DECAY
    )
    new_back, moment_back, square_back = adamw(
        w_back, m_back, v_back, summed_back, float(full_inner) ** (-0.5), WEIGHT_DECAY
    )
    return (
        mixed,
        input_grad,
        new_qkv,
        moment_qkv,
        square_qkv,
        new_out,
        moment_out,
        square_out,
        new_in,
        moment_in,
        square_in,
        new_back,
        moment_back,
        square_back,
        new_vectors,
        moment_vectors,
        square_vectors,
    )


def solution(mesh):
    placed = (
        P(("dp", "tensor"), None),
        P(("dp", "tensor"), None),
        P("dp", None),
        P(None, "dp", "tensor"),
        P(None, "dp", "tensor"),
        P(None, "dp", "tensor"),
        P("tensor", "dp"),
        P("tensor", "dp"),
        P("tensor", "dp"),
        P("dp", "tensor"),
        P("dp", "tensor"),
        P("dp", "tensor"),
        P("tensor", "dp"),
        P("tensor", "dp"),
        P("tensor", "dp"),
        P(None, ("dp", "tensor")),
        P(None, ("dp", "tensor")),
        P(None, ("dp", "tensor")),
    )
    return jax.shard_map(
        on_device,
        mesh=mesh,
        in_specs=placed,
        out_specs=(
            P(("dp", "tensor"), None),
            P(("dp", "tensor"), None),
            P(None, "dp", "tensor"),
            P(None, "dp", "tensor"),
            P(None, "dp", "tensor"),
            P("tensor", "dp"),
            P("tensor", "dp"),
            P("tensor", "dp"),
            P("dp", "tensor"),
            P("dp", "tensor"),
            P("dp", "tensor"),
            P("tensor", "dp"),
            P("tensor", "dp"),
            P("tensor", "dp"),
            P(None, ("dp", "tensor")),
            P(None, ("dp", "tensor")),
            P(None, ("dp", "tensor")),
        ),
        check_vma=False,
    )
```
